32 devices in a mesh: seq: 8 (over z, x), kv: 4 (over y, core).
Axes of the slice: x: 2, y: 2, z: 4, core: 2. Of those that a mesh axis runs over, the one named last changes fastest.
Arguments:
- inputs: bfloat16 [4, 1024, 2048], P(None, 'seq'), may hold values from -6 to 6
- cotangent: bfloat16 [4, 1024, 2048], P(None, 'seq'), may hold values from -6 to 6
- bucket_sizes: int32 [4, 4], replicated, may hold values from 32 to 928, as said below
- true_lengths: int32 [4, 4], replicated, may hold values from 1 to 928, as said below
- attention_gain: bfloat16 [2048], P('seq'), may hold values from 0.099609375 to 1.8984375
- feedforward_gain: bfloat16 [2048], P('seq'), may hold values from 0.099609375 to 1.8984375
- query_gain: bfloat16 [128], replicated, may hold values from 0.099609375 to 1.8984375
- key_gain: bfloat16 [128], replicated, may hold values from 0.099609375 to 1.8984375
- query_weight: bfloat16 [2048, 2048], P('seq', 'kv'), may hold values from -0.125 to 0.125
- key_matrix: bfloat16 [2048, 1024], P('seq', 'kv'), may hold values from -0.125 to 0.125
- value_matrix: bfloat16 [2048, 1024], P('seq', 'kv'), may hold values from -0.125 to 0.125
- headgate_weight: bfloat16 [2048, 16], P('seq', 'kv'), may hold values from -0.125 to 0.125
- output_weight: bfloat16 [2048, 2048], P('kv', 'seq'), may hold values from -1 to 1
- gate_weight: bfloat16 [2048, 6144], P('seq', 'kv'), may hold values from -0.125 to 0.125
- up_weight: bfloat16 [2048, 6144], P('seq', 'kv'), may hold values from -0.125 to 0.125
- down_weight: bfloat16 [6144, 2048], P('kv', 'seq'), may hold values from -0.078125 to 0.078125
Outputs:
- block_output: bfloat16 [4, 1024, 2048], P(None, 'seq')
- input_grad: bfloat16 [4, 1024, 2048], P(None, 'seq')
- attention_gain_grad: float32 [2048], P('seq')
- feedforward_gain_grad: float32 [2048], P('seq')
- query_gain_grad: float32 [128], replicated
- key_gain_grad: float32 [128], replicated
- query_weight_grad: float32 [2048, 2048], P('seq', 'kv')
- key_weight_grad: float32 [2048, 1024], P('seq', 'kv')
- value_weight_grad: float32 [2048, 1024], P('seq', 'kv')
- headgate_weight_grad: float32 [2048, 16], P('seq', 'kv')
- output_weight_grad: float32 [2048, 2048], P('kv', 'seq')
- gate_weight_grad: float32 [2048, 6144], P('seq', 'kv')
- up_weight_grad: float32 [2048, 6144], P('seq', 'kv')
- down_weight_grad: float32 [6144, 2048], P('kv', 'seq')
The draws below stay inside these ranges and needn't reach their ends.
Inputs may be any that keep to these rules, and one draw needn't show every extreme that they name: `bucket_sizes`: each micro-batch's 4 buckets are positive multiples of 32 tokens laid end to end that fill its 1024 tokens; the second bucket starts among the first 128 tokens and ends among the last 128. `true_lengths`: each true length is at least its bucket's size minus 128 / 4 plus 1, and at most the bucket's size.
All inputs are finite; a program needn't handle non-finite values.
Results may differ from the reference program's by a relative error of at most 0.024.
Values may be sent and summed in bfloat16 or wider, within the bound.
A program may use at most 256 MiB of HBM per device.

```python
import math
import jax
import jax.numpy as jnp
from jax import lax

MODEL_WIDTH = 2048
QUERY_HEADS = 16
KEY_VALUE_HEADS = 8
HEAD_SIZE = 128
FF = 6144
TOK_DEV = 128
MB = 4
NSEG = 4
TOKENS = 1024


def widest_batch(key):
    return jax.random.randint(jax.random.fold_in(key, 13), (), 0, MB)


def bucket_layout(key):
    quantum = TOK_DEV // 4
    chosen = jnp.arange(MB) == widest_batch(key)
    head = jax.random.randint(jax.random.fold_in(key, 11), (MB,), 1, 4)
    tail = jax.random.randint(jax.random.fold_in(key, 12), (MB,), 2, 4)
    head = jnp.where(chosen, 1, head)
    tail = jnp.where(chosen, 2, tail)
    middle = TOKENS // quantum - head - tail
    single = jnp.ones((MB,), jnp.int32)
    return (jnp.stack([head, middle, single, tail - 1], axis=1) * quantum).astype(jnp.int32)


def draw_bucket_sizes(key, part):
    sizes = bucket_layout(key)
    return sizes


def draw_true_lengths(key, part):
    sizes = bucket_layout(key)
    chosen = (jnp.arange(MB) == widest_batch(key))[:, None]
    column = jnp.arange(NSEG)[None, :]
    key = jax.random.fold_in(key, 5)
    padding = jax.random.randint(key, sizes.shape, 0, TOK_DEV // 4)
    padding = jnp.where(chosen & (column == 1), 0, padding)
    padding = jnp.where(chosen & (column == 2), TOK_DEV // 4 - 1, padding)
    return (sizes - padding).astype(jnp.int32)


def block_scale(key, dims, shards, smallest, largest):
    def one(dim, blocks):
        steps = jax.random.uniform(jax.random.fold_in(jax.random.fold_in(key, 6), dim), (blocks,), jnp.float32, smallest / len(shards), largest / len(shards))
        return jnp.repeat(jnp.exp(steps), dims[dim] // blocks).reshape((-1,) + (1,) * (len(dims) - dim - 1))

    factor_of = one(*shards[0])
    for cut in shards[1:]:
        factor_of = factor_of * one(*cut)
    return factor_of


def normal_values(own_key, dims, scale, bound, split=(), kind=jnp.bfloat16):
    entries = scale * jax.random.normal(own_key, dims, jnp.float32)
    if split:
        entries = entries * block_scale(own_key, dims, split, -0.22, 0.18)
    return jnp.clip(entries, -bound, bound).astype(kind)


def setup_inputs(seed: int = 0) -> dict:
    splits = jax.random.split(jax.random.key(seed), 17)
    inputs = normal_values(splits[0], (MB, TOKENS, MODEL_WIDTH), 1.0, 6.0, ((1, 8),))
    cotangent = normal_values(splits[1], (MB, TOKENS, MODEL_WIDTH), 1.0, 6.0, ((1, 8),))
    bucket_sizes = draw_bucket_sizes(jax.random.fold_in(splits[16], 71), 0)
    true_lengths = draw_true_lengths(jax.random.fold_in(splits[16], 71), 0)
    attention_gain = jnp.clip(1.0 + 0.18 * jax.random.normal(splits[4], (MODEL_WIDTH,), jnp.float32), 0.099609375, 1.8984375).astype(jnp.bfloat16)
    feedforward_gain = jnp.clip(1.0 + 0.18 * jax.random.normal(splits[5], (MODEL_WIDTH,), jnp.float32), 0.099609375, 1.8984375).astype(jnp.bfloat16)
    query_gain = jnp.clip(1.0 + 0.18 * jax.random.normal(splits[6], (HEAD_SIZE,), jnp.float32), 0.099609375, 1.8984375).astype(jnp.bfloat16)
    key_gain = jnp.clip(1.0 + 0.18 * jax.random.normal(splits[7], (HEAD_SIZE,), jnp.float32), 0.099609375, 1.8984375).astype(jnp.bfloat16)
    query_weight = normal_values(splits[8], (MODEL_WIDTH, QUERY_HEADS * HEAD_SIZE), MODEL_WIDTH ** -0.5, 0.125, ((0, 8), (1, 4)))
    key_matrix = normal_values(splits[9], (MODEL_WIDTH, KEY_VALUE_HEADS * HEAD_SIZE), MODEL_WIDTH ** -0.5, 0.125, ((0, 8), (1, 4)))
    value_matrix = normal_values(splits[10], (MODEL_WIDTH, KEY_VALUE_HEADS * HEAD_SIZE), MODEL_WIDTH ** -0.5, 0.125, ((0, 8), (1, 4)))
    headgate_weight = normal_values(splits[11], (MODEL_WIDTH, QUERY_HEADS), MODEL_WIDTH ** -0.5, 0.125, ((0, 8), (1, 4)))
    output_weight = normal_values(splits[12], (QUERY_HEADS * HEAD_SIZE, MODEL_WIDTH), (QUERY_HEADS * HEAD_SIZE // 64) ** -0.5, 1.0, ((0, 4), (1, 8)))
    gate_weight = normal_values(splits[13], (MODEL_WIDTH, FF), MODEL_WIDTH ** -0.5, 0.125, ((0, 8), (1, 4)))
    up_weight = normal_values(splits[14], (MODEL_WIDTH, FF), MODEL_WIDTH ** -0.5, 0.125, ((0, 8), (1, 4)))
    down_weight = normal_values(splits[15], (FF, MODEL_WIDTH), FF ** -0.5, 0.078125, ((0, 4), (1, 8)))
    return {"inputs": inputs, "cotangent": cotangent, "bucket_sizes": bucket_sizes, "true_lengths": true_lengths, "attention_gain": attention_gain, "feedforward_gain": feedforward_gain, "query_gain": query_gain, "key_gain": key_gain, "query_weight": query_weight, "key_matrix": key_matrix, "value_matrix": value_matrix, "headgate_weight": headgate_weight, "output_weight": output_weight, "gate_weight": gate_weight, "up_weight": up_weight, "down_weight": down_weight}


EPS = 1e-06
ROPE_BASE = 1000000.0
MASKED = -1e+30

@jax.custom_vjp
def low(v):
    return lax.optimization_barrier(v.astype(jnp.bfloat16)).astype(jnp.float32)

@jax.custom_vjp
def reduced_backward(v):
    return v

def low_keep(v):
    return (low(v), None)

def low_pass(kept, grad):
    return (grad,)

def back_keep(v):
    return (v, None)

def back_low(kept, grad):
    return (low(grad),)
low.defvjp(low_keep, low_pass)
reduced_backward.defvjp(back_keep, back_low)

def rms_scale(values):
    return lax.rsqrt(lax.optimization_barrier(jnp.mean(values * values, axis=-1, keepdims=True)) + EPS)

def rope_tables(positions, width):
    half = width // 2
    steps = jnp.arange(half, dtype=jnp.float32) * (2.0 / width)
    inverse = jnp.exp(-steps * math.log(ROPE_BASE))
    angles = positions.astype(jnp.float32)[:, None] * inverse[None, :]
    cosine = jnp.cos(angles)
    sine = jnp.sin(angles)
    return (jnp.concatenate([cosine, cosine], axis=-1), jnp.concatenate([sine, sine], axis=-1))

def rotate_forward(values, cosine, sine):
    half = values.shape[-1] // 2
    turned = jnp.concatenate([-values[..., half:], values[..., :half]], axis=-1)
    return values * cosine[:, None, :] + turned * sine[:, None, :]

def token_layout(index, buckets, lengths):
    ends = jnp.cumsum(buckets).astype(jnp.int32)
    starts = (ends - buckets).astype(jnp.int32)
    member = (index[:, None] >= starts[None, :]) & (index[:, None] < ends[None, :])
    labels = jnp.arange(buckets.shape[0], dtype=jnp.int32)
    segment = lax.optimization_barrier(jnp.sum(jnp.where(member, labels[None, :], 0), axis=1)).astype(jnp.int32)
    position = (index - lax.optimization_barrier(jnp.sum(jnp.where(member, starts[None, :], 0), axis=1))).astype(jnp.int32)
    limit = lax.optimization_barrier(jnp.sum(jnp.where(member, lengths[None, :], 0), axis=1)).astype(jnp.int32)
    return (segment, position, position < limit)

def attention(query, key, value_rows, segment, valid):
    item_count = query.shape[0]
    block = math.gcd(item_count, 512)
    head_groups = QUERY_HEADS // KEY_VALUE_HEADS
    keys = jnp.repeat(key, head_groups, axis=1)
    values = jnp.repeat(value_rows, head_groups, axis=1)
    scale = HEAD_SIZE ** (-0.5)
    highest_precision = lax.Precision.HIGHEST
    key_index = jnp.arange(item_count, dtype=jnp.int32)

    def one_block(start):
        rows = lax.dynamic_slice_in_dim(query, start, block, 0)
        row_segment = lax.dynamic_slice_in_dim(segment, start, block, 0)
        row_index = start + jnp.arange(block, dtype=jnp.int32)
        scores = reduced_backward(jnp.einsum('qhd,shd->hqs', rows, keys, precision=highest_precision) * scale)
        allowed = (row_segment[:, None] == segment[None, :]) & (key_index[None, :] <= row_index[:, None]) & valid[None, :]
        masked = jnp.where(allowed[None], scores, MASKED)
        total = jax.nn.logsumexp(masked, axis=-1, keepdims=True)
        weights = jnp.where(allowed[None], jnp.exp(masked - total), 0.0)
        return jnp.einsum('hqs,shd->qhd', low(weights), values, precision=highest_precision)
    starts = (jnp.arange(item_count // block) * block).astype(jnp.int32)
    result = lax.map(jax.checkpoint(one_block), starts)
    return result.reshape(item_count, QUERY_HEADS, HEAD_SIZE)

def block_forward(values, buckets, lengths, params):
    att_gain, ffn_gain, q_gain, k_gain, w_query, key_projection_weight, value_projection_weight, w_head, w_output, w_gate, w_up, w_down = params
    highest_precision = lax.Precision.HIGHEST
    item_count = values.shape[0]
    index = jnp.arange(item_count, dtype=jnp.int32)
    segment, position, valid = token_layout(index, buckets, lengths)
    cosine, sine = rope_tables(position, HEAD_SIZE)
    normed_input = low(values * rms_scale(values) * att_gain)
    query = reduced_backward(jnp.dot(normed_input, w_query, precision=highest_precision)).reshape(item_count, QUERY_HEADS, HEAD_SIZE)
    key = reduced_backward(jnp.dot(normed_input, key_projection_weight, precision=highest_precision)).reshape(item_count, KEY_VALUE_HEADS, HEAD_SIZE)
    value_rows = reduced_backward(jnp.dot(normed_input, value_projection_weight, precision=highest_precision)).reshape(item_count, KEY_VALUE_HEADS, HEAD_SIZE)
    query = low(rotate_forward(query * rms_scale(query) * q_gain, cosine, sine))
    key = low(rotate_forward(key * rms_scale(key) * k_gain, cosine, sine))
    value_rows = low(value_rows)
    logits = reduced_backward(jnp.dot(normed_input, w_head, precision=highest_precision))
    gate = jax.nn.sigmoid(logits)
    attended = reduced_backward(attention(query, key, value_rows, segment, valid))
    mixed = low((attended * gate[:, :, None]).reshape(item_count, QUERY_HEADS * HEAD_SIZE))
    hidden = values + reduced_backward(jnp.dot(mixed, w_output, precision=highest_precision))
    inner = low(hidden * rms_scale(hidden) * ffn_gain)
    gated = reduced_backward(jnp.dot(inner, w_gate, precision=highest_precision))
    upward = reduced_backward(jnp.dot(inner, w_up, precision=highest_precision))
    product = low(jax.nn.silu(gated) * upward)
    return hidden + reduced_backward(jnp.dot(product, w_down, precision=highest_precision))

def reference(inputs, cotangent, bucket_sizes, true_lengths, attention_gain, feedforward_gain, query_gain, key_gain, query_weight, key_matrix, value_matrix, headgate_weight, output_weight, gate_weight, up_weight, down_weight):
    weights = tuple((item.astype(jnp.float32) for item in (attention_gain, feedforward_gain, query_gain, key_gain, query_weight, key_matrix, value_matrix, headgate_weight, output_weight, gate_weight, up_weight, down_weight)))

    def forward(values, params):

        def one_batch(item):
            rows, buckets, lengths = item
            return block_forward(rows, buckets, lengths, params)
        return lax.map(jax.checkpoint(one_batch), (values, bucket_sizes, true_lengths))
    outputs, pullback = jax.vjp(forward, inputs.astype(jnp.float32), weights)
    input_grad, grads = pullback(cotangent.astype(jnp.float32))
    return (outputs.astype(jnp.bfloat16), input_grad.astype(jnp.bfloat16), grads[0], grads[1], grads[2], grads[3], grads[4], grads[5], grads[6], grads[7], grads[8], grads[9], grads[10], grads[11])
```

```python
import functools
import math

import jax
import jax.numpy as jnp
from jax import lax
from jax.experimental import pallas as pl
from jax.experimental.pallas import tpu as pltpu
from jax.sharding import PartitionSpec as P

HEAD_SIZE = 128


EPS = 1e-06
ROPE_BASE = 1000000.0
MASKED = -1e30


def rms_scale(values):
    return lax.rsqrt(jnp.mean(values * values, axis=-1, keepdims=True) + EPS)


def norm_backward(grad, normal, factor):
    return factor * (grad - normal * jnp.mean(grad * normal, axis=-1, keepdims=True))


def rope_tables(positions, width):
    half = width // 2
    steps = jnp.arange(half, dtype=jnp.float32) * (2.0 / width)
    inverse = jnp.exp(-steps * math.log(ROPE_BASE))
    angles = positions.astype(jnp.float32)[:, None] * inverse[None, :]
    cosine = jnp.cos(angles)
    sine = jnp.sin(angles)
    return (jnp.concatenate([cosine, cosine], axis=-1), jnp.concatenate([sine, sine], axis=-1))


def rotate_forward(values, cosine, sine):
    half = values.shape[-1] // 2
    turned = jnp.concatenate([-values[..., half:], values[..., :half]], axis=-1)
    return values * cosine[:, None, :] + turned * sine[:, None, :]


def rotate_backward(grad, cosine, sine):
    half = grad.shape[-1] // 2
    moved = grad * sine[:, None, :]
    return grad * cosine[:, None, :] + jnp.concatenate(
        [moved[..., half:], -moved[..., :half]], axis=-1
    )


def token_layout(index, buckets, lengths):
    ends = jnp.cumsum(buckets)
    starts = ends - buckets
    member = (index[:, None] >= starts[None, :]) & (index[:, None] < ends[None, :])
    labels = jnp.arange(buckets.shape[0], dtype=jnp.int32)
    segment = jnp.sum(jnp.where(member, labels[None, :], 0), axis=1)
    position = index - jnp.sum(jnp.where(member, starts[None, :], 0), axis=1)
    limit = jnp.sum(jnp.where(member, lengths[None, :], 0), axis=1)
    return (segment, position, position < limit)


def outer_sum(left, right):
    return lax.dot_general(
        left, right, (((0,), (0,)), ((), ())), preferred_element_type=jnp.float32
    )


def times_transpose(left, weight):
    return lax.dot_general(
        left, weight, (((1,), (1,)), ((), ())), preferred_element_type=jnp.float32
    )


def block_scores(query_kg, key_block, start, row_index, row_segment, buckets, lengths, scale):
    key_index = start + jnp.arange(key_block.shape[0], dtype=jnp.int32)
    key_segment, key_position, key_valid = token_layout(key_index, buckets, lengths)
    allowed = (
        (row_segment[:, None] == key_segment[None, :])
        & (key_index[None, :] <= row_index[:, None])
        & key_valid[None, :]
    )
    raw = (
        jnp.einsum("kgtd,skd->kgts", query_kg, key_block, preferred_element_type=jnp.float32)
        * scale
    )
    return (jnp.where(allowed, raw, MASKED), allowed)


def split_blocks(keys, values, block):
    blocks = keys.shape[0] // block
    key_blocks = keys.reshape(blocks, block, keys.shape[1], keys.shape[2])
    value_blocks = values.reshape(blocks, block, values.shape[1], values.shape[2])
    starts = jnp.arange(blocks) * block
    return (key_blocks, value_blocks, starts)


def attention_forward(
    query_kg, keys, values, row_index, row_segment, buckets, lengths, block, scale
):
    key_blocks, value_blocks, starts = split_blocks(keys, values, block)

    def first_pass(carry, item):
        running_max, total = carry
        key_block, start = item
        masked, allowed = block_scores(
            query_kg, key_block, start, row_index, row_segment, buckets, lengths, scale
        )
        new_max = jnp.maximum(running_max, jnp.max(masked, axis=-1))
        total = total * jnp.exp(running_max - new_max) + jnp.sum(
            jnp.where(allowed, jnp.exp(masked - new_max[..., None]), 0.0), axis=-1
        )
        return ((new_max, total), None)

    begin = (
        jnp.full(query_kg.shape[:3], MASKED, jnp.float32),
        jnp.zeros(query_kg.shape[:3], jnp.float32),
    )
    (running_max, total), unused = lax.scan(first_pass, begin, (key_blocks, starts))
    log_total = running_max + jnp.log(total)

    def second_pass(accumulated, item):
        key_block, value_block, start = item
        masked, allowed = block_scores(
            query_kg, key_block, start, row_index, row_segment, buckets, lengths, scale
        )
        weights = jnp.where(allowed, jnp.exp(masked - log_total[..., None]), 0.0).astype(
            jnp.bfloat16
        )
        return (
            accumulated
            + jnp.einsum(
                "kgts,skd->kgtd", weights, value_block, preferred_element_type=jnp.float32
            ),
            None,
        )

    attended, unused = lax.scan(
        second_pass, jnp.zeros(query_kg.shape, jnp.float32), (key_blocks, value_blocks, starts)
    )
    return (attended, log_total)


def attention_backward(
    query_kg,
    grad_kg,
    log_total,
    delta,
    keys,
    values,
    row_index,
    row_segment,
    buckets,
    lengths,
    block,
    scale,
):
    key_blocks, value_blocks, starts = split_blocks(keys, values, block)

    def step(grad_query, item):
        key_block, value_block, start = item
        masked, allowed = block_scores(
            query_kg, key_block, start, row_index, row_segment, buckets, lengths, scale
        )
        weights = jnp.where(allowed, jnp.exp(masked - log_total[..., None]), 0.0)
        grad_weights = jnp.einsum(
            "kgtd,skd->kgts", grad_kg, value_block, preferred_element_type=jnp.float32
        )
        grad_scores = (weights * (grad_weights - delta[..., None])).astype(jnp.bfloat16)
        grad_query = grad_query + scale * jnp.einsum(
            "kgts,skd->kgtd", grad_scores, key_block, preferred_element_type=jnp.float32
        )
        grad_key = scale * jnp.einsum(
            "kgts,kgtd->skd", grad_scores, query_kg, preferred_element_type=jnp.float32
        )
        grad_value = jnp.einsum(
            "kgts,kgtd->skd",
            weights.astype(jnp.bfloat16),
            grad_kg,
            preferred_element_type=jnp.float32,
        )
        return (grad_query, (grad_key, grad_value))

    grad_query, (grad_keys, grad_values) = lax.scan(
        step, jnp.zeros(query_kg.shape, jnp.float32), (key_blocks, value_blocks, starts)
    )
    return (grad_query, grad_keys.reshape(keys.shape), grad_values.reshape(values.shape))


def local(
    inputs,
    cotangent,
    bucket_sizes,
    true_lengths,
    attention_gain,
    feedforward_gain,
    query_gain,
    key_gain,
    query_weight,
    key_matrix,
    value_matrix,
    headgate_weight,
    output_weight,
    gate_weight,
    up_weight,
    down_weight,
):
    batches, rows, width = inputs.shape
    seq_count = lax.axis_size("seq")
    block = math.gcd(rows * seq_count, 512)
    local_heads = query_weight.shape[1] // HEAD_SIZE
    local_groups = key_matrix.shape[1] // HEAD_SIZE
    group = local_heads // local_groups
    scale = HEAD_SIZE ** (-0.5)
    row_index = lax.axis_index("seq") * rows + jnp.arange(rows, dtype=jnp.int32)
    gain_query = query_gain.astype(jnp.float32)
    gain_key = key_gain.astype(jnp.float32)
    sum_attention_gain = jnp.zeros((width,), jnp.float32)
    sum_feedforward_gain = jnp.zeros((width,), jnp.float32)
    sum_query = jnp.zeros((width, query_weight.shape[1]), jnp.float32)
    sum_key = jnp.zeros((width, key_matrix.shape[1]), jnp.float32)
    sum_value = jnp.zeros((width, value_matrix.shape[1]), jnp.float32)
    sum_headgate = jnp.zeros((width, headgate_weight.shape[1]), jnp.float32)
    sum_output = jnp.zeros((output_weight.shape[0], width), jnp.float32)
    sum_gate = jnp.zeros((width, gate_weight.shape[1]), jnp.float32)
    sum_upward = jnp.zeros((width, up_weight.shape[1]), jnp.float32)
    sum_down = jnp.zeros((down_weight.shape[0], width), jnp.float32)
    sum_query_gain = jnp.zeros((HEAD_SIZE,), jnp.float32)
    sum_key_gain = jnp.zeros((HEAD_SIZE,), jnp.float32)
    results = []
    input_grads = []
    for batch in range(batches):
        gathered = (
            lax.all_gather(attention_gain, "seq", axis=0, tiled=True),
            lax.all_gather(feedforward_gain, "seq", axis=0, tiled=True),
            lax.all_gather(query_weight, "seq", axis=0, tiled=True),
            lax.all_gather(key_matrix, "seq", axis=0, tiled=True),
            lax.all_gather(value_matrix, "seq", axis=0, tiled=True),
            lax.all_gather(headgate_weight, "seq", axis=0, tiled=True),
            lax.all_gather(output_weight, "seq", axis=1, tiled=True),
            lax.all_gather(gate_weight, "seq", axis=0, tiled=True),
            lax.all_gather(up_weight, "seq", axis=0, tiled=True),
            lax.all_gather(down_weight, "seq", axis=1, tiled=True),
        )
        (
            gain_a,
            gain_f,
            w_query,
            key_projection_weight,
            value_projection_weight,
            w_head,
            w_output,
            w_gate,
            w_up,
            w_down,
        ) = gathered
        gain_a = gain_a.astype(jnp.float32)
        gain_f = gain_f.astype(jnp.float32)
        buckets = bucket_sizes[batch]
        lengths = true_lengths[batch]
        row_segment, row_position, row_valid = token_layout(row_index, buckets, lengths)
        cosine, sine = rope_tables(row_position, HEAD_SIZE)
        current = inputs[batch].astype(jnp.float32)
        scale_a = rms_scale(current)
        normal_a = current * scale_a
        normed_input = (normal_a * gain_a).astype(jnp.bfloat16)
        query_proj = jnp.dot(normed_input, w_query, preferred_element_type=jnp.float32).reshape(
            rows, local_heads, HEAD_SIZE
        )
        key_proj = jnp.dot(
            normed_input, key_projection_weight, preferred_element_type=jnp.float32
        ).reshape(rows, local_groups, HEAD_SIZE)
        value_proj = jnp.dot(
            normed_input, value_projection_weight, preferred_element_type=jnp.float32
        )
        query_scale = rms_scale(query_proj)
        query_normal = query_proj * query_scale
        key_scale = rms_scale(key_proj)
        key_normal = key_proj * key_scale
        query_rot = rotate_forward(query_normal * gain_query, cosine, sine).astype(jnp.bfloat16)
        key_rot = rotate_forward(key_normal * gain_key, cosine, sine).astype(jnp.bfloat16)
        value_low = value_proj.astype(jnp.bfloat16).reshape(rows, local_groups, HEAD_SIZE)
        logits = jnp.dot(normed_input, w_head, preferred_element_type=jnp.float32)
        gate = jax.nn.sigmoid(logits)
        all_keys, all_values = (
            lax.all_gather(key_rot, "seq", axis=0, tiled=True),
            lax.all_gather(value_low, "seq", axis=0, tiled=True),
        )
        query_kg = query_rot.reshape(rows, local_groups, group, HEAD_SIZE).transpose(1, 2, 0, 3)
        attended_kg, log_total = attention_forward(
            query_kg, all_keys, all_values, row_index, row_segment, buckets, lengths, block, scale
        )
        attended = attended_kg.transpose(2, 0, 1, 3).reshape(rows, local_heads, HEAD_SIZE)
        mixed = (
            (attended * gate[:, :, None])
            .astype(jnp.bfloat16)
            .reshape(rows, local_heads * HEAD_SIZE)
        )
        hidden = current + lax.psum(
            jnp.dot(mixed, w_output, preferred_element_type=jnp.float32).astype(jnp.bfloat16), "kv"
        ).astype(jnp.float32)
        scale_f = rms_scale(hidden)
        normal_f = hidden * scale_f
        inner = (normal_f * gain_f).astype(jnp.bfloat16)
        gated = jnp.dot(inner, w_gate, preferred_element_type=jnp.float32)
        upward = jnp.dot(inner, w_up, preferred_element_type=jnp.float32)
        sigma = jax.nn.sigmoid(gated)
        swish = gated * sigma
        product = (swish * upward).astype(jnp.bfloat16)
        output = hidden + lax.psum(
            jnp.dot(product, w_down, preferred_element_type=jnp.float32).astype(jnp.bfloat16), "kv"
        ).astype(jnp.float32)
        results.append(output.astype(jnp.bfloat16))
        grad_out = cotangent[batch].astype(jnp.float32)
        grad_low = grad_out.astype(jnp.bfloat16)
        sum_down = sum_down + outer_sum(product, grad_low)
        grad_product = times_transpose(grad_low, w_down)
        grad_gated = (grad_product * upward * sigma * (1.0 + gated * (1.0 - sigma))).astype(
            jnp.bfloat16
        )
        grad_upward = (grad_product * swish).astype(jnp.bfloat16)
        sum_gate = sum_gate + outer_sum(inner, grad_gated)
        sum_upward = sum_upward + outer_sum(inner, grad_upward)
        grad_inner = lax.psum(
            (times_transpose(grad_gated, w_gate) + times_transpose(grad_upward, w_up)).astype(
                jnp.bfloat16
            ),
            "kv",
        ).astype(jnp.float32)
        sum_feedforward_gain = sum_feedforward_gain + jnp.sum(grad_inner * normal_f, axis=0)
        grad_hidden = grad_out + norm_backward(grad_inner * gain_f, normal_f, scale_f)
        grad_branch = grad_hidden.astype(jnp.bfloat16)
        sum_output = sum_output + outer_sum(mixed, grad_branch)
        grad_mixed = times_transpose(grad_branch, w_output).reshape(rows, local_heads, HEAD_SIZE)
        grad_heads = (grad_mixed * gate[:, :, None]).astype(jnp.bfloat16)
        grad_logits = (jnp.sum(grad_mixed * attended, axis=-1) * gate * (1.0 - gate)).astype(
            jnp.bfloat16
        )
        back_keys = lax.all_gather(key_rot, "seq", axis=0, tiled=True)
        back_values = lax.all_gather(value_low, "seq", axis=0, tiled=True)
        grad_kg = grad_heads.reshape(rows, local_groups, group, HEAD_SIZE).transpose(1, 2, 0, 3)
        delta = jnp.sum(grad_kg.astype(jnp.float32) * attended_kg, axis=-1)
        grad_query_kg, grad_keys, grad_values = attention_backward(
            query_kg,
            grad_kg,
            log_total,
            delta,
            back_keys,
            back_values,
            row_index,
            row_segment,
            buckets,
            lengths,
            block,
            scale,
        )
        local_keys, local_values = (
            lax.psum_scatter(
                grad_keys.astype(jnp.bfloat16), "seq", scatter_dimension=0, tiled=True
            ).astype(jnp.float32),
            lax.psum_scatter(
                grad_values.astype(jnp.bfloat16), "seq", scatter_dimension=0, tiled=True
            ).astype(jnp.float32),
        )
        grad_query_rot = grad_query_kg.transpose(2, 0, 1, 3).reshape(rows, local_heads, HEAD_SIZE)
        grad_query_norm = rotate_backward(grad_query_rot, cosine, sine)
        sum_query_gain = sum_query_gain + jnp.sum(grad_query_norm * query_normal, axis=(0, 1))
        grad_query = (
            norm_backward(grad_query_norm * gain_query, query_normal, query_scale)
            .astype(jnp.bfloat16)
            .reshape(rows, local_heads * HEAD_SIZE)
        )
        grad_key_norm = rotate_backward(local_keys, cosine, sine)
        sum_key_gain = sum_key_gain + jnp.sum(grad_key_norm * key_normal, axis=(0, 1))
        grad_key = (
            norm_backward(grad_key_norm * gain_key, key_normal, key_scale)
            .astype(jnp.bfloat16)
            .reshape(rows, local_groups * HEAD_SIZE)
        )
        grad_value = local_values.astype(jnp.bfloat16).reshape(rows, local_groups * HEAD_SIZE)
        sum_query = sum_query + outer_sum(normed_input, grad_query)
        sum_key = sum_key + outer_sum(normed_input, grad_key)
        sum_value = sum_value + outer_sum(normed_input, grad_value)
        sum_headgate = sum_headgate + outer_sum(normed_input, grad_logits)
        grad_partial = (
            times_transpose(grad_query, w_query)
            + times_transpose(grad_key, key_projection_weight)
            + times_transpose(grad_value, value_projection_weight)
            + times_transpose(grad_logits, w_head)
        )
        grad_normed = lax.psum(grad_partial.astype(jnp.bfloat16), "kv").astype(jnp.float32)
        sum_attention_gain = sum_attention_gain + jnp.sum(grad_normed * normal_a, axis=0)
        grad_input = grad_hidden + norm_backward(grad_normed * gain_a, normal_a, scale_a)
        input_grads.append(grad_input.astype(jnp.bfloat16))
    (
        attention_total,
        feedforward_total,
        query_total,
        key_total,
        value_total,
        headgate_total,
        output_total,
        gate_total,
        upward_total,
        down_total,
    ) = (
        lax.psum_scatter(
            sum_attention_gain.astype(jnp.bfloat16), "seq", scatter_dimension=0, tiled=True
        ).astype(jnp.float32),
        lax.psum_scatter(
            sum_feedforward_gain.astype(jnp.bfloat16), "seq", scatter_dimension=0, tiled=True
        ).astype(jnp.float32),
        lax.psum_scatter(
            sum_query.astype(jnp.bfloat16), "seq", scatter_dimension=0, tiled=True
        ).astype(jnp.float32),
        lax.psum_scatter(
            sum_key.astype(jnp.bfloat16), "seq", scatter_dimension=0, tiled=True
        ).astype(jnp.float32),
        lax.psum_scatter(
            sum_value.astype(jnp.bfloat16), "seq", scatter_dimension=0, tiled=True
        ).astype(jnp.float32),
        lax.psum_scatter(
            sum_headgate.astype(jnp.bfloat16), "seq", scatter_dimension=0, tiled=True
        ).astype(jnp.float32),
        lax.psum_scatter(
            sum_output.astype(jnp.bfloat16), "seq", scatter_dimension=1, tiled=True
        ).astype(jnp.float32),
        lax.psum_scatter(
            sum_gate.astype(jnp.bfloat16), "seq", scatter_dimension=0, tiled=True
        ).astype(jnp.float32),
        lax.psum_scatter(
            sum_upward.astype(jnp.bfloat16), "seq", scatter_dimension=0, tiled=True
        ).astype(jnp.float32),
        lax.psum_scatter(
            sum_down.astype(jnp.bfloat16), "seq", scatter_dimension=1, tiled=True
        ).astype(jnp.float32),
    )
    query_gain_total, key_gain_total = lax.psum((sum_query_gain, sum_key_gain), ("seq", "kv"))
    return (
        jnp.stack(results, axis=0),
        jnp.stack(input_grads, axis=0),
        attention_total,
        feedforward_total,
        query_gain_total,
        key_gain_total,
        query_total,
        key_total,
        value_total,
        headgate_total,
        output_total,
        gate_total,
        upward_total,
        down_total,
    )


BF = jnp.bfloat16
F32 = jnp.float32
ANY = pl.BlockSpec(memory_space=pl.ANY)
VM = pl.BlockSpec(memory_space=pltpu.VMEM)
DMA = pltpu.SemaphoreType.DMA


def place():
    s = lax.axis_index("seq")
    k = lax.axis_index("kv")
    return (lax.div(s, 2), lax.rem(s, 2), lax.div(k, 2), lax.rem(k, 2))


def device(l, x, y, c):
    return (l * 2 + x, y * 2 + c)


def remote(src, dst, send, recv, target):
    return pltpu.make_async_remote_copy(
        src_ref=src,
        dst_ref=dst,
        send_sem=send,
        recv_sem=recv,
        device_id=target,
        device_id_type=pl.DeviceIdType.MESH,
    )


def greet(partners):
    barrier = pltpu.get_barrier_semaphore()
    count = 0
    for target, there in partners:

        def call(target=target):
            pl.semaphore_signal(
                barrier, inc=1, device_id=target, device_id_type=pl.DeviceIdType.MESH
            )

        if there is None:
            call()
            count = count + 1
        else:
            pl.when(there)(call)
            count = count + jnp.where(there, 1, 0)
    pl.semaphore_wait(barrier, count)


class Line:
    def __init__(self, length, g, ag_send, ag_recv, land=None, rs_send=None, rs_recv=None):
        self.n = length
        self.g, self.ag_send, self.ag_recv = g, ag_send, ag_recv
        self.land, self.rs_send, self.rs_recv = land, rs_send, rs_recv
        self.l, self.x, self.y, self.c = place()

    def partners(self):
        l, x, y, c = self.l, self.x, self.y, self.c
        return [
            (device(l - 1, x, y, c), l >= 1),
            (device(l + 1, x, y, c), l <= self.n - 2),
        ]

    def block(self, item, b):
        return self.g.at[item, pl.ds(2 * b, 2)]

    def _ag(self, item, way, b):
        step = -1 if way == 0 else 1
        return remote(
            self.block(item, b),
            self.block(item, b),
            self.ag_send.at[item, way, b],
            self.ag_recv.at[item, b],
            device(self.l + step, self.x, self.y, self.c),
        )

    def ag_start(self, item):
        l = self.l
        pl.when(l >= 1)(lambda: self._ag(item, 0, l).start())
        pl.when(l <= self.n - 2)(lambda: self._ag(item, 1, l).start())

    def ag_step(self, item, t):
        l, n = self.l, self.n

        @pl.when(l + t <= n - 1)
        def _():
            self._ag(item, 0, l + t).wait_recv()
            pl.when(l >= 1)(lambda: self._ag(item, 0, l + t).start())

        @pl.when(l - t >= 0)
        def _():
            self._ag(item, 1, l - t).wait_recv()
            pl.when(l <= n - 2)(lambda: self._ag(item, 1, l - t).start())

    def ag_end(self, item):
        l, n = self.l, self.n
        for b in range(n):
            pl.when((l >= 1) & (l <= b))(lambda b=b: self._ag(item, 0, b).wait_send())
            pl.when((l <= n - 2) & (l >= b))(lambda b=b: self._ag(item, 1, b).wait_send())

    def _slot(self, item, slot):
        return self.land.at[item, pl.ds(2 * slot, 2)]

    def _rs(self, item, way, o):
        if way == 0:
            target = self.l - 1
            slot = jnp.where(target == o, self.n, o)
        else:
            target = self.l + 1
            slot = o
        return remote(
            self.block(item, o),
            self._slot(item, slot),
            self.rs_send.at[item, way, o],
            self.rs_recv.at[item, slot],
            device(target, self.x, self.y, self.c),
        )

    def _take(self, item, o, slot):
        here = self._slot(item, slot)
        pltpu.make_async_copy(here, here, self.rs_recv.at[item, slot]).wait()
        for h in range(2):
            total = self.g[item, 2 * o + h].astype(F32) + self.land[item, 2 * slot + h].astype(F32)
            self.g[item, 2 * o + h] = total.astype(BF)

    def rs_step(self, item, q):
        l, n = self.l, self.n
        right, left = n - q, q - 1

        @pl.when(l < right)
        def _():
            pl.when(l >= 1)(lambda: self._take(item, right, right))
            self._rs(item, 1, right).start()

        @pl.when(l > left)
        def _():
            pl.when(l <= n - 2)(lambda: self._take(item, left, left))
            self._rs(item, 0, left).start()

    def rs_final(self, item):
        l, n = self.l, self.n
        pl.when(l >= 1)(lambda: self._take(item, l, l))
        pl.when(l <= n - 2)(lambda: self._take(item, l, n))

    def rs_end(self, item):
        l, n = self.l, self.n
        for o in range(n):
            pl.when(l < o)(lambda o=o: self._rs(item, 1, o).wait_send())
            pl.when(l > o)(lambda o=o: self._rs(item, 0, o).wait_send())


def each(count, body):
    def step(i, unused):
        body(i)
        return 0

    lax.fori_loop(0, count, step, 0)


class Pair:
    def __init__(self, line, refs, send, recv, local, half):
        self.line, self.refs = line, refs
        self.send, self.recv, self.local, self.half = send, recv, local, half

    def partner(self):
        line = self.line
        return (device(line.l, 1 - line.x, line.y, line.c), None)

    def _part(self, ref, kind, j, x):
        at = pl.multiple_of(x * self.half + j * 256, 256)
        return ref.at[pl.ds(at, 256), :] if kind == 2 else ref.at[:, pl.ds(at, 256)]

    def _copies(self, item, kind, j):
        line = self.line
        mine = line.g.at[item, 2 * line.l + line.x]
        out = remote(
            self._part(self.refs[kind], kind, j, 1 - line.x),
            mine,
            self.send.at[item],
            self.recv.at[item],
            self.partner()[0],
        )
        here = pltpu.make_async_copy(
            self._part(self.refs[kind], kind, j, line.x), mine, self.local.at[item]
        )
        return out, here

    def start(self, item, kind, j):
        for copy in self._copies(item, kind, j):
            copy.start()

    def end(self, item, kind, j):
        out, here = self._copies(item, kind, j)
        here.wait()
        out.wait_send()
        out.wait_recv()


class Back(Pair):
    def _copies(self, item, kind, j):
        line = self.line
        home = self._part(self.refs[kind], kind, j, line.x)
        out = remote(
            line.g.at[item, 2 * line.l + 1 - line.x],
            home,
            self.send.at[item],
            self.recv.at[item],
            self.partner()[0],
        )
        here = pltpu.make_async_copy(
            line.g.at[item, 2 * line.l + line.x], home, self.local.at[item]
        )
        return out, here


def back_wait(back, item, kind, j):
    line = back.line
    out, here = back._copies(item, kind, j)
    here.wait()
    out.wait_send()
    there = back._part(back.refs[kind], kind, j, 1 - line.x)
    pltpu.make_async_copy(there, there, back.recv.at[item]).wait()


def dot(a, b):
    return lax.dot_general(a, b, (((1,), (0,)), ((), ())), preferred_element_type=F32)


def dot_t(a, b):
    return lax.dot_general(a, b, (((1,), (1,)), ((), ())), preferred_element_type=F32)


def front_kernel(
    n, x_ref, z_ref, wq, wkv, wo, x_all, z_all, g, p_send, p_recv, p_loc, ag_send, ag_recv, t_send, t_recv, t_loc
):
    line = Line(n, g, ag_send, ag_recv)
    pair = Pair(line, (wq, wkv, wo), p_send, p_recv, p_loc, 256)
    l, x, y, c = line.l, line.x, line.y, line.c
    across, mate = device(l, 1 - x, y, c), device(l, x, y, 1 - c)
    greet(line.partners() + [(across, None), (mate, None)])
    for item in range(3):
        pair.start(item, item, 0)

    def token(i, src, dst):
        own = pltpu.make_async_copy(src, dst.at[:, x], t_loc.at[i])
        out = remote(
            src.at[pl.ds(2 * c, 2)], dst.at[pl.ds(2 * c, 2), x], t_send.at[i, 0], t_recv.at[i, 0], across
        )
        part = dst.at[pl.ds(2 * c, 2), 1 - x]
        on = remote(part, part, t_send.at[i, 1], t_recv.at[i, 1], mate)
        return own, out, on

    tokens = [token(0, x_ref, x_all), token(1, z_ref, z_all)]
    for own, out, on in tokens:
        own.start()
        out.start()
    for item in range(3):
        pair.end(item, item, 0)
        line.ag_start(item)
    for i, (own, out, on) in enumerate(tokens):
        out.wait_recv()
        on.start()
    for t in range(1, n):
        for item in range(3):
            line.ag_step(item, t)
    for own, out, on in tokens:
        own.wait()
        out.wait_send()
        on.wait()
    for item in range(3):
        line.ag_end(item)


def front(n, x_in, z_in, wq, wkv, wo):
    b, r, d = x_in.shape
    whole = jax.ShapeDtypeStruct((b, 2, r, d), BF)
    return pl.pallas_call(
        functools.partial(front_kernel, n),
        out_shape=(whole, whole, jax.ShapeDtypeStruct((3, 2 * n, 256, 256), BF)),
        in_specs=[ANY] * 5,
        out_specs=(ANY, ANY, ANY),
        scratch_shapes=[
            DMA((3,)),
            DMA((3,)),
            DMA((3,)),
            DMA((3, 2, n)),
            DMA((3, n)),
            DMA((2, 2)),
            DMA((2, 2)),
            DMA((2,)),
        ],
        compiler_params=pltpu.CompilerParams(collective_id=0, has_side_effects=True),
        name="front",
    )(x_in, z_in, wq, wkv, wo)


def keys_kernel(n, own_ref, out_ref, send, recv, local):
    l, x, y, c = place()
    left, right = device(l - 1, x, y, c), device(l + 1, x, y, c)
    greet([(left, l >= 1), (right, l <= n - 2)])
    own = pltpu.make_async_copy(own_ref, out_ref.at[l], local)
    own.start()

    def copy(b, src):
        return remote(src, out_ref.at[b], send.at[b], recv.at[b], right)

    pl.when(l <= n - 2)(lambda: copy(l, own_ref).start())
    for t in range(1, n):

        @pl.when(l - t >= 0)
        def _():
            b = l - t
            copy(b, out_ref.at[b]).wait_recv()
            pl.when(l <= n - 2)(lambda: copy(b, out_ref.at[b]).start())

    for b in range(n):
        pl.when((l >= b) & (l <= n - 2))(lambda b=b: copy(b, out_ref.at[b]).wait_send())
    own.wait()


def keys_forward(n, own):
    return pl.pallas_call(
        functools.partial(keys_kernel, n),
        out_shape=jax.ShapeDtypeStruct((n,) + own.shape, BF),
        in_specs=[VM],
        out_specs=ANY,
        scratch_shapes=[DMA((n,)), DMA((n,)), DMA],
        compiler_params=pltpu.CompilerParams(collective_id=1, has_side_effects=True),
        name="keys",
    )(own)


def keys_back_kernel(n, part_ref, out_ref, work, land, send, recv, local):
    l, x, y, c = place()
    left, right = device(l - 1, x, y, c), device(l + 1, x, y, c)
    greet([(left, l >= 1), (right, l <= n - 2)])
    load = pltpu.make_async_copy(part_ref, work, local)
    load.start()
    load.wait()

    def copy(o):
        return remote(work.at[o], land.at[o], send.at[o], recv.at[o], left)

    def take(o):
        copy(o).wait_recv()

        def add(i, unused):
            at = pl.ds(pl.multiple_of(i * 128, 128), 128)
            work[o, at] = (work[o, at].astype(F32) + land[o, at].astype(F32)).astype(BF)
            return 0

        lax.fori_loop(0, work.shape[1] // 128, add, 0)

    for o in range(n - 1):

        @pl.when(l > o)
        def _(o=o):
            pl.when(l <= n - 2)(lambda: take(o))
            copy(o).start()

    pl.when(l <= n - 2)(lambda: take(l))
    out_ref[...] = work[l]
    for o in range(n - 1):
        pl.when(l > o)(lambda o=o: copy(o).wait_send())


def keys_back(n, parts):
    return pl.pallas_call(
        functools.partial(keys_back_kernel, n),
        out_shape=jax.ShapeDtypeStruct(parts.shape[1:], BF),
        in_specs=[ANY],
        out_specs=VM,
        scratch_shapes=[
            pltpu.VMEM(parts.shape, BF),
            pltpu.VMEM(parts.shape, BF),
            DMA((n,)),
            DMA((n,)),
            DMA,
        ],
        compiler_params=pltpu.CompilerParams(
            collective_id=2, has_side_effects=True, vmem_limit_bytes=40 * 2**20
        ),
        name="keys_back",
    )(parts)


class Group:
    def __init__(self):
        self.l, self.x, self.y, self.c = place()
        self.mate = device(self.l, self.x, self.y, 1 - self.c)

    def other(self, i):
        x = 1 - self.x if i & 1 else self.x
        y = 1 - self.y if i & 2 else self.y
        return x, y

    def chip(self, i):
        x, y = self.other(i)
        return device(self.l, x, y, self.c)

    def partners(self):
        return [(self.mate, None)] + [(self.chip(i), None) for i in (1, 2, 3)]


def sum_kernel(m, part_ref, out_ref, core_land, low, chip_land, c_send, c_recv, s_send, s_recv):
    group = Group()
    x, y, c = group.x, group.y, group.c
    greet(group.partners())
    pairs = [(i, b) for b in range(4) for i in range(m)]

    def to_mate(i, b):
        return remote(
            part_ref.at[i, b, :, :, 1 - c],
            core_land.at[i, b],
            c_send.at[i, b],
            c_recv.at[i, b],
            group.mate,
        )

    def to_chip(i, b, o):
        ox, oy = group.other(o)
        return remote(
            low.at[i, b, ox, oy],
            chip_land.at[i, o - 1, b],
            s_send.at[i, b, o - 1],
            s_recv.at[i, b, o - 1],
            group.chip(o),
        )

    for i, b in pairs:
        to_mate(i, b).start()
    for i, b in pairs:
        to_mate(i, b).wait_recv()
        for u in range(2):
            for v in range(2):
                low[i, b, u, v] = (
                    part_ref[i, b, u, v, c].astype(F32) + core_land[i, b, u, v].astype(F32)
                ).astype(BF)
        for o in (3, 1, 2):
            to_chip(i, b, o).start()
    for i, b in pairs:
        total = low[i, b, x, y].astype(F32)
        for o in (1, 2, 3):
            to_chip(i, b, o).wait_recv()
            total = total + chip_land[i, o - 1, b].astype(F32)
        out_ref[i, b] = total
    for i, b in pairs:
        to_mate(i, b).wait_send()
        for o in (1, 2, 3):
            to_chip(i, b, o).wait_send()


def group_sum(part, collective):
    m, d = part.shape[0], part.shape[-1]
    return pl.pallas_call(
        functools.partial(sum_kernel, m),
        out_shape=jax.ShapeDtypeStruct((m, 4, 32, d), F32),
        in_specs=[VM],
        out_specs=VM,
        scratch_shapes=[
            pltpu.VMEM((m, 4, 2, 2, 32, d), BF),
            pltpu.VMEM((m, 4, 2, 2, 32, d), BF),
            pltpu.VMEM((m, 3, 4, 32, d), BF),
            DMA((m, 4)),
            DMA((m, 4)),
            DMA((m, 4, 3)),
            DMA((m, 4, 3)),
        ],
        compiler_params=pltpu.CompilerParams(
            collective_id=collective, has_side_effects=True, vmem_limit_bytes=56 * 2**20
        ),
        name=f"group_sum{m}",
    )(part)


def spread_kernel(own_ref, out_ref, s_send, s_recv, c_send, c_recv, local):
    group = Group()
    x, y, c = group.x, group.y, group.c
    greet(group.partners())
    mine = out_ref.at[:, x, y, c]
    keep = pltpu.make_async_copy(own_ref, mine, local)
    keep.start()

    def to_chip(o):
        return remote(own_ref, mine, s_send.at[o - 1], s_recv.at[o - 1], group.chip(o))

    def to_mate(o):
        ox, oy = group.other(o)
        part = out_ref.at[:, ox, oy, c]
        src = own_ref if o == 0 else part
        return remote(src, part, c_send.at[o], c_recv.at[o], group.mate)

    for o in (3, 1, 2):
        to_chip(o).start()
    to_mate(0).start()
    for o in (1, 2, 3):
        to_chip(o).wait_recv()
        to_mate(o).start()
    keep.wait()
    for o in (1, 2, 3):
        to_chip(o).wait_send()
    for o in range(4):
        to_mate(o).wait()


def group_spread(own, collective):
    b, r, d = own.shape
    return pl.pallas_call(
        spread_kernel,
        out_shape=jax.ShapeDtypeStruct((b, 2, 2, 2, r, d), own.dtype),
        in_specs=[VM],
        out_specs=ANY,
        scratch_shapes=[DMA((3,)), DMA((3,)), DMA((4,)), DMA((4,)), DMA],
        compiler_params=pltpu.CompilerParams(collective_id=collective, has_side_effects=True),
        name="group_spread",
    )(own)


def home_kernel(own_ref, out_ref, s_send, s_recv, local):
    group = Group()
    l, x, y, c = group.l, group.x, group.y, group.c
    others = [device(l, x, y, 1 - c), device(l, x, 1 - y, c), device(l, x, 1 - y, 1 - c)]
    greet([(o, None) for o in others])
    mine = out_ref.at[:, :, y, c]
    keep = pltpu.make_async_copy(own_ref, mine, local)
    keep.start()
    copies = [
        remote(own_ref, mine, s_send.at[i], s_recv.at[i], o) for i, o in enumerate(others)
    ]
    for copy in copies:
        copy.start()
    keep.wait()
    for copy in copies:
        copy.wait()


def home(own):
    m, b, r, d = own.shape
    return pl.pallas_call(
        home_kernel,
        out_shape=jax.ShapeDtypeStruct((m, b, 2, 2, r, d), own.dtype),
        in_specs=[VM],
        out_specs=ANY,
        scratch_shapes=[DMA((3,)), DMA((3,)), DMA],
        compiler_params=pltpu.CompilerParams(collective_id=7, has_side_effects=True),
        name="home",
    )(own)


def rows_kernel(n, part_ref, dq, dkv, do, g, land, rs_send, rs_recv, b_send, b_recv, b_loc, local):
    line = Line(n, g, None, None, land, rs_send, rs_recv)
    back = Back(line, (dq, dkv, do), b_send, b_recv, b_loc, 256)
    greet(line.partners() + [back.partner()])
    load = pltpu.make_async_copy(part_ref, g, local)
    load.start()
    load.wait()
    for q in range(1, n):
        each(3, lambda item, q=q: line.rs_step(item, q))
    each(3, line.rs_final)
    for item in range(3):
        back.start(item, item, 0)
    for item in range(3):
        back_wait(back, item, item, 0)
    each(3, line.rs_end)


def rows_sum(n, parts):
    return pl.pallas_call(
        functools.partial(rows_kernel, n),
        out_shape=(
            jax.ShapeDtypeStruct((256, 512), BF),
            jax.ShapeDtypeStruct((256, 512), BF),
            jax.ShapeDtypeStruct((512, 256), BF),
        ),
        in_specs=[ANY],
        out_specs=(ANY, ANY, ANY),
        scratch_shapes=[
            pltpu.VMEM((3, 2 * n, 256, 256), BF),
            pltpu.VMEM((3, 2 * n + 2, 256, 256), BF),
            DMA((3, 2, n)),
            DMA((3, n + 1)),
            DMA((3,)),
            DMA((3,)),
            DMA((3,)),
            DMA,
        ],
        compiler_params=pltpu.CompilerParams(
            collective_id=8, has_side_effects=True, vmem_limit_bytes=40 * 2**20
        ),
        name="rows_sum",
    )(parts)


def ffn_kernel(
    n,
    chunks,
    inner_ref,
    dz_ref,
    wg,
    wu,
    wd,
    out_ref,
    din_ref,
    dgw,
    duw,
    ddw,
    inner_t,
    out_acc,
    din_acc,
    g,
    land,
    low,
    prod_t,
    p_send,
    p_recv,
    p_loc,
    ag_send,
    ag_recv,
    rs_send,
    rs_recv,
    b_send,
    b_recv,
    b_loc,
    o_loc,
):
    line = Line(n, g, ag_send, ag_recv, land, rs_send, rs_recv)
    half = chunks * 256
    pair = Pair(line, (wg, wu, wd), p_send, p_recv, p_loc, half)
    back = Back(line, (dgw, duw, ddw), b_send, b_recv, b_loc, half)
    greet(line.partners() + [pair.partner()])
    blocks = 2 * n
    for j in range(chunks):
        for kind in range(3):
            pair.start(3 * j + kind, kind, j)

    def turn(i, unused):
        m, s = lax.div(i, blocks), lax.rem(i, blocks)
        tile = inner_ref[m, :, pl.ds(pl.multiple_of(s * 256, 256), 256)]
        inner_t[s, :, pl.ds(pl.multiple_of(m * 256, 256), 256)] = tile.T
        return 0

    for j in range(chunks):
        for kind in range(3):
            pair.end(3 * j + kind, kind, j)
            line.ag_start(3 * j + kind)
    lax.fori_loop(0, 4 * blocks, turn, 0)

    def compute(j):
        base = 3 * j

        def rows(m, unused):
            a = inner_ref[m]
            d = dz_ref[m]
            gated = dot(a, g[base].reshape(blocks * 256, 256))
            upward = dot(a, g[base + 1].reshape(blocks * 256, 256))
            grad = dot_t(d[:, :256], g[base + 2, 0])
            for s in range(1, blocks):
                grad = grad + dot_t(d[:, s * 256 : (s + 1) * 256], g[base + 2, s])
            sigma = jax.nn.sigmoid(gated)
            swish = gated * sigma
            product = (swish * upward).astype(BF)
            d_gated = (grad * upward * sigma * (1.0 + gated * (1.0 - sigma))).astype(BF)
            d_upward = (grad * swish).astype(BF)
            at = pl.ds(pl.multiple_of(m * 256, 256), 256)
            low[0, at] = d_gated
            low[1, at] = d_upward
            prod_t[:, at] = product.T
            for s in range(blocks):
                cols = slice(s * 256, (s + 1) * 256)
                o = dot(product, g[base + 2, s])
                i = dot_t(d_gated, g[base, s]) + dot_t(d_upward, g[base + 1, s])
                if j == 0:
                    out_acc[m, :, cols] = o
                    din_acc[m, :, cols] = i
                else:
                    out_acc[m, :, cols] += o
                    din_acc[m, :, cols] += i
            return 0

        lax.fori_loop(0, 4, rows, 0)

        def weights(s, unused):
            t = inner_t[s]
            g[base, s] = dot(t, low[0]).astype(BF)
            g[base + 1, s] = dot(t, low[1]).astype(BF)
            z = dz_ref[:, :, pl.ds(pl.multiple_of(s * 256, 256), 256)].reshape(1024, 256)
            g[base + 2, s] = dot(prod_t[...], z).astype(BF)
            return 0

        lax.fori_loop(0, blocks, weights, 0)

    def items(j, body):
        each(3, lambda i: body(3 * j + i))

    for j in range(chunks):
        for t in range(1, n):
            items(j, lambda item, t=t: line.ag_step(item, t))
            if j > 0:
                items(j - 1, lambda item, t=t: line.rs_step(item, t))
        items(j, line.ag_end)
        compute(j)
        if j > 0:
            items(j - 1, line.rs_final)
            for kind in range(3):
                back.start(3 * j - 3 + kind, kind, j - 1)
    last = chunks - 1

    def flush(m, unused):
        inner_ref[m] = out_acc[m].astype(BF)
        dz_ref[m] = din_acc[m].astype(BF)
        return 0

    for t in range(1, n):
        items(last, lambda item, t=t: line.rs_step(item, t))
    lax.fori_loop(0, 4, flush, 0)
    outs = [
        pltpu.make_async_copy(inner_ref, out_ref, o_loc.at[0]),
        pltpu.make_async_copy(dz_ref, din_ref, o_loc.at[1]),
    ]
    for copy in outs:
        copy.start()
    items(last, line.rs_final)
    for kind in range(3):
        back.start(3 * last + kind, kind, last)
    for j in range(chunks):
        for kind in range(3):
            back_wait(back, 3 * j + kind, kind, j)
    for j in range(chunks):
        items(j, line.rs_end)
    for copy in outs:
        copy.wait()


def ffn(n, inner, dz, wg, wu, wd):
    d, hid = wg.shape[0] * 2 * n, wg.shape[1]
    chunks = hid // 512
    items = 3 * chunks
    tokens = jax.ShapeDtypeStruct((4, 256, d), BF)
    return pl.pallas_call(
        lambda inner_any, dz_any, *rest: ffn_load(n, chunks, inner_any, dz_any, *rest),
        out_shape=(
            tokens,
            tokens,
            jax.ShapeDtypeStruct(wg.shape, BF),
            jax.ShapeDtypeStruct(wu.shape, BF),
            jax.ShapeDtypeStruct(wd.shape, BF),
        ),
        in_specs=[ANY] * 5,
        out_specs=(ANY,) * 5,
        scratch_shapes=[
            pltpu.VMEM((4, 256, d), BF),
            pltpu.VMEM((4, 256, d), BF),
            DMA((2,)),
            pltpu.VMEM((2 * n, 256, 1024), BF),
            pltpu.VMEM((4, 256, d), F32),
            pltpu.VMEM((4, 256, d), F32),
            pltpu.VMEM((items, 2 * n, 256, 256), BF),
            pltpu.VMEM((items, 2 * n + 2, 256, 256), BF),
            pltpu.VMEM((2, 1024, 256), BF),
            pltpu.VMEM((256, 1024), BF),
            DMA((items,)),
            DMA((items,)),
            DMA((items,)),
            DMA((items, 2, n)),
            DMA((items, n)),
            DMA((items, 2, n)),
            DMA((items, n + 1)),
            DMA((items,)),
            DMA((items,)),
            DMA((items,)),
            DMA((2,)),
        ],
        compiler_params=pltpu.CompilerParams(
            collective_id=9, has_side_effects=True, vmem_limit_bytes=62 * 2**20
        ),
        name="ffn",
    )(inner, dz, wg, wu, wd)


def ffn_load(n, chunks, inner_any, dz_any, wg, wu, wd, out, din, dgw, duw, ddw, inner_v, dz_v, in_loc, *rest):
    loads = [
        pltpu.make_async_copy(inner_any, inner_v, in_loc.at[0]),
        pltpu.make_async_copy(dz_any, dz_v, in_loc.at[1]),
    ]
    for copy in loads:
        copy.start()
    for copy in loads:
        copy.wait()
    ffn_kernel(n, chunks, inner_v, dz_v, wg, wu, wd, out, din, dgw, duw, ddw, *rest)


def fast_local(
    inputs,
    cotangent,
    bucket_sizes,
    true_lengths,
    attention_gain,
    feedforward_gain,
    query_gain,
    key_gain,
    query_weight,
    key_matrix,
    value_matrix,
    headgate_weight,
    output_weight,
    gate_weight,
    up_weight,
    down_weight,
):
    batches, rows, width = inputs.shape
    n = lax.axis_size("seq") // 2
    seq, kv = lax.axis_index("seq"), lax.axis_index("kv")
    l, x = seq // 2, seq % 2
    scale = HEAD_SIZE ** (-0.5)
    span = 2 * rows
    gain_query = query_gain.astype(F32)
    gain_key = key_gain.astype(F32)

    small = jnp.concatenate(
        [headgate_weight.T, attention_gain[None], feedforward_gain[None]], axis=0
    )
    small = lax.all_gather(small, "seq", axis=1, tiled=True)
    w_head = lax.dynamic_slice_in_dim(small, x * 2, 2, 0)
    gain_a = small[4].astype(F32)
    gain_f = small[5].astype(F32)
    paired = jnp.concatenate(
        [key_matrix[:, :128], value_matrix[:, :128], key_matrix[:, 128:], value_matrix[:, 128:]],
        axis=1,
    )
    x_all, z_all, g = front(n, inputs, cotangent, query_weight, paired, output_weight)
    w_query = g[0].reshape(width, 256)
    w_keys = g[1].reshape(width, 256)
    w_output = g[2]

    def own_rows(values):
        return lax.dynamic_slice_in_dim(values, kv * 32, 32, 1)

    row_index = l * span + jnp.arange(span, dtype=jnp.int32)
    key_index = jnp.arange(n * span, dtype=jnp.int32)
    layouts = [token_layout(row_index, bucket_sizes[b], true_lengths[b]) for b in range(batches)]
    key_layouts = [
        token_layout(key_index, bucket_sizes[b], true_lengths[b]) for b in range(batches)
    ]
    positions = jnp.concatenate([item[1] for item in layouts])
    allowed = jnp.stack(
        [
            (mine[0][:, None] == theirs[0][None, :])
            & (key_index[None, :] <= row_index[:, None])
            & theirs[2][None, :]
            for mine, theirs in zip(layouts, key_layouts)
        ]
    )[:, None]
    cosine, sine = rope_tables(positions, HEAD_SIZE)

    current = x_all.reshape(batches * span, width).astype(F32)
    normed = (current * rms_scale(current) * gain_a).astype(BF)
    query_proj = jnp.dot(normed, w_query, preferred_element_type=F32).reshape(-1, 2, HEAD_SIZE)
    keys_proj = jnp.dot(normed, w_keys, preferred_element_type=F32)
    key_proj = keys_proj[:, :HEAD_SIZE].reshape(-1, 1, HEAD_SIZE)
    value_low = keys_proj[:, HEAD_SIZE:].astype(BF)
    query_scale = rms_scale(query_proj)
    query_normal = query_proj * query_scale
    key_scale = rms_scale(key_proj)
    key_normal = key_proj * key_scale
    query_rot = rotate_forward(query_normal * gain_query, cosine, sine).astype(BF)
    key_rot = rotate_forward(key_normal * gain_key, cosine, sine).astype(BF)
    gate = jax.nn.sigmoid(times_transpose(normed, w_head))
    own_keys = jnp.concatenate([key_rot.reshape(-1, HEAD_SIZE), value_low], axis=1)
    all_keys = keys_forward(n, own_keys).reshape(n, batches, span, 256)
    seen = (jnp.arange(n) <= l)[:, None, None, None]
    all_keys = jnp.where(seen, all_keys, 0).transpose(1, 0, 2, 3).reshape(batches, n * span, 256)
    keys, values = all_keys[..., :HEAD_SIZE], all_keys[..., HEAD_SIZE:]
    query = query_rot.reshape(batches, span, 2, HEAD_SIZE).transpose(0, 2, 1, 3)

    def weights_of(log_total=None):
        raw = jnp.einsum("bhtd,bsd->bhts", query, keys, preferred_element_type=F32) * scale
        if log_total is None:
            return jnp.where(allowed, jnp.exp(raw), 0.0)
        return jnp.where(allowed, jnp.exp(raw - log_total), 0.0)

    spread = weights_of()
    log_total = jnp.log(jnp.sum(spread, axis=-1, keepdims=True))
    weights = weights_of(log_total)
    attended = jnp.einsum("bhts,bsd->bhtd", weights.astype(BF), values, preferred_element_type=F32)
    gate_heads = gate.reshape(batches, span, 2).transpose(0, 2, 1)[..., None]
    mixed = (attended * gate_heads).astype(BF).transpose(0, 2, 1, 3).reshape(-1, 256)
    branch = jnp.concatenate(
        [jnp.dot(mixed, w_output[s], preferred_element_type=F32) for s in range(2 * n)], axis=1
    ).astype(BF)
    split = (batches, 2, 2, 2, 32, width)
    own_x = own_rows(inputs).astype(F32)
    hidden = own_x + group_sum(branch.reshape((1,) + split), 3)[0]
    scale_f = rms_scale(hidden)
    normal_f = hidden * scale_f
    inner = group_spread((normal_f * gain_f).astype(BF), 4)
    out_part, din_part, d_gate, d_up, d_down = ffn(
        n,
        inner.reshape(batches, span, width),
        z_all.reshape(batches, span, width),
        gate_weight,
        up_weight,
        down_weight,
    )
    sums = group_sum(jnp.stack([out_part.reshape(split), din_part.reshape(split)]), 5)
    own_out = (hidden + sums[0]).astype(BF)
    grad_inner = sums[1]
    own_dz = own_rows(cotangent).astype(F32)
    sum_feedforward_gain = jnp.sum(grad_inner * normal_f, axis=(0, 1))
    grad_hidden = own_dz + norm_backward(grad_inner * gain_f, normal_f, scale_f)
    grad_branch = group_spread(grad_hidden.astype(BF), 6).reshape(-1, width)
    d_output = jnp.stack(
        [outer_sum(mixed, grad_branch[:, s * 256 : (s + 1) * 256]).astype(BF) for s in range(2 * n)]
    )
    grad_mixed = sum(
        times_transpose(grad_branch[:, s * 256 : (s + 1) * 256], w_output[s]) for s in range(2 * n)
    )
    grad_mixed = grad_mixed.reshape(batches, span, 2, HEAD_SIZE).transpose(0, 2, 1, 3)
    grad_heads = (grad_mixed * gate_heads).astype(BF)
    grad_logits = (
        jnp.sum(grad_mixed * attended, axis=-1, keepdims=True) * gate_heads * (1.0 - gate_heads)
    ).astype(BF)
    delta = jnp.sum(grad_heads.astype(F32) * attended, axis=-1, keepdims=True)
    grad_weights = jnp.einsum("bhtd,bsd->bhts", grad_heads, values, preferred_element_type=F32)
    grad_scores = (weights * (grad_weights - delta)).astype(BF)
    grad_query = scale * jnp.einsum(
        "bhts,bsd->bhtd", grad_scores, keys, preferred_element_type=F32
    )
    grad_keys = scale * jnp.einsum(
        "bhts,bhtd->bsd", grad_scores, query, preferred_element_type=F32
    )
    grad_values = jnp.einsum(
        "bhts,bhtd->bsd", weights.astype(BF), grad_heads, preferred_element_type=F32
    )
    grad_pair = jnp.concatenate([grad_keys, grad_values], axis=-1).astype(BF)
    grad_pair = grad_pair.reshape(batches, n, span, 256).transpose(1, 0, 2, 3)
    local_pair = keys_back(n, grad_pair.reshape(n, batches * span, 256)).astype(F32)

    grad_query_rot = grad_query.transpose(0, 2, 1, 3).reshape(-1, 2, HEAD_SIZE)
    grad_query_norm = rotate_backward(grad_query_rot, cosine, sine)
    sum_query_gain = jnp.sum(grad_query_norm * query_normal, axis=(0, 1))
    d_query = (
        norm_backward(grad_query_norm * gain_query, query_normal, query_scale)
        .astype(BF)
        .reshape(-1, 256)
    )
    grad_key_norm = rotate_backward(local_pair[:, None, :HEAD_SIZE], cosine, sine)
    sum_key_gain = jnp.sum(grad_key_norm * key_normal, axis=(0, 1))
    d_key = norm_backward(grad_key_norm * gain_key, key_normal, key_scale).astype(BF)
    d_pair = jnp.concatenate(
        [d_key.reshape(-1, HEAD_SIZE), local_pair[:, HEAD_SIZE:].astype(BF)], axis=1
    )
    logits_low = grad_logits[..., 0].transpose(0, 2, 1).reshape(-1, 2)
    d_head = outer_sum(logits_low, normed)
    d_head = jnp.where(jnp.arange(2)[:, None, None] == x, d_head[None], 0.0).reshape(4, width)
    d_query_weight = outer_sum(normed, d_query).astype(BF).reshape(2 * n, 256, 256)
    d_pair_weight = outer_sum(normed, d_pair).astype(BF).reshape(2 * n, 256, 256)
    grad_partial = (
        times_transpose(d_query, w_query)
        + times_transpose(d_pair, w_keys)
        + jnp.dot(logits_low, w_head, preferred_element_type=F32)
    ).astype(BF)
    grad_normed = group_sum(grad_partial.reshape((1,) + split), 10)[0]
    dq, dkv, do = rows_sum(n, jnp.stack([d_query_weight, d_pair_weight, d_output]))
    scale_a = rms_scale(own_x)
    normal_a = own_x * scale_a
    sum_attention_gain = jnp.sum(grad_normed * normal_a, axis=(0, 1))
    own_grad = (grad_hidden + norm_backward(grad_normed * gain_a, normal_a, scale_a)).astype(BF)
    outs = home(jnp.stack([own_out, own_grad])).reshape(2, batches, rows, width)
    gains = lax.psum(
        jnp.concatenate([sum_attention_gain, sum_feedforward_gain, sum_query_gain, sum_key_gain]),
        ("seq", "kv"),
    )
    head_total = lax.psum(d_head, "seq")
    own_width = width // (2 * n)

    def cut(values):
        return lax.dynamic_slice_in_dim(values, seq * own_width, own_width, values.ndim - 1)

    return (
        outs[0],
        outs[1],
        cut(gains[:width]),
        cut(gains[width : 2 * width]),
        gains[2 * width : 2 * width + HEAD_SIZE],
        gains[2 * width + HEAD_SIZE :],
        dq.astype(F32),
        jnp.concatenate([dkv[:, :128], dkv[:, 256:384]], axis=1).astype(F32),
        jnp.concatenate([dkv[:, 128:256], dkv[:, 384:]], axis=1).astype(F32),
        cut(head_total).T,
        do.astype(F32),
        d_gate.astype(F32),
        d_up.astype(F32),
        d_down.astype(F32),
    )


def solution(mesh):
    chosen = fast_local if dict(mesh.shape) == {"seq": 8, "kv": 4} else local
    in_specs = (
        P(None, "seq", None),
        P(None, "seq", None),
        P(),
        P(),
        P("seq"),
        P("seq"),
        P(),
        P(),
        P("seq", "kv"),
        P("seq", "kv"),
        P("seq", "kv"),
        P("seq", "kv"),
        P("kv", "seq"),
        P("seq", "kv"),
        P("seq", "kv"),
        P("kv", "seq"),
    )
    out_specs = (
        P(None, "seq", None),
        P(None, "seq", None),
        P("seq"),
        P("seq"),
        P(),
        P(),
        P("seq", "kv"),
        P("seq", "kv"),
        P("seq", "kv"),
        P("seq", "kv"),
        P("kv", "seq"),
        P("seq", "kv"),
        P("seq", "kv"),
        P("kv", "seq"),
    )
    return jax.shard_map(chosen, mesh=mesh, in_specs=in_specs, out_specs=out_specs, check_vma=False)
```

```python
import functools
import math

import jax
import jax.numpy as jnp
from jax import lax
from jax.experimental import pallas as pl
from jax.experimental.pallas import tpu as pltpu
from jax.sharding import PartitionSpec as P

HEAD_SIZE = 128


EPS = 1e-06
ROPE_BASE = 1000000.0
MASKED = -1e30


def rms_scale(values):
    return lax.rsqrt(jnp.mean(values * values, axis=-1, keepdims=True) + EPS)


def norm_backward(grad, normal, factor):
    return factor * (grad - normal * jnp.mean(grad * normal, axis=-1, keepdims=True))


def rope_tables(positions, width):
    half = width // 2
    steps = jnp.arange(half, dtype=jnp.float32) * (2.0 / width)
    inverse = jnp.exp(-steps * math.log(ROPE_BASE))
    angles = positions.astype(jnp.float32)[:, None] * inverse[None, :]
    cosine = jnp.cos(angles)
    sine = jnp.sin(angles)
    return (jnp.concatenate([cosine, cosine], axis=-1), jnp.concatenate([sine, sine], axis=-1))


def rotate_forward(values, cosine, sine):
    half = values.shape[-1] // 2
    turned = jnp.concatenate([-values[..., half:], values[..., :half]], axis=-1)
    return values * cosine[:, None, :] + turned * sine[:, None, :]


def rotate_backward(grad, cosine, sine):
    half = grad.shape[-1] // 2
    moved = grad * sine[:, None, :]
    return grad * cosine[:, None, :] + jnp.concatenate(
        [moved[..., half:], -moved[..., :half]], axis=-1
    )


def token_layout(index, buckets, lengths):
    ends = jnp.cumsum(buckets)
    starts = ends - buckets
    member = (index[:, None] >= starts[None, :]) & (index[:, None] < ends[None, :])
    labels = jnp.arange(buckets.shape[0], dtype=jnp.int32)
    segment = jnp.sum(jnp.where(member, labels[None, :], 0), axis=1)
    position = index - jnp.sum(jnp.where(member, starts[None, :], 0), axis=1)
    limit = jnp.sum(jnp.where(member, lengths[None, :], 0), axis=1)
    return (segment, position, position < limit)


def outer_sum(left, right):
    return lax.dot_general(
        left, right, (((0,), (0,)), ((), ())), preferred_element_type=jnp.float32
    )


def times_transpose(left, weight):
    return lax.dot_general(
        left, weight, (((1,), (1,)), ((), ())), preferred_element_type=jnp.float32
    )


def block_scores(query_kg, key_block, start, row_index, row_segment, buckets, lengths, scale):
    key_index = start + jnp.arange(key_block.shape[0], dtype=jnp.int32)
    key_segment, key_position, key_valid = token_layout(key_index, buckets, lengths)
    allowed = (
        (row_segment[:, None] == key_segment[None, :])
        & (key_index[None, :] <= row_index[:, None])
        & key_valid[None, :]
    )
    raw = (
        jnp.einsum("kgtd,skd->kgts", query_kg, key_block, preferred_element_type=jnp.float32)
        * scale
    )
    return (jnp.where(allowed, raw, MASKED), allowed)


def split_blocks(keys, values, block):
    blocks = keys.shape[0] // block
    key_blocks = keys.reshape(blocks, block, keys.shape[1], keys.shape[2])
    value_blocks = values.reshape(blocks, block, values.shape[1], values.shape[2])
    starts = jnp.arange(blocks) * block
    return (key_blocks, value_blocks, starts)


def attention_forward(
    query_kg, keys, values, row_index, row_segment, buckets, lengths, block, scale
):
    key_blocks, value_blocks, starts = split_blocks(keys, values, block)

    def first_pass(carry, item):
        running_max, total = carry
        key_block, start = item
        masked, allowed = block_scores(
            query_kg, key_block, start, row_index, row_segment, buckets, lengths, scale
        )
        new_max = jnp.maximum(running_max, jnp.max(masked, axis=-1))
        total = total * jnp.exp(running_max - new_max) + jnp.sum(
            jnp.where(allowed, jnp.exp(masked - new_max[..., None]), 0.0), axis=-1
        )
        return ((new_max, total), None)

    begin = (
        jnp.full(query_kg.shape[:3], MASKED, jnp.float32),
        jnp.zeros(query_kg.shape[:3], jnp.float32),
    )
    (running_max, total), unused = lax.scan(first_pass, begin, (key_blocks, starts))
    log_total = running_max + jnp.log(total)

    def second_pass(accumulated, item):
        key_block, value_block, start = item
        masked, allowed = block_scores(
            query_kg, key_block, start, row_index, row_segment, buckets, lengths, scale
        )
        weights = jnp.where(allowed, jnp.exp(masked - log_total[..., None]), 0.0).astype(
            jnp.bfloat16
        )
        return (
            accumulated
            + jnp.einsum(
                "kgts,skd->kgtd", weights, value_block, preferred_element_type=jnp.float32
            ),
            None,
        )

    attended, unused = lax.scan(
        second_pass, jnp.zeros(query_kg.shape, jnp.float32), (key_blocks, value_blocks, starts)
    )
    return (attended, log_total)


def attention_backward(
    query_kg,
    grad_kg,
    log_total,
    delta,
    keys,
    values,
    row_index,
    row_segment,
    buckets,
    lengths,
    block,
    scale,
):
    key_blocks, value_blocks, starts = split_blocks(keys, values, block)

    def step(grad_query, item):
        key_block, value_block, start = item
        masked, allowed = block_scores(
            query_kg, key_block, start, row_index, row_segment, buckets, lengths, scale
        )
        weights = jnp.where(allowed, jnp.exp(masked - log_total[..., None]), 0.0)
        grad_weights = jnp.einsum(
            "kgtd,skd->kgts", grad_kg, value_block, preferred_element_type=jnp.float32
        )
        grad_scores = (weights * (grad_weights - delta[..., None])).astype(jnp.bfloat16)
        grad_query = grad_query + scale * jnp.einsum(
            "kgts,skd->kgtd", grad_scores, key_block, preferred_element_type=jnp.float32
        )
        grad_key = scale * jnp.einsum(
            "kgts,kgtd->skd", grad_scores, query_kg, preferred_element_type=jnp.float32
        )
        grad_value = jnp.einsum(
            "kgts,kgtd->skd",
            weights.astype(jnp.bfloat16),
            grad_kg,
            preferred_element_type=jnp.float32,
        )
        return (grad_query, (grad_key, grad_value))

    grad_query, (grad_keys, grad_values) = lax.scan(
        step, jnp.zeros(query_kg.shape, jnp.float32), (key_blocks, value_blocks, starts)
    )
    return (grad_query, grad_keys.reshape(keys.shape), grad_values.reshape(values.shape))


def local(
    inputs,
    cotangent,
    bucket_sizes,
    true_lengths,
    attention_gain,
    feedforward_gain,
    query_gain,
    key_gain,
    query_weight,
    key_matrix,
    value_matrix,
    headgate_weight,
    output_weight,
    gate_weight,
    up_weight,
    down_weight,
):
    batches, rows, width = inputs.shape
    seq_count = lax.axis_size("seq")
    block = math.gcd(rows * seq_count, 512)
    local_heads = query_weight.shape[1] // HEAD_SIZE
    local_groups = key_matrix.shape[1] // HEAD_SIZE
    group = local_heads // local_groups
    scale = HEAD_SIZE ** (-0.5)
    row_index = lax.axis_index("seq") * rows + jnp.arange(rows, dtype=jnp.int32)
    gain_query = query_gain.astype(jnp.float32)
    gain_key = key_gain.astype(jnp.float32)
    sum_attention_gain = jnp.zeros((width,), jnp.float32)
    sum_feedforward_gain = jnp.zeros((width,), jnp.float32)
    sum_query = jnp.zeros((width, query_weight.shape[1]), jnp.float32)
    sum_key = jnp.zeros((width, key_matrix.shape[1]), jnp.float32)
    sum_value = jnp.zeros((width, value_matrix.shape[1]), jnp.float32)
    sum_headgate = jnp.zeros((width, headgate_weight.shape[1]), jnp.float32)
    sum_output = jnp.zeros((output_weight.shape[0], width), jnp.float32)
    sum_gate = jnp.zeros((width, gate_weight.shape[1]), jnp.float32)
    sum_upward = jnp.zeros((width, up_weight.shape[1]), jnp.float32)
    sum_down = jnp.zeros((down_weight.shape[0], width), jnp.float32)
    sum_query_gain = jnp.zeros((HEAD_SIZE,), jnp.float32)
    sum_key_gain = jnp.zeros((HEAD_SIZE,), jnp.float32)
    results = []
    input_grads = []
    for batch in range(batches):
        gathered = (
            lax.all_gather(attention_gain, "seq", axis=0, tiled=True),
            lax.all_gather(feedforward_gain, "seq", axis=0, tiled=True),
            lax.all_gather(query_weight, "seq", axis=0, tiled=True),
            lax.all_gather(key_matrix, "seq", axis=0, tiled=True),
            lax.all_gather(value_matrix, "seq", axis=0, tiled=True),
            lax.all_gather(headgate_weight, "seq", axis=0, tiled=True),
            lax.all_gather(output_weight, "seq", axis=1, tiled=True),
            lax.all_gather(gate_weight, "seq", axis=0, tiled=True),
            lax.all_gather(up_weight, "seq", axis=0, tiled=True),
            lax.all_gather(down_weight, "seq", axis=1, tiled=True),
        )
        (
            gain_a,
            gain_f,
            w_query,
            key_projection_weight,
            value_projection_weight,
            w_head,
            w_output,
            w_gate,
            w_up,
            w_down,
        ) = gathered
        gain_a = gain_a.astype(jnp.float32)
        gain_f = gain_f.astype(jnp.float32)
        buckets = bucket_sizes[batch]
        lengths = true_lengths[batch]
        row_segment, row_position, row_valid = token_layout(row_index, buckets, lengths)
        cosine, sine = rope_tables(row_position, HEAD_SIZE)
        current = inputs[batch].astype(jnp.float32)
        scale_a = rms_scale(current)
        normal_a = current * scale_a
        normed_input = (normal_a * gain_a).astype(jnp.bfloat16)
        query_proj = jnp.dot(normed_input, w_query, preferred_element_type=jnp.float32).reshape(
            rows, local_heads, HEAD_SIZE
        )
        key_proj = jnp.dot(
            normed_input, key_projection_weight, preferred_element_type=jnp.float32
        ).reshape(rows, local_groups, HEAD_SIZE)
        value_proj = jnp.dot(
            normed_input, value_projection_weight, preferred_element_type=jnp.float32
        )
        query_scale = rms_scale(query_proj)
        query_normal = query_proj * query_scale
        key_scale = rms_scale(key_proj)
        key_normal = key_proj * key_scale
        query_rot = rotate_forward(query_normal * gain_query, cosine, sine).astype(jnp.bfloat16)
        key_rot = rotate_forward(key_normal * gain_key, cosine, sine).astype(jnp.bfloat16)
        value_low = value_proj.astype(jnp.bfloat16).reshape(rows, local_groups, HEAD_SIZE)
        logits = jnp.dot(normed_input, w_head, preferred_element_type=jnp.float32)
        gate = jax.nn.sigmoid(logits)
        all_keys, all_values = (
            lax.all_gather(key_rot, "seq", axis=0, tiled=True),
            lax.all_gather(value_low, "seq", axis=0, tiled=True),
        )
        query_kg = query_rot.reshape(rows, local_groups, group, HEAD_SIZE).transpose(1, 2, 0, 3)
        attended_kg, log_total = attention_forward(
            query_kg, all_keys, all_values, row_index, row_segment, buckets, lengths, block, scale
        )
        attended = attended_kg.transpose(2, 0, 1, 3).reshape(rows, local_heads, HEAD_SIZE)
        mixed = (
            (attended * gate[:, :, None])
            .astype(jnp.bfloat16)
            .reshape(rows, local_heads * HEAD_SIZE)
        )
        hidden = current + lax.psum(
            jnp.dot(mixed, w_output, preferred_element_type=jnp.float32).astype(jnp.bfloat16), "kv"
        ).astype(jnp.float32)
        scale_f = rms_scale(hidden)
        normal_f = hidden * scale_f
        inner = (normal_f * gain_f).astype(jnp.bfloat16)
        gated = jnp.dot(inner, w_gate, preferred_element_type=jnp.float32)
        upward = jnp.dot(inner, w_up, preferred_element_type=jnp.float32)
        sigma = jax.nn.sigmoid(gated)
        swish = gated * sigma
        product = (swish * upward).astype(jnp.bfloat16)
        output = hidden + lax.psum(
            jnp.dot(product, w_down, preferred_element_type=jnp.float32).astype(jnp.bfloat16), "kv"
        ).astype(jnp.float32)
        results.append(output.astype(jnp.bfloat16))
        grad_out = cotangent[batch].astype(jnp.float32)
        grad_low = grad_out.astype(jnp.bfloat16)
        sum_down = sum_down + outer_sum(product, grad_low)
        grad_product = times_transpose(grad_low, w_down)
        grad_gated = (grad_product * upward * sigma * (1.0 + gated * (1.0 - sigma))).astype(
            jnp.bfloat16
        )
        grad_upward = (grad_product * swish).astype(jnp.bfloat16)
        sum_gate = sum_gate + outer_sum(inner, grad_gated)
        sum_upward = sum_upward + outer_sum(inner, grad_upward)
        grad_inner = lax.psum(
            (times_transpose(grad_gated, w_gate) + times_transpose(grad_upward, w_up)).astype(
                jnp.bfloat16
            ),
            "kv",
        ).astype(jnp.float32)
        sum_feedforward_gain = sum_feedforward_gain + jnp.sum(grad_inner * normal_f, axis=0)
        grad_hidden = grad_out + norm_backward(grad_inner * gain_f, normal_f, scale_f)
        grad_branch = grad_hidden.astype(jnp.bfloat16)
        sum_output = sum_output + outer_sum(mixed, grad_branch)
        grad_mixed = times_transpose(grad_branch, w_output).reshape(rows, local_heads, HEAD_SIZE)
        grad_heads = (grad_mixed * gate[:, :, None]).astype(jnp.bfloat16)
        grad_logits = (jnp.sum(grad_mixed * attended, axis=-1) * gate * (1.0 - gate)).astype(
            jnp.bfloat16
        )
        back_keys = lax.all_gather(key_rot, "seq", axis=0, tiled=True)
        back_values = lax.all_gather(value_low, "seq", axis=0, tiled=True)
        grad_kg = grad_heads.reshape(rows, local_groups, group, HEAD_SIZE).transpose(1, 2, 0, 3)
        delta = jnp.sum(grad_kg.astype(jnp.float32) * attended_kg, axis=-1)
        grad_query_kg, grad_keys, grad_values = attention_backward(
            query_kg,
            grad_kg,
            log_total,
            delta,
            back_keys,
            back_values,
            row_index,
            row_segment,
            buckets,
            lengths,
            block,
            scale,
        )
        local_keys, local_values = (
            lax.psum_scatter(
                grad_keys.astype(jnp.bfloat16), "seq", scatter_dimension=0, tiled=True
            ).astype(jnp.float32),
            lax.psum_scatter(
                grad_values.astype(jnp.bfloat16), "seq", scatter_dimension=0, tiled=True
            ).astype(jnp.float32),
        )
        grad_query_rot = grad_query_kg.transpose(2, 0, 1, 3).reshape(rows, local_heads, HEAD_SIZE)
        grad_query_norm = rotate_backward(grad_query_rot, cosine, sine)
        sum_query_gain = sum_query_gain + jnp.sum(grad_query_norm * query_normal, axis=(0, 1))
        grad_query = (
            norm_backward(grad_query_norm * gain_query, query_normal, query_scale)
            .astype(jnp.bfloat16)
            .reshape(rows, local_heads * HEAD_SIZE)
        )
        grad_key_norm = rotate_backward(local_keys, cosine, sine)
        sum_key_gain = sum_key_gain + jnp.sum(grad_key_norm * key_normal, axis=(0, 1))
        grad_key = (
            norm_backward(grad_key_norm * gain_key, key_normal, key_scale)
            .astype(jnp.bfloat16)
            .reshape(rows, local_groups * HEAD_SIZE)
        )
        grad_value = local_values.astype(jnp.bfloat16).reshape(rows, local_groups * HEAD_SIZE)
        sum_query = sum_query + outer_sum(normed_input, grad_query)
        sum_key = sum_key + outer_sum(normed_input, grad_key)
        sum_value = sum_value + outer_sum(normed_input, grad_value)
        sum_headgate = sum_headgate + outer_sum(normed_input, grad_logits)
        grad_partial = (
            times_transpose(grad_query, w_query)
            + times_transpose(grad_key, key_projection_weight)
            + times_transpose(grad_value, value_projection_weight)
            + times_transpose(grad_logits, w_head)
        )
        grad_normed = lax.psum(grad_partial.astype(jnp.bfloat16), "kv").astype(jnp.float32)
        sum_attention_gain = sum_attention_gain + jnp.sum(grad_normed * normal_a, axis=0)
        grad_input = grad_hidden + norm_backward(grad_normed * gain_a, normal_a, scale_a)
        input_grads.append(grad_input.astype(jnp.bfloat16))
    (
        attention_total,
        feedforward_total,
        query_total,
        key_total,
        value_total,
        headgate_total,
        output_total,
        gate_total,
        upward_total,
        down_total,
    ) = (
        lax.psum_scatter(
            sum_attention_gain.astype(jnp.bfloat16), "seq", scatter_dimension=0, tiled=True
        ).astype(jnp.float32),
        lax.psum_scatter(
            sum_feedforward_gain.astype(jnp.bfloat16), "seq", scatter_dimension=0, tiled=True
        ).astype(jnp.float32),
        lax.psum_scatter(
            sum_query.astype(jnp.bfloat16), "seq", scatter_dimension=0, tiled=True
        ).astype(jnp.float32),
        lax.psum_scatter(
            sum_key.astype(jnp.bfloat16), "seq", scatter_dimension=0, tiled=True
        ).astype(jnp.float32),
        lax.psum_scatter(
            sum_value.astype(jnp.bfloat16), "seq", scatter_dimension=0, tiled=True
        ).astype(jnp.float32),
        lax.psum_scatter(
            sum_headgate.astype(jnp.bfloat16), "seq", scatter_dimension=0, tiled=True
        ).astype(jnp.float32),
        lax.psum_scatter(
            sum_output.astype(jnp.bfloat16), "seq", scatter_dimension=1, tiled=True
        ).astype(jnp.float32),
        lax.psum_scatter(
            sum_gate.astype(jnp.bfloat16), "seq", scatter_dimension=0, tiled=True
        ).astype(jnp.float32),
        lax.psum_scatter(
            sum_upward.astype(jnp.bfloat16), "seq", scatter_dimension=0, tiled=True
        ).astype(jnp.float32),
        lax.psum_scatter(
            sum_down.astype(jnp.bfloat16), "seq", scatter_dimension=1, tiled=True
        ).astype(jnp.float32),
    )
    query_gain_total, key_gain_total = lax.psum((sum_query_gain, sum_key_gain), ("seq", "kv"))
    return (
        jnp.stack(results, axis=0),
        jnp.stack(input_grads, axis=0),
        attention_total,
        feedforward_total,
        query_gain_total,
        key_gain_total,
        query_total,
        key_total,
        value_total,
        headgate_total,
        output_total,
        gate_total,
        upward_total,
        down_total,
    )


BF = jnp.bfloat16
F32 = jnp.float32
ANY = pl.BlockSpec(memory_space=pl.ANY)
VM = pl.BlockSpec(memory_space=pltpu.VMEM)
DMA = pltpu.SemaphoreType.DMA


def place():
    s = lax.axis_index("seq")
    k = lax.axis_index("kv")
    return (lax.div(s, 2), lax.rem(s, 2), lax.div(k, 2), lax.rem(k, 2))


def device(l, x, y, c):
    return (l * 2 + x, y * 2 + c)


def remote(src, dst, send, recv, target):
    return pltpu.make_async_remote_copy(
        src_ref=src,
        dst_ref=dst,
        send_sem=send,
        recv_sem=recv,
        device_id=target,
        device_id_type=pl.DeviceIdType.MESH,
    )


def greet(partners):
    barrier = pltpu.get_barrier_semaphore()
    count = 0
    for target, there in partners:

        def call(target=target):
            pl.semaphore_signal(
                barrier, inc=1, device_id=target, device_id_type=pl.DeviceIdType.MESH
            )

        if there is None:
            call()
            count = count + 1
        else:
            pl.when(there)(call)
            count = count + jnp.where(there, 1, 0)
    pl.semaphore_wait(barrier, count)


class Line:
    def __init__(self, length, g, ag_send, ag_recv, land=None, rs_send=None, rs_recv=None):
        self.n = length
        self.g, self.ag_send, self.ag_recv = g, ag_send, ag_recv
        self.land, self.rs_send, self.rs_recv = land, rs_send, rs_recv
        self.l, self.x, self.y, self.c = place()

    def partners(self):
        l, x, y, c = self.l, self.x, self.y, self.c
        return [
            (device(l - 1, x, y, c), l >= 1),
            (device(l + 1, x, y, c), l <= self.n - 2),
        ]

    def block(self, item, b):
        return self.g.at[item, pl.ds(2 * b, 2)]

    def _ag(self, item, way, b):
        step = -1 if way == 0 else 1
        return remote(
            self.block(item, b),
            self.block(item, b),
            self.ag_send.at[item, way, b],
            self.ag_recv.at[item, b],
            device(self.l + step, self.x, self.y, self.c),
        )

    def ag_start(self, item):
        l = self.l
        pl.when(l >= 1)(lambda: self._ag(item, 0, l).start())
        pl.when(l <= self.n - 2)(lambda: self._ag(item, 1, l).start())

    def ag_step(self, item, t):
        l, n = self.l, self.n

        @pl.when(l + t <= n - 1)
        def _():
            self._ag(item, 0, l + t).wait_recv()
            pl.when(l >= 1)(lambda: self._ag(item, 0, l + t).start())

        @pl.when(l - t >= 0)
        def _():
            self._ag(item, 1, l - t).wait_recv()
            pl.when(l <= n - 2)(lambda: self._ag(item, 1, l - t).start())

    def pump(self, item, t):
        l, n = self.l, self.n

        @pl.when((l + t <= n - 1) & (l >= 1))
        def _():
            self._ag(item, 0, l + t).wait_recv()
            self._ag(item, 0, l + t).start()

        @pl.when((l - t >= 0) & (l <= n - 2))
        def _():
            self._ag(item, 1, l - t).wait_recv()
            self._ag(item, 1, l - t).start()

    def collect(self, item):
        l, n = self.l, self.n
        for t in range(1, n):
            pl.when(l == 0)(lambda t=t: self._ag(item, 0, t).wait_recv())
            pl.when(l == n - 1)(lambda t=t: self._ag(item, 1, n - 1 - t).wait_recv())

    def ag_end(self, item):
        l, n = self.l, self.n
        for b in range(n):
            pl.when((l >= 1) & (l <= b))(lambda b=b: self._ag(item, 0, b).wait_send())
            pl.when((l <= n - 2) & (l >= b))(lambda b=b: self._ag(item, 1, b).wait_send())

    def _slot(self, item, slot):
        return self.land.at[item, pl.ds(2 * slot, 2)]

    def _rs(self, item, way, o):
        if way == 0:
            target = self.l - 1
            slot = jnp.where(target == o, self.n, o)
        else:
            target = self.l + 1
            slot = o
        return remote(
            self.block(item, o),
            self._slot(item, slot),
            self.rs_send.at[item, way, o],
            self.rs_recv.at[item, slot],
            device(target, self.x, self.y, self.c),
        )

    def _take(self, item, o, slot):
        here = self._slot(item, slot)
        pltpu.make_async_copy(here, here, self.rs_recv.at[item, slot]).wait()
        for h in range(2):
            total = self.g[item, 2 * o + h].astype(F32) + self.land[item, 2 * slot + h].astype(F32)
            self.g[item, 2 * o + h] = total.astype(BF)

    def rs_step(self, item, q):
        l, n = self.l, self.n
        right, left = n - q, q - 1

        @pl.when(l < right)
        def _():
            pl.when(l >= 1)(lambda: self._take(item, right, right))
            self._rs(item, 1, right).start()

        @pl.when(l > left)
        def _():
            pl.when(l <= n - 2)(lambda: self._take(item, left, left))
            self._rs(item, 0, left).start()

    def rs_final(self, item):
        l, n = self.l, self.n
        pl.when(l >= 1)(lambda: self._take(item, l, l))
        pl.when(l <= n - 2)(lambda: self._take(item, l, n))

    def rs_end(self, item):
        l, n = self.l, self.n
        for o in range(n):
            pl.when(l < o)(lambda o=o: self._rs(item, 1, o).wait_send())
            pl.when(l > o)(lambda o=o: self._rs(item, 0, o).wait_send())


def each(count, body):
    def step(i, unused):
        body(i)
        return 0

    lax.fori_loop(0, count, step, 0)


class Pair:
    def __init__(self, line, refs, send, recv, local, half):
        self.line, self.refs = line, refs
        self.send, self.recv, self.local, self.half = send, recv, local, half

    def partner(self):
        line = self.line
        return (device(line.l, 1 - line.x, line.y, line.c), None)

    def _part(self, ref, kind, j, x):
        at = pl.multiple_of(x * self.half + j * 256, 256)
        return ref.at[pl.ds(at, 256), :] if kind == 2 else ref.at[:, pl.ds(at, 256)]

    def _copies(self, item, kind, j):
        line = self.line
        mine = line.g.at[item, 2 * line.l + line.x]
        out = remote(
            self._part(self.refs[kind], kind, j, 1 - line.x),
            mine,
            self.send.at[item],
            self.recv.at[item],
            self.partner()[0],
        )
        here = pltpu.make_async_copy(
            self._part(self.refs[kind], kind, j, line.x), mine, self.local.at[item]
        )
        return out, here

    def start(self, item, kind, j):
        for copy in self._copies(item, kind, j):
            copy.start()

    def end(self, item, kind, j):
        out, here = self._copies(item, kind, j)
        here.wait()
        out.wait_send()
        out.wait_recv()


class Back(Pair):
    def _copies(self, item, kind, j):
        line = self.line
        home = self._part(self.refs[kind], kind, j, line.x)
        out = remote(
            line.g.at[item, 2 * line.l + 1 - line.x],
            home,
            self.send.at[item],
            self.recv.at[item],
            self.partner()[0],
        )
        here = pltpu.make_async_copy(
            line.g.at[item, 2 * line.l + line.x], home, self.local.at[item]
        )
        return out, here


def back_wait(back, item, kind, j):
    line = back.line
    out, here = back._copies(item, kind, j)
    here.wait()
    out.wait_send()
    there = back._part(back.refs[kind], kind, j, 1 - line.x)
    pltpu.make_async_copy(there, there, back.recv.at[item]).wait()


def dot(a, b):
    return lax.dot_general(a, b, (((1,), (0,)), ((), ())), preferred_element_type=F32)


def dot_t(a, b):
    return lax.dot_general(a, b, (((1,), (1,)), ((), ())), preferred_element_type=F32)


def head_kernel(
    n,
    x_any,
    z_any,
    wq,
    wkv,
    wo,
    wg,
    wu,
    wd,
    small,
    cos_ref,
    sin_ref,
    row_lo,
    row_hi,
    g_out,
    own_out,
    normed_out,
    kv_out,
    q_out,
    qp_out,
    kp_out,
    gate_out,
    att_out,
    lse_out,
    hidden_out,
    inner_out,
    dz_out,
    small_out,
    x_v,
    normed,
    g,
    own_g,
    small_g,
    gain_row,
    heads_row,
    kv,
    q_v,
    qp,
    kp,
    gate_v,
    att,
    tot,
    part,
    core_land,
    low,
    chip_land,
    inner,
    hidden,
    p_send,
    p_recv,
    p_loc,
    ag_send,
    ag_recv,
    sp_sem,
    sa_send,
    sa_recv,
    t_send,
    t_recv,
    z_send,
    z_recv,
    kv_send,
    kv_recv,
    c_send,
    c_recv,
    s_send,
    s_recv,
    i_send,
    i_recv,
    j_send,
    j_recv,
    o_loc,
):
    line = Line(n, g, ag_send, ag_recv)
    l, x, y, c = line.l, line.x, line.y, line.c
    k = y * 2 + c
    group = Group()
    across, mate = device(l, 1 - x, y, c), group.mate
    right = device(l + 1, x, y, c)
    tiny = Line(n, small_g, sa_send, sa_recv)
    scale = HEAD_SIZE ** (-0.5)
    late = 9
    first = Pair(line, (wq, wkv, wo), p_send, p_recv, p_loc, 256)
    rest = Pair(line, (wg, wu, wd), p_send, p_recv, p_loc, 768)

    def swap(item):
        if item < 3:
            return first, item, item, 0
        return rest, item, item % 3, item // 3 - 1

    def swap_start(item):
        pair, item, kind, j = swap(item)
        pair.start(item, kind, j)

    def swap_end(item):
        pair, item, kind, j = swap(item)
        pair.end(item, kind, j)

    outs = []

    def put(src, dst):
        copy = pltpu.make_async_copy(src, dst, o_loc.at[len(outs)])
        copy.start()
        outs.append(copy)

    greet(line.partners() + [(mate, None)] + [(group.chip(i), None) for i in (1, 2, 3)])

    small_here = small_g.at[0, 2 * l + x]
    small_out_copy = remote(small, small_here, sp_sem.at[0], sp_sem.at[1], across)
    small_own = pltpu.make_async_copy(small, small_here, sp_sem.at[2])
    small_out_copy.start()
    small_own.start()
    swap_start(0)
    swap_start(1)
    own_x = pltpu.make_async_copy(x_any, x_v.at[:, x], t_send.at[2])
    own_x.start()
    halves = pl.ds(2 * c, 2)
    x_out = remote(x_any.at[halves], x_v.at[halves, x], t_send.at[0], t_recv.at[0], across)
    x_part = x_v.at[halves, 1 - x]
    x_on = remote(x_part, x_part, t_send.at[1], t_recv.at[1], mate)
    x_out.start()
    for item in range(2, 6):
        swap_start(item)
    z_out = remote(z_any.at[halves], dz_out.at[halves], z_send.at[0], z_recv.at[0], across)
    z_part = dz_out.at[halves]
    z_on = remote(z_part, z_part, z_send.at[1], z_recv.at[1], mate)
    z_out.start()
    for item in range(6, 12):
        swap_start(item)

    small_own.wait()
    small_out_copy.wait()
    tiny.ag_start(0)
    for item in range(3):
        swap_end(item)
        line.ag_start(item)
    for t in range(1, n):
        tiny.ag_step(0, t)
    for s in range(2 * n):
        cols = slice(s * 256, (s + 1) * 256)
        heads_row[:, cols] = small_g[0, s]
        gain_row[:, cols] = small_g[0, s, 4:6, :].astype(F32)

    def norm(m, side):
        v = x_v[m, side].reshape(128, 256 * 2 * n).astype(F32)
        mean = jnp.mean(v * v, axis=-1, keepdims=True)
        v = v * lax.rsqrt(mean + EPS) * gain_row[0:1, :]
        normed[m, side] = v.astype(BF)

    own_x.wait()
    each(4, lambda m: norm(m, x))
    line.pump(0, 1)
    line.pump(1, 1)
    x_out.wait_recv()
    x_on.start()
    line.pump(0, 2)
    line.pump(1, 2)
    line.pump(2, 1)
    x_on.wait_recv()
    each(4, lambda m: norm(m, 1 - x))
    for item in (3, 4):
        swap_end(item)
        line.ag_start(item)
    for item in (0, 1):
        line.pump(item, 3)
        line.collect(item)
    line.pump(2, 2)

    def project(m):
        a = normed[m].reshape(256, 256 * 2 * n)
        qf = dot(a, g[0].reshape(256 * 2 * n, 256))
        kf = dot(a, g[1].reshape(256 * 2 * n, 256))
        gate_v[m] = jax.nn.sigmoid(dot_t(a, heads_row[...]))
        qp[m] = qf
        kp[m] = kf[:, :128]
        cosine, sine = cos_ref[m], sin_ref[m]

        def turn(u, gain):
            u = u * lax.rsqrt(jnp.mean(u * u, axis=-1, keepdims=True) + EPS) * gain
            return (u * cosine + pltpu.roll(u, 64, 1) * sine).astype(BF)

        gains = small[8:10, :128].astype(F32)
        q_v[m, :256] = turn(qf[:, :128], gains[0:1])
        q_v[m, 256:] = turn(qf[:, 128:], gains[0:1])
        kv[l, m, :, :128] = turn(kf[:, :128], gains[1:2])
        kv[l, m, :, 128:] = kf[:, 128:].astype(BF)
        pl.when(l <= n - 2)(lambda: send_kv(l, m).start())

    def send_kv(b, m):
        return remote(kv.at[b, m], kv.at[b, m], kv_send.at[b, m], kv_recv.at[b, m], right)

    each(4, project)
    put(normed, normed_out)
    put(qp, qp_out)
    put(kp, kp_out)
    put(gate_v, gate_out)
    put(q_v, q_out)

    def attend(m, b, diagonal):
        pair = kv[b, m]
        raw = dot_t(q_v[m], pair[:, :128]) * scale
        lo = row_lo[m][:, :1] - b * 256
        hi = row_hi[m][:, :1] - b * 256
        column = lax.broadcasted_iota(jnp.int32, (512, 256), 1)
        allowed = (column >= jnp.concatenate([lo, lo], axis=0)) & (
            column < jnp.concatenate([hi, hi], axis=0)
        )
        e = jnp.where(allowed, jnp.exp(raw), 0.0)
        total = jnp.sum(e, axis=-1, keepdims=True)
        value = dot(e.astype(BF), pair[:, 128:])
        total = jnp.broadcast_to(total, (512, 128))
        if diagonal:
            tot[m] = total
            att[m] = value
        else:
            tot[m] += total
            att[m] += value

    def kv_round(t):
        @pl.when(l - t >= 0)
        def _():
            b = l - t

            def take(m):
                send_kv(b, m).wait_recv()
                pl.when(l <= n - 2)(lambda: send_kv(b, m).start())

            each(4, take)
            each(4, lambda m: attend(m, b, False))

    line.pump(2, 3)
    each(4, lambda m: attend(m, l, True))
    line.pump(3, 1)
    line.pump(4, 1)
    kv_round(1)
    for item in (5,):
        swap_end(item)
        line.ag_start(item)
    line.pump(3, 2)
    line.pump(4, 2)
    line.pump(3, 3)
    kv_round(2)
    swap_end(6)
    line.ag_start(6)
    line.pump(4, 3)
    line.pump(5, 1)
    line.pump(5, 2)
    kv_round(3)
    line.collect(2)

    def mate_copy(m):
        return remote(
            part.at[m, :, :, 1 - c], core_land.at[m], c_send.at[m], c_recv.at[m], mate
        )

    def branch(m):
        total = tot[m]
        lse = jnp.log(total)
        value = att[m] / total
        att[m] = value
        tot[m] = lse
        gates = gate_v[m]
        lo, hi = gates[:, 0:2], gates[:, 2:4]
        gates = jnp.where(x == 0, lo, hi)
        mixed = jnp.concatenate(
            [value[:256] * gates[:, 0:1], value[256:] * gates[:, 1:2]], axis=1
        ).astype(BF)
        for s in range(2 * n):
            part[m, :, :, :, :, s * 256 : (s + 1) * 256] = (
                dot(mixed, g[2, s]).astype(BF).reshape(2, 2, 2, 32, 256)
            )
        mate_copy(m).start()

    each(4, branch)
    put(att, att_out)
    put(tot, lse_out)
    put(kv, kv_out)
    swap_end(7)
    line.ag_start(7)
    line.pump(5, 3)
    line.pump(6, 1)

    def chip_copy(m, o):
        ox, oy = group.other(o)
        return remote(
            low.at[m, ox, oy],
            chip_land.at[o - 1, m],
            s_send.at[m, o - 1],
            s_recv.at[m, o - 1],
            group.chip(o),
        )

    def to_chips(m):
        mate_copy(m).wait_recv()
        for u in range(2):
            for v in range(2):
                low[m, u, v] = (
                    part[m, u, v, c].astype(F32) + core_land[m, u, v].astype(F32)
                ).astype(BF)
        for o in (3, 1, 2):
            chip_copy(m, o).start()

    each(4, to_chips)
    line.pump(6, 2)
    swap_end(8)
    line.ag_start(8)
    line.pump(6, 3)
    line.pump(7, 1)

    def inner_copy(m, o):
        here = inner.at[m, x, y, c]
        return remote(
            here, here, i_send.at[m, o - 1], i_recv.at[m, o - 1], group.chip(o)
        )

    def inner_mate(m, o):
        ox, oy = group.other(o)
        there = inner.at[m, ox, oy, c]
        return remote(there, there, j_send.at[m, o], j_recv.at[m, o], mate)

    def finish(m):
        total = low[m, x, y].astype(F32)
        for o in (1, 2, 3):
            chip_copy(m, o).wait_recv()
            total = total + chip_land[o - 1, m].astype(F32)
        h = x_v[m, x, k].astype(F32) + total
        hidden[m] = h
        mean = jnp.mean(h * h, axis=-1, keepdims=True)
        inner[m, x, y, c] = (h * lax.rsqrt(mean + EPS) * gain_row[1:2, :]).astype(BF)
        for o in (3, 1, 2):
            inner_copy(m, o).start()
        inner_mate(m, 0).start()

    each(4, finish)
    put(hidden, hidden_out)
    line.pump(7, 2)
    line.pump(7, 3)
    line.pump(8, 1)
    z_out.wait_recv()
    z_on.start()

    def pass_on(m):
        for o in (1, 2, 3):
            inner_copy(m, o).wait_recv()
            inner_mate(m, o).start()

    each(4, pass_on)
    line.pump(8, 2)
    for item in (9, 10, 11):
        swap_end(item)
        put(g.at[item, pl.ds(2 * l, 2)], own_out.at[item - 9])
    line.pump(8, 3)

    def arrive(m):
        for o in range(4):
            inner_mate(m, o).wait_recv()

    each(4, arrive)
    put(inner, inner_out)
    put(small_g, small_out)
    for item in range(3, 9):
        line.collect(item)
    put(g.at[pl.ds(0, 9)], g_out)

    small_out_copy_done = None
    own_waits = [x_out, x_on, z_out, z_on]
    for copy in own_waits:
        copy.wait_send()
    z_on.wait_recv()
    tiny.ag_end(0)
    each(9, line.ag_end)

    def drain(m):
        mate_copy(m).wait_send()
        for o in (1, 2, 3):
            chip_copy(m, o).wait_send()
            inner_copy(m, o).wait_send()
        for o in range(4):
            inner_mate(m, o).wait_send()
        for b in range(n):
            pl.when((l >= b) & (l <= n - 2))(lambda b=b: send_kv(b, m).wait_send())

    each(4, drain)
    for copy in outs:
        copy.wait()


def head(n, x_in, z_in, wq, wkv, wo, wg, wu, wd, small, cosine, sine, row_lo, row_hi):
    d = x_in.shape[-1]
    m = 2 * n
    bf = lambda *shape: jax.ShapeDtypeStruct(shape, BF)
    f32 = lambda *shape: jax.ShapeDtypeStruct(shape, F32)
    vb = lambda *shape: pltpu.VMEM(shape, BF)
    vf = lambda *shape: pltpu.VMEM(shape, F32)
    return pl.pallas_call(
        functools.partial(head_kernel, n),
        out_shape=(
            bf(9, m, 256, 256),
            bf(3, 2, 256, 256),
            bf(4, 2, 128, d),
            bf(n, 4, 256, 256),
            bf(4, 512, 128),
            f32(4, 256, 256),
            f32(4, 256, 128),
            f32(4, 256, 16),
            f32(4, 512, 128),
            f32(4, 512, 128),
            f32(4, 32, d),
            bf(4, 2, 2, 2, 32, d),
            bf(4, 4, 32, d),
            bf(1, m, 16, 256),
        ),
        in_specs=[ANY] * 8 + [VM] * 5,
        out_specs=(ANY,) * 14,
        scratch_shapes=[
            vb(4, 2, 4, 32, d),
            vb(4, 2, 128, d),
            vb(12, m, 256, 256),
            vb(1, 16, 128),
            vb(1, m, 16, 256),
            vf(2, d),
            vb(16, d),
            vb(n, 4, 256, 256),
            vb(4, 512, 128),
            vf(4, 256, 256),
            vf(4, 256, 128),
            vf(4, 256, 16),
            vf(4, 512, 128),
            vf(4, 512, 128),
            vb(4, 2, 2, 2, 32, d),
            vb(4, 2, 2, 32, d),
            vb(4, 2, 2, 32, d),
            vb(3, 4, 32, d),
            vb(4, 2, 2, 2, 32, d),
            vf(4, 32, d),
            DMA((12,)),
            DMA((12,)),
            DMA((12,)),
            DMA((12, 2, n)),
            DMA((12, n)),
            DMA((3,)),
            DMA((1, 2, n)),
            DMA((1, n)),
            DMA((3,)),
            DMA((2,)),
            DMA((2,)),
            DMA((2,)),
            DMA((n, 4)),
            DMA((n, 4)),
            DMA((4,)),
            DMA((4,)),
            DMA((4, 3)),
            DMA((4, 3)),
            DMA((4, 3)),
            DMA((4, 3)),
            DMA((4, 4)),
            DMA((4, 4)),
            DMA((16,)),
        ],
        compiler_params=pltpu.CompilerParams(
            collective_id=0, has_side_effects=True, vmem_limit_bytes=62 * 2**20
        ),
        name="head",
    )(x_in, z_in, wq, wkv, wo, wg, wu, wd, small, cosine, sine, row_lo, row_hi)


def keys_back_kernel(n, part_ref, out_ref, work, land, send, recv, local):
    l, x, y, c = place()
    left, right = device(l - 1, x, y, c), device(l + 1, x, y, c)
    greet([(left, l >= 1), (right, l <= n - 2)])
    load = pltpu.make_async_copy(part_ref, work, local)
    load.start()
    load.wait()

    def copy(o):
        return remote(work.at[o], land.at[o], send.at[o], recv.at[o], left)

    def take(o):
        copy(o).wait_recv()

        def add(i, unused):
            at = pl.ds(pl.multiple_of(i * 128, 128), 128)
            work[o, at] = (work[o, at].astype(F32) + land[o, at].astype(F32)).astype(BF)
            return 0

        lax.fori_loop(0, work.shape[1] // 128, add, 0)

    for o in range(n - 1):

        @pl.when(l > o)
        def _(o=o):
            pl.when(l <= n - 2)(lambda: take(o))
            copy(o).start()

    pl.when(l <= n - 2)(lambda: take(l))
    out_ref[...] = work[l]
    for o in range(n - 1):
        pl.when(l > o)(lambda o=o: copy(o).wait_send())


def keys_back(n, parts):
    return pl.pallas_call(
        functools.partial(keys_back_kernel, n),
        out_shape=jax.ShapeDtypeStruct(parts.shape[1:], BF),
        in_specs=[ANY],
        out_specs=VM,
        scratch_shapes=[
            pltpu.VMEM(parts.shape, BF),
            pltpu.VMEM(parts.shape, BF),
            DMA((n,)),
            DMA((n,)),
            DMA,
        ],
        compiler_params=pltpu.CompilerParams(
            collective_id=2, has_side_effects=True, vmem_limit_bytes=40 * 2**20
        ),
        name="keys_back",
    )(parts)


class Group:
    def __init__(self):
        self.l, self.x, self.y, self.c = place()
        self.mate = device(self.l, self.x, self.y, 1 - self.c)

    def other(self, i):
        x = 1 - self.x if i & 1 else self.x
        y = 1 - self.y if i & 2 else self.y
        return x, y

    def chip(self, i):
        x, y = self.other(i)
        return device(self.l, x, y, self.c)

    def partners(self):
        return [(self.mate, None)] + [(self.chip(i), None) for i in (1, 2, 3)]


def sum_kernel(m, part_ref, out_ref, core_land, low, chip_land, c_send, c_recv, s_send, s_recv):
    group = Group()
    x, y, c = group.x, group.y, group.c
    greet(group.partners())
    pairs = [(i, b) for b in range(4) for i in range(m)]

    def to_mate(i, b):
        return remote(
            part_ref.at[i, b, :, :, 1 - c],
            core_land.at[i, b],
            c_send.at[i, b],
            c_recv.at[i, b],
            group.mate,
        )

    def to_chip(i, b, o):
        ox, oy = group.other(o)
        return remote(
            low.at[i, b, ox, oy],
            chip_land.at[i, o - 1, b],
            s_send.at[i, b, o - 1],
            s_recv.at[i, b, o - 1],
            group.chip(o),
        )

    for i, b in pairs:
        to_mate(i, b).start()
    for i, b in pairs:
        to_mate(i, b).wait_recv()
        for u in range(2):
            for v in range(2):
                low[i, b, u, v] = (
                    part_ref[i, b, u, v, c].astype(F32) + core_land[i, b, u, v].astype(F32)
                ).astype(BF)
        for o in (3, 1, 2):
            to_chip(i, b, o).start()
    for i, b in pairs:
        total = low[i, b, x, y].astype(F32)
        for o in (1, 2, 3):
            to_chip(i, b, o).wait_recv()
            total = total + chip_land[i, o - 1, b].astype(F32)
        out_ref[i, b] = total
    for i, b in pairs:
        to_mate(i, b).wait_send()
        for o in (1, 2, 3):
            to_chip(i, b, o).wait_send()


def group_sum(part, collective):
    m, d = part.shape[0], part.shape[-1]
    return pl.pallas_call(
        functools.partial(sum_kernel, m),
        out_shape=jax.ShapeDtypeStruct((m, 4, 32, d), F32),
        in_specs=[VM],
        out_specs=VM,
        scratch_shapes=[
            pltpu.VMEM((m, 4, 2, 2, 32, d), BF),
            pltpu.VMEM((m, 4, 2, 2, 32, d), BF),
            pltpu.VMEM((m, 3, 4, 32, d), BF),
            DMA((m, 4)),
            DMA((m, 4)),
            DMA((m, 4, 3)),
            DMA((m, 4, 3)),
        ],
        compiler_params=pltpu.CompilerParams(
            collective_id=collective, has_side_effects=True, vmem_limit_bytes=56 * 2**20
        ),
        name=f"group_sum{m}",
    )(part)


def spread_kernel(own_ref, out_ref, s_send, s_recv, c_send, c_recv, local):
    group = Group()
    x, y, c = group.x, group.y, group.c
    greet(group.partners())
    mine = out_ref.at[:, x, y, c]
    keep = pltpu.make_async_copy(own_ref, mine, local)
    keep.start()

    def to_chip(o):
        return remote(own_ref, mine, s_send.at[o - 1], s_recv.at[o - 1], group.chip(o))

    def to_mate(o):
        ox, oy = group.other(o)
        part = out_ref.at[:, ox, oy, c]
        src = own_ref if o == 0 else part
        return remote(src, part, c_send.at[o], c_recv.at[o], group.mate)

    for o in (3, 1, 2):
        to_chip(o).start()
    to_mate(0).start()
    for o in (1, 2, 3):
        to_chip(o).wait_recv()
        to_mate(o).start()
    keep.wait()
    for o in (1, 2, 3):
        to_chip(o).wait_send()
    for o in range(4):
        to_mate(o).wait()


def group_spread(own, collective):
    b, r, d = own.shape
    return pl.pallas_call(
        spread_kernel,
        out_shape=jax.ShapeDtypeStruct((b, 2, 2, 2, r, d), own.dtype),
        in_specs=[VM],
        out_specs=ANY,
        scratch_shapes=[DMA((3,)), DMA((3,)), DMA((4,)), DMA((4,)), DMA],
        compiler_params=pltpu.CompilerParams(collective_id=collective, has_side_effects=True),
        name="group_spread",
    )(own)


def home_kernel(own_ref, out_ref, s_send, s_recv, local):
    group = Group()
    l, x, y, c = group.l, group.x, group.y, group.c
    others = [device(l, x, y, 1 - c), device(l, x, 1 - y, c), device(l, x, 1 - y, 1 - c)]
    greet([(o, None) for o in others])
    mine = out_ref.at[:, :, y, c]
    keep = pltpu.make_async_copy(own_ref, mine, local)
    keep.start()
    copies = [
        remote(own_ref, mine, s_send.at[i], s_recv.at[i], o) for i, o in enumerate(others)
    ]
    for copy in copies:
        copy.start()
    keep.wait()
    for copy in copies:
        copy.wait()


def home(own):
    m, b, r, d = own.shape
    return pl.pallas_call(
        home_kernel,
        out_shape=jax.ShapeDtypeStruct((m, b, 2, 2, r, d), own.dtype),
        in_specs=[VM],
        out_specs=ANY,
        scratch_shapes=[DMA((3,)), DMA((3,)), DMA],
        compiler_params=pltpu.CompilerParams(collective_id=7, has_side_effects=True),
        name="home",
    )(own)


def rows_kernel(
    n, part_ref, ffn_ref, dq, dkv, do, dg, du, dd, g, land, rs_send, rs_recv, b_send, b_recv, b_loc, local
):
    line = Line(n, g, None, None, land, rs_send, rs_recv)
    small = Back(line, (dq, dkv, do), b_send, b_recv, b_loc, 256)
    large = Back(line, (dg, du, dd), b_send, b_recv, b_loc, 512)
    greet(line.partners() + [small.partner()])
    loads = [
        pltpu.make_async_copy(ffn_ref, g.at[pl.ds(3, 6)], local.at[1]),
        pltpu.make_async_copy(part_ref, g.at[pl.ds(0, 3)], local.at[0]),
    ]
    for load in loads:
        load.start()
    for load in loads:
        load.wait()
    for q in range(1, n):
        each(9, lambda item, q=q: line.rs_step(item, q))
    each(9, line.rs_final)
    for item in range(9):
        if item < 3:
            small.start(item, item, 0)
        else:
            large.start(item, item % 3, item // 3 - 1)
    for item in range(9):
        if item < 3:
            back_wait(small, item, item, 0)
        else:
            back_wait(large, item, item % 3, item // 3 - 1)
    each(9, line.rs_end)


def rows_sum(n, parts, ffn_parts):
    bf = lambda *shape: jax.ShapeDtypeStruct(shape, BF)
    return pl.pallas_call(
        functools.partial(rows_kernel, n),
        out_shape=(bf(256, 512), bf(256, 512), bf(512, 256), bf(256, 1024), bf(256, 1024), bf(1024, 256)),
        in_specs=[ANY] * 2,
        out_specs=(ANY,) * 6,
        scratch_shapes=[
            pltpu.VMEM((9, 2 * n, 256, 256), BF),
            pltpu.VMEM((9, 2 * n + 2, 256, 256), BF),
            DMA((9, 2, n)),
            DMA((9, n + 1)),
            DMA((9,)),
            DMA((9,)),
            DMA((9,)),
            DMA((2,)),
        ],
        compiler_params=pltpu.CompilerParams(
            collective_id=8, has_side_effects=True, vmem_limit_bytes=40 * 2**20
        ),
        name="rows_sum",
    )(parts, ffn_parts)


def ffn_kernel(
    n,
    inner_any,
    z_own,
    z_other,
    g_in,
    own_in,
    out_ref,
    din_ref,
    part_out,
    dgw,
    duw,
    ddw,
    inner_ref,
    dz_ref,
    inner_t,
    out_acc,
    din_acc,
    g,
    land,
    low,
    prod_t,
    ag_send,
    ag_recv,
    rs_send,
    rs_recv,
    b_send,
    b_recv,
    b_loc,
    in_loc,
    o_loc,
):
    chunks = 3
    line = Line(n, g, ag_send, ag_recv, land, rs_send, rs_recv)
    l, x = line.l, line.x
    blocks = 2 * n
    width = blocks * 256
    back = Back(line, (dgw, duw, ddw), b_send, b_recv, b_loc, 256)
    loads = [
        pltpu.make_async_copy(own_in, g.at[pl.ds(6, 3), pl.ds(2 * l, 2)], in_loc.at[0]),
        pltpu.make_async_copy(inner_any, inner_ref, in_loc.at[1]),
        pltpu.make_async_copy(z_own, dz_ref.at[:, x], in_loc.at[2]),
        pltpu.make_async_copy(z_other, dz_ref.at[:, 1 - x], in_loc.at[3]),
        pltpu.make_async_copy(g_in.at[pl.ds(3, 6)], g.at[pl.ds(0, 6)], in_loc.at[4]),
    ]
    for copy in loads:
        copy.start()
    greet(line.partners() + [back.partner()])
    loads[0].wait()
    for item in range(6, 9):
        line.ag_start(item)
    for copy in loads[1:]:
        copy.wait()

    def turn(i, unused):
        m, s = lax.div(i, blocks), lax.rem(i, blocks)
        tile = inner_ref[m, :, pl.ds(pl.multiple_of(s * 256, 256), 256)]
        inner_t[s, :, pl.ds(pl.multiple_of(m * 256, 256), 256)] = tile.T
        return 0

    lax.fori_loop(0, 4 * blocks, turn, 0)

    def compute(j):
        base = 3 * j

        def rows(m, unused):
            a = inner_ref[m]
            d = dz_ref[m].reshape(256, width)
            gated = dot(a, g[base].reshape(width, 256))
            upward = dot(a, g[base + 1].reshape(width, 256))
            grad = dot_t(d[:, :256], g[base + 2, 0])
            for s in range(1, blocks):
                grad = grad + dot_t(d[:, s * 256 : (s + 1) * 256], g[base + 2, s])
            sigma = jax.nn.sigmoid(gated)
            swish = gated * sigma
            product = (swish * upward).astype(BF)
            d_gated = (grad * upward * sigma * (1.0 + gated * (1.0 - sigma))).astype(BF)
            d_upward = (grad * swish).astype(BF)
            at = pl.ds(pl.multiple_of(m * 256, 256), 256)
            low[0, at] = d_gated
            low[1, at] = d_upward
            prod_t[:, at] = product.T
            for s in range(blocks):
                cols = slice(s * 256, (s + 1) * 256)
                o = dot(product, g[base + 2, s])
                i = dot_t(d_gated, g[base, s]) + dot_t(d_upward, g[base + 1, s])
                if j == 0:
                    out_acc[m, :, cols] = o
                    din_acc[m, :, cols] = i
                else:
                    out_acc[m, :, cols] += o
                    din_acc[m, :, cols] += i
            return 0

        lax.fori_loop(0, 4, rows, 0)

        def weights(s, unused):
            t = inner_t[s]
            g[base, s] = dot(t, low[0]).astype(BF)
            g[base + 1, s] = dot(t, low[1]).astype(BF)
            z = dz_ref[:, :, :, :, pl.ds(pl.multiple_of(s * 256, 256), 256)].reshape(1024, 256)
            g[base + 2, s] = dot(prod_t[...], z).astype(BF)
            return 0

        lax.fori_loop(0, blocks, weights, 0)

    def items(j, body):
        each(3, lambda i: body(3 * j + i))

    compute(0)
    for t in range(1, n):
        items(2, lambda item, t=t: line.pump(item, t))
        items(0, lambda item, t=t: line.rs_step(item, t))
    compute(1)
    items(0, line.rs_final)
    for kind in range(3):
        back.start(kind, kind, 0)
    items(2, line.collect)
    items(2, line.ag_end)
    compute(2)
    parts = pltpu.make_async_copy(g.at[pl.ds(3, 6)], part_out, o_loc.at[2])
    parts.start()

    def flush(m, unused):
        inner_ref[m] = out_acc[m].astype(BF)
        dz_ref[m] = din_acc[m].astype(BF).reshape(2, 4, 32, width)
        return 0

    lax.fori_loop(0, 4, flush, 0)
    outs = [
        pltpu.make_async_copy(inner_ref, out_ref, o_loc.at[0]),
        pltpu.make_async_copy(dz_ref, din_ref, o_loc.at[1]),
        parts,
    ]
    for copy in outs[:2]:
        copy.start()
    for kind in range(3):
        back_wait(back, kind, kind, 0)
    items(0, line.rs_end)
    for copy in outs:
        copy.wait()


def ffn(n, inner, z_own, z_other, g_in, own_in):
    d = inner.shape[-1]
    m = 2 * n
    bf = lambda *shape: jax.ShapeDtypeStruct(shape, BF)
    vb = lambda *shape: pltpu.VMEM(shape, BF)
    return pl.pallas_call(
        functools.partial(ffn_kernel, n),
        out_shape=(
            bf(4, 256, d),
            bf(4, 2, 4, 32, d),
            bf(6, m, 256, 256),
            bf(256, 512),
            bf(256, 512),
            bf(512, 256),
        ),
        in_specs=[ANY] * 5,
        out_specs=(ANY,) * 6,
        scratch_shapes=[
            vb(4, 256, d),
            vb(4, 2, 4, 32, d),
            vb(m, 256, 1024),
            pltpu.VMEM((4, 256, d), F32),
            pltpu.VMEM((4, 256, d), F32),
            vb(9, m, 256, 256),
            vb(3, m + 2, 256, 256),
            vb(2, 1024, 256),
            vb(256, 1024),
            DMA((9, 2, n)),
            DMA((9, n)),
            DMA((3, 2, n)),
            DMA((3, n + 1)),
            DMA((3,)),
            DMA((3,)),
            DMA((3,)),
            DMA((5,)),
            DMA((3,)),
        ],
        compiler_params=pltpu.CompilerParams(
            collective_id=9, has_side_effects=True, vmem_limit_bytes=62 * 2**20
        ),
        name="ffn",
    )(inner, z_own, z_other, g_in, own_in)


def row_layout(index, buckets, lengths):
    ends = jnp.cumsum(buckets)
    starts = ends - buckets
    member = (index[:, None] >= starts[None, :]) & (index[:, None] < ends[None, :])
    position = index - jnp.sum(jnp.where(member, starts[None, :], 0), axis=1)
    limit = jnp.sum(jnp.where(member, lengths[None, :], 0), axis=1)
    return (None, position, limit)


def fast_local(
    inputs,
    cotangent,
    bucket_sizes,
    true_lengths,
    attention_gain,
    feedforward_gain,
    query_gain,
    key_gain,
    query_weight,
    key_matrix,
    value_matrix,
    headgate_weight,
    output_weight,
    gate_weight,
    up_weight,
    down_weight,
):
    batches, rows, width = inputs.shape
    n = lax.axis_size("seq") // 2
    seq, kv = lax.axis_index("seq"), lax.axis_index("kv")
    l, x = seq // 2, seq % 2
    scale = HEAD_SIZE ** (-0.5)
    span = 2 * rows
    gain_query = query_gain.astype(F32)
    gain_key = key_gain.astype(F32)

    own_small = jnp.concatenate(
        [
            headgate_weight.T,
            attention_gain[None],
            feedforward_gain[None],
            jnp.zeros((2, 256), BF),
            jnp.pad(jnp.stack([query_gain, key_gain]), ((0, 0), (0, 128))),
            jnp.zeros((6, 256), BF),
        ],
        axis=0,
    )
    paired = jnp.concatenate(
        [key_matrix[:, :128], value_matrix[:, :128], key_matrix[:, 128:], value_matrix[:, 128:]],
        axis=1,
    )

    def own_rows(values):
        return lax.dynamic_slice_in_dim(values, kv * 32, 32, 1)

    row_index = l * span + jnp.arange(span, dtype=jnp.int32)
    key_index = jnp.arange(n * span, dtype=jnp.int32)
    layouts = [row_layout(row_index, bucket_sizes[b], true_lengths[b]) for b in range(batches)]
    positions = jnp.concatenate([item[1] for item in layouts])
    row_lo = jnp.stack([row_index - item[1] for item in layouts])
    limits = jnp.stack([item[2] for item in layouts])
    row_hi = jnp.minimum(row_index + 1, row_lo + limits)
    allowed = (
        (key_index[None, None, :] >= row_lo[:, :, None])
        & (key_index[None, None, :] < row_hi[:, :, None])
    )[:, None]
    cosine, sine = rope_tables(positions, HEAD_SIZE)
    signed = sine * jnp.where(jnp.arange(HEAD_SIZE) < HEAD_SIZE // 2, -1.0, 1.0)
    (
        g_all,
        g_own,
        normed,
        all_keys,
        query,
        query_proj,
        key_proj,
        gate,
        attended,
        log_total,
        hidden,
        inner,
        z_other,
        small,
    ) = head(
        n,
        inputs.reshape(batches, 4, 32, width),
        cotangent.reshape(batches, 4, 32, width),
        query_weight,
        paired,
        output_weight,
        gate_weight,
        up_weight,
        down_weight,
        own_small,
        cosine.reshape(batches, span, HEAD_SIZE),
        signed.reshape(batches, span, HEAD_SIZE),
        jnp.broadcast_to(row_lo[:, :, None], (batches, span, 128)),
        jnp.broadcast_to(row_hi[:, :, None], (batches, span, 128)),
    )
    small = small[0].transpose(1, 0, 2).reshape(16, width)
    w_head = lax.dynamic_slice_in_dim(small, x * 2, 2, 0)
    gain_a = small[4].astype(F32)
    gain_f = small[5].astype(F32)
    w_query = g_all[0].reshape(width, 256)
    w_keys = g_all[1].reshape(width, 256)
    w_output = g_all[2]
    normed = normed.reshape(batches * span, width)
    query_proj = query_proj.reshape(-1, 2, HEAD_SIZE)
    key_proj = key_proj.reshape(-1, 1, HEAD_SIZE)
    query_scale = rms_scale(query_proj)
    query_normal = query_proj * query_scale
    key_scale = rms_scale(key_proj)
    key_normal = key_proj * key_scale
    gate = lax.dynamic_slice_in_dim(gate, x * 2, 2, 2)
    seen = (jnp.arange(n) <= l)[:, None, None, None]
    all_keys = jnp.where(seen, all_keys, 0).transpose(1, 0, 2, 3).reshape(batches, n * span, 256)
    keys, values = all_keys[..., :HEAD_SIZE], all_keys[..., HEAD_SIZE:]
    query = query.reshape(batches, 2, span, HEAD_SIZE)
    attended = attended.reshape(batches, 2, span, HEAD_SIZE)
    log_total = log_total[..., :1].reshape(batches, 2, span, 1)
    raw = jnp.einsum("bhtd,bsd->bhts", query, keys, preferred_element_type=F32) * scale
    weights = jnp.where(allowed, jnp.exp(raw - log_total), 0.0)
    gate_heads = gate.transpose(0, 2, 1)[..., None]
    mixed = (attended * gate_heads).astype(BF).transpose(0, 2, 1, 3).reshape(-1, 256)
    split = (batches, 2, 2, 2, 32, width)
    own_x = own_rows(inputs).astype(F32)
    scale_f = rms_scale(hidden)
    normal_f = hidden * scale_f
    out_part, din_part, ffn_parts, d_gate, d_up, d_down = ffn(
        n,
        inner.reshape(batches, span, width),
        cotangent.reshape(batches, 4, 32, width),
        z_other,
        g_all,
        g_own,
    )
    sums = group_sum(jnp.stack([out_part.reshape(split), din_part.reshape(split)]), 5)
    own_out = (hidden + sums[0]).astype(BF)
    grad_inner = sums[1]
    own_dz = own_rows(cotangent).astype(F32)
    sum_feedforward_gain = jnp.sum(grad_inner * normal_f, axis=(0, 1))
    grad_hidden = own_dz + norm_backward(grad_inner * gain_f, normal_f, scale_f)
    grad_branch = group_spread(grad_hidden.astype(BF), 6).reshape(-1, width)
    d_output = jnp.stack(
        [outer_sum(mixed, grad_branch[:, s * 256 : (s + 1) * 256]).astype(BF) for s in range(2 * n)]
    )
    grad_mixed = sum(
        times_transpose(grad_branch[:, s * 256 : (s + 1) * 256], w_output[s]) for s in range(2 * n)
    )
    grad_mixed = grad_mixed.reshape(batches, span, 2, HEAD_SIZE).transpose(0, 2, 1, 3)
    grad_heads = (grad_mixed * gate_heads).astype(BF)
    grad_logits = (
        jnp.sum(grad_mixed * attended, axis=-1, keepdims=True) * gate_heads * (1.0 - gate_heads)
    ).astype(BF)
    delta = jnp.sum(grad_heads.astype(F32) * attended, axis=-1, keepdims=True)
    grad_weights = jnp.einsum("bhtd,bsd->bhts", grad_heads, values, preferred_element_type=F32)
    grad_scores = (weights * (grad_weights - delta)).astype(BF)
    grad_query = scale * jnp.einsum(
        "bhts,bsd->bhtd", grad_scores, keys, preferred_element_type=F32
    )
    grad_keys = scale * jnp.einsum(
        "bhts,bhtd->bsd", grad_scores, query, preferred_element_type=F32
    )
    grad_values = jnp.einsum(
        "bhts,bhtd->bsd", weights.astype(BF), grad_heads, preferred_element_type=F32
    )
    grad_pair = jnp.concatenate([grad_keys, grad_values], axis=-1).astype(BF)
    grad_pair = grad_pair.reshape(batches, n, span, 256).transpose(1, 0, 2, 3)
    local_pair = keys_back(n, grad_pair.reshape(n, batches * span, 256)).astype(F32)

    grad_query_rot = grad_query.transpose(0, 2, 1, 3).reshape(-1, 2, HEAD_SIZE)
    grad_query_norm = rotate_backward(grad_query_rot, cosine, sine)
    sum_query_gain = jnp.sum(grad_query_norm * query_normal, axis=(0, 1))
    d_query = (
        norm_backward(grad_query_norm * gain_query, query_normal, query_scale)
        .astype(BF)
        .reshape(-1, 256)
    )
    grad_key_norm = rotate_backward(local_pair[:, None, :HEAD_SIZE], cosine, sine)
    sum_key_gain = jnp.sum(grad_key_norm * key_normal, axis=(0, 1))
    d_key = norm_backward(grad_key_norm * gain_key, key_normal, key_scale).astype(BF)
    d_pair = jnp.concatenate(
        [d_key.reshape(-1, HEAD_SIZE), local_pair[:, HEAD_SIZE:].astype(BF)], axis=1
    )
    logits_low = grad_logits[..., 0].transpose(0, 2, 1).reshape(-1, 2)
    d_head = outer_sum(logits_low, normed)
    d_head = jnp.where(jnp.arange(2)[:, None, None] == x, d_head[None], 0.0).reshape(4, width)
    d_query_weight = outer_sum(normed, d_query).astype(BF).reshape(2 * n, 256, 256)
    d_pair_weight = outer_sum(normed, d_pair).astype(BF).reshape(2 * n, 256, 256)
    grad_partial = (
        times_transpose(d_query, w_query)
        + times_transpose(d_pair, w_keys)
        + jnp.dot(logits_low, w_head, preferred_element_type=F32)
    ).astype(BF)
    grad_normed = group_sum(grad_partial.reshape((1,) + split), 10)[0]
    dq, dkv, do, d_gate2, d_up2, d_down2 = rows_sum(
        n, jnp.stack([d_query_weight, d_pair_weight, d_output]), ffn_parts
    )
    scale_a = rms_scale(own_x)
    normal_a = own_x * scale_a
    sum_attention_gain = jnp.sum(grad_normed * normal_a, axis=(0, 1))
    own_grad = (grad_hidden + norm_backward(grad_normed * gain_a, normal_a, scale_a)).astype(BF)
    outs = home(jnp.stack([own_out, own_grad])).reshape(2, batches, rows, width)
    gains = lax.psum(
        jnp.concatenate([sum_attention_gain, sum_feedforward_gain, sum_query_gain, sum_key_gain]),
        ("seq", "kv"),
    )
    head_total = lax.psum(d_head, "seq")
    own_width = width // (2 * n)

    def joined(first, rest, axis):
        a, b = jnp.split(first.astype(F32), 2, axis=axis)
        c, d = jnp.split(rest.astype(F32), 2, axis=axis)
        return jnp.concatenate([a, c, b, d], axis=axis)

    def cut(values):
        return lax.dynamic_slice_in_dim(values, seq * own_width, own_width, values.ndim - 1)

    return (
        outs[0],
        outs[1],
        cut(gains[:width]),
        cut(gains[width : 2 * width]),
        gains[2 * width : 2 * width + HEAD_SIZE],
        gains[2 * width + HEAD_SIZE :],
        dq.astype(F32),
        jnp.concatenate([dkv[:, :128], dkv[:, 256:384]], axis=1).astype(F32),
        jnp.concatenate([dkv[:, 128:256], dkv[:, 384:]], axis=1).astype(F32),
        cut(head_total).T,
        do.astype(F32),
        joined(d_gate, d_gate2, 1),
        joined(d_up, d_up2, 1),
        joined(d_down, d_down2, 0),
    )


def solution(mesh):
    chosen = fast_local if dict(mesh.shape) == {"seq": 8, "kv": 4} else local
    in_specs = (
        P(None, "seq", None),
        P(None, "seq", None),
        P(),
        P(),
        P("seq"),
        P("seq"),
        P(),
        P(),
        P("seq", "kv"),
        P("seq", "kv"),
        P("seq", "kv"),
        P("seq", "kv"),
        P("kv", "seq"),
        P("seq", "kv"),
        P("seq", "kv"),
        P("kv", "seq"),
    )
    out_specs = (
        P(None, "seq", None),
        P(None, "seq", None),
        P("seq"),
        P("seq"),
        P(),
        P(),
        P("seq", "kv"),
        P("seq", "kv"),
        P("seq", "kv"),
        P("seq", "kv"),
        P("kv", "seq"),
        P("seq", "kv"),
        P("seq", "kv"),
        P("kv", "seq"),
    )
    return jax.shard_map(chosen, mesh=mesh, in_specs=in_specs, out_specs=out_specs, check_vma=False)
```

```python
import functools
import math

import jax
import jax.numpy as jnp
from jax import lax
from jax.experimental import pallas as pl
from jax.experimental.pallas import tpu as pltpu
from jax.sharding import PartitionSpec as P

HEAD_SIZE = 128


EPS = 1e-06
ROPE_BASE = 1000000.0
MASKED = -1e30


def rms_scale(values):
    return lax.rsqrt(jnp.mean(values * values, axis=-1, keepdims=True) + EPS)


def norm_backward(grad, normal, factor):
    return factor * (grad - normal * jnp.mean(grad * normal, axis=-1, keepdims=True))


def rope_tables(positions, width):
    half = width // 2
    steps = jnp.arange(half, dtype=jnp.float32) * (2.0 / width)
    inverse = jnp.exp(-steps * math.log(ROPE_BASE))
    angles = positions.astype(jnp.float32)[:, None] * inverse[None, :]
    cosine = jnp.cos(angles)
    sine = jnp.sin(angles)
    return (jnp.concatenate([cosine, cosine], axis=-1), jnp.concatenate([sine, sine], axis=-1))


def rotate_forward(values, cosine, sine):
    half = values.shape[-1] // 2
    turned = jnp.concatenate([-values[..., half:], values[..., :half]], axis=-1)
    return values * cosine[:, None, :] + turned * sine[:, None, :]


def rotate_backward(grad, cosine, sine):
    half = grad.shape[-1] // 2
    moved = grad * sine[:, None, :]
    return grad * cosine[:, None, :] + jnp.concatenate(
        [moved[..., half:], -moved[..., :half]], axis=-1
    )


def token_layout(index, buckets, lengths):
    ends = jnp.cumsum(buckets)
    starts = ends - buckets
    member = (index[:, None] >= starts[None, :]) & (index[:, None] < ends[None, :])
    labels = jnp.arange(buckets.shape[0], dtype=jnp.int32)
    segment = jnp.sum(jnp.where(member, labels[None, :], 0), axis=1)
    position = index - jnp.sum(jnp.where(member, starts[None, :], 0), axis=1)
    limit = jnp.sum(jnp.where(member, lengths[None, :], 0), axis=1)
    return (segment, position, position < limit)


def outer_sum(left, right):
    return lax.dot_general(
        left, right, (((0,), (0,)), ((), ())), preferred_element_type=jnp.float32
    )


def times_transpose(left, weight):
    return lax.dot_general(
        left, weight, (((1,), (1,)), ((), ())), preferred_element_type=jnp.float32
    )


def block_scores(query_kg, key_block, start, row_index, row_segment, buckets, lengths, scale):
    key_index = start + jnp.arange(key_block.shape[0], dtype=jnp.int32)
    key_segment, key_position, key_valid = token_layout(key_index, buckets, lengths)
    allowed = (
        (row_segment[:, None] == key_segment[None, :])
        & (key_index[None, :] <= row_index[:, None])
        & key_valid[None, :]
    )
    raw = (
        jnp.einsum("kgtd,skd->kgts", query_kg, key_block, preferred_element_type=jnp.float32)
        * scale
    )
    return (jnp.where(allowed, raw, MASKED), allowed)


def split_blocks(keys, values, block):
    blocks = keys.shape[0] // block
    key_blocks = keys.reshape(blocks, block, keys.shape[1], keys.shape[2])
    value_blocks = values.reshape(blocks, block, values.shape[1], values.shape[2])
    starts = jnp.arange(blocks) * block
    return (key_blocks, value_blocks, starts)


def attention_forward(
    query_kg, keys, values, row_index, row_segment, buckets, lengths, block, scale
):
    key_blocks, value_blocks, starts = split_blocks(keys, values, block)

    def first_pass(carry, item):
        running_max, total = carry
        key_block, start = item
        masked, allowed = block_scores(
            query_kg, key_block, start, row_index, row_segment, buckets, lengths, scale
        )
        new_max = jnp.maximum(running_max, jnp.max(masked, axis=-1))
        total = total * jnp.exp(running_max - new_max) + jnp.sum(
            jnp.where(allowed, jnp.exp(masked - new_max[..., None]), 0.0), axis=-1
        )
        return ((new_max, total), None)

    begin = (
        jnp.full(query_kg.shape[:3], MASKED, jnp.float32),
        jnp.zeros(query_kg.shape[:3], jnp.float32),
    )
    (running_max, total), unused = lax.scan(first_pass, begin, (key_blocks, starts))
    log_total = running_max + jnp.log(total)

    def second_pass(accumulated, item):
        key_block, value_block, start = item
        masked, allowed = block_scores(
            query_kg, key_block, start, row_index, row_segment, buckets, lengths, scale
        )
        weights = jnp.where(allowed, jnp.exp(masked - log_total[..., None]), 0.0).astype(
            jnp.bfloat16
        )
        return (
            accumulated
            + jnp.einsum(
                "kgts,skd->kgtd", weights, value_block, preferred_element_type=jnp.float32
            ),
            None,
        )

    attended, unused = lax.scan(
        second_pass, jnp.zeros(query_kg.shape, jnp.float32), (key_blocks, value_blocks, starts)
    )
    return (attended, log_total)


def attention_backward(
    query_kg,
    grad_kg,
    log_total,
    delta,
    keys,
    values,
    row_index,
    row_segment,
    buckets,
    lengths,
    block,
    scale,
):
    key_blocks, value_blocks, starts = split_blocks(keys, values, block)

    def step(grad_query, item):
        key_block, value_block, start = item
        masked, allowed = block_scores(
            query_kg, key_block, start, row_index, row_segment, buckets, lengths, scale
        )
        weights = jnp.where(allowed, jnp.exp(masked - log_total[..., None]), 0.0)
        grad_weights = jnp.einsum(
            "kgtd,skd->kgts", grad_kg, value_block, preferred_element_type=jnp.float32
        )
        grad_scores = (weights * (grad_weights - delta[..., None])).astype(jnp.bfloat16)
        grad_query = grad_query + scale * jnp.einsum(
            "kgts,skd->kgtd", grad_scores, key_block, preferred_element_type=jnp.float32
        )
        grad_key = scale * jnp.einsum(
            "kgts,kgtd->skd", grad_scores, query_kg, preferred_element_type=jnp.float32
        )
        grad_value = jnp.einsum(
            "kgts,kgtd->skd",
            weights.astype(jnp.bfloat16),
            grad_kg,
            preferred_element_type=jnp.float32,
        )
        return (grad_query, (grad_key, grad_value))

    grad_query, (grad_keys, grad_values) = lax.scan(
        step, jnp.zeros(query_kg.shape, jnp.float32), (key_blocks, value_blocks, starts)
    )
    return (grad_query, grad_keys.reshape(keys.shape), grad_values.reshape(values.shape))


def local(
    inputs,
    cotangent,
    bucket_sizes,
    true_lengths,
    attention_gain,
    feedforward_gain,
    query_gain,
    key_gain,
    query_weight,
    key_matrix,
    value_matrix,
    headgate_weight,
    output_weight,
    gate_weight,
    up_weight,
    down_weight,
):
    batches, rows, width = inputs.shape
    seq_count = lax.axis_size("seq")
    block = math.gcd(rows * seq_count, 512)
    local_heads = query_weight.shape[1] // HEAD_SIZE
    local_groups = key_matrix.shape[1] // HEAD_SIZE
    group = local_heads // local_groups
    scale = HEAD_SIZE ** (-0.5)
    row_index = lax.axis_index("seq") * rows + jnp.arange(rows, dtype=jnp.int32)
    gain_query = query_gain.astype(jnp.float32)
    gain_key = key_gain.astype(jnp.float32)
    sum_attention_gain = jnp.zeros((width,), jnp.float32)
    sum_feedforward_gain = jnp.zeros((width,), jnp.float32)
    sum_query = jnp.zeros((width, query_weight.shape[1]), jnp.float32)
    sum_key = jnp.zeros((width, key_matrix.shape[1]), jnp.float32)
    sum_value = jnp.zeros((width, value_matrix.shape[1]), jnp.float32)
    sum_headgate = jnp.zeros((width, headgate_weight.shape[1]), jnp.float32)
    sum_output = jnp.zeros((output_weight.shape[0], width), jnp.float32)
    sum_gate = jnp.zeros((width, gate_weight.shape[1]), jnp.float32)
    sum_upward = jnp.zeros((width, up_weight.shape[1]), jnp.float32)
    sum_down = jnp.zeros((down_weight.shape[0], width), jnp.float32)
    sum_query_gain = jnp.zeros((HEAD_SIZE,), jnp.float32)
    sum_key_gain = jnp.zeros((HEAD_SIZE,), jnp.float32)
    results = []
    input_grads = []
    for batch in range(batches):
        gathered = (
            lax.all_gather(attention_gain, "seq", axis=0, tiled=True),
            lax.all_gather(feedforward_gain, "seq", axis=0, tiled=True),
            lax.all_gather(query_weight, "seq", axis=0, tiled=True),
            lax.all_gather(key_matrix, "seq", axis=0, tiled=True),
            lax.all_gather(value_matrix, "seq", axis=0, tiled=True),
            lax.all_gather(headgate_weight, "seq", axis=0, tiled=True),
            lax.all_gather(output_weight, "seq", axis=1, tiled=True),
            lax.all_gather(gate_weight, "seq", axis=0, tiled=True),
            lax.all_gather(up_weight, "seq", axis=0, tiled=True),
            lax.all_gather(down_weight, "seq", axis=1, tiled=True),
        )
        (
            gain_a,
            gain_f,
            w_query,
            key_projection_weight,
            value_projection_weight,
            w_head,
            w_output,
            w_gate,
            w_up,
            w_down,
        ) = gathered
        gain_a = gain_a.astype(jnp.float32)
        gain_f = gain_f.astype(jnp.float32)
        buckets = bucket_sizes[batch]
        lengths = true_lengths[batch]
        row_segment, row_position, row_valid = token_layout(row_index, buckets, lengths)
        cosine, sine = rope_tables(row_position, HEAD_SIZE)
        current = inputs[batch].astype(jnp.float32)
        scale_a = rms_scale(current)
        normal_a = current * scale_a
        normed_input = (normal_a * gain_a).astype(jnp.bfloat16)
        query_proj = jnp.dot(normed_input, w_query, preferred_element_type=jnp.float32).reshape(
            rows, local_heads, HEAD_SIZE
        )
        key_proj = jnp.dot(
            normed_input, key_projection_weight, preferred_element_type=jnp.float32
        ).reshape(rows, local_groups, HEAD_SIZE)
        value_proj = jnp.dot(
            normed_input, value_projection_weight, preferred_element_type=jnp.float32
        )
        query_scale = rms_scale(query_proj)
        query_normal = query_proj * query_scale
        key_scale = rms_scale(key_proj)
        key_normal = key_proj * key_scale
        query_rot = rotate_forward(query_normal * gain_query, cosine, sine).astype(jnp.bfloat16)
        key_rot = rotate_forward(key_normal * gain_key, cosine, sine).astype(jnp.bfloat16)
        value_low = value_proj.astype(jnp.bfloat16).reshape(rows, local_groups, HEAD_SIZE)
        logits = jnp.dot(normed_input, w_head, preferred_element_type=jnp.float32)
        gate = jax.nn.sigmoid(logits)
        all_keys, all_values = (
            lax.all_gather(key_rot, "seq", axis=0, tiled=True),
            lax.all_gather(value_low, "seq", axis=0, tiled=True),
        )
        query_kg = query_rot.reshape(rows, local_groups, group, HEAD_SIZE).transpose(1, 2, 0, 3)
        attended_kg, log_total = attention_forward(
            query_kg, all_keys, all_values, row_index, row_segment, buckets, lengths, block, scale
        )
        attended = attended_kg.transpose(2, 0, 1, 3).reshape(rows, local_heads, HEAD_SIZE)
        mixed = (
            (attended * gate[:, :, None])
            .astype(jnp.bfloat16)
            .reshape(rows, local_heads * HEAD_SIZE)
        )
        hidden = current + lax.psum(
            jnp.dot(mixed, w_output, preferred_element_type=jnp.float32).astype(jnp.bfloat16), "kv"
        ).astype(jnp.float32)
        scale_f = rms_scale(hidden)
        normal_f = hidden * scale_f
        inner = (normal_f * gain_f).astype(jnp.bfloat16)
        gated = jnp.dot(inner, w_gate, preferred_element_type=jnp.float32)
        upward = jnp.dot(inner, w_up, preferred_element_type=jnp.float32)
        sigma = jax.nn.sigmoid(gated)
        swish = gated * sigma
        product = (swish * upward).astype(jnp.bfloat16)
        output = hidden + lax.psum(
            jnp.dot(product, w_down, preferred_element_type=jnp.float32).astype(jnp.bfloat16), "kv"
        ).astype(jnp.float32)
        results.append(output.astype(jnp.bfloat16))
        grad_out = cotangent[batch].astype(jnp.float32)
        grad_low = grad_out.astype(jnp.bfloat16)
        sum_down = sum_down + outer_sum(product, grad_low)
        grad_product = times_transpose(grad_low, w_down)
        grad_gated = (grad_product * upward * sigma * (1.0 + gated * (1.0 - sigma))).astype(
            jnp.bfloat16
        )
        grad_upward = (grad_product * swish).astype(jnp.bfloat16)
        sum_gate = sum_gate + outer_sum(inner, grad_gated)
        sum_upward = sum_upward + outer_sum(inner, grad_upward)
        grad_inner = lax.psum(
            (times_transpose(grad_gated, w_gate) + times_transpose(grad_upward, w_up)).astype(
                jnp.bfloat16
            ),
            "kv",
        ).astype(jnp.float32)
        sum_feedforward_gain = sum_feedforward_gain + jnp.sum(grad_inner * normal_f, axis=0)
        grad_hidden = grad_out + norm_backward(grad_inner * gain_f, normal_f, scale_f)
        grad_branch = grad_hidden.astype(jnp.bfloat16)
        sum_output = sum_output + outer_sum(mixed, grad_branch)
        grad_mixed = times_transpose(grad_branch, w_output).reshape(rows, local_heads, HEAD_SIZE)
        grad_heads = (grad_mixed * gate[:, :, None]).astype(jnp.bfloat16)
        grad_logits = (jnp.sum(grad_mixed * attended, axis=-1) * gate * (1.0 - gate)).astype(
            jnp.bfloat16
        )
        back_keys = lax.all_gather(key_rot, "seq", axis=0, tiled=True)
        back_values = lax.all_gather(value_low, "seq", axis=0, tiled=True)
        grad_kg = grad_heads.reshape(rows, local_groups, group, HEAD_SIZE).transpose(1, 2, 0, 3)
        delta = jnp.sum(grad_kg.astype(jnp.float32) * attended_kg, axis=-1)
        grad_query_kg, grad_keys, grad_values = attention_backward(
            query_kg,
            grad_kg,
            log_total,
            delta,
            back_keys,
            back_values,
            row_index,
            row_segment,
            buckets,
            lengths,
            block,
            scale,
        )
        local_keys, local_values = (
            lax.psum_scatter(
                grad_keys.astype(jnp.bfloat16), "seq", scatter_dimension=0, tiled=True
            ).astype(jnp.float32),
            lax.psum_scatter(
                grad_values.astype(jnp.bfloat16), "seq", scatter_dimension=0, tiled=True
            ).astype(jnp.float32),
        )
        grad_query_rot = grad_query_kg.transpose(2, 0, 1, 3).reshape(rows, local_heads, HEAD_SIZE)
        grad_query_norm = rotate_backward(grad_query_rot, cosine, sine)
        sum_query_gain = sum_query_gain + jnp.sum(grad_query_norm * query_normal, axis=(0, 1))
        grad_query = (
            norm_backward(grad_query_norm * gain_query, query_normal, query_scale)
            .astype(jnp.bfloat16)
            .reshape(rows, local_heads * HEAD_SIZE)
        )
        grad_key_norm = rotate_backward(local_keys, cosine, sine)
        sum_key_gain = sum_key_gain + jnp.sum(grad_key_norm * key_normal, axis=(0, 1))
        grad_key = (
            norm_backward(grad_key_norm * gain_key, key_normal, key_scale)
            .astype(jnp.bfloat16)
            .reshape(rows, local_groups * HEAD_SIZE)
        )
        grad_value = local_values.astype(jnp.bfloat16).reshape(rows, local_groups * HEAD_SIZE)
        sum_query = sum_query + outer_sum(normed_input, grad_query)
        sum_key = sum_key + outer_sum(normed_input, grad_key)
        sum_value = sum_value + outer_sum(normed_input, grad_value)
        sum_headgate = sum_headgate + outer_sum(normed_input, grad_logits)
        grad_partial = (
            times_transpose(grad_query, w_query)
            + times_transpose(grad_key, key_projection_weight)
            + times_transpose(grad_value, value_projection_weight)
            + times_transpose(grad_logits, w_head)
        )
        grad_normed = lax.psum(grad_partial.astype(jnp.bfloat16), "kv").astype(jnp.float32)
        sum_attention_gain = sum_attention_gain + jnp.sum(grad_normed * normal_a, axis=0)
        grad_input = grad_hidden + norm_backward(grad_normed * gain_a, normal_a, scale_a)
        input_grads.append(grad_input.astype(jnp.bfloat16))
    (
        attention_total,
        feedforward_total,
        query_total,
        key_total,
        value_total,
        headgate_total,
        output_total,
        gate_total,
        upward_total,
        down_total,
    ) = (
        lax.psum_scatter(
            sum_attention_gain.astype(jnp.bfloat16), "seq", scatter_dimension=0, tiled=True
        ).astype(jnp.float32),
        lax.psum_scatter(
            sum_feedforward_gain.astype(jnp.bfloat16), "seq", scatter_dimension=0, tiled=True
        ).astype(jnp.float32),
        lax.psum_scatter(
            sum_query.astype(jnp.bfloat16), "seq", scatter_dimension=0, tiled=True
        ).astype(jnp.float32),
        lax.psum_scatter(
            sum_key.astype(jnp.bfloat16), "seq", scatter_dimension=0, tiled=True
        ).astype(jnp.float32),
        lax.psum_scatter(
            sum_value.astype(jnp.bfloat16), "seq", scatter_dimension=0, tiled=True
        ).astype(jnp.float32),
        lax.psum_scatter(
            sum_headgate.astype(jnp.bfloat16), "seq", scatter_dimension=0, tiled=True
        ).astype(jnp.float32),
        lax.psum_scatter(
            sum_output.astype(jnp.bfloat16), "seq", scatter_dimension=1, tiled=True
        ).astype(jnp.float32),
        lax.psum_scatter(
            sum_gate.astype(jnp.bfloat16), "seq", scatter_dimension=0, tiled=True
        ).astype(jnp.float32),
        lax.psum_scatter(
            sum_upward.astype(jnp.bfloat16), "seq", scatter_dimension=0, tiled=True
        ).astype(jnp.float32),
        lax.psum_scatter(
            sum_down.astype(jnp.bfloat16), "seq", scatter_dimension=1, tiled=True
        ).astype(jnp.float32),
    )
    query_gain_total, key_gain_total = lax.psum((sum_query_gain, sum_key_gain), ("seq", "kv"))
    return (
        jnp.stack(results, axis=0),
        jnp.stack(input_grads, axis=0),
        attention_total,
        feedforward_total,
        query_gain_total,
        key_gain_total,
        query_total,
        key_total,
        value_total,
        headgate_total,
        output_total,
        gate_total,
        upward_total,
        down_total,
    )


BF = jnp.bfloat16
F32 = jnp.float32
ANY = pl.BlockSpec(memory_space=pl.ANY)
VM = pl.BlockSpec(memory_space=pltpu.VMEM)
DMA = pltpu.SemaphoreType.DMA


def place():
    s = lax.axis_index("seq")
    k = lax.axis_index("kv")
    return (lax.div(s, 2), lax.rem(s, 2), lax.div(k, 2), lax.rem(k, 2))


def device(l, x, y, c):
    return (l * 2 + x, y * 2 + c)


def remote(src, dst, send, recv, target):
    return pltpu.make_async_remote_copy(
        src_ref=src,
        dst_ref=dst,
        send_sem=send,
        recv_sem=recv,
        device_id=target,
        device_id_type=pl.DeviceIdType.MESH,
    )


def greet(partners):
    barrier = pltpu.get_barrier_semaphore()
    count = 0
    for target, there in partners:

        def call(target=target):
            pl.semaphore_signal(
                barrier, inc=1, device_id=target, device_id_type=pl.DeviceIdType.MESH
            )

        if there is None:
            call()
            count = count + 1
        else:
            pl.when(there)(call)
            count = count + jnp.where(there, 1, 0)
    pl.semaphore_wait(barrier, count)


class Line:
    def __init__(self, length, g, ag_send, ag_recv, land=None, rs_send=None, rs_recv=None):
        self.n = length
        self.g, self.ag_send, self.ag_recv = g, ag_send, ag_recv
        self.land, self.rs_send, self.rs_recv = land, rs_send, rs_recv
        self.l, self.x, self.y, self.c = place()

    def partners(self):
        l, x, y, c = self.l, self.x, self.y, self.c
        return [
            (device(l - 1, x, y, c), l >= 1),
            (device(l + 1, x, y, c), l <= self.n - 2),
        ]

    def block(self, item, b):
        return self.g.at[item, pl.ds(2 * b, 2)]

    def _ag(self, item, way, b):
        step = -1 if way == 0 else 1
        return remote(
            self.block(item, b),
            self.block(item, b),
            self.ag_send.at[item, way, b],
            self.ag_recv.at[item, b],
            device(self.l + step, self.x, self.y, self.c),
        )

    def ag_start(self, item):
        l = self.l
        pl.when(l >= 1)(lambda: self._ag(item, 0, l).start())
        pl.when(l <= self.n - 2)(lambda: self._ag(item, 1, l).start())

    def ag_step(self, item, t):
        l, n = self.l, self.n

        @pl.when(l + t <= n - 1)
        def _():
            self._ag(item, 0, l + t).wait_recv()
            pl.when(l >= 1)(lambda: self._ag(item, 0, l + t).start())

        @pl.when(l - t >= 0)
        def _():
            self._ag(item, 1, l - t).wait_recv()
            pl.when(l <= n - 2)(lambda: self._ag(item, 1, l - t).start())

    def pump(self, item, t):
        l, n = self.l, self.n

        @pl.when((l + t <= n - 1) & (l >= 1))
        def _():
            self._ag(item, 0, l + t).wait_recv()
            self._ag(item, 0, l + t).start()

        @pl.when((l - t >= 0) & (l <= n - 2))
        def _():
            self._ag(item, 1, l - t).wait_recv()
            self._ag(item, 1, l - t).start()

    def collect(self, item):
        l, n = self.l, self.n
        for t in range(1, n):
            pl.when(l == 0)(lambda t=t: self._ag(item, 0, t).wait_recv())
            pl.when(l == n - 1)(lambda t=t: self._ag(item, 1, n - 1 - t).wait_recv())

    def ag_end(self, item):
        l, n = self.l, self.n
        for b in range(n):
            pl.when((l >= 1) & (l <= b))(lambda b=b: self._ag(item, 0, b).wait_send())
            pl.when((l <= n - 2) & (l >= b))(lambda b=b: self._ag(item, 1, b).wait_send())

    def _slot(self, item, slot):
        return self.land.at[item, pl.ds(2 * slot, 2)]

    def _rs(self, item, way, o):
        if way == 0:
            target = self.l - 1
            slot = jnp.where(target == o, self.n, o)
        else:
            target = self.l + 1
            slot = o
        return remote(
            self.block(item, o),
            self._slot(item, slot),
            self.rs_send.at[item, way, o],
            self.rs_recv.at[item, slot],
            device(target, self.x, self.y, self.c),
        )

    def _take(self, item, o, slot):
        here = self._slot(item, slot)
        pltpu.make_async_copy(here, here, self.rs_recv.at[item, slot]).wait()
        for h in range(2):
            total = self.g[item, 2 * o + h].astype(F32) + self.land[item, 2 * slot + h].astype(F32)
            self.g[item, 2 * o + h] = total.astype(BF)

    def rs_step(self, item, q):
        l, n = self.l, self.n
        right, left = n - q, q - 1

        @pl.when(l < right)
        def _():
            pl.when(l >= 1)(lambda: self._take(item, right, right))
            self._rs(item, 1, right).start()

        @pl.when(l > left)
        def _():
            pl.when(l <= n - 2)(lambda: self._take(item, left, left))
            self._rs(item, 0, left).start()

    def rs_fire(self, item):
        l, n = self.l, self.n
        for o in range(n - 1, 0, -1):
            pl.when(l == 0)(lambda o=o: self._rs(item, 1, o).start())
            pl.when(l == n - 1)(lambda o=o: self._rs(item, 0, n - 1 - o).start())

    def rs_mid(self, item, q):
        l, n = self.l, self.n
        right, left = n - q, q - 1

        @pl.when((l < right) & (l >= 1))
        def _():
            self._take(item, right, right)
            self._rs(item, 1, right).start()

        @pl.when((l > left) & (l <= n - 2))
        def _():
            self._take(item, left, left)
            self._rs(item, 0, left).start()

    def rs_final(self, item):
        l, n = self.l, self.n
        pl.when(l >= 1)(lambda: self._take(item, l, l))
        pl.when(l <= n - 2)(lambda: self._take(item, l, n))

    def rs_end(self, item):
        l, n = self.l, self.n
        for o in range(n):
            pl.when(l < o)(lambda o=o: self._rs(item, 1, o).wait_send())
            pl.when(l > o)(lambda o=o: self._rs(item, 0, o).wait_send())


def each(count, body):
    def step(i, unused):
        body(i)
        return 0

    lax.fori_loop(0, count, step, 0)


class Pair:
    def __init__(self, line, refs, send, recv, local, half):
        self.line, self.refs = line, refs
        self.send, self.recv, self.local, self.half = send, recv, local, half

    def partner(self):
        line = self.line
        return (device(line.l, 1 - line.x, line.y, line.c), None)

    def _part(self, ref, kind, j, x):
        at = pl.multiple_of(x * self.half + j * 256, 256)
        return ref.at[pl.ds(at, 256), :] if kind == 2 else ref.at[:, pl.ds(at, 256)]

    def _copies(self, item, kind, j):
        line = self.line
        mine = line.g.at[item, 2 * line.l + line.x]
        out = remote(
            self._part(self.refs[kind], kind, j, 1 - line.x),
            mine,
            self.send.at[item],
            self.recv.at[item],
            self.partner()[0],
        )
        here = pltpu.make_async_copy(
            self._part(self.refs[kind], kind, j, line.x), mine, self.local.at[item]
        )
        return out, here

    def start(self, item, kind, j):
        for copy in self._copies(item, kind, j):
            copy.start()

    def end(self, item, kind, j):
        out, here = self._copies(item, kind, j)
        here.wait()
        out.wait_send()
        out.wait_recv()


class Back(Pair):
    def _copies(self, item, kind, j):
        line = self.line
        home = self._part(self.refs[kind], kind, j, line.x)
        out = remote(
            line.g.at[item, 2 * line.l + 1 - line.x],
            home,
            self.send.at[item],
            self.recv.at[item],
            self.partner()[0],
        )
        here = pltpu.make_async_copy(
            line.g.at[item, 2 * line.l + line.x], home, self.local.at[item]
        )
        return out, here


def back_wait(back, item, kind, j):
    line = back.line
    out, here = back._copies(item, kind, j)
    here.wait()
    out.wait_send()
    there = back._part(back.refs[kind], kind, j, 1 - line.x)
    pltpu.make_async_copy(there, there, back.recv.at[item]).wait()


def dot(a, b):
    return lax.dot_general(a, b, (((1,), (0,)), ((), ())), preferred_element_type=F32)


def dot_t(a, b):
    return lax.dot_general(a, b, (((1,), (1,)), ((), ())), preferred_element_type=F32)


def head_kernel(
    n,
    x_any,
    z_any,
    wq,
    wkv,
    wo,
    wg,
    wu,
    wd,
    small,
    cos_ref,
    sin_ref,
    row_lo,
    row_hi,
    g_out,
    own_out,
    normed_out,
    kv_out,
    q_out,
    qp_out,
    kp_out,
    gate_out,
    att_out,
    lse_out,
    hidden_out,
    inner_out,
    dz_out,
    small_out,
    x_v,
    normed,
    normed_t,
    g,
    small_g,
    gain_row,
    heads_row,
    kv,
    q_v,
    qp,
    kp,
    gate_v,
    att,
    tot,
    part,
    core_land,
    low,
    chip_land,
    inner,
    hidden,
    p_send,
    p_recv,
    p_loc,
    ag_send,
    ag_recv,
    sp_sem,
    sa_send,
    sa_recv,
    t_send,
    t_recv,
    z_send,
    z_recv,
    kv_send,
    kv_recv,
    c_send,
    c_recv,
    s_send,
    s_recv,
    i_send,
    i_recv,
    j_send,
    j_recv,
    o_loc,
):
    line = Line(n, g, ag_send, ag_recv)
    l, x, y, c = line.l, line.x, line.y, line.c
    k = y * 2 + c
    group = Group()
    across, mate = device(l, 1 - x, y, c), group.mate
    right = device(l + 1, x, y, c)
    tiny = Line(n, small_g, sa_send, sa_recv)
    scale = HEAD_SIZE ** (-0.5)
    late = 9
    first = Pair(line, (wq, wkv, wo), p_send, p_recv, p_loc, 256)
    rest = Pair(line, (wg, wu, wd), p_send, p_recv, p_loc, 768)

    def swap(item):
        if item < 3:
            return first, item, item, 0
        return rest, item, item % 3, item // 3 - 1

    def swap_start(item):
        pair, item, kind, j = swap(item)
        pair.start(item, kind, j)

    def swap_end(item):
        pair, item, kind, j = swap(item)
        pair.end(item, kind, j)

    outs = []

    def put(src, dst):
        copy = pltpu.make_async_copy(src, dst, o_loc.at[len(outs)])
        copy.start()
        outs.append(copy)

    greet(line.partners() + [(mate, None)] + [(group.chip(i), None) for i in (1, 2, 3)])

    small_here = small_g.at[0, 2 * l + x]
    small_out_copy = remote(small, small_here, sp_sem.at[0], sp_sem.at[1], across)
    small_own = pltpu.make_async_copy(small, small_here, sp_sem.at[2])
    small_out_copy.start()
    small_own.start()
    swap_start(0)
    swap_start(1)
    own_x = pltpu.make_async_copy(x_any, x_v.at[:, x], t_send.at[2])
    own_x.start()
    halves = pl.ds(2 * c, 2)
    x_out = remote(x_any.at[halves], x_v.at[halves, x], t_send.at[0], t_recv.at[0], across)
    x_part = x_v.at[halves, 1 - x]
    x_on = remote(x_part, x_part, t_send.at[1], t_recv.at[1], mate)
    x_out.start()
    for item in range(2, 6):
        swap_start(item)
    z_out = remote(z_any.at[halves], dz_out.at[halves], z_send.at[0], z_recv.at[0], across)
    z_part = dz_out.at[halves]
    z_on = remote(z_part, z_part, z_send.at[1], z_recv.at[1], mate)
    z_out.start()
    for item in range(6, 12):
        swap_start(item)

    small_own.wait()
    small_out_copy.wait()
    tiny.ag_start(0)
    for item in range(3):
        swap_end(item)
        line.ag_start(item)
    for t in range(1, n):
        tiny.ag_step(0, t)
    for s in range(2 * n):
        cols = slice(s * 256, (s + 1) * 256)
        heads_row[:, cols] = small_g[0, s]
        gain_row[:, cols] = small_g[0, s, 4:6, :].astype(F32)

    def norm(m, side):
        v = x_v[m, side].reshape(128, 256 * 2 * n).astype(F32)
        mean = jnp.mean(v * v, axis=-1, keepdims=True)
        v = v * lax.rsqrt(mean + EPS) * gain_row[0:1, :]
        normed[m, side] = v.astype(BF)

    own_x.wait()
    each(4, lambda m: norm(m, x))
    line.pump(0, 1)
    line.pump(1, 1)
    x_out.wait_recv()
    x_on.start()
    line.pump(0, 2)
    line.pump(1, 2)
    line.pump(2, 1)
    x_on.wait_recv()
    each(4, lambda m: norm(m, 1 - x))
    for item in (3, 4):
        swap_end(item)
        line.ag_start(item)
    for item in (0, 1):
        line.pump(item, 3)
        line.collect(item)
    line.pump(2, 2)

    def project(m):
        a = normed[m].reshape(256, 256 * 2 * n)
        qf = dot(a, g[0].reshape(256 * 2 * n, 256))
        kf = dot(a, g[1].reshape(256 * 2 * n, 256))
        gate_v[m] = jax.nn.sigmoid(dot_t(a, heads_row[...]))
        qp[m] = qf
        kp[m] = kf[:, :128]
        cosine, sine = cos_ref[m], sin_ref[m]

        def turn(u, gain):
            u = u * lax.rsqrt(jnp.mean(u * u, axis=-1, keepdims=True) + EPS) * gain
            return (u * cosine + pltpu.roll(u, 64, 1) * sine).astype(BF)

        gains = small[8:10, :128].astype(F32)
        q_v[m, :256] = turn(qf[:, :128], gains[0:1])
        q_v[m, 256:] = turn(qf[:, 128:], gains[0:1])
        kv[l, m, :, :128] = turn(kf[:, :128], gains[1:2])
        kv[l, m, :, 128:] = kf[:, 128:].astype(BF)
        pl.when(l <= n - 2)(lambda: send_kv(l, m).start())

    def send_kv(b, m):
        return remote(kv.at[b, m], kv.at[b, m], kv_send.at[b, m], kv_recv.at[b, m], right)

    each(4, project)
    put(qp, qp_out)
    put(kp, kp_out)
    put(gate_v, gate_out)
    put(q_v, q_out)

    def attend(m, b, diagonal):
        pair = kv[b, m]
        raw = dot_t(q_v[m], pair[:, :128]) * scale
        lo = row_lo[m][:, :1] - b * 256
        hi = row_hi[m][:, :1] - b * 256
        column = lax.broadcasted_iota(jnp.int32, (512, 256), 1)
        allowed = (column >= jnp.concatenate([lo, lo], axis=0)) & (
            column < jnp.concatenate([hi, hi], axis=0)
        )
        e = jnp.where(allowed, jnp.exp(raw), 0.0)
        total = jnp.sum(e, axis=-1, keepdims=True)
        value = dot(e.astype(BF), pair[:, 128:])
        total = jnp.broadcast_to(total, (512, 128))
        if diagonal:
            tot[m] = total
            att[m] = value
        else:
            tot[m] += total
            att[m] += value

    def kv_round(t):
        @pl.when(l - t >= 0)
        def _():
            b = l - t

            def take(m):
                send_kv(b, m).wait_recv()
                pl.when(l <= n - 2)(lambda: send_kv(b, m).start())

            each(4, take)
            each(4, lambda m: attend(m, b, False))

    line.pump(2, 3)
    each(4, lambda m: attend(m, l, True))

    def turned(i):
        m, s = lax.div(i, 2 * n), lax.rem(i, 2 * n)
        tile = normed[m, :, :, pl.ds(pl.multiple_of(s * 256, 256), 256)].reshape(256, 256)
        normed_t[s, :, pl.ds(pl.multiple_of(m * 256, 256), 256)] = tile.T

    each(8 * n, turned)
    put(normed_t, normed_out)
    line.pump(3, 1)
    line.pump(4, 1)
    kv_round(1)
    for item in (5,):
        swap_end(item)
        line.ag_start(item)
    line.pump(3, 2)
    line.pump(4, 2)
    line.pump(3, 3)
    kv_round(2)
    swap_end(6)
    line.ag_start(6)
    line.pump(4, 3)
    line.pump(5, 1)
    line.pump(5, 2)
    kv_round(3)
    line.collect(2)

    def mate_copy(m):
        return remote(
            part.at[m, :, :, 1 - c], core_land.at[m], c_send.at[m], c_recv.at[m], mate
        )

    def branch(m):
        total = tot[m]
        lse = jnp.log(total)
        value = att[m] / total
        att[m] = value
        tot[m] = lse
        gates = gate_v[m]
        lo, hi = gates[:, 0:2], gates[:, 2:4]
        gates = jnp.where(x == 0, lo, hi)
        mixed = jnp.concatenate(
            [value[:256] * gates[:, 0:1], value[256:] * gates[:, 1:2]], axis=1
        ).astype(BF)
        for s in range(2 * n):
            part[m, :, :, :, :, s * 256 : (s + 1) * 256] = (
                dot(mixed, g[2, s]).astype(BF).reshape(2, 2, 2, 32, 256)
            )
        mate_copy(m).start()

    each(4, branch)
    put(att, att_out)
    put(tot, lse_out)
    put(kv, kv_out)
    swap_end(7)
    line.ag_start(7)
    line.pump(5, 3)
    line.pump(6, 1)

    def chip_copy(m, o):
        ox, oy = group.other(o)
        return remote(
            low.at[m, ox, oy],
            chip_land.at[o - 1, m],
            s_send.at[m, o - 1],
            s_recv.at[m, o - 1],
            group.chip(o),
        )

    def to_chips(m):
        mate_copy(m).wait_recv()
        for u in range(2):
            for v in range(2):
                low[m, u, v] = (
                    part[m, u, v, c].astype(F32) + core_land[m, u, v].astype(F32)
                ).astype(BF)
        for o in (3, 1, 2):
            chip_copy(m, o).start()

    each(4, to_chips)
    line.pump(6, 2)
    swap_end(8)
    line.ag_start(8)
    line.pump(6, 3)
    line.pump(7, 1)

    def inner_copy(m, o):
        here = inner.at[m, x, y, c]
        return remote(
            here, here, i_send.at[m, o - 1], i_recv.at[m, o - 1], group.chip(o)
        )

    def inner_mate(m, o):
        ox, oy = group.other(o)
        there = inner.at[m, ox, oy, c]
        return remote(there, there, j_send.at[m, o], j_recv.at[m, o], mate)

    def finish(m):
        total = low[m, x, y].astype(F32)
        for o in (1, 2, 3):
            chip_copy(m, o).wait_recv()
            total = total + chip_land[o - 1, m].astype(F32)
        h = x_v[m, x, k].astype(F32) + total
        hidden[m] = h
        mean = jnp.mean(h * h, axis=-1, keepdims=True)
        inner[m, x, y, c] = (h * lax.rsqrt(mean + EPS) * gain_row[1:2, :]).astype(BF)
        for o in (3, 1, 2):
            inner_copy(m, o).start()
        inner_mate(m, 0).start()

    each(4, finish)
    put(hidden, hidden_out)
    line.pump(7, 2)
    line.pump(7, 3)
    line.pump(8, 1)
    z_out.wait_recv()
    z_on.start()

    def pass_on(m):
        for o in (1, 2, 3):
            inner_copy(m, o).wait_recv()
            inner_mate(m, o).start()

    each(4, pass_on)
    line.pump(8, 2)
    for item in (9, 10, 11):
        swap_end(item)
        put(g.at[item, pl.ds(2 * l, 2)], own_out.at[item - 9])
    line.pump(8, 3)

    def arrive(m):
        for o in range(4):
            inner_mate(m, o).wait_recv()

    each(4, arrive)
    put(inner, inner_out)
    put(small_g, small_out)
    for item in range(3, 9):
        line.collect(item)
    put(g.at[pl.ds(0, 9)], g_out)

    small_out_copy_done = None
    own_waits = [x_out, x_on, z_out, z_on]
    for copy in own_waits:
        copy.wait_send()
    z_on.wait_recv()
    tiny.ag_end(0)
    each(9, line.ag_end)

    def drain(m):
        mate_copy(m).wait_send()
        for o in (1, 2, 3):
            chip_copy(m, o).wait_send()
            inner_copy(m, o).wait_send()
        for o in range(4):
            inner_mate(m, o).wait_send()
        for b in range(n):
            pl.when((l >= b) & (l <= n - 2))(lambda b=b: send_kv(b, m).wait_send())

    each(4, drain)
    for copy in outs:
        copy.wait()


def head(n, x_in, z_in, wq, wkv, wo, wg, wu, wd, small, cosine, sine, row_lo, row_hi):
    d = x_in.shape[-1]
    m = 2 * n
    bf = lambda *shape: jax.ShapeDtypeStruct(shape, BF)
    f32 = lambda *shape: jax.ShapeDtypeStruct(shape, F32)
    vb = lambda *shape: pltpu.VMEM(shape, BF)
    vf = lambda *shape: pltpu.VMEM(shape, F32)
    return pl.pallas_call(
        functools.partial(head_kernel, n),
        out_shape=(
            bf(9, m, 256, 256),
            bf(3, 2, 256, 256),
            bf(m, 256, 1024),
            bf(n, 4, 256, 256),
            bf(4, 512, 128),
            f32(4, 256, 256),
            f32(4, 256, 128),
            f32(4, 256, 16),
            f32(4, 512, 128),
            f32(4, 512, 128),
            f32(4, 32, d),
            bf(4, 2, 2, 2, 32, d),
            bf(4, 4, 32, d),
            bf(1, m, 16, 256),
        ),
        in_specs=[ANY] * 8 + [VM] * 5,
        out_specs=(ANY,) * 14,
        scratch_shapes=[
            vb(4, 2, 4, 32, d),
            vb(4, 2, 128, d),
            vb(m, 256, 1024),
            vb(12, m, 256, 256),
            vb(1, m, 16, 256),
            vf(2, d),
            vb(16, d),
            vb(n, 4, 256, 256),
            vb(4, 512, 128),
            vf(4, 256, 256),
            vf(4, 256, 128),
            vf(4, 256, 16),
            vf(4, 512, 128),
            vf(4, 512, 128),
            vb(4, 2, 2, 2, 32, d),
            vb(4, 2, 2, 32, d),
            vb(4, 2, 2, 32, d),
            vb(3, 4, 32, d),
            vb(4, 2, 2, 2, 32, d),
            vf(4, 32, d),
            DMA((12,)),
            DMA((12,)),
            DMA((12,)),
            DMA((12, 2, n)),
            DMA((12, n)),
            DMA((3,)),
            DMA((1, 2, n)),
            DMA((1, n)),
            DMA((3,)),
            DMA((2,)),
            DMA((2,)),
            DMA((2,)),
            DMA((n, 4)),
            DMA((n, 4)),
            DMA((4,)),
            DMA((4,)),
            DMA((4, 3)),
            DMA((4, 3)),
            DMA((4, 3)),
            DMA((4, 3)),
            DMA((4, 4)),
            DMA((4, 4)),
            DMA((16,)),
        ],
        compiler_params=pltpu.CompilerParams(
            collective_id=0, has_side_effects=True, vmem_limit_bytes=62 * 2**20
        ),
        name="head",
    )(x_in, z_in, wq, wkv, wo, wg, wu, wd, small, cosine, sine, row_lo, row_hi)


class Group:
    def __init__(self):
        self.l, self.x, self.y, self.c = place()
        self.mate = device(self.l, self.x, self.y, 1 - self.c)

    def other(self, i):
        x = 1 - self.x if i & 1 else self.x
        y = 1 - self.y if i & 2 else self.y
        return x, y

    def chip(self, i):
        x, y = self.other(i)
        return device(self.l, x, y, self.c)

    def partners(self):
        return [(self.mate, None)] + [(self.chip(i), None) for i in (1, 2, 3)]


def ffn_kernel(
    n,
    inner_any,
    z_own,
    z_other,
    g_in,
    own_in,
    out_ref,
    din_ref,
    part_out,
    dgw,
    duw,
    ddw,
    inner_ref,
    dz_ref,
    inner_t,
    out_acc,
    din_acc,
    g,
    land,
    low,
    prod_t,
    ag_send,
    ag_recv,
    rs_send,
    rs_recv,
    b_send,
    b_recv,
    b_loc,
    in_loc,
    o_loc,
):
    chunks = 3
    line = Line(n, g, ag_send, ag_recv, land, rs_send, rs_recv)
    l, x = line.l, line.x
    blocks = 2 * n
    width = blocks * 256
    back = Back(line, (dgw, duw, ddw), b_send, b_recv, b_loc, 256)
    loads = [
        pltpu.make_async_copy(own_in, g.at[pl.ds(6, 3), pl.ds(2 * l, 2)], in_loc.at[0]),
        pltpu.make_async_copy(inner_any, inner_ref, in_loc.at[1]),
        pltpu.make_async_copy(z_own, dz_ref.at[:, x], in_loc.at[2]),
        pltpu.make_async_copy(z_other, dz_ref.at[:, 1 - x], in_loc.at[3]),
        pltpu.make_async_copy(g_in.at[pl.ds(3, 6)], g.at[pl.ds(0, 6)], in_loc.at[4]),
    ]
    for copy in loads:
        copy.start()
    greet(line.partners() + [back.partner()])
    loads[0].wait()
    for item in range(6, 9):
        line.ag_start(item)
    for copy in loads[1:]:
        copy.wait()

    def turn(i, unused):
        m, s = lax.div(i, blocks), lax.rem(i, blocks)
        tile = inner_ref[m, :, pl.ds(pl.multiple_of(s * 256, 256), 256)]
        inner_t[s, :, pl.ds(pl.multiple_of(m * 256, 256), 256)] = tile.T
        return 0

    lax.fori_loop(0, 4 * blocks, turn, 0)

    def compute(j):
        base = 3 * j

        def rows(m, unused):
            a = inner_ref[m]
            d = dz_ref[m].reshape(256, width)
            gated = dot(a, g[base].reshape(width, 256))
            upward = dot(a, g[base + 1].reshape(width, 256))
            grad = dot_t(d[:, :256], g[base + 2, 0])
            for s in range(1, blocks):
                grad = grad + dot_t(d[:, s * 256 : (s + 1) * 256], g[base + 2, s])
            sigma = jax.nn.sigmoid(gated)
            swish = gated * sigma
            product = (swish * upward).astype(BF)
            d_gated = (grad * upward * sigma * (1.0 + gated * (1.0 - sigma))).astype(BF)
            d_upward = (grad * swish).astype(BF)
            at = pl.ds(pl.multiple_of(m * 256, 256), 256)
            low[0, at] = d_gated
            low[1, at] = d_upward
            prod_t[:, at] = product.T
            for s in range(blocks):
                cols = slice(s * 256, (s + 1) * 256)
                o = dot(product, g[base + 2, s])
                i = dot_t(d_gated, g[base, s]) + dot_t(d_upward, g[base + 1, s])
                if j == 0:
                    out_acc[m, :, cols] = o
                    din_acc[m, :, cols] = i
                else:
                    out_acc[m, :, cols] += o
                    din_acc[m, :, cols] += i
            return 0

        lax.fori_loop(0, 4, rows, 0)

        def weights(s, unused):
            t = inner_t[s]
            g[base, s] = dot(t, low[0]).astype(BF)
            g[base + 1, s] = dot(t, low[1]).astype(BF)
            z = dz_ref[:, :, :, :, pl.ds(pl.multiple_of(s * 256, 256), 256)].reshape(1024, 256)
            g[base + 2, s] = dot(prod_t[...], z).astype(BF)
            return 0

        lax.fori_loop(0, blocks, weights, 0)

    def items(j, body):
        each(3, lambda i: body(3 * j + i))

    compute(0)
    for t in range(1, n):
        items(2, lambda item, t=t: line.pump(item, t))
        items(0, lambda item, t=t: line.rs_step(item, t))
    compute(1)
    items(0, line.rs_final)
    for kind in range(3):
        back.start(kind, kind, 0)
    items(2, line.collect)
    items(2, line.ag_end)
    compute(2)
    parts = pltpu.make_async_copy(g.at[pl.ds(3, 6)], part_out, o_loc.at[2])
    parts.start()

    def flush(m, unused):
        inner_ref[m] = out_acc[m].astype(BF)
        dz_ref[m] = din_acc[m].astype(BF).reshape(2, 4, 32, width)
        return 0

    lax.fori_loop(0, 4, flush, 0)
    outs = [
        pltpu.make_async_copy(inner_ref, out_ref, o_loc.at[0]),
        pltpu.make_async_copy(dz_ref, din_ref, o_loc.at[1]),
        parts,
    ]
    for copy in outs[:2]:
        copy.start()
    for kind in range(3):
        back_wait(back, kind, kind, 0)
    items(0, line.rs_end)
    for copy in outs:
        copy.wait()


def ffn(n, inner, z_own, z_other, g_in, own_in):
    d = inner.shape[-1]
    m = 2 * n
    bf = lambda *shape: jax.ShapeDtypeStruct(shape, BF)
    vb = lambda *shape: pltpu.VMEM(shape, BF)
    return pl.pallas_call(
        functools.partial(ffn_kernel, n),
        out_shape=(
            bf(4, 256, d),
            bf(4, 2, 4, 32, d),
            bf(6, m, 256, 256),
            bf(256, 512),
            bf(256, 512),
            bf(512, 256),
        ),
        in_specs=[ANY] * 5,
        out_specs=(ANY,) * 6,
        scratch_shapes=[
            vb(4, 256, d),
            vb(4, 2, 4, 32, d),
            vb(m, 256, 1024),
            pltpu.VMEM((4, 256, d), F32),
            pltpu.VMEM((4, 256, d), F32),
            vb(9, m, 256, 256),
            vb(3, m + 2, 256, 256),
            vb(2, 1024, 256),
            vb(256, 1024),
            DMA((9, 2, n)),
            DMA((9, n)),
            DMA((3, 2, n)),
            DMA((3, n + 1)),
            DMA((3,)),
            DMA((3,)),
            DMA((3,)),
            DMA((5,)),
            DMA((3,)),
        ],
        compiler_params=pltpu.CompilerParams(
            collective_id=9, has_side_effects=True, vmem_limit_bytes=62 * 2**20
        ),
        name="ffn",
    )(inner, z_own, z_other, g_in, own_in)


def tail_kernel(
    n,
    din_any,
    out_any,
    x_any,
    z_any,
    hidden_any,
    ffn_parts,
    normed_any,
    g_any,
    kv_any,
    q_any,
    qp_any,
    kp_any,
    att_any,
    lse_any,
    gate_ref,
    small_g,
    small,
    cos_ref,
    sin_ref,
    row_lo,
    row_hi,
    res_out,
    grad_out,
    dq_out,
    dkv_out,
    do_out,
    dg_out,
    du_out,
    dd_out,
    sums_out,
    g,
    land,
    w,
    normed_t,
    dbr,
    kv,
    kv_land,
    q_v,
    qp,
    kp,
    att,
    lse,
    core_land,
    chip_land,
    low,
    hidden,
    d_hid,
    own_z,
    own_x,
    own_res,
    own_grad,
    mixed_t,
    dql,
    dpl,
    dl,
    dl_t,
    gain_row,
    gain_sum,
    head_sum,
    sums,
    sum_c,
    sum_x,
    sum_y,
    sum_l,
    loads,
    rs_send,
    rs_recv,
    b_send,
    b_recv,
    b_loc,
    kv_send,
    kv_recv,
    c_send,
    c_recv,
    s_send,
    s_recv,
    i_send,
    i_recv,
    j_send,
    j_recv,
    h_send,
    h_recv,
    t_send,
    t_recv,
    o_loc,
):
    line = Line(n, g, None, None, land, rs_send, rs_recv)
    l, x, y, c = line.l, line.x, line.y, line.c
    k = y * 2 + c
    group = Group()
    mate = group.mate
    left = device(l - 1, x, y, c)
    blocks = 2 * n
    width = blocks * 256
    scale = HEAD_SIZE ** (-0.5)
    first = Back(line, (dq_out, dkv_out, do_out), b_send, b_recv, b_loc, 256)
    rest = Back(line, (dg_out, du_out, dd_out), b_send, b_recv, b_loc, 512)

    def backward(item):
        if item < 3:
            return first, item, item, 0
        return rest, item, item % 3, item // 3 - 1

    pending = {}

    def load(name, src, dst):
        copy = pltpu.make_async_copy(src, dst, loads.at[len(pending)])
        copy.start()
        pending[name] = copy

    load("din", din_any.at[:, :, :, c], low)
    load("hidden", hidden_any, hidden)
    load("z", z_any.at[:, k], own_z)
    load("ffn", ffn_parts, g.at[pl.ds(3, 6)])
    load("w", g_any.at[pl.ds(0, 3)], w)
    load("kv", kv_any, kv)
    load("q", q_any, q_v)
    load("att", att_any, att)
    load("lse", lse_any, lse)
    load("qp", qp_any, qp)
    load("kp", kp_any, kp)
    load("normed", normed_any, normed_t)
    load("x", x_any.at[:, k], own_x)

    others = [device(lax.rem(l + d, n), x, y, c) for d in range(1, n)]
    greet(
        [(o, None) for o in others] + [(mate, None)] + [(group.chip(i), None) for i in (1, 2, 3)]
    )

    def mate_copy(r, src, m):
        return remote(
            src.at[m, :, :, 1 - c], core_land.at[r % 2, m], c_send.at[r, m], c_recv.at[r, m], mate
        )

    def chip_copy(r, m, o):
        ox, oy = group.other(o)
        return remote(
            low.at[m, ox, oy],
            chip_land.at[r % 2, o - 1, m],
            s_send.at[r, m, o - 1],
            s_recv.at[r, m, o - 1],
            group.chip(o),
        )

    def to_chips(r, src, m, own):
        mate_copy(r, src, m).wait_recv()
        for u in range(2):
            for v in range(2):
                low[m, u, v] = (
                    own(m, u, v).astype(F32) + core_land[r % 2, m, u, v].astype(F32)
                ).astype(BF)
        for o in (3, 1, 2):
            chip_copy(r, m, o).start()

    def total_of(r, m):
        total = low[m, x, y].astype(F32)
        for o in (1, 2, 3):
            chip_copy(r, m, o).wait_recv()
            total = total + chip_land[r % 2, o - 1, m].astype(F32)
        return total

    def group_end(r, src):
        def done(m):
            mate_copy(r, src, m).wait_send()
            for o in (1, 2, 3):
                chip_copy(r, m, o).wait_send()

        each(4, done)

    each(4, lambda m: mate_copy(0, din_any, m).start())
    pending["ffn"].wait()
    line.rs_fire(3)
    line.rs_fire(4)
    for s in range(blocks):
        cols = slice(s * 256, (s + 1) * 256)
        gain_row[:, cols] = small_g[0, s, 4:6, :].astype(F32)
    gain_sum[...] = jnp.zeros_like(gain_sum)
    head_sum[...] = jnp.zeros_like(head_sum)
    pending["din"].wait()
    pending["hidden"].wait()
    pending["z"].wait()
    each(4, lambda m: to_chips(0, din_any, m, lambda m, u, v: low[m, u, v]))
    line.rs_mid(3, 1)

    def spread(m, o):
        here = dbr.at[m, x, y, c]
        return remote(here, here, i_send.at[m, o - 1], i_recv.at[m, o - 1], group.chip(o))

    def spread_mate(m, o):
        ox, oy = group.other(o)
        there = dbr.at[m, ox, oy, c]
        return remote(there, there, j_send.at[m, o], j_recv.at[m, o], mate)

    def finish(m):
        total = total_of(0, m)
        h = hidden[m]
        r = lax.rsqrt(jnp.mean(h * h, axis=-1, keepdims=True) + EPS)
        normal = h * r
        gain_sum[1:2] += jnp.sum(total * normal, axis=0, keepdims=True)
        e = total * gain_row[1:2, :]
        grad = own_z[m].astype(F32) + r * (
            e - normal * jnp.mean(e * normal, axis=-1, keepdims=True)
        )
        d_hid[m] = grad
        dbr[m, x, y, c] = grad.astype(BF)
        for o in (3, 1, 2):
            spread(m, o).start()
        spread_mate(m, 0).start()

    each(4, finish)
    line.rs_mid(3, 2)
    line.rs_fire(5)
    line.rs_mid(4, 1)
    line.rs_mid(3, 3)
    for name in ("w", "kv", "q", "att", "lse", "qp", "kp", "normed", "x"):
        pending[name].wait()
    line.rs_mid(4, 2)

    def pass_on(m):
        for o in (1, 2, 3):
            spread(m, o).wait_recv()
            spread_mate(m, o).start()

    each(4, pass_on)
    group_end(0, din_any)
    own_low = pltpu.make_async_copy(out_any.at[:, :, :, c], low, o_loc.at[0])
    own_low.start()
    each(4, lambda m: mate_copy(1, out_any, m).start())
    line.rs_fire(6)
    line.rs_mid(4, 3)

    def arrive(m):
        for o in range(4):
            spread_mate(m, o).wait_recv()

    def attend_back(m):
        arrive(m)
        d = dbr[m].reshape(256, width)
        gm = dot_t(d[:, :256], w[2, 0])
        for s in range(1, blocks):
            gm = gm + dot_t(d[:, s * 256 : (s + 1) * 256], w[2, s])
        gates = gate_ref[m]
        gates = jnp.where(x == 0, gates[:, 0:2], gates[:, 2:4])
        g0, g1 = gates[:, 0:1], gates[:, 1:2]
        a0, a1 = att[m, :256], att[m, 256:]
        d0, d1 = gm[:, :128], gm[:, 128:]
        l0 = jnp.sum(d0 * a0, axis=-1, keepdims=True) * g0 * (1.0 - g0)
        l1 = jnp.sum(d1 * a1, axis=-1, keepdims=True) * g1 * (1.0 - g1)
        lane = lax.broadcasted_iota(jnp.int32, (256, 128), 1)
        logits = jnp.where(lane == 2 * x, l0, 0.0) + jnp.where(lane == 2 * x + 1, l1, 0.0)
        logits = logits.astype(BF)
        dl[m] = logits
        at = pl.ds(pl.multiple_of(m * 256, 256), 256)
        dl_t[:, at] = logits.T
        mixed = jnp.concatenate([a0 * g0, a1 * g1], axis=1).astype(BF)
        mixed_t[:, at] = mixed.T
        da = jnp.concatenate([d0 * g0, d1 * g1], axis=0).astype(BF)
        delta = jnp.sum(da.astype(F32) * att[m], axis=-1, keepdims=True)
        log_total = lse[m][:, :1]
        qm = q_v[m]
        att[m] = jnp.zeros((512, 128), F32)

        def block(b, unused):
            pair = kv[b, m]
            keys, values = pair[:, :128], pair[:, 128:]
            raw = dot_t(qm, keys) * scale
            lo = row_lo[m][:, :1] - b * 256
            hi = row_hi[m][:, :1] - b * 256
            column = lax.broadcasted_iota(jnp.int32, (512, 256), 1)
            allowed = (column >= jnp.concatenate([lo, lo], axis=0)) & (
                column < jnp.concatenate([hi, hi], axis=0)
            )
            p = jnp.where(allowed, jnp.exp(raw - log_total), 0.0)
            ds = (p * (dot_t(da, values) - delta)).astype(BF)
            att[m] += dot(ds, keys)
            dk = dot(ds.T, qm) * scale
            dv = dot(p.astype(BF).T, da)
            kv[b, m] = jnp.concatenate([dk, dv], axis=1).astype(BF)
            return 0

        lax.fori_loop(0, l + 1, block, 0)

    def kv_copy(b, m):
        return remote(
            kv.at[b, m], kv_land.at[b, m], kv_send.at[b, m], kv_recv.at[b, m], left
        )

    def kv_step(m):
        for b in range(n - 1):

            @pl.when(l > b)
            def _(b=b):
                @pl.when(l <= n - 2)
                def _():
                    kv_copy(b, m).wait_recv()
                    kv[b, m] = (kv[b, m].astype(F32) + kv_land[b, m].astype(F32)).astype(BF)

                kv_copy(b, m).start()

    def normal_back(u, d_rot, gain, cosine, sine):
        d = d_rot * cosine - pltpu.roll(d_rot, 64, 1) * sine
        r = lax.rsqrt(jnp.mean(u * u, axis=-1, keepdims=True) + EPS)
        normal = u * r
        e = d * gain
        grad = r * (e - normal * jnp.mean(e * normal, axis=-1, keepdims=True))
        return grad.astype(BF), jnp.sum(d * normal, axis=0, keepdims=True)

    gains = small[8:10, :128].astype(F32)

    def query_back(m):
        for h in range(2):
            cols = slice(h * 128, (h + 1) * 128)
            grad, total = normal_back(
                qp[m][:, cols],
                att[m, h * 256 : (h + 1) * 256] * scale,
                gains[0:1],
                cos_ref[m],
                sin_ref[m],
            )
            dql[m, :, cols] = grad
            head_sum[0:1, :128] += total

    attend_back(0)
    line.rs_mid(5, 1)
    attend_back(1)
    kv_step(0)
    line.rs_mid(5, 2)
    line.rs_fire(7)
    attend_back(2)
    kv_step(1)
    line.rs_mid(5, 3)
    line.rs_mid(6, 1)
    attend_back(3)
    kv_step(2)
    kv_step(3)
    line.rs_mid(6, 2)
    line.rs_fire(8)
    each(4, query_back)

    def output_weights(s, unused):
        z = dbr[:, :, :, :, :, pl.ds(pl.multiple_of(s * 256, 256), 256)].reshape(1024, 256)
        g[2, s] = dot(mixed_t[...], z).astype(BF)
        return 0

    def query_weights(s, unused):
        g[0, s] = dot(normed_t[s], dql[...].reshape(1024, 256)).astype(BF)
        sums[1, s] = dot_t(dl_t[:16], normed_t[s])[:8]
        return 0

    lax.fori_loop(0, blocks, output_weights, 0)
    line.rs_fire(2)
    lax.fori_loop(0, blocks, query_weights, 0)
    line.rs_fire(0)
    line.rs_mid(6, 3)
    line.rs_mid(7, 1)
    own_low.wait()
    each(4, lambda m: to_chips(1, out_any, m, lambda m, u, v: low[m, u, v]))
    line.rs_mid(7, 2)

    def key_back(m):
        pl.when(l <= n - 2)(lambda: kv_copy(l, m).wait_recv())
        pair = kv[l, m].astype(F32)
        pair = pair + jnp.where(l <= n - 2, kv_land[l, m].astype(F32), 0.0)
        grad, total = normal_back(kp[m], pair[:, :128], gains[1:2], cos_ref[m], sin_ref[m])
        dpl[m, :, :128] = grad
        dpl[m, :, 128:] = pair[:, 128:].astype(BF)
        head_sum[0:1, 128:] += total

    each(4, key_back)

    def key_weights(s, unused):
        g[1, s] = dot(normed_t[s], dpl[...].reshape(1024, 256)).astype(BF)
        return 0

    lax.fori_loop(0, blocks, key_weights, 0)
    line.rs_fire(1)

    def finish_out(m):
        own_res[m] = (hidden[m] + total_of(1, m)).astype(BF)

    each(4, finish_out)
    group_end(1, out_any)

    def normed_back(m):
        a, b, e = dql[m], dpl[m], dl[m][:, :16]
        for s in range(blocks):
            part = dot_t(a, w[0, s]) + dot_t(b, w[1, s]) + dot(e, small_g[0, s])
            dbr[m, :, :, :, :, s * 256 : (s + 1) * 256] = part.astype(BF).reshape(
                2, 2, 2, 32, 256
            )
        mate_copy(2, dbr, m).start()

    def home(i, own, out):
        mine = out.at[:, k]
        there = out.at[:, (1 - y) * 2 + c]
        keep = pltpu.make_async_copy(own, mine, o_loc.at[1 + i])
        over = remote(own, mine, h_send.at[i, 0], h_recv.at[i, 0], group.chip(2))
        beside = remote(own, mine, h_send.at[i, 1], h_recv.at[i, 1], mate)
        on = remote(there, there, h_send.at[i, 2], h_recv.at[i, 2], mate)
        return keep, over, beside, on

    def drain_spread(m):
        for o in (1, 2, 3):
            spread(m, o).wait_send()
        for o in range(4):
            spread_mate(m, o).wait_send()

    each(4, drain_spread)
    each(4, normed_back)
    res_home = home(0, own_res, res_out)
    for copy in res_home[:3]:
        copy.start()
    line.rs_mid(7, 3)
    line.rs_mid(8, 1)
    line.rs_mid(8, 2)
    each(4, lambda m: to_chips(2, dbr, m, lambda m, u, v: dbr[m, u, v, c]))
    line.rs_mid(8, 3)
    line.rs_mid(2, 1)

    def finish_grad(m):
        total = total_of(2, m)
        v = own_x[m].astype(F32)
        r = lax.rsqrt(jnp.mean(v * v, axis=-1, keepdims=True) + EPS)
        normal = v * r
        gain_sum[0:1] += jnp.sum(total * normal, axis=0, keepdims=True)
        e = total * gain_row[0:1, :]
        own_grad[m] = (
            d_hid[m] + r * (e - normal * jnp.mean(e * normal, axis=-1, keepdims=True))
        ).astype(BF)

    each(4, finish_grad)
    for s in range(blocks):
        sums[0, s, 0:2] = gain_sum[0:2, s * 256 : (s + 1) * 256]
        sums[0, s, 2:3] = head_sum[0:1]
        sums[0, s, 3:8] = jnp.zeros((5, 256), F32)
    small_c = remote(sums.at[0], sum_c, t_send.at[0], t_recv.at[0], mate)
    small_x = remote(sums, sum_x, t_send.at[1], t_recv.at[1], group.chip(1))
    small_y = remote(sums.at[0], sum_y, t_send.at[2], t_recv.at[2], group.chip(2))
    small_c.start()
    grad_home = home(1, own_grad, grad_out)
    for copy in grad_home[:3]:
        copy.start()
    res_home[1].wait_recv()
    res_home[3].start()
    line.rs_mid(2, 2)
    line.rs_mid(2, 3)
    small_c.wait()
    sums[0] = sums[0] + sum_c[...]
    small_x.start()
    line.rs_mid(0, 1)
    line.rs_mid(0, 2)
    small_x.wait()
    sums[...] = sums[...] + sum_x[...]
    small_y.start()
    line.rs_mid(0, 3)
    line.rs_mid(1, 1)
    small_y.wait()
    sums[0] = sums[0] + sum_y[...]

    def small_line(d):
        to = lax.rem(l + d, n)
        return remote(
            sums.at[:, pl.ds(2 * to, 2)],
            sum_l.at[l],
            t_send.at[2 + d],
            t_recv.at[2 + d],
            device(to, x, y, c),
        )

    for d in range(1, n):
        small_line(d).start()
    sum_l[l] = sums[:, pl.ds(2 * l, 2)]
    line.rs_mid(1, 2)
    line.rs_mid(1, 3)
    grad_home[1].wait_recv()
    grad_home[3].start()
    for item in (3, 4, 5, 6, 7, 8, 2, 0, 1):
        line.rs_final(item)
        back, item, kind, j = backward(item)
        back.start(item, kind, j)
    for d in range(1, n):
        small_line(d).wait()
    total = sum_l[0, :, x]
    for i in range(1, n):
        total = total + sum_l[i, :, x]
    sums_out[...] = total
    for item in (3, 4, 5, 6, 7, 8, 2, 0, 1):
        back, item, kind, j = backward(item)
        back_wait(back, item, kind, j)
    for copies in (res_home, grad_home):
        keep, over, beside, on = copies
        keep.wait()
        over.wait_send()
        beside.wait()
        on.wait()
    group_end(2, dbr)

    def drain(m):
        for b in range(n - 1):
            pl.when(l > b)(lambda b=b: kv_copy(b, m).wait_send())

    each(4, drain)
    each(9, line.rs_end)


def tail(n, din, out, x_in, z_in, hidden, ffn_parts, normed_t, g_all, kv, q, qp, kp, att, lse, gate, small_g, small, cosine, sine, row_lo, row_hi):
    d = x_in.shape[-1]
    m = 2 * n
    bf = lambda *shape: jax.ShapeDtypeStruct(shape, BF)
    vb = lambda *shape: pltpu.VMEM(shape, BF)
    vf = lambda *shape: pltpu.VMEM(shape, F32)
    return pl.pallas_call(
        functools.partial(tail_kernel, n),
        out_shape=(
            bf(4, 4, 32, d),
            bf(4, 4, 32, d),
            bf(256, 512),
            bf(256, 512),
            bf(512, 256),
            bf(256, 1024),
            bf(256, 1024),
            bf(1024, 256),
            jax.ShapeDtypeStruct((2, 8, 256), F32),
        ),
        in_specs=[ANY] * 14 + [VM] * 7,
        out_specs=(ANY,) * 8 + (VM,),
        scratch_shapes=[
            vb(9, m, 256, 256),
            vb(9, m + 2, 256, 256),
            vb(3, m, 256, 256),
            vb(m, 256, 1024),
            vb(4, 2, 2, 2, 32, d),
            vb(n, 4, 256, 256),
            vb(n, 4, 256, 256),
            vb(4, 512, 128),
            vf(4, 256, 256),
            vf(4, 256, 128),
            vf(4, 512, 128),
            vf(4, 512, 128),
            vb(2, 4, 2, 2, 32, d),
            vb(2, 3, 4, 32, d),
            vb(4, 2, 2, 32, d),
            vf(4, 32, d),
            vf(4, 32, d),
            vb(4, 32, d),
            vb(4, 32, d),
            vb(4, 32, d),
            vb(4, 32, d),
            vb(256, 1024),
            vb(4, 256, 256),
            vb(4, 256, 256),
            vb(4, 256, 128),
            vb(128, 1024),
            vf(2, d),
            vf(2, d),
            vf(1, 256),
            vf(2, m, 8, 256),
            vf(m, 8, 256),
            vf(2, m, 8, 256),
            vf(m, 8, 256),
            vf(n, 2, 2, 8, 256),
            DMA((13,)),
            DMA((9, 2, n)),
            DMA((9, n + 1)),
            DMA((9,)),
            DMA((9,)),
            DMA((9,)),
            DMA((n, 4)),
            DMA((n, 4)),
            DMA((3, 4)),
            DMA((3, 4)),
            DMA((3, 4, 3)),
            DMA((3, 4, 3)),
            DMA((4, 3)),
            DMA((4, 3)),
            DMA((4, 4)),
            DMA((4, 4)),
            DMA((2, 3)),
            DMA((2, 3)),
            DMA((3 + n,)),
            DMA((3 + n,)),
            DMA((3,)),
        ],
        compiler_params=pltpu.CompilerParams(
            collective_id=10, has_side_effects=True, vmem_limit_bytes=63 * 2**20
        ),
        name="tail",
    )(din, out, x_in, z_in, hidden, ffn_parts, normed_t, g_all, kv, q, qp, kp, att, lse, gate, small_g, small, cosine, sine, row_lo, row_hi)


def row_layout(index, buckets, lengths):
    ends = jnp.cumsum(buckets)
    starts = ends - buckets
    member = (index[:, None] >= starts[None, :]) & (index[:, None] < ends[None, :])
    position = index - jnp.sum(jnp.where(member, starts[None, :], 0), axis=1)
    limit = jnp.sum(jnp.where(member, lengths[None, :], 0), axis=1)
    return (None, position, limit)


def fast_local(
    inputs,
    cotangent,
    bucket_sizes,
    true_lengths,
    attention_gain,
    feedforward_gain,
    query_gain,
    key_gain,
    query_weight,
    key_matrix,
    value_matrix,
    headgate_weight,
    output_weight,
    gate_weight,
    up_weight,
    down_weight,
):
    batches, rows, width = inputs.shape
    n = lax.axis_size("seq") // 2
    seq, kv = lax.axis_index("seq"), lax.axis_index("kv")
    l, x = seq // 2, seq % 2
    scale = HEAD_SIZE ** (-0.5)
    span = 2 * rows
    gain_query = query_gain.astype(F32)
    gain_key = key_gain.astype(F32)

    own_small = jnp.concatenate(
        [
            headgate_weight.T,
            attention_gain[None],
            feedforward_gain[None],
            jnp.zeros((2, 256), BF),
            jnp.pad(jnp.stack([query_gain, key_gain]), ((0, 0), (0, 128))),
            jnp.zeros((6, 256), BF),
        ],
        axis=0,
    )
    paired = jnp.concatenate(
        [key_matrix[:, :128], value_matrix[:, :128], key_matrix[:, 128:], value_matrix[:, 128:]],
        axis=1,
    )

    row_index = l * span + jnp.arange(span, dtype=jnp.int32)
    layouts = [row_layout(row_index, bucket_sizes[b], true_lengths[b]) for b in range(batches)]
    positions = jnp.concatenate([item[1] for item in layouts])
    row_lo = jnp.stack([row_index - item[1] for item in layouts])
    limits = jnp.stack([item[2] for item in layouts])
    row_hi = jnp.minimum(row_index + 1, row_lo + limits)
    cosine, sine = rope_tables(positions, HEAD_SIZE)
    signed = sine * jnp.where(jnp.arange(HEAD_SIZE) < HEAD_SIZE // 2, -1.0, 1.0)
    x_split = inputs.reshape(batches, 4, 32, width)
    z_split = cotangent.reshape(batches, 4, 32, width)
    cosine = cosine.reshape(batches, span, HEAD_SIZE)
    signed = signed.reshape(batches, span, HEAD_SIZE)
    row_lo = jnp.broadcast_to(row_lo[:, :, None], (batches, span, 128))
    row_hi = jnp.broadcast_to(row_hi[:, :, None], (batches, span, 128))
    (g_all, g_own, normed_t, kv_all, query, query_proj, key_proj, gate, attended, log_total, hidden, inner, z_other, small) = head(
        n,
        x_split,
        z_split,
        query_weight,
        paired,
        output_weight,
        gate_weight,
        up_weight,
        down_weight,
        own_small,
        cosine,
        signed,
        row_lo,
        row_hi,
    )
    split = (batches, 2, 2, 2, 32, width)
    out_part, din_part, ffn_parts, d_gate, d_up, d_down = ffn(
        n, inner.reshape(batches, span, width), z_split, z_other, g_all, g_own
    )
    (own_out, own_grad, dq, dkv, do, d_gate2, d_up2, d_down2, sums) = tail(
        n,
        din_part.reshape(split),
        out_part.reshape(split),
        x_split,
        z_split,
        hidden,
        ffn_parts,
        normed_t,
        g_all,
        kv_all,
        query,
        query_proj,
        key_proj,
        attended,
        log_total,
        gate,
        small,
        own_small,
        cosine,
        signed,
        row_lo,
        row_hi,
    )

    def joined(first, rest, axis):
        a, b = jnp.split(first.astype(F32), 2, axis=axis)
        c, d = jnp.split(rest.astype(F32), 2, axis=axis)
        return jnp.concatenate([a, c, b, d], axis=axis)

    return (
        own_out.reshape(batches, rows, width),
        own_grad.reshape(batches, rows, width),
        sums[0, 0],
        sums[0, 1],
        sums[0, 2, :HEAD_SIZE],
        sums[0, 2, HEAD_SIZE:],
        dq.astype(F32),
        jnp.concatenate([dkv[:, :128], dkv[:, 256:384]], axis=1).astype(F32),
        jnp.concatenate([dkv[:, 128:256], dkv[:, 384:]], axis=1).astype(F32),
        sums[1, :4].T,
        do.astype(F32),
        joined(d_gate, d_gate2, 1),
        joined(d_up, d_up2, 1),
        joined(d_down, d_down2, 0),
    )


def solution(mesh):
    chosen = fast_local if dict(mesh.shape) == {"seq": 8, "kv": 4} else local
    in_specs = (
        P(None, "seq", None),
        P(None, "seq", None),
        P(),
        P(),
        P("seq"),
        P("seq"),
        P(),
        P(),
        P("seq", "kv"),
        P("seq", "kv"),
        P("seq", "kv"),
        P("seq", "kv"),
        P("kv", "seq"),
        P("seq", "kv"),
        P("seq", "kv"),
        P("kv", "seq"),
    )
    out_specs = (
        P(None, "seq", None),
        P(None, "seq", None),
        P("seq"),
        P("seq"),
        P(),
        P(),
        P("seq", "kv"),
        P("seq", "kv"),
        P("seq", "kv"),
        P("seq", "kv"),
        P("kv", "seq"),
        P("seq", "kv"),
        P("seq", "kv"),
        P("kv", "seq"),
    )
    return jax.shard_map(chosen, mesh=mesh, in_specs=in_specs, out_specs=out_specs, check_vma=False)
```

```python
import functools
import math

import jax
import jax.numpy as jnp
from jax import lax
from jax.experimental import pallas as pl
from jax.experimental.pallas import tpu as pltpu
from jax.sharding import PartitionSpec as P

HEAD_SIZE = 128


EPS = 1e-06
ROPE_BASE = 1000000.0
MASKED = -1e30


def rms_scale(values):
    return lax.rsqrt(jnp.mean(values * values, axis=-1, keepdims=True) + EPS)


def norm_backward(grad, normal, factor):
    return factor * (grad - normal * jnp.mean(grad * normal, axis=-1, keepdims=True))


def rope_tables(positions, width):
    half = width // 2
    steps = jnp.arange(half, dtype=jnp.float32) * (2.0 / width)
    inverse = jnp.exp(-steps * math.log(ROPE_BASE))
    angles = positions.astype(jnp.float32)[:, None] * inverse[None, :]
    cosine = jnp.cos(angles)
    sine = jnp.sin(angles)
    return (jnp.concatenate([cosine, cosine], axis=-1), jnp.concatenate([sine, sine], axis=-1))


def rotate_forward(values, cosine, sine):
    half = values.shape[-1] // 2
    turned = jnp.concatenate([-values[..., half:], values[..., :half]], axis=-1)
    return values * cosine[:, None, :] + turned * sine[:, None, :]


def rotate_backward(grad, cosine, sine):
    half = grad.shape[-1] // 2
    moved = grad * sine[:, None, :]
    return grad * cosine[:, None, :] + jnp.concatenate(
        [moved[..., half:], -moved[..., :half]], axis=-1
    )


def token_layout(index, buckets, lengths):
    ends = jnp.cumsum(buckets)
    starts = ends - buckets
    member = (index[:, None] >= starts[None, :]) & (index[:, None] < ends[None, :])
    labels = jnp.arange(buckets.shape[0], dtype=jnp.int32)
    segment = jnp.sum(jnp.where(member, labels[None, :], 0), axis=1)
    position = index - jnp.sum(jnp.where(member, starts[None, :], 0), axis=1)
    limit = jnp.sum(jnp.where(member, lengths[None, :], 0), axis=1)
    return (segment, position, position < limit)


def outer_sum(left, right):
    return lax.dot_general(
        left, right, (((0,), (0,)), ((), ())), preferred_element_type=jnp.float32
    )


def times_transpose(left, weight):
    return lax.dot_general(
        left, weight, (((1,), (1,)), ((), ())), preferred_element_type=jnp.float32
    )


def block_scores(query_kg, key_block, start, row_index, row_segment, buckets, lengths, scale):
    key_index = start + jnp.arange(key_block.shape[0], dtype=jnp.int32)
    key_segment, key_position, key_valid = token_layout(key_index, buckets, lengths)
    allowed = (
        (row_segment[:, None] == key_segment[None, :])
        & (key_index[None, :] <= row_index[:, None])
        & key_valid[None, :]
    )
    raw = (
        jnp.einsum("kgtd,skd->kgts", query_kg, key_block, preferred_element_type=jnp.float32)
        * scale
    )
    return (jnp.where(allowed, raw, MASKED), allowed)


def split_blocks(keys, values, block):
    blocks = keys.shape[0] // block
    key_blocks = keys.reshape(blocks, block, keys.shape[1], keys.shape[2])
    value_blocks = values.reshape(blocks, block, values.shape[1], values.shape[2])
    starts = jnp.arange(blocks) * block
    return (key_blocks, value_blocks, starts)


def attention_forward(
    query_kg, keys, values, row_index, row_segment, buckets, lengths, block, scale
):
    key_blocks, value_blocks, starts = split_blocks(keys, values, block)

    def first_pass(carry, item):
        running_max, total = carry
        key_block, start = item
        masked, allowed = block_scores(
            query_kg, key_block, start, row_index, row_segment, buckets, lengths, scale
        )
        new_max = jnp.maximum(running_max, jnp.max(masked, axis=-1))
        total = total * jnp.exp(running_max - new_max) + jnp.sum(
            jnp.where(allowed, jnp.exp(masked - new_max[..., None]), 0.0), axis=-1
        )
        return ((new_max, total), None)

    begin = (
        jnp.full(query_kg.shape[:3], MASKED, jnp.float32),
        jnp.zeros(query_kg.shape[:3], jnp.float32),
    )
    (running_max, total), unused = lax.scan(first_pass, begin, (key_blocks, starts))
    log_total = running_max + jnp.log(total)

    def second_pass(accumulated, item):
        key_block, value_block, start = item
        masked, allowed = block_scores(
            query_kg, key_block, start, row_index, row_segment, buckets, lengths, scale
        )
        weights = jnp.where(allowed, jnp.exp(masked - log_total[..., None]), 0.0).astype(
            jnp.bfloat16
        )
        return (
            accumulated
            + jnp.einsum(
                "kgts,skd->kgtd", weights, value_block, preferred_element_type=jnp.float32
            ),
            None,
        )

    attended, unused = lax.scan(
        second_pass, jnp.zeros(query_kg.shape, jnp.float32), (key_blocks, value_blocks, starts)
    )
    return (attended, log_total)


def attention_backward(
    query_kg,
    grad_kg,
    log_total,
    delta,
    keys,
    values,
    row_index,
    row_segment,
    buckets,
    lengths,
    block,
    scale,
):
    key_blocks, value_blocks, starts = split_blocks(keys, values, block)

    def step(grad_query, item):
        key_block, value_block, start = item
        masked, allowed = block_scores(
            query_kg, key_block, start, row_index, row_segment, buckets, lengths, scale
        )
        weights = jnp.where(allowed, jnp.exp(masked - log_total[..., None]), 0.0)
        grad_weights = jnp.einsum(
            "kgtd,skd->kgts", grad_kg, value_block, preferred_element_type=jnp.float32
        )
        grad_scores = (weights * (grad_weights - delta[..., None])).astype(jnp.bfloat16)
        grad_query = grad_query + scale * jnp.einsum(
            "kgts,skd->kgtd", grad_scores, key_block, preferred_element_type=jnp.float32
        )
        grad_key = scale * jnp.einsum(
            "kgts,kgtd->skd", grad_scores, query_kg, preferred_element_type=jnp.float32
        )
        grad_value = jnp.einsum(
            "kgts,kgtd->skd",
            weights.astype(jnp.bfloat16),
            grad_kg,
            preferred_element_type=jnp.float32,
        )
        return (grad_query, (grad_key, grad_value))

    grad_query, (grad_keys, grad_values) = lax.scan(
        step, jnp.zeros(query_kg.shape, jnp.float32), (key_blocks, value_blocks, starts)
    )
    return (grad_query, grad_keys.reshape(keys.shape), grad_values.reshape(values.shape))


def local(
    inputs,
    cotangent,
    bucket_sizes,
    true_lengths,
    attention_gain,
    feedforward_gain,
    query_gain,
    key_gain,
    query_weight,
    key_matrix,
    value_matrix,
    headgate_weight,
    output_weight,
    gate_weight,
    up_weight,
    down_weight,
):
    batches, rows, width = inputs.shape
    seq_count = lax.axis_size("seq")
    block = math.gcd(rows * seq_count, 512)
    local_heads = query_weight.shape[1] // HEAD_SIZE
    local_groups = key_matrix.shape[1] // HEAD_SIZE
    group = local_heads // local_groups
    scale = HEAD_SIZE ** (-0.5)
    row_index = lax.axis_index("seq") * rows + jnp.arange(rows, dtype=jnp.int32)
    gain_query = query_gain.astype(jnp.float32)
    gain_key = key_gain.astype(jnp.float32)
    sum_attention_gain = jnp.zeros((width,), jnp.float32)
    sum_feedforward_gain = jnp.zeros((width,), jnp.float32)
    sum_query = jnp.zeros((width, query_weight.shape[1]), jnp.float32)
    sum_key = jnp.zeros((width, key_matrix.shape[1]), jnp.float32)
    sum_value = jnp.zeros((width, value_matrix.shape[1]), jnp.float32)
    sum_headgate = jnp.zeros((width, headgate_weight.shape[1]), jnp.float32)
    sum_output = jnp.zeros((output_weight.shape[0], width), jnp.float32)
    sum_gate = jnp.zeros((width, gate_weight.shape[1]), jnp.float32)
    sum_upward = jnp.zeros((width, up_weight.shape[1]), jnp.float32)
    sum_down = jnp.zeros((down_weight.shape[0], width), jnp.float32)
    sum_query_gain = jnp.zeros((HEAD_SIZE,), jnp.float32)
    sum_key_gain = jnp.zeros((HEAD_SIZE,), jnp.float32)
    results = []
    input_grads = []
    for batch in range(batches):
        gathered = (
            lax.all_gather(attention_gain, "seq", axis=0, tiled=True),
            lax.all_gather(feedforward_gain, "seq", axis=0, tiled=True),
            lax.all_gather(query_weight, "seq", axis=0, tiled=True),
            lax.all_gather(key_matrix, "seq", axis=0, tiled=True),
            lax.all_gather(value_matrix, "seq", axis=0, tiled=True),
            lax.all_gather(headgate_weight, "seq", axis=0, tiled=True),
            lax.all_gather(output_weight, "seq", axis=1, tiled=True),
            lax.all_gather(gate_weight, "seq", axis=0, tiled=True),
            lax.all_gather(up_weight, "seq", axis=0, tiled=True),
            lax.all_gather(down_weight, "seq", axis=1, tiled=True),
        )
        (
            gain_a,
            gain_f,
            w_query,
            key_projection_weight,
            value_projection_weight,
            w_head,
            w_output,
            w_gate,
            w_up,
            w_down,
        ) = gathered
        gain_a = gain_a.astype(jnp.float32)
        gain_f = gain_f.astype(jnp.float32)
        buckets = bucket_sizes[batch]
        lengths = true_lengths[batch]
        row_segment, row_position, row_valid = token_layout(row_index, buckets, lengths)
        cosine, sine = rope_tables(row_position, HEAD_SIZE)
        current = inputs[batch].astype(jnp.float32)
        scale_a = rms_scale(current)
        normal_a = current * scale_a
        normed_input = (normal_a * gain_a).astype(jnp.bfloat16)
        query_proj = jnp.dot(normed_input, w_query, preferred_element_type=jnp.float32).reshape(
            rows, local_heads, HEAD_SIZE
        )
        key_proj = jnp.dot(
            normed_input, key_projection_weight, preferred_element_type=jnp.float32
        ).reshape(rows, local_groups, HEAD_SIZE)
        value_proj = jnp.dot(
            normed_input, value_projection_weight, preferred_element_type=jnp.float32
        )
        query_scale = rms_scale(query_proj)
        query_normal = query_proj * query_scale
        key_scale = rms_scale(key_proj)
        key_normal = key_proj * key_scale
        query_rot = rotate_forward(query_normal * gain_query, cosine, sine).astype(jnp.bfloat16)
        key_rot = rotate_forward(key_normal * gain_key, cosine, sine).astype(jnp.bfloat16)
        value_low = value_proj.astype(jnp.bfloat16).reshape(rows, local_groups, HEAD_SIZE)
        logits = jnp.dot(normed_input, w_head, preferred_element_type=jnp.float32)
        gate = jax.nn.sigmoid(logits)
        all_keys, all_values = (
            lax.all_gather(key_rot, "seq", axis=0, tiled=True),
            lax.all_gather(value_low, "seq", axis=0, tiled=True),
        )
        query_kg = query_rot.reshape(rows, local_groups, group, HEAD_SIZE).transpose(1, 2, 0, 3)
        attended_kg, log_total = attention_forward(
            query_kg, all_keys, all_values, row_index, row_segment, buckets, lengths, block, scale
        )
        attended = attended_kg.transpose(2, 0, 1, 3).reshape(rows, local_heads, HEAD_SIZE)
        mixed = (
            (attended * gate[:, :, None])
            .astype(jnp.bfloat16)
            .reshape(rows, local_heads * HEAD_SIZE)
        )
        hidden = current + lax.psum(
            jnp.dot(mixed, w_output, preferred_element_type=jnp.float32).astype(jnp.bfloat16), "kv"
        ).astype(jnp.float32)
        scale_f = rms_scale(hidden)
        normal_f = hidden * scale_f
        inner = (normal_f * gain_f).astype(jnp.bfloat16)
        gated = jnp.dot(inner, w_gate, preferred_element_type=jnp.float32)
        upward = jnp.dot(inner, w_up, preferred_element_type=jnp.float32)
        sigma = jax.nn.sigmoid(gated)
        swish = gated * sigma
        product = (swish * upward).astype(jnp.bfloat16)
        output = hidden + lax.psum(
            jnp.dot(product, w_down, preferred_element_type=jnp.float32).astype(jnp.bfloat16), "kv"
        ).astype(jnp.float32)
        results.append(output.astype(jnp.bfloat16))
        grad_out = cotangent[batch].astype(jnp.float32)
        grad_low = grad_out.astype(jnp.bfloat16)
        sum_down = sum_down + outer_sum(product, grad_low)
        grad_product = times_transpose(grad_low, w_down)
        grad_gated = (grad_product * upward * sigma * (1.0 + gated * (1.0 - sigma))).astype(
            jnp.bfloat16
        )
        grad_upward = (grad_product * swish).astype(jnp.bfloat16)
        sum_gate = sum_gate + outer_sum(inner, grad_gated)
        sum_upward = sum_upward + outer_sum(inner, grad_upward)
        grad_inner = lax.psum(
            (times_transpose(grad_gated, w_gate) + times_transpose(grad_upward, w_up)).astype(
                jnp.bfloat16
            ),
            "kv",
        ).astype(jnp.float32)
        sum_feedforward_gain = sum_feedforward_gain + jnp.sum(grad_inner * normal_f, axis=0)
        grad_hidden = grad_out + norm_backward(grad_inner * gain_f, normal_f, scale_f)
        grad_branch = grad_hidden.astype(jnp.bfloat16)
        sum_output = sum_output + outer_sum(mixed, grad_branch)
        grad_mixed = times_transpose(grad_branch, w_output).reshape(rows, local_heads, HEAD_SIZE)
        grad_heads = (grad_mixed * gate[:, :, None]).astype(jnp.bfloat16)
        grad_logits = (jnp.sum(grad_mixed * attended, axis=-1) * gate * (1.0 - gate)).astype(
            jnp.bfloat16
        )
        back_keys = lax.all_gather(key_rot, "seq", axis=0, tiled=True)
        back_values = lax.all_gather(value_low, "seq", axis=0, tiled=True)
        grad_kg = grad_heads.reshape(rows, local_groups, group, HEAD_SIZE).transpose(1, 2, 0, 3)
        delta = jnp.sum(grad_kg.astype(jnp.float32) * attended_kg, axis=-1)
        grad_query_kg, grad_keys, grad_values = attention_backward(
            query_kg,
            grad_kg,
            log_total,
            delta,
            back_keys,
            back_values,
            row_index,
            row_segment,
            buckets,
            lengths,
            block,
            scale,
        )
        local_keys, local_values = (
            lax.psum_scatter(
                grad_keys.astype(jnp.bfloat16), "seq", scatter_dimension=0, tiled=True
            ).astype(jnp.float32),
            lax.psum_scatter(
                grad_values.astype(jnp.bfloat16), "seq", scatter_dimension=0, tiled=True
            ).astype(jnp.float32),
        )
        grad_query_rot = grad_query_kg.transpose(2, 0, 1, 3).reshape(rows, local_heads, HEAD_SIZE)
        grad_query_norm = rotate_backward(grad_query_rot, cosine, sine)
        sum_query_gain = sum_query_gain + jnp.sum(grad_query_norm * query_normal, axis=(0, 1))
        grad_query = (
            norm_backward(grad_query_norm * gain_query, query_normal, query_scale)
            .astype(jnp.bfloat16)
            .reshape(rows, local_heads * HEAD_SIZE)
        )
        grad_key_norm = rotate_backward(local_keys, cosine, sine)
        sum_key_gain = sum_key_gain + jnp.sum(grad_key_norm * key_normal, axis=(0, 1))
        grad_key = (
            norm_backward(grad_key_norm * gain_key, key_normal, key_scale)
            .astype(jnp.bfloat16)
            .reshape(rows, local_groups * HEAD_SIZE)
        )
        grad_value = local_values.astype(jnp.bfloat16).reshape(rows, local_groups * HEAD_SIZE)
        sum_query = sum_query + outer_sum(normed_input, grad_query)
        sum_key = sum_key + outer_sum(normed_input, grad_key)
        sum_value = sum_value + outer_sum(normed_input, grad_value)
        sum_headgate = sum_headgate + outer_sum(normed_input, grad_logits)
        grad_partial = (
            times_transpose(grad_query, w_query)
            + times_transpose(grad_key, key_projection_weight)
            + times_transpose(grad_value, value_projection_weight)
            + times_transpose(grad_logits, w_head)
        )
        grad_normed = lax.psum(grad_partial.astype(jnp.bfloat16), "kv").astype(jnp.float32)
        sum_attention_gain = sum_attention_gain + jnp.sum(grad_normed * normal_a, axis=0)
        grad_input = grad_hidden + norm_backward(grad_normed * gain_a, normal_a, scale_a)
        input_grads.append(grad_input.astype(jnp.bfloat16))
    (
        attention_total,
        feedforward_total,
        query_total,
        key_total,
        value_total,
        headgate_total,
        output_total,
        gate_total,
        upward_total,
        down_total,
    ) = (
        lax.psum_scatter(
            sum_attention_gain.astype(jnp.bfloat16), "seq", scatter_dimension=0, tiled=True
        ).astype(jnp.float32),
        lax.psum_scatter(
            sum_feedforward_gain.astype(jnp.bfloat16), "seq", scatter_dimension=0, tiled=True
        ).astype(jnp.float32),
        lax.psum_scatter(
            sum_query.astype(jnp.bfloat16), "seq", scatter_dimension=0, tiled=True
        ).astype(jnp.float32),
        lax.psum_scatter(
            sum_key.astype(jnp.bfloat16), "seq", scatter_dimension=0, tiled=True
        ).astype(jnp.float32),
        lax.psum_scatter(
            sum_value.astype(jnp.bfloat16), "seq", scatter_dimension=0, tiled=True
        ).astype(jnp.float32),
        lax.psum_scatter(
            sum_headgate.astype(jnp.bfloat16), "seq", scatter_dimension=0, tiled=True
        ).astype(jnp.float32),
        lax.psum_scatter(
            sum_output.astype(jnp.bfloat16), "seq", scatter_dimension=1, tiled=True
        ).astype(jnp.float32),
        lax.psum_scatter(
            sum_gate.astype(jnp.bfloat16), "seq", scatter_dimension=0, tiled=True
        ).astype(jnp.float32),
        lax.psum_scatter(
            sum_upward.astype(jnp.bfloat16), "seq", scatter_dimension=0, tiled=True
        ).astype(jnp.float32),
        lax.psum_scatter(
            sum_down.astype(jnp.bfloat16), "seq", scatter_dimension=1, tiled=True
        ).astype(jnp.float32),
    )
    query_gain_total, key_gain_total = lax.psum((sum_query_gain, sum_key_gain), ("seq", "kv"))
    return (
        jnp.stack(results, axis=0),
        jnp.stack(input_grads, axis=0),
        attention_total,
        feedforward_total,
        query_gain_total,
        key_gain_total,
        query_total,
        key_total,
        value_total,
        headgate_total,
        output_total,
        gate_total,
        upward_total,
        down_total,
    )


BF = jnp.bfloat16
F32 = jnp.float32
ANY = pl.BlockSpec(memory_space=pl.ANY)
VM = pl.BlockSpec(memory_space=pltpu.VMEM)
DMA = pltpu.SemaphoreType.DMA


def place():
    s = lax.axis_index("seq")
    k = lax.axis_index("kv")
    return (lax.div(s, 2), lax.rem(s, 2), lax.div(k, 2), lax.rem(k, 2))


def device(l, x, y, c):
    return (l * 2 + x, y * 2 + c)


def remote(src, dst, send, recv, target):
    return pltpu.make_async_remote_copy(
        src_ref=src,
        dst_ref=dst,
        send_sem=send,
        recv_sem=recv,
        device_id=target,
        device_id_type=pl.DeviceIdType.MESH,
    )


def greet(partners):
    barrier = pltpu.get_barrier_semaphore()
    count = 0
    for target, there in partners:

        def call(target=target):
            pl.semaphore_signal(
                barrier, inc=1, device_id=target, device_id_type=pl.DeviceIdType.MESH
            )

        if there is None:
            call()
            count = count + 1
        else:
            pl.when(there)(call)
            count = count + jnp.where(there, 1, 0)
    pl.semaphore_wait(barrier, count)


class Line:
    def __init__(self, length, g, ag_send, ag_recv, land=None, rs_send=None, rs_recv=None):
        self.n = length
        self.g, self.ag_send, self.ag_recv = g, ag_send, ag_recv
        self.land, self.rs_send, self.rs_recv = land, rs_send, rs_recv
        self.l, self.x, self.y, self.c = place()

    def partners(self):
        l, x, y, c = self.l, self.x, self.y, self.c
        return [
            (device(l - 1, x, y, c), l >= 1),
            (device(l + 1, x, y, c), l <= self.n - 2),
        ]

    def block(self, item, b):
        return self.g.at[item, pl.ds(2 * b, 2)]

    def _ag(self, item, way, b):
        step = -1 if way == 0 else 1
        return remote(
            self.block(item, b),
            self.block(item, b),
            self.ag_send.at[item, way, b],
            self.ag_recv.at[item, b],
            device(self.l + step, self.x, self.y, self.c),
        )

    def ag_start(self, item):
        l = self.l
        pl.when(l >= 1)(lambda: self._ag(item, 0, l).start())
        pl.when(l <= self.n - 2)(lambda: self._ag(item, 1, l).start())

    def ag_left(self, item):
        pl.when(self.l >= 1)(lambda: self._ag(item, 0, self.l).start())

    def ag_right(self, item):
        pl.when(self.l <= self.n - 2)(lambda: self._ag(item, 1, self.l).start())

    def ag_step(self, item, t):
        l, n = self.l, self.n

        @pl.when(l + t <= n - 1)
        def _():
            self._ag(item, 0, l + t).wait_recv()
            pl.when(l >= 1)(lambda: self._ag(item, 0, l + t).start())

        @pl.when(l - t >= 0)
        def _():
            self._ag(item, 1, l - t).wait_recv()
            pl.when(l <= n - 2)(lambda: self._ag(item, 1, l - t).start())

    def pump(self, item, t):
        l, n = self.l, self.n

        @pl.when((l + t <= n - 1) & (l >= 1))
        def _():
            self._ag(item, 0, l + t).wait_recv()
            self._ag(item, 0, l + t).start()

        @pl.when((l - t >= 0) & (l <= n - 2))
        def _():
            self._ag(item, 1, l - t).wait_recv()
            self._ag(item, 1, l - t).start()

    def collect(self, item):
        l, n = self.l, self.n
        for t in range(1, n):
            pl.when(l == 0)(lambda t=t: self._ag(item, 0, t).wait_recv())
            pl.when(l == n - 1)(lambda t=t: self._ag(item, 1, n - 1 - t).wait_recv())

    def ag_end(self, item):
        l, n = self.l, self.n
        for b in range(n):
            pl.when((l >= 1) & (l <= b))(lambda b=b: self._ag(item, 0, b).wait_send())
            pl.when((l <= n - 2) & (l >= b))(lambda b=b: self._ag(item, 1, b).wait_send())

    def _slot(self, item, slot):
        return self.land.at[item, pl.ds(2 * slot, 2)]

    def _rs(self, item, way, o):
        if way == 0:
            target = self.l - 1
            slot = jnp.where(target == o, self.n, o)
        else:
            target = self.l + 1
            slot = o
        return remote(
            self.block(item, o),
            self._slot(item, slot),
            self.rs_send.at[item, way, o],
            self.rs_recv.at[item, slot],
            device(target, self.x, self.y, self.c),
        )

    def _take(self, item, o, slot):
        here = self._slot(item, slot)
        pltpu.make_async_copy(here, here, self.rs_recv.at[item, slot]).wait()
        for h in range(2):
            total = self.g[item, 2 * o + h].astype(F32) + self.land[item, 2 * slot + h].astype(F32)
            self.g[item, 2 * o + h] = total.astype(BF)

    def rs_step(self, item, q):
        l, n = self.l, self.n
        right, left = n - q, q - 1

        @pl.when(l < right)
        def _():
            pl.when(l >= 1)(lambda: self._take(item, right, right))
            self._rs(item, 1, right).start()

        @pl.when(l > left)
        def _():
            pl.when(l <= n - 2)(lambda: self._take(item, left, left))
            self._rs(item, 0, left).start()

    def rs_fire(self, item):
        l, n = self.l, self.n
        for o in range(n - 1, 0, -1):
            pl.when(l == 0)(lambda o=o: self._rs(item, 1, o).start())
            pl.when(l == n - 1)(lambda o=o: self._rs(item, 0, n - 1 - o).start())

    def rs_mid(self, item, q):
        l, n = self.l, self.n
        right, left = n - q, q - 1

        @pl.when((l < right) & (l >= 1))
        def _():
            self._take(item, right, right)
            self._rs(item, 1, right).start()

        @pl.when((l > left) & (l <= n - 2))
        def _():
            self._take(item, left, left)
            self._rs(item, 0, left).start()

    def rs_near(self, item):
        l, n = self.l, self.n

        @pl.when(l == 1)
        def _():
            for o in range(n - 1, 1, -1):
                self._take(item, o, o)
                self._rs(item, 1, o).start()

        @pl.when(l == n - 2)
        def _():
            for o in range(n - 2):
                self._take(item, o, o)
                self._rs(item, 0, o).start()

    def rs_far(self, item):
        l, n = self.l, self.n

        @pl.when(l == 1)
        def _():
            self._take(item, 0, 0)
            self._rs(item, 0, 0).start()

        @pl.when(l == n - 2)
        def _():
            self._take(item, n - 1, n - 1)
            self._rs(item, 1, n - 1).start()

    def rs_final(self, item):
        l, n = self.l, self.n
        pl.when(l >= 1)(lambda: self._take(item, l, l))
        pl.when(l <= n - 2)(lambda: self._take(item, l, n))

    def rs_end(self, item):
        l, n = self.l, self.n
        for o in range(n):
            pl.when(l < o)(lambda o=o: self._rs(item, 1, o).wait_send())
            pl.when(l > o)(lambda o=o: self._rs(item, 0, o).wait_send())


def each(count, body):
    def step(i, unused):
        body(i)
        return 0

    lax.fori_loop(0, count, step, 0)


class Pair:
    def __init__(self, line, refs, send, recv, local, half):
        self.line, self.refs = line, refs
        self.send, self.recv, self.local, self.half = send, recv, local, half

    def partner(self):
        line = self.line
        return (device(line.l, 1 - line.x, line.y, line.c), None)

    def _part(self, ref, kind, j, x):
        half = self.half if isinstance(self.half, int) else self.half[kind]
        at = pl.multiple_of(x * half + j * 256, 256)
        return ref.at[pl.ds(at, 256), :] if kind == 2 else ref.at[:, pl.ds(at, 256)]

    def _copies(self, item, kind, j):
        line = self.line
        mine = line.g.at[item, 2 * line.l + line.x]
        out = remote(
            self._part(self.refs[kind], kind, j, 1 - line.x),
            mine,
            self.send.at[item],
            self.recv.at[item],
            self.partner()[0],
        )
        here = pltpu.make_async_copy(
            self._part(self.refs[kind], kind, j, line.x), mine, self.local.at[item]
        )
        return out, here

    def start(self, item, kind, j):
        for copy in self._copies(item, kind, j):
            copy.start()

    def end(self, item, kind, j):
        out, here = self._copies(item, kind, j)
        here.wait()
        out.wait_send()
        out.wait_recv()


class Back(Pair):
    def _copies(self, item, kind, j):
        line = self.line
        home = self._part(self.refs[kind], kind, j, line.x)
        out = remote(
            line.g.at[item, 2 * line.l + 1 - line.x],
            home,
            self.send.at[item],
            self.recv.at[item],
            self.partner()[0],
        )
        here = pltpu.make_async_copy(
            line.g.at[item, 2 * line.l + line.x], home, self.local.at[item]
        )
        return out, here


def back_wait(back, item, kind, j):
    line = back.line
    out, here = back._copies(item, kind, j)
    here.wait()
    out.wait_send()
    there = back._part(back.refs[kind], kind, j, 1 - line.x)
    pltpu.make_async_copy(there, there, back.recv.at[item]).wait()


def dot(a, b):
    return lax.dot_general(a, b, (((1,), (0,)), ((), ())), preferred_element_type=F32)


def dot_t(a, b):
    return lax.dot_general(a, b, (((1,), (1,)), ((), ())), preferred_element_type=F32)


def head_kernel(
    n,
    x_any,
    z_any,
    wq,
    wkv,
    wo,
    wg,
    wu,
    wd,
    small,
    cos_ref,
    sin_ref,
    row_lo,
    row_hi,
    g_out,
    own_out,
    normed_out,
    kv_out,
    q_out,
    qp_out,
    kp_out,
    gate_out,
    att_out,
    lse_out,
    hidden_out,
    inner_out,
    dz_out,
    small_out,
    x_v,
    normed,
    normed_t,
    g,
    small_g,
    gain_row,
    heads_row,
    kv,
    q_v,
    qp,
    kp,
    gate_v,
    att,
    tot,
    part,
    core_land,
    low,
    chip_land,
    inner,
    hidden,
    p_send,
    p_recv,
    p_loc,
    ag_send,
    ag_recv,
    sp_sem,
    sa_send,
    sa_recv,
    t_send,
    t_recv,
    z_send,
    z_recv,
    kv_send,
    kv_recv,
    c_send,
    c_recv,
    s_send,
    s_recv,
    i_send,
    i_recv,
    j_send,
    j_recv,
    o_loc,
):
    line = Line(n, g, ag_send, ag_recv)
    l, x, y, c = line.l, line.x, line.y, line.c
    k = y * 2 + c
    group = Group()
    across, mate = device(l, 1 - x, y, c), group.mate
    right = device(l + 1, x, y, c)
    tiny = Line(n, small_g, sa_send, sa_recv)
    scale = HEAD_SIZE ** (-0.5)
    late = 9
    first = Pair(line, (wq, wkv, wo), p_send, p_recv, p_loc, 256)
    rest = Pair(line, (wg, wu, wd), p_send, p_recv, p_loc, 768)

    def swap(item):
        if item < 3:
            return first, item, item, 0
        return rest, item, item % 3, item // 3 - 1

    def swap_start(item):
        pair, item, kind, j = swap(item)
        pair.start(item, kind, j)

    def swap_end(item):
        pair, item, kind, j = swap(item)
        pair.end(item, kind, j)

    outs = []

    def put(src, dst):
        copy = pltpu.make_async_copy(src, dst, o_loc.at[len(outs)])
        copy.start()
        outs.append(copy)

    greet(line.partners() + [(mate, None)] + [(group.chip(i), None) for i in (1, 2, 3)])

    small_here = small_g.at[0, 2 * l + x]
    small_out_copy = remote(small, small_here, sp_sem.at[0], sp_sem.at[1], across)
    small_own = pltpu.make_async_copy(small, small_here, sp_sem.at[2])
    small_out_copy.start()
    small_own.start()
    swap_start(0)
    swap_start(1)
    swap_start(2)
    own_x = pltpu.make_async_copy(x_any, x_v.at[:, x], t_send.at[2])
    own_x.start()
    halves = pl.ds(2 * c, 2)
    x_out = remote(x_any.at[halves], x_v.at[halves, x], t_send.at[0], t_recv.at[0], across)
    x_part = x_v.at[halves, 1 - x]
    x_on = remote(x_part, x_part, t_send.at[1], t_recv.at[1], mate)
    x_out.start()
    for item in range(3, 6):
        swap_start(item)
    z_out = remote(z_any.at[halves], dz_out.at[halves], z_send.at[0], z_recv.at[0], across)
    z_part = dz_out.at[halves]
    z_on = remote(z_part, z_part, z_send.at[1], z_recv.at[1], mate)
    z_out.start()
    for item in range(6, 12):
        swap_start(item)

    small_own.wait()
    small_out_copy.wait()
    tiny.ag_start(0)
    for item in (0, 1):
        swap_end(item)
        line.ag_start(item)
    for t in range(1, n):
        tiny.ag_step(0, t)
    line.pump(0, 1)
    line.pump(1, 1)
    swap_end(2)
    for s in range(2 * n):
        cols = slice(s * 256, (s + 1) * 256)
        heads_row[:, cols] = small_g[0, s]
        gain_row[:, cols] = small_g[0, s, 4:6, :].astype(F32)

    def norm(m, side):
        v = x_v[m, side].reshape(128, 256 * 2 * n).astype(F32)
        mean = jnp.mean(v * v, axis=-1, keepdims=True)
        v = v * lax.rsqrt(mean + EPS) * gain_row[0:1, :]
        normed[m, side] = v.astype(BF)

    own_x.wait()
    each(4, lambda m: norm(m, x))
    line.pump(0, 2)
    line.pump(1, 2)
    line.ag_start(2)
    x_out.wait_recv()
    x_on.start()
    line.pump(2, 1)
    for item in (3, 4, 5):
        swap_end(item)
        line.ag_left(item)
    x_on.wait_recv()
    each(4, lambda m: norm(m, 1 - x))
    for item in (0, 1):
        line.collect(item)

    def project(m):
        a = normed[m].reshape(256, 256 * 2 * n)
        qf = dot(a, g[0].reshape(256 * 2 * n, 256))
        kf = dot(a, g[1].reshape(256 * 2 * n, 256))
        gate_v[m] = jax.nn.sigmoid(dot_t(a, heads_row[...]))
        qp[m] = qf
        kp[m] = kf[:, :128]
        cosine, sine = cos_ref[m], sin_ref[m]

        def turn(u, gain):
            u = u * lax.rsqrt(jnp.mean(u * u, axis=-1, keepdims=True) + EPS) * gain
            return (u * cosine + pltpu.roll(u, 64, 1) * sine).astype(BF)

        gains = small[8:10, :128].astype(F32)
        q_v[m, :256] = turn(qf[:, :128], gains[0:1])
        q_v[m, 256:] = turn(qf[:, 128:], gains[0:1])
        kv[l, m, :, :128] = turn(kf[:, :128], gains[1:2])
        kv[l, m, :, 128:] = kf[:, 128:].astype(BF)

    def send_kv(b, m):
        return remote(kv.at[b, m], kv.at[b, m], kv_send.at[b, m], kv_recv.at[b, m], right)

    each(4, project)
    put(qp, qp_out)
    put(kp, kp_out)
    put(gate_v, gate_out)
    put(q_v, q_out)

    def attend(m, b, diagonal):
        pair = kv[b, m]
        raw = dot_t(q_v[m], pair[:, :128]) * scale
        lo = row_lo[m][:, :1] - b * 256
        hi = row_hi[m][:, :1] - b * 256
        column = lax.broadcasted_iota(jnp.int32, (512, 256), 1)
        allowed = (column >= jnp.concatenate([lo, lo], axis=0)) & (
            column < jnp.concatenate([hi, hi], axis=0)
        )
        e = jnp.where(allowed, jnp.exp(raw), 0.0)
        total = jnp.sum(e, axis=-1, keepdims=True)
        value = dot(e.astype(BF), pair[:, 128:])
        total = jnp.broadcast_to(total, (512, 128))
        if diagonal:
            tot[m] = total
            att[m] = value
        else:
            tot[m] += total
            att[m] += value

    line.pump(2, 2)

    def turned(i):
        m, s = lax.div(i, 2 * n), lax.rem(i, 2 * n)
        tile = normed[m, :, :, pl.ds(pl.multiple_of(s * 256, 256), 256)].reshape(256, 256)
        normed_t[s, :, pl.ds(pl.multiple_of(m * 256, 256), 256)] = tile.T

    def mate_copy(m):
        return remote(
            part.at[m, :, :, 1 - c], core_land.at[m], c_send.at[m], c_recv.at[m], mate
        )

    def branch(m):
        total = tot[m]
        lse = jnp.log(total)
        value = att[m] / total
        att[m] = value
        tot[m] = lse
        gates = gate_v[m]
        lo, hi = gates[:, 0:2], gates[:, 2:4]
        gates = jnp.where(x == 0, lo, hi)
        mixed = jnp.concatenate(
            [value[:256] * gates[:, 0:1], value[256:] * gates[:, 1:2]], axis=1
        ).astype(BF)
        for s in range(2 * n):
            part[m, :, :, :, :, s * 256 : (s + 1) * 256] = (
                dot(mixed, g[2, s]).astype(BF).reshape(2, 2, 2, 32, 256)
            )
        mate_copy(m).start()

    def chip_copy(m, o):
        ox, oy = group.other(o)
        return remote(
            low.at[m, ox, oy],
            chip_land.at[o - 1, m],
            s_send.at[m, o - 1],
            s_recv.at[m, o - 1],
            group.chip(o),
        )

    def to_chips(m):
        mate_copy(m).wait_recv()
        for u in range(2):
            for v in range(2):
                low[m, u, v] = (
                    part[m, u, v, c].astype(F32) + core_land[m, u, v].astype(F32)
                ).astype(BF)
        for o in (3, 1, 2):
            chip_copy(m, o).start()

    def ahead(m):
        pl.when(l <= n - 2)(lambda: send_kv(l, m).start())
        attend(m, l, True)

        def step(t, unused):
            b = l - t
            send_kv(b, m).wait_recv()
            pl.when(l <= n - 2)(lambda: send_kv(b, m).start())
            attend(m, b, False)
            return 0

        lax.fori_loop(1, l + 1, step, 0)

    for m in range(4):
        ahead(m)
        if m == 0:
            each(8 * n, turned)
            line.collect(2)
        branch(m)
        if m > 0:
            to_chips(m - 1)
    to_chips(3)
    for item in (3, 4, 5):
        line.ag_right(item)
    put(normed_t, normed_out)
    put(att, att_out)
    put(tot, lse_out)
    put(kv, kv_out)
    line.pump(3, 1)

    def inner_copy(m, o):
        here = inner.at[m, x, y, c]
        return remote(
            here, here, i_send.at[m, o - 1], i_recv.at[m, o - 1], group.chip(o)
        )

    def inner_mate(m, o):
        ox, oy = group.other(o)
        there = inner.at[m, ox, oy, c]
        return remote(there, there, j_send.at[m, o], j_recv.at[m, o], mate)

    def finish(m):
        total = low[m, x, y].astype(F32)
        for o in (1, 2, 3):
            chip_copy(m, o).wait_recv()
            total = total + chip_land[o - 1, m].astype(F32)
        h = x_v[m, x, k].astype(F32) + total
        hidden[m] = h
        mean = jnp.mean(h * h, axis=-1, keepdims=True)
        inner[m, x, y, c] = (h * lax.rsqrt(mean + EPS) * gain_row[1:2, :]).astype(BF)
        for o in (3, 1, 2):
            inner_copy(m, o).start()
        inner_mate(m, 0).start()

    each(4, finish)
    put(hidden, hidden_out)
    line.pump(3, 2)
    line.pump(4, 1)
    z_out.wait_recv()
    z_on.start()
    line.pump(4, 2)

    def pass_on(m):
        for o in (1, 2, 3):
            inner_copy(m, o).wait_recv()
            inner_mate(m, o).start()

    each(4, pass_on)
    line.pump(5, 1)
    for item in range(6, 12):
        swap_end(item)
        put(g.at[item, pl.ds(2 * l, 2)], own_out.at[item - 6])
    line.pump(5, 2)

    def arrive(m):
        for o in range(4):
            inner_mate(m, o).wait_recv()

    each(4, arrive)
    put(inner, inner_out)
    put(small_g, small_out)
    for item in range(3, 6):
        line.collect(item)
    put(g.at[pl.ds(0, 6)], g_out)

    small_out_copy_done = None
    own_waits = [x_out, x_on, z_out, z_on]
    for copy in own_waits:
        copy.wait_send()
    z_on.wait_recv()
    tiny.ag_end(0)
    each(6, line.ag_end)

    def drain(m):
        mate_copy(m).wait_send()
        for o in (1, 2, 3):
            chip_copy(m, o).wait_send()
            inner_copy(m, o).wait_send()
        for o in range(4):
            inner_mate(m, o).wait_send()
        for b in range(n):
            pl.when((l >= b) & (l <= n - 2))(lambda b=b: send_kv(b, m).wait_send())

    each(4, drain)
    for copy in outs:
        copy.wait()


def head(n, x_in, z_in, wq, wkv, wo, wg, wu, wd, small, cosine, sine, row_lo, row_hi):
    d = x_in.shape[-1]
    m = 2 * n
    bf = lambda *shape: jax.ShapeDtypeStruct(shape, BF)
    f32 = lambda *shape: jax.ShapeDtypeStruct(shape, F32)
    vb = lambda *shape: pltpu.VMEM(shape, BF)
    vf = lambda *shape: pltpu.VMEM(shape, F32)
    return pl.pallas_call(
        functools.partial(head_kernel, n),
        out_shape=(
            bf(6, m, 256, 256),
            bf(6, 2, 256, 256),
            bf(m, 256, 1024),
            bf(n, 4, 256, 256),
            bf(4, 512, 128),
            f32(4, 256, 256),
            f32(4, 256, 128),
            f32(4, 256, 16),
            f32(4, 512, 128),
            f32(4, 512, 128),
            f32(4, 32, d),
            bf(4, 2, 2, 2, 32, d),
            bf(4, 4, 32, d),
            bf(1, m, 16, 256),
        ),
        in_specs=[ANY] * 8 + [VM] * 5,
        out_specs=(ANY,) * 14,
        scratch_shapes=[
            vb(4, 2, 4, 32, d),
            vb(4, 2, 128, d),
            vb(m, 256, 1024),
            vb(12, m, 256, 256),
            vb(1, m, 16, 256),
            vf(2, d),
            vb(16, d),
            vb(n, 4, 256, 256),
            vb(4, 512, 128),
            vf(4, 256, 256),
            vf(4, 256, 128),
            vf(4, 256, 16),
            vf(4, 512, 128),
            vf(4, 512, 128),
            vb(4, 2, 2, 2, 32, d),
            vb(4, 2, 2, 32, d),
            vb(4, 2, 2, 32, d),
            vb(3, 4, 32, d),
            vb(4, 2, 2, 2, 32, d),
            vf(4, 32, d),
            DMA((12,)),
            DMA((12,)),
            DMA((12,)),
            DMA((12, 2, n)),
            DMA((12, n)),
            DMA((3,)),
            DMA((1, 2, n)),
            DMA((1, n)),
            DMA((3,)),
            DMA((2,)),
            DMA((2,)),
            DMA((2,)),
            DMA((n, 4)),
            DMA((n, 4)),
            DMA((4,)),
            DMA((4,)),
            DMA((4, 3)),
            DMA((4, 3)),
            DMA((4, 3)),
            DMA((4, 3)),
            DMA((4, 4)),
            DMA((4, 4)),
            DMA((24,)),
        ],
        compiler_params=pltpu.CompilerParams(
            collective_id=0, has_side_effects=True, vmem_limit_bytes=62 * 2**20
        ),
        name="head",
    )(x_in, z_in, wq, wkv, wo, wg, wu, wd, small, cosine, sine, row_lo, row_hi)


class Group:
    def __init__(self):
        self.l, self.x, self.y, self.c = place()
        self.mate = device(self.l, self.x, self.y, 1 - self.c)

    def other(self, i):
        x = 1 - self.x if i & 1 else self.x
        y = 1 - self.y if i & 2 else self.y
        return x, y

    def chip(self, i):
        x, y = self.other(i)
        return device(self.l, x, y, self.c)

    def partners(self):
        return [(self.mate, None)] + [(self.chip(i), None) for i in (1, 2, 3)]


def ffn_kernel(
    n,
    inner_any,
    z_own,
    z_other,
    g_in,
    own_in,
    out_ref,
    din_ref,
    part_out,
    dgw,
    duw,
    ddw,
    inner_ref,
    dz_ref,
    inner_t,
    out_acc,
    din_acc,
    g,
    land,
    low,
    prod_t,
    ag_send,
    ag_recv,
    rs_send,
    rs_recv,
    b_send,
    b_recv,
    b_loc,
    in_loc,
    o_loc,
):
    chunks = 3
    line = Line(n, g, ag_send, ag_recv, land, rs_send, rs_recv)
    l, x = line.l, line.x
    blocks = 2 * n
    width = blocks * 256
    back = Back(line, (dgw, duw, ddw), b_send, b_recv, b_loc, (512, 512, 256))
    loads = [
        pltpu.make_async_copy(own_in, g.at[pl.ds(3, 6), pl.ds(2 * l, 2)], in_loc.at[0]),
        pltpu.make_async_copy(inner_any, inner_ref, in_loc.at[1]),
        pltpu.make_async_copy(z_own, dz_ref.at[:, x], in_loc.at[2]),
        pltpu.make_async_copy(z_other, dz_ref.at[:, 1 - x], in_loc.at[3]),
        pltpu.make_async_copy(g_in.at[pl.ds(3, 3)], g.at[pl.ds(0, 3)], in_loc.at[4]),
    ]
    for copy in loads:
        copy.start()
    greet(line.partners() + [back.partner()])
    loads[0].wait()
    for item in range(3, 6):
        line.ag_start(item)
    for copy in loads[1:]:
        copy.wait()

    def turn(i, unused):
        m, s = lax.div(i, blocks), lax.rem(i, blocks)
        tile = inner_ref[m, :, pl.ds(pl.multiple_of(s * 256, 256), 256)]
        inner_t[s, :, pl.ds(pl.multiple_of(m * 256, 256), 256)] = tile.T
        return 0

    lax.fori_loop(0, 4 * blocks, turn, 0)

    def compute(j):
        base = 3 * j

        def rows(m, unused):
            a = inner_ref[m]
            d = dz_ref[m].reshape(256, width)
            gated = dot(a, g[base].reshape(width, 256))
            upward = dot(a, g[base + 1].reshape(width, 256))
            grad = dot_t(d[:, :256], g[base + 2, 0])
            for s in range(1, blocks):
                grad = grad + dot_t(d[:, s * 256 : (s + 1) * 256], g[base + 2, s])
            sigma = jax.nn.sigmoid(gated)
            swish = gated * sigma
            product = (swish * upward).astype(BF)
            d_gated = (grad * upward * sigma * (1.0 + gated * (1.0 - sigma))).astype(BF)
            d_upward = (grad * swish).astype(BF)
            at = pl.ds(pl.multiple_of(m * 256, 256), 256)
            low[0, at] = d_gated
            low[1, at] = d_upward
            prod_t[:, at] = product.T
            for s in range(blocks):
                cols = slice(s * 256, (s + 1) * 256)
                o = dot(product, g[base + 2, s])
                i = dot_t(d_gated, g[base, s]) + dot_t(d_upward, g[base + 1, s])
                if j == 0:
                    out_acc[m, :, cols] = o
                    din_acc[m, :, cols] = i
                else:
                    out_acc[m, :, cols] += o
                    din_acc[m, :, cols] += i
            return 0

        lax.fori_loop(0, 4, rows, 0)

        def weights(s, unused):
            t = inner_t[s]
            g[base, s] = dot(t, low[0]).astype(BF)
            g[base + 1, s] = dot(t, low[1]).astype(BF)
            z = dz_ref[:, :, :, :, pl.ds(pl.multiple_of(s * 256, 256), 256)].reshape(1024, 256)
            g[base + 2, s] = dot(prod_t[...], z).astype(BF)
            return 0

        lax.fori_loop(0, blocks, weights, 0)

    def homeward(item):
        line.rs_final(item)
        back.start(item, item % 3, item // 3)

    compute(0)
    for item in (0, 1, 2):
        line.rs_fire(item)
    for t in (1, 2):
        for item in (3, 4, 5):
            line.pump(item, t)
    for item in (6, 7, 8):
        line.ag_start(item)
    line.rs_near(0)
    line.rs_near(1)
    line.rs_far(0)
    for item in (3, 4, 5):
        line.collect(item)
        line.ag_end(item)
    compute(1)
    for item in (3, 4):
        line.rs_fire(item)
    for item in (6, 7, 8):
        line.pump(item, 1)
    line.rs_near(2)
    line.rs_far(1)
    for item in (6, 7, 8):
        line.pump(item, 2)
    homeward(0)
    line.rs_near(3)
    line.rs_far(2)
    homeward(1)
    line.rs_near(4)
    line.rs_far(3)
    homeward(2)
    line.rs_far(4)
    for item in (6, 7, 8):
        line.collect(item)
        line.ag_end(item)
    compute(2)
    parts = pltpu.make_async_copy(g.at[pl.ds(5, 4)], part_out, o_loc.at[2])
    parts.start()

    def flush(m, unused):
        inner_ref[m] = out_acc[m].astype(BF)
        dz_ref[m] = din_acc[m].astype(BF).reshape(2, 4, 32, width)
        return 0

    lax.fori_loop(0, 4, flush, 0)
    outs = [
        pltpu.make_async_copy(inner_ref, out_ref, o_loc.at[0]),
        pltpu.make_async_copy(dz_ref, din_ref, o_loc.at[1]),
        parts,
    ]
    for copy in outs[:2]:
        copy.start()
    homeward(3)
    homeward(4)
    for item in range(5):
        back_wait(back, item, item % 3, item // 3)
    each(5, line.rs_end)
    for copy in outs:
        copy.wait()


def ffn(n, inner, z_own, z_other, g_in, own_in):
    d = inner.shape[-1]
    m = 2 * n
    bf = lambda *shape: jax.ShapeDtypeStruct(shape, BF)
    vb = lambda *shape: pltpu.VMEM(shape, BF)
    return pl.pallas_call(
        functools.partial(ffn_kernel, n),
        out_shape=(
            bf(4, 256, d),
            bf(4, 2, 4, 32, d),
            bf(4, m, 256, 256),
            bf(256, 1024),
            bf(256, 1024),
            bf(512, 256),
        ),
        in_specs=[ANY] * 5,
        out_specs=(ANY,) * 6,
        scratch_shapes=[
            vb(4, 256, d),
            vb(4, 2, 4, 32, d),
            vb(m, 256, 1024),
            pltpu.VMEM((4, 256, d), F32),
            pltpu.VMEM((4, 256, d), F32),
            vb(9, m, 256, 256),
            vb(5, m + 2, 256, 256),
            vb(2, 1024, 256),
            vb(256, 1024),
            DMA((9, 2, n)),
            DMA((9, n)),
            DMA((5, 2, n)),
            DMA((5, n + 1)),
            DMA((5,)),
            DMA((5,)),
            DMA((5,)),
            DMA((5,)),
            DMA((3,)),
        ],
        compiler_params=pltpu.CompilerParams(
            collective_id=9, has_side_effects=True, vmem_limit_bytes=62 * 2**20
        ),
        name="ffn",
    )(inner, z_own, z_other, g_in, own_in)


def tail_kernel(
    n,
    din_any,
    out_any,
    x_any,
    z_any,
    hidden_any,
    ffn_parts,
    normed_any,
    g_any,
    kv_any,
    q_any,
    qp_any,
    kp_any,
    att_any,
    lse_any,
    gate_ref,
    small_g,
    small,
    cos_ref,
    sin_ref,
    row_lo,
    row_hi,
    res_out,
    grad_out,
    dq_out,
    dkv_out,
    do_out,
    dg_out,
    du_out,
    dd_out,
    sums_out,
    g,
    land,
    w,
    normed_t,
    dbr,
    kv,
    kv_land,
    q_v,
    qp,
    kp,
    att,
    lse,
    core_land,
    chip_land,
    low,
    hidden,
    d_hid,
    own_z,
    own_x,
    own_res,
    own_grad,
    mixed_t,
    dql,
    dpl,
    dl,
    dl_t,
    gain_row,
    gain_sum,
    head_sum,
    sums,
    sum_c,
    sum_x,
    sum_y,
    sum_l,
    loads,
    rs_send,
    rs_recv,
    b_send,
    b_recv,
    b_loc,
    kv_send,
    kv_recv,
    c_send,
    c_recv,
    s_send,
    s_recv,
    i_send,
    i_recv,
    j_send,
    j_recv,
    h_send,
    h_recv,
    t_send,
    t_recv,
    o_loc,
):
    line = Line(n, g, None, None, land, rs_send, rs_recv)
    l, x, y, c = line.l, line.x, line.y, line.c
    k = y * 2 + c
    group = Group()
    mate = group.mate
    left = device(l - 1, x, y, c)
    blocks = 2 * n
    width = blocks * 256
    scale = HEAD_SIZE ** (-0.5)
    first = Back(line, (dq_out, dkv_out, do_out), b_send, b_recv, b_loc, 256)
    rest = Back(line, (dg_out, du_out, dd_out), b_send, b_recv, b_loc, (256, 256, 512))

    def backward(item):
        if item < 3:
            return first, item, item, 0
        return rest, item, (item + 2) % 3, 1 if item == 6 else 0

    def homeward(item):
        line.rs_final(item)
        back, item, kind, j = backward(item)
        back.start(item, kind, j)

    pending = {}

    def load(name, src, dst):
        copy = pltpu.make_async_copy(src, dst, loads.at[len(pending)])
        copy.start()
        pending[name] = copy

    load("din", din_any.at[:, :, :, c], low)
    load("hidden", hidden_any, hidden)
    load("z", z_any.at[:, k], own_z)
    load("ffn", ffn_parts, g.at[pl.ds(3, 4)])
    load("w", g_any.at[pl.ds(0, 3)], w)
    load("kv", kv_any, kv)
    load("q", q_any, q_v)
    load("att", att_any, att)
    load("lse", lse_any, lse)
    load("qp", qp_any, qp)
    load("kp", kp_any, kp)
    load("normed", normed_any, normed_t)
    load("x", x_any.at[:, k], own_x)

    others = [device(lax.rem(l + d, n), x, y, c) for d in range(1, n)]
    greet(
        [(o, None) for o in others] + [(mate, None)] + [(group.chip(i), None) for i in (1, 2, 3)]
    )

    def mate_copy(r, src, m):
        return remote(
            src.at[m, :, :, 1 - c], core_land.at[r % 2, m], c_send.at[r, m], c_recv.at[r, m], mate
        )

    def chip_copy(r, m, o):
        ox, oy = group.other(o)
        return remote(
            low.at[m, ox, oy],
            chip_land.at[r % 2, o - 1, m],
            s_send.at[r, m, o - 1],
            s_recv.at[r, m, o - 1],
            group.chip(o),
        )

    def to_chips(r, src, m, own):
        mate_copy(r, src, m).wait_recv()
        for u in range(2):
            for v in range(2):
                low[m, u, v] = (
                    own(m, u, v).astype(F32) + core_land[r % 2, m, u, v].astype(F32)
                ).astype(BF)
        for o in (3, 1, 2):
            chip_copy(r, m, o).start()

    def total_of(r, m):
        total = low[m, x, y].astype(F32)
        for o in (1, 2, 3):
            chip_copy(r, m, o).wait_recv()
            total = total + chip_land[r % 2, o - 1, m].astype(F32)
        return total

    def group_end(r, src):
        def done(m):
            mate_copy(r, src, m).wait_send()
            for o in (1, 2, 3):
                chip_copy(r, m, o).wait_send()

        each(4, done)

    each(4, lambda m: mate_copy(0, din_any, m).start())
    pending["ffn"].wait()
    line.rs_fire(3)
    line.rs_fire(4)
    for s in range(blocks):
        cols = slice(s * 256, (s + 1) * 256)
        gain_row[:, cols] = small_g[0, s, 4:6, :].astype(F32)
    gain_sum[...] = jnp.zeros_like(gain_sum)
    head_sum[...] = jnp.zeros_like(head_sum)
    pending["din"].wait()
    pending["hidden"].wait()
    pending["z"].wait()
    each(4, lambda m: to_chips(0, din_any, m, lambda m, u, v: low[m, u, v]))
    line.rs_near(3)

    def spread(m, o):
        here = dbr.at[m, x, y, c]
        return remote(here, here, i_send.at[m, o - 1], i_recv.at[m, o - 1], group.chip(o))

    def spread_mate(m, o):
        ox, oy = group.other(o)
        there = dbr.at[m, ox, oy, c]
        return remote(there, there, j_send.at[m, o], j_recv.at[m, o], mate)

    def finish(m):
        total = total_of(0, m)
        h = hidden[m]
        r = lax.rsqrt(jnp.mean(h * h, axis=-1, keepdims=True) + EPS)
        normal = h * r
        gain_sum[1:2] += jnp.sum(total * normal, axis=0, keepdims=True)
        e = total * gain_row[1:2, :]
        grad = own_z[m].astype(F32) + r * (
            e - normal * jnp.mean(e * normal, axis=-1, keepdims=True)
        )
        d_hid[m] = grad
        dbr[m, x, y, c] = grad.astype(BF)
        for o in (3, 1, 2):
            spread(m, o).start()
        spread_mate(m, 0).start()

    each(4, finish)
    line.rs_fire(5)
    for name in ("w", "kv", "q", "att", "lse", "qp", "kp", "normed", "x"):
        pending[name].wait()
    line.rs_near(4)
    line.rs_far(3)

    def pass_on(m):
        for o in (1, 2, 3):
            spread(m, o).wait_recv()
            spread_mate(m, o).start()

    each(4, pass_on)
    group_end(0, din_any)
    own_low = pltpu.make_async_copy(out_any.at[:, :, :, c], low, o_loc.at[0])
    own_low.start()
    each(4, lambda m: mate_copy(1, out_any, m).start())
    line.rs_far(4)

    def arrive(m):
        for o in range(4):
            spread_mate(m, o).wait_recv()

    def attend_back(m):
        arrive(m)
        d = dbr[m].reshape(256, width)
        gm = dot_t(d[:, :256], w[2, 0])
        for s in range(1, blocks):
            gm = gm + dot_t(d[:, s * 256 : (s + 1) * 256], w[2, s])
        gates = gate_ref[m]
        gates = jnp.where(x == 0, gates[:, 0:2], gates[:, 2:4])
        g0, g1 = gates[:, 0:1], gates[:, 1:2]
        a0, a1 = att[m, :256], att[m, 256:]
        d0, d1 = gm[:, :128], gm[:, 128:]
        l0 = jnp.sum(d0 * a0, axis=-1, keepdims=True) * g0 * (1.0 - g0)
        l1 = jnp.sum(d1 * a1, axis=-1, keepdims=True) * g1 * (1.0 - g1)
        lane = lax.broadcasted_iota(jnp.int32, (256, 128), 1)
        logits = jnp.where(lane == 2 * x, l0, 0.0) + jnp.where(lane == 2 * x + 1, l1, 0.0)
        logits = logits.astype(BF)
        dl[m] = logits
        at = pl.ds(pl.multiple_of(m * 256, 256), 256)
        dl_t[:, at] = logits.T
        mixed = jnp.concatenate([a0 * g0, a1 * g1], axis=1).astype(BF)
        mixed_t[:, at] = mixed.T
        da = jnp.concatenate([d0 * g0, d1 * g1], axis=0).astype(BF)
        delta = jnp.sum(da.astype(F32) * att[m], axis=-1, keepdims=True)
        log_total = lse[m][:, :1]
        qm = q_v[m]
        att[m] = jnp.zeros((512, 128), F32)

        def block(b, unused):
            pair = kv[b, m]
            keys, values = pair[:, :128], pair[:, 128:]
            raw = dot_t(qm, keys) * scale
            lo = row_lo[m][:, :1] - b * 256
            hi = row_hi[m][:, :1] - b * 256
            column = lax.broadcasted_iota(jnp.int32, (512, 256), 1)
            allowed = (column >= jnp.concatenate([lo, lo], axis=0)) & (
                column < jnp.concatenate([hi, hi], axis=0)
            )
            p = jnp.where(allowed, jnp.exp(raw - log_total), 0.0)
            ds = (p * (dot_t(da, values) - delta)).astype(BF)
            att[m] += dot(ds, keys)
            dk = dot(ds.T, qm) * scale
            dv = dot(p.astype(BF).T, da)
            kv[b, m] = jnp.concatenate([dk, dv], axis=1).astype(BF)
            return 0

        lax.fori_loop(0, l + 1, block, 0)

    def kv_copy(b, m):
        return remote(
            kv.at[b, m], kv_land.at[b, m], kv_send.at[b, m], kv_recv.at[b, m], left
        )

    def kv_step(m):
        for b in range(n - 1):

            @pl.when(l > b)
            def _(b=b):
                @pl.when(l <= n - 2)
                def _():
                    kv_copy(b, m).wait_recv()
                    kv[b, m] = (kv[b, m].astype(F32) + kv_land[b, m].astype(F32)).astype(BF)

                kv_copy(b, m).start()

    def normal_back(u, d_rot, gain, cosine, sine):
        d = d_rot * cosine - pltpu.roll(d_rot, 64, 1) * sine
        r = lax.rsqrt(jnp.mean(u * u, axis=-1, keepdims=True) + EPS)
        normal = u * r
        e = d * gain
        grad = r * (e - normal * jnp.mean(e * normal, axis=-1, keepdims=True))
        return grad.astype(BF), jnp.sum(d * normal, axis=0, keepdims=True)

    gains = small[8:10, :128].astype(F32)

    def query_back(m):
        for h in range(2):
            cols = slice(h * 128, (h + 1) * 128)
            grad, total = normal_back(
                qp[m][:, cols],
                att[m, h * 256 : (h + 1) * 256] * scale,
                gains[0:1],
                cos_ref[m],
                sin_ref[m],
            )
            dql[m, :, cols] = grad
            head_sum[0:1, :128] += total

    attend_back(0)
    attend_back(1)
    kv_step(0)
    attend_back(2)
    kv_step(1)
    attend_back(3)
    kv_step(2)
    kv_step(3)
    line.rs_fire(6)
    each(4, query_back)

    def output_weights(s, unused):
        z = dbr[:, :, :, :, :, pl.ds(pl.multiple_of(s * 256, 256), 256)].reshape(1024, 256)
        g[2, s] = dot(mixed_t[...], z).astype(BF)
        return 0

    def query_weights(s, unused):
        g[0, s] = dot(normed_t[s], dql[...].reshape(1024, 256)).astype(BF)
        sums[1, s] = dot_t(dl_t[:16], normed_t[s])[:8]
        return 0

    lax.fori_loop(0, blocks, output_weights, 0)
    line.rs_fire(2)
    lax.fori_loop(0, blocks, query_weights, 0)
    line.rs_fire(0)
    line.rs_near(5)
    homeward(3)
    own_low.wait()
    each(4, lambda m: to_chips(1, out_any, m, lambda m, u, v: low[m, u, v]))
    line.rs_near(6)
    line.rs_far(5)
    homeward(4)

    def key_back(m):
        pl.when(l <= n - 2)(lambda: kv_copy(l, m).wait_recv())
        pair = kv[l, m].astype(F32)
        pair = pair + jnp.where(l <= n - 2, kv_land[l, m].astype(F32), 0.0)
        grad, total = normal_back(kp[m], pair[:, :128], gains[1:2], cos_ref[m], sin_ref[m])
        dpl[m, :, :128] = grad
        dpl[m, :, 128:] = pair[:, 128:].astype(BF)
        head_sum[0:1, 128:] += total

    each(4, key_back)

    def key_weights(s, unused):
        g[1, s] = dot(normed_t[s], dpl[...].reshape(1024, 256)).astype(BF)
        return 0

    lax.fori_loop(0, blocks, key_weights, 0)
    line.rs_fire(1)

    def finish_out(m):
        own_res[m] = (hidden[m] + total_of(1, m)).astype(BF)

    each(4, finish_out)
    group_end(1, out_any)

    def normed_back(m):
        a, b, e = dql[m], dpl[m], dl[m][:, :16]
        for s in range(blocks):
            part = dot_t(a, w[0, s]) + dot_t(b, w[1, s]) + dot(e, small_g[0, s])
            dbr[m, :, :, :, :, s * 256 : (s + 1) * 256] = part.astype(BF).reshape(
                2, 2, 2, 32, 256
            )
        mate_copy(2, dbr, m).start()

    def home(i, own, out):
        mine = out.at[:, k]
        there = out.at[:, (1 - y) * 2 + c]
        keep = pltpu.make_async_copy(own, mine, o_loc.at[1 + i])
        over = remote(own, mine, h_send.at[i, 0], h_recv.at[i, 0], group.chip(2))
        beside = remote(own, mine, h_send.at[i, 1], h_recv.at[i, 1], mate)
        on = remote(there, there, h_send.at[i, 2], h_recv.at[i, 2], mate)
        return keep, over, beside, on

    def drain_spread(m):
        for o in (1, 2, 3):
            spread(m, o).wait_send()
        for o in range(4):
            spread_mate(m, o).wait_send()

    each(4, drain_spread)
    each(4, normed_back)
    res_home = home(0, own_res, res_out)
    for copy in res_home[:3]:
        copy.start()
    line.rs_near(2)
    line.rs_far(6)
    homeward(5)
    each(4, lambda m: to_chips(2, dbr, m, lambda m, u, v: dbr[m, u, v, c]))
    line.rs_near(0)
    line.rs_far(2)

    def finish_grad(m):
        total = total_of(2, m)
        v = own_x[m].astype(F32)
        r = lax.rsqrt(jnp.mean(v * v, axis=-1, keepdims=True) + EPS)
        normal = v * r
        gain_sum[0:1] += jnp.sum(total * normal, axis=0, keepdims=True)
        e = total * gain_row[0:1, :]
        own_grad[m] = (
            d_hid[m] + r * (e - normal * jnp.mean(e * normal, axis=-1, keepdims=True))
        ).astype(BF)

    each(4, finish_grad)
    for s in range(blocks):
        sums[0, s, 0:2] = gain_sum[0:2, s * 256 : (s + 1) * 256]
        sums[0, s, 2:3] = head_sum[0:1]
        sums[0, s, 3:8] = jnp.zeros((5, 256), F32)
    small_c = remote(sums.at[0], sum_c, t_send.at[0], t_recv.at[0], mate)
    small_x = remote(sums, sum_x, t_send.at[1], t_recv.at[1], group.chip(1))
    small_y = remote(sums.at[0], sum_y, t_send.at[2], t_recv.at[2], group.chip(2))
    small_c.start()
    grad_home = home(1, own_grad, grad_out)
    for copy in grad_home[:3]:
        copy.start()
    res_home[1].wait_recv()
    res_home[3].start()
    small_c.wait()
    sums[0] = sums[0] + sum_c[...]
    small_x.start()
    line.rs_near(1)
    line.rs_far(0)
    homeward(6)
    small_x.wait()
    sums[...] = sums[...] + sum_x[...]
    small_y.start()
    homeward(2)
    small_y.wait()
    sums[0] = sums[0] + sum_y[...]

    def small_line(d):
        to = lax.rem(l + d, n)
        return remote(
            sums.at[:, pl.ds(2 * to, 2)],
            sum_l.at[l],
            t_send.at[2 + d],
            t_recv.at[2 + d],
            device(to, x, y, c),
        )

    for d in range(1, n):
        small_line(d).start()
    sum_l[l] = sums[:, pl.ds(2 * l, 2)]
    line.rs_far(1)
    grad_home[1].wait_recv()
    grad_home[3].start()
    homeward(0)
    homeward(1)
    for d in range(1, n):
        small_line(d).wait()
    total = sum_l[0, :, x]
    for i in range(1, n):
        total = total + sum_l[i, :, x]
    sums_out[...] = total
    for item in (3, 4, 5, 6, 2, 0, 1):
        back, item, kind, j = backward(item)
        back_wait(back, item, kind, j)
    for copies in (res_home, grad_home):
        keep, over, beside, on = copies
        keep.wait()
        over.wait_send()
        beside.wait()
        on.wait()
    group_end(2, dbr)

    def drain(m):
        for b in range(n - 1):
            pl.when(l > b)(lambda b=b: kv_copy(b, m).wait_send())

    each(4, drain)
    each(7, line.rs_end)


def tail(n, din, out, x_in, z_in, hidden, ffn_parts, normed_t, g_all, kv, q, qp, kp, att, lse, gate, small_g, small, cosine, sine, row_lo, row_hi):
    d = x_in.shape[-1]
    m = 2 * n
    bf = lambda *shape: jax.ShapeDtypeStruct(shape, BF)
    vb = lambda *shape: pltpu.VMEM(shape, BF)
    vf = lambda *shape: pltpu.VMEM(shape, F32)
    return pl.pallas_call(
        functools.partial(tail_kernel, n),
        out_shape=(
            bf(4, 4, 32, d),
            bf(4, 4, 32, d),
            bf(256, 512),
            bf(256, 512),
            bf(512, 256),
            bf(256, 512),
            bf(256, 512),
            bf(1024, 256),
            jax.ShapeDtypeStruct((2, 8, 256), F32),
        ),
        in_specs=[ANY] * 14 + [VM] * 7,
        out_specs=(ANY,) * 8 + (VM,),
        scratch_shapes=[
            vb(7, m, 256, 256),
            vb(7, m + 2, 256, 256),
            vb(3, m, 256, 256),
            vb(m, 256, 1024),
            vb(4, 2, 2, 2, 32, d),
            vb(n, 4, 256, 256),
            vb(n, 4, 256, 256),
            vb(4, 512, 128),
            vf(4, 256, 256),
            vf(4, 256, 128),
            vf(4, 512, 128),
            vf(4, 512, 128),
            vb(2, 4, 2, 2, 32, d),
            vb(2, 3, 4, 32, d),
            vb(4, 2, 2, 32, d),
            vf(4, 32, d),
            vf(4, 32, d),
            vb(4, 32, d),
            vb(4, 32, d),
            vb(4, 32, d),
            vb(4, 32, d),
            vb(256, 1024),
            vb(4, 256, 256),
            vb(4, 256, 256),
            vb(4, 256, 128),
            vb(128, 1024),
            vf(2, d),
            vf(2, d),
            vf(1, 256),
            vf(2, m, 8, 256),
            vf(m, 8, 256),
            vf(2, m, 8, 256),
            vf(m, 8, 256),
            vf(n, 2, 2, 8, 256),
            DMA((13,)),
            DMA((7, 2, n)),
            DMA((7, n + 1)),
            DMA((7,)),
            DMA((7,)),
            DMA((7,)),
            DMA((n, 4)),
            DMA((n, 4)),
            DMA((3, 4)),
            DMA((3, 4)),
            DMA((3, 4, 3)),
            DMA((3, 4, 3)),
            DMA((4, 3)),
            DMA((4, 3)),
            DMA((4, 4)),
            DMA((4, 4)),
            DMA((2, 3)),
            DMA((2, 3)),
            DMA((3 + n,)),
            DMA((3 + n,)),
            DMA((3,)),
        ],
        compiler_params=pltpu.CompilerParams(
            collective_id=10, has_side_effects=True, vmem_limit_bytes=63 * 2**20
        ),
        name="tail",
    )(din, out, x_in, z_in, hidden, ffn_parts, normed_t, g_all, kv, q, qp, kp, att, lse, gate, small_g, small, cosine, sine, row_lo, row_hi)


def row_layout(index, buckets, lengths):
    ends = jnp.cumsum(buckets)
    starts = ends - buckets
    member = (index[:, None] >= starts[None, :]) & (index[:, None] < ends[None, :])
    position = index - jnp.sum(jnp.where(member, starts[None, :], 0), axis=1)
    limit = jnp.sum(jnp.where(member, lengths[None, :], 0), axis=1)
    return (None, position, limit)


def fast_local(
    inputs,
    cotangent,
    bucket_sizes,
    true_lengths,
    attention_gain,
    feedforward_gain,
    query_gain,
    key_gain,
    query_weight,
    key_matrix,
    value_matrix,
    headgate_weight,
    output_weight,
    gate_weight,
    up_weight,
    down_weight,
):
    batches, rows, width = inputs.shape
    n = lax.axis_size("seq") // 2
    seq, kv = lax.axis_index("seq"), lax.axis_index("kv")
    l, x = seq // 2, seq % 2
    scale = HEAD_SIZE ** (-0.5)
    span = 2 * rows
    gain_query = query_gain.astype(F32)
    gain_key = key_gain.astype(F32)

    own_small = jnp.concatenate(
        [
            headgate_weight.T,
            attention_gain[None],
            feedforward_gain[None],
            jnp.zeros((2, 256), BF),
            jnp.pad(jnp.stack([query_gain, key_gain]), ((0, 0), (0, 128))),
            jnp.zeros((6, 256), BF),
        ],
        axis=0,
    )
    paired = jnp.concatenate(
        [key_matrix[:, :128], value_matrix[:, :128], key_matrix[:, 128:], value_matrix[:, 128:]],
        axis=1,
    )

    row_index = l * span + jnp.arange(span, dtype=jnp.int32)
    layouts = [row_layout(row_index, bucket_sizes[b], true_lengths[b]) for b in range(batches)]
    positions = jnp.concatenate([item[1] for item in layouts])
    row_lo = jnp.stack([row_index - item[1] for item in layouts])
    limits = jnp.stack([item[2] for item in layouts])
    row_hi = jnp.minimum(row_index + 1, row_lo + limits)
    cosine, sine = rope_tables(positions, HEAD_SIZE)
    signed = sine * jnp.where(jnp.arange(HEAD_SIZE) < HEAD_SIZE // 2, -1.0, 1.0)
    x_split = inputs.reshape(batches, 4, 32, width)
    z_split = cotangent.reshape(batches, 4, 32, width)
    cosine = cosine.reshape(batches, span, HEAD_SIZE)
    signed = signed.reshape(batches, span, HEAD_SIZE)
    row_lo = jnp.broadcast_to(row_lo[:, :, None], (batches, span, 128))
    row_hi = jnp.broadcast_to(row_hi[:, :, None], (batches, span, 128))
    (g_all, g_own, normed_t, kv_all, query, query_proj, key_proj, gate, attended, log_total, hidden, inner, z_other, small) = head(
        n,
        x_split,
        z_split,
        query_weight,
        paired,
        output_weight,
        gate_weight,
        up_weight,
        down_weight,
        own_small,
        cosine,
        signed,
        row_lo,
        row_hi,
    )
    split = (batches, 2, 2, 2, 32, width)
    out_part, din_part, ffn_parts, d_gate, d_up, d_down = ffn(
        n, inner.reshape(batches, span, width), z_split, z_other, g_all, g_own
    )
    (own_out, own_grad, dq, dkv, do, d_gate2, d_up2, d_down2, sums) = tail(
        n,
        din_part.reshape(split),
        out_part.reshape(split),
        x_split,
        z_split,
        hidden,
        ffn_parts,
        normed_t,
        g_all,
        kv_all,
        query,
        query_proj,
        key_proj,
        attended,
        log_total,
        gate,
        small,
        own_small,
        cosine,
        signed,
        row_lo,
        row_hi,
    )

    def joined(first, rest, axis):
        a, b = jnp.split(first.astype(F32), 2, axis=axis)
        c, d = jnp.split(rest.astype(F32), 2, axis=axis)
        return jnp.concatenate([a, c, b, d], axis=axis)

    return (
        own_out.reshape(batches, rows, width),
        own_grad.reshape(batches, rows, width),
        sums[0, 0],
        sums[0, 1],
        sums[0, 2, :HEAD_SIZE],
        sums[0, 2, HEAD_SIZE:],
        dq.astype(F32),
        jnp.concatenate([dkv[:, :128], dkv[:, 256:384]], axis=1).astype(F32),
        jnp.concatenate([dkv[:, 128:256], dkv[:, 384:]], axis=1).astype(F32),
        sums[1, :4].T,
        do.astype(F32),
        joined(d_gate, d_gate2, 1),
        joined(d_up, d_up2, 1),
        joined(d_down, d_down2, 0),
    )


def solution(mesh):
    chosen = fast_local if dict(mesh.shape) == {"seq": 8, "kv": 4} else local
    in_specs = (
        P(None, "seq", None),
        P(None, "seq", None),
        P(),
        P(),
        P("seq"),
        P("seq"),
        P(),
        P(),
        P("seq", "kv"),
        P("seq", "kv"),
        P("seq", "kv"),
        P("seq", "kv"),
        P("kv", "seq"),
        P("seq", "kv"),
        P("seq", "kv"),
        P("kv", "seq"),
    )
    out_specs = (
        P(None, "seq", None),
        P(None, "seq", None),
        P("seq"),
        P("seq"),
        P(),
        P(),
        P("seq", "kv"),
        P("seq", "kv"),
        P("seq", "kv"),
        P("seq", "kv"),
        P("kv", "seq"),
        P("seq", "kv"),
        P("seq", "kv"),
        P("kv", "seq"),
    )
    return jax.shard_map(chosen, mesh=mesh, in_specs=in_specs, out_specs=out_specs, check_vma=False)
```

```python
import functools
import math

import jax
import jax.numpy as jnp
from jax import lax
from jax.experimental import pallas as pl
from jax.experimental.pallas import tpu as pltpu
from jax.sharding import PartitionSpec as P

HEAD_SIZE = 128


EPS = 1e-06
ROPE_BASE = 1000000.0
MASKED = -1e30


def rms_scale(values):
    return lax.rsqrt(jnp.mean(values * values, axis=-1, keepdims=True) + EPS)


def norm_backward(grad, normal, factor):
    return factor * (grad - normal * jnp.mean(grad * normal, axis=-1, keepdims=True))


def rope_tables(positions, width):
    half = width // 2
    steps = jnp.arange(half, dtype=jnp.float32) * (2.0 / width)
    inverse = jnp.exp(-steps * math.log(ROPE_BASE))
    angles = positions.astype(jnp.float32)[:, None] * inverse[None, :]
    cosine = jnp.cos(angles)
    sine = jnp.sin(angles)
    return (jnp.concatenate([cosine, cosine], axis=-1), jnp.concatenate([sine, sine], axis=-1))


def rotate_forward(values, cosine, sine):
    half = values.shape[-1] // 2
    turned = jnp.concatenate([-values[..., half:], values[..., :half]], axis=-1)
    return values * cosine[:, None, :] + turned * sine[:, None, :]


def rotate_backward(grad, cosine, sine):
    half = grad.shape[-1] // 2
    moved = grad * sine[:, None, :]
    return grad * cosine[:, None, :] + jnp.concatenate(
        [moved[..., half:], -moved[..., :half]], axis=-1
    )


def token_layout(index, buckets, lengths):
    ends = jnp.cumsum(buckets)
    starts = ends - buckets
    member = (index[:, None] >= starts[None, :]) & (index[:, None] < ends[None, :])
    labels = jnp.arange(buckets.shape[0], dtype=jnp.int32)
    segment = jnp.sum(jnp.where(member, labels[None, :], 0), axis=1)
    position = index - jnp.sum(jnp.where(member, starts[None, :], 0), axis=1)
    limit = jnp.sum(jnp.where(member, lengths[None, :], 0), axis=1)
    return (segment, position, position < limit)


def outer_sum(left, right):
    return lax.dot_general(
        left, right, (((0,), (0,)), ((), ())), preferred_element_type=jnp.float32
    )


def times_transpose(left, weight):
    return lax.dot_general(
        left, weight, (((1,), (1,)), ((), ())), preferred_element_type=jnp.float32
    )


def block_scores(query_kg, key_block, start, row_index, row_segment, buckets, lengths, scale):
    key_index = start + jnp.arange(key_block.shape[0], dtype=jnp.int32)
    key_segment, key_position, key_valid = token_layout(key_index, buckets, lengths)
    allowed = (
        (row_segment[:, None] == key_segment[None, :])
        & (key_index[None, :] <= row_index[:, None])
        & key_valid[None, :]
    )
    raw = (
        jnp.einsum("kgtd,skd->kgts", query_kg, key_block, preferred_element_type=jnp.float32)
        * scale
    )
    return (jnp.where(allowed, raw, MASKED), allowed)


def split_blocks(keys, values, block):
    blocks = keys.shape[0] // block
    key_blocks = keys.reshape(blocks, block, keys.shape[1], keys.shape[2])
    value_blocks = values.reshape(blocks, block, values.shape[1], values.shape[2])
    starts = jnp.arange(blocks) * block
    return (key_blocks, value_blocks, starts)


def attention_forward(
    query_kg, keys, values, row_index, row_segment, buckets, lengths, block, scale
):
    key_blocks, value_blocks, starts = split_blocks(keys, values, block)

    def first_pass(carry, item):
        running_max, total = carry
        key_block, start = item
        masked, allowed = block_scores(
            query_kg, key_block, start, row_index, row_segment, buckets, lengths, scale
        )
        new_max = jnp.maximum(running_max, jnp.max(masked, axis=-1))
        total = total * jnp.exp(running_max - new_max) + jnp.sum(
            jnp.where(allowed, jnp.exp(masked - new_max[..., None]), 0.0), axis=-1
        )
        return ((new_max, total), None)

    begin = (
        jnp.full(query_kg.shape[:3], MASKED, jnp.float32),
        jnp.zeros(query_kg.shape[:3], jnp.float32),
    )
    (running_max, total), unused = lax.scan(first_pass, begin, (key_blocks, starts))
    log_total = running_max + jnp.log(total)

    def second_pass(accumulated, item):
        key_block, value_block, start = item
        masked, allowed = block_scores(
            query_kg, key_block, start, row_index, row_segment, buckets, lengths, scale
        )
        weights = jnp.where(allowed, jnp.exp(masked - log_total[..., None]), 0.0).astype(
            jnp.bfloat16
        )
        return (
            accumulated
            + jnp.einsum(
                "kgts,skd->kgtd", weights, value_block, preferred_element_type=jnp.float32
            ),
            None,
        )

    attended, unused = lax.scan(
        second_pass, jnp.zeros(query_kg.shape, jnp.float32), (key_blocks, value_blocks, starts)
    )
    return (attended, log_total)


def attention_backward(
    query_kg,
    grad_kg,
    log_total,
    delta,
    keys,
    values,
    row_index,
    row_segment,
    buckets,
    lengths,
    block,
    scale,
):
    key_blocks, value_blocks, starts = split_blocks(keys, values, block)

    def step(grad_query, item):
        key_block, value_block, start = item
        masked, allowed = block_scores(
            query_kg, key_block, start, row_index, row_segment, buckets, lengths, scale
        )
        weights = jnp.where(allowed, jnp.exp(masked - log_total[..., None]), 0.0)
        grad_weights = jnp.einsum(
            "kgtd,skd->kgts", grad_kg, value_block, preferred_element_type=jnp.float32
        )
        grad_scores = (weights * (grad_weights - delta[..., None])).astype(jnp.bfloat16)
        grad_query = grad_query + scale * jnp.einsum(
            "kgts,skd->kgtd", grad_scores, key_block, preferred_element_type=jnp.float32
        )
        grad_key = scale * jnp.einsum(
            "kgts,kgtd->skd", grad_scores, query_kg, preferred_element_type=jnp.float32
        )
        grad_value = jnp.einsum(
            "kgts,kgtd->skd",
            weights.astype(jnp.bfloat16),
            grad_kg,
            preferred_element_type=jnp.float32,
        )
        return (grad_query, (grad_key, grad_value))

    grad_query, (grad_keys, grad_values) = lax.scan(
        step, jnp.zeros(query_kg.shape, jnp.float32), (key_blocks, value_blocks, starts)
    )
    return (grad_query, grad_keys.reshape(keys.shape), grad_values.reshape(values.shape))


def local(
    inputs,
    cotangent,
    bucket_sizes,
    true_lengths,
    attention_gain,
    feedforward_gain,
    query_gain,
    key_gain,
    query_weight,
    key_matrix,
    value_matrix,
    headgate_weight,
    output_weight,
    gate_weight,
    up_weight,
    down_weight,
):
    batches, rows, width = inputs.shape
    seq_count = lax.axis_size("seq")
    block = math.gcd(rows * seq_count, 512)
    local_heads = query_weight.shape[1] // HEAD_SIZE
    local_groups = key_matrix.shape[1] // HEAD_SIZE
    group = local_heads // local_groups
    scale = HEAD_SIZE ** (-0.5)
    row_index = lax.axis_index("seq") * rows + jnp.arange(rows, dtype=jnp.int32)
    gain_query = query_gain.astype(jnp.float32)
    gain_key = key_gain.astype(jnp.float32)
    sum_attention_gain = jnp.zeros((width,), jnp.float32)
    sum_feedforward_gain = jnp.zeros((width,), jnp.float32)
    sum_query = jnp.zeros((width, query_weight.shape[1]), jnp.float32)
    sum_key = jnp.zeros((width, key_matrix.shape[1]), jnp.float32)
    sum_value = jnp.zeros((width, value_matrix.shape[1]), jnp.float32)
    sum_headgate = jnp.zeros((width, headgate_weight.shape[1]), jnp.float32)
    sum_output = jnp.zeros((output_weight.shape[0], width), jnp.float32)
    sum_gate = jnp.zeros((width, gate_weight.shape[1]), jnp.float32)
    sum_upward = jnp.zeros((width, up_weight.shape[1]), jnp.float32)
    sum_down = jnp.zeros((down_weight.shape[0], width), jnp.float32)
    sum_query_gain = jnp.zeros((HEAD_SIZE,), jnp.float32)
    sum_key_gain = jnp.zeros((HEAD_SIZE,), jnp.float32)
    results = []
    input_grads = []
    for batch in range(batches):
        gathered = (
            lax.all_gather(attention_gain, "seq", axis=0, tiled=True),
            lax.all_gather(feedforward_gain, "seq", axis=0, tiled=True),
            lax.all_gather(query_weight, "seq", axis=0, tiled=True),
            lax.all_gather(key_matrix, "seq", axis=0, tiled=True),
            lax.all_gather(value_matrix, "seq", axis=0, tiled=True),
            lax.all_gather(headgate_weight, "seq", axis=0, tiled=True),
            lax.all_gather(output_weight, "seq", axis=1, tiled=True),
            lax.all_gather(gate_weight, "seq", axis=0, tiled=True),
            lax.all_gather(up_weight, "seq", axis=0, tiled=True),
            lax.all_gather(down_weight, "seq", axis=1, tiled=True),
        )
        (
            gain_a,
            gain_f,
            w_query,
            key_projection_weight,
            value_projection_weight,
            w_head,
            w_output,
            w_gate,
            w_up,
            w_down,
        ) = gathered
        gain_a = gain_a.astype(jnp.float32)
        gain_f = gain_f.astype(jnp.float32)
        buckets = bucket_sizes[batch]
        lengths = true_lengths[batch]
        row_segment, row_position, row_valid = token_layout(row_index, buckets, lengths)
        cosine, sine = rope_tables(row_position, HEAD_SIZE)
        current = inputs[batch].astype(jnp.float32)
        scale_a = rms_scale(current)
        normal_a = current * scale_a
        normed_input = (normal_a * gain_a).astype(jnp.bfloat16)
        query_proj = jnp.dot(normed_input, w_query, preferred_element_type=jnp.float32).reshape(
            rows, local_heads, HEAD_SIZE
        )
        key_proj = jnp.dot(
            normed_input, key_projection_weight, preferred_element_type=jnp.float32
        ).reshape(rows, local_groups, HEAD_SIZE)
        value_proj = jnp.dot(
            normed_input, value_projection_weight, preferred_element_type=jnp.float32
        )
        query_scale = rms_scale(query_proj)
        query_normal = query_proj * query_scale
        key_scale = rms_scale(key_proj)
        key_normal = key_proj * key_scale
        query_rot = rotate_forward(query_normal * gain_query, cosine, sine).astype(jnp.bfloat16)
        key_rot = rotate_forward(key_normal * gain_key, cosine, sine).astype(jnp.bfloat16)
        value_low = value_proj.astype(jnp.bfloat16).reshape(rows, local_groups, HEAD_SIZE)
        logits = jnp.dot(normed_input, w_head, preferred_element_type=jnp.float32)
        gate = jax.nn.sigmoid(logits)
        all_keys, all_values = (
            lax.all_gather(key_rot, "seq", axis=0, tiled=True),
            lax.all_gather(value_low, "seq", axis=0, tiled=True),
        )
        query_kg = query_rot.reshape(rows, local_groups, group, HEAD_SIZE).transpose(1, 2, 0, 3)
        attended_kg, log_total = attention_forward(
            query_kg, all_keys, all_values, row_index, row_segment, buckets, lengths, block, scale
        )
        attended = attended_kg.transpose(2, 0, 1, 3).reshape(rows, local_heads, HEAD_SIZE)
        mixed = (
            (attended * gate[:, :, None])
            .astype(jnp.bfloat16)
            .reshape(rows, local_heads * HEAD_SIZE)
        )
        hidden = current + lax.psum(
            jnp.dot(mixed, w_output, preferred_element_type=jnp.float32).astype(jnp.bfloat16), "kv"
        ).astype(jnp.float32)
        scale_f = rms_scale(hidden)
        normal_f = hidden * scale_f
        inner = (normal_f * gain_f).astype(jnp.bfloat16)
        gated = jnp.dot(inner, w_gate, preferred_element_type=jnp.float32)
        upward = jnp.dot(inner, w_up, preferred_element_type=jnp.float32)
        sigma = jax.nn.sigmoid(gated)
        swish = gated * sigma
        product = (swish * upward).astype(jnp.bfloat16)
        output = hidden + lax.psum(
            jnp.dot(product, w_down, preferred_element_type=jnp.float32).astype(jnp.bfloat16), "kv"
        ).astype(jnp.float32)
        results.append(output.astype(jnp.bfloat16))
        grad_out = cotangent[batch].astype(jnp.float32)
        grad_low = grad_out.astype(jnp.bfloat16)
        sum_down = sum_down + outer_sum(product, grad_low)
        grad_product = times_transpose(grad_low, w_down)
        grad_gated = (grad_product * upward * sigma * (1.0 + gated * (1.0 - sigma))).astype(
            jnp.bfloat16
        )
        grad_upward = (grad_product * swish).astype(jnp.bfloat16)
        sum_gate = sum_gate + outer_sum(inner, grad_gated)
        sum_upward = sum_upward + outer_sum(inner, grad_upward)
        grad_inner = lax.psum(
            (times_transpose(grad_gated, w_gate) + times_transpose(grad_upward, w_up)).astype(
                jnp.bfloat16
            ),
            "kv",
        ).astype(jnp.float32)
        sum_feedforward_gain = sum_feedforward_gain + jnp.sum(grad_inner * normal_f, axis=0)
        grad_hidden = grad_out + norm_backward(grad_inner * gain_f, normal_f, scale_f)
        grad_branch = grad_hidden.astype(jnp.bfloat16)
        sum_output = sum_output + outer_sum(mixed, grad_branch)
        grad_mixed = times_transpose(grad_branch, w_output).reshape(rows, local_heads, HEAD_SIZE)
        grad_heads = (grad_mixed * gate[:, :, None]).astype(jnp.bfloat16)
        grad_logits = (jnp.sum(grad_mixed * attended, axis=-1) * gate * (1.0 - gate)).astype(
            jnp.bfloat16
        )
        back_keys = lax.all_gather(key_rot, "seq", axis=0, tiled=True)
        back_values = lax.all_gather(value_low, "seq", axis=0, tiled=True)
        grad_kg = grad_heads.reshape(rows, local_groups, group, HEAD_SIZE).transpose(1, 2, 0, 3)
        delta = jnp.sum(grad_kg.astype(jnp.float32) * attended_kg, axis=-1)
        grad_query_kg, grad_keys, grad_values = attention_backward(
            query_kg,
            grad_kg,
            log_total,
            delta,
            back_keys,
            back_values,
            row_index,
            row_segment,
            buckets,
            lengths,
            block,
            scale,
        )
        local_keys, local_values = (
            lax.psum_scatter(
                grad_keys.astype(jnp.bfloat16), "seq", scatter_dimension=0, tiled=True
            ).astype(jnp.float32),
            lax.psum_scatter(
                grad_values.astype(jnp.bfloat16), "seq", scatter_dimension=0, tiled=True
            ).astype(jnp.float32),
        )
        grad_query_rot = grad_query_kg.transpose(2, 0, 1, 3).reshape(rows, local_heads, HEAD_SIZE)
        grad_query_norm = rotate_backward(grad_query_rot, cosine, sine)
        sum_query_gain = sum_query_gain + jnp.sum(grad_query_norm * query_normal, axis=(0, 1))
        grad_query = (
            norm_backward(grad_query_norm * gain_query, query_normal, query_scale)
            .astype(jnp.bfloat16)
            .reshape(rows, local_heads * HEAD_SIZE)
        )
        grad_key_norm = rotate_backward(local_keys, cosine, sine)
        sum_key_gain = sum_key_gain + jnp.sum(grad_key_norm * key_normal, axis=(0, 1))
        grad_key = (
            norm_backward(grad_key_norm * gain_key, key_normal, key_scale)
            .astype(jnp.bfloat16)
            .reshape(rows, local_groups * HEAD_SIZE)
        )
        grad_value = local_values.astype(jnp.bfloat16).reshape(rows, local_groups * HEAD_SIZE)
        sum_query = sum_query + outer_sum(normed_input, grad_query)
        sum_key = sum_key + outer_sum(normed_input, grad_key)
        sum_value = sum_value + outer_sum(normed_input, grad_value)
        sum_headgate = sum_headgate + outer_sum(normed_input, grad_logits)
        grad_partial = (
            times_transpose(grad_query, w_query)
            + times_transpose(grad_key, key_projection_weight)
            + times_transpose(grad_value, value_projection_weight)
            + times_transpose(grad_logits, w_head)
        )
        grad_normed = lax.psum(grad_partial.astype(jnp.bfloat16), "kv").astype(jnp.float32)
        sum_attention_gain = sum_attention_gain + jnp.sum(grad_normed * normal_a, axis=0)
        grad_input = grad_hidden + norm_backward(grad_normed * gain_a, normal_a, scale_a)
        input_grads.append(grad_input.astype(jnp.bfloat16))
    (
        attention_total,
        feedforward_total,
        query_total,
        key_total,
        value_total,
        headgate_total,
        output_total,
        gate_total,
        upward_total,
        down_total,
    ) = (
        lax.psum_scatter(
            sum_attention_gain.astype(jnp.bfloat16), "seq", scatter_dimension=0, tiled=True
        ).astype(jnp.float32),
        lax.psum_scatter(
            sum_feedforward_gain.astype(jnp.bfloat16), "seq", scatter_dimension=0, tiled=True
        ).astype(jnp.float32),
        lax.psum_scatter(
            sum_query.astype(jnp.bfloat16), "seq", scatter_dimension=0, tiled=True
        ).astype(jnp.float32),
        lax.psum_scatter(
            sum_key.astype(jnp.bfloat16), "seq", scatter_dimension=0, tiled=True
        ).astype(jnp.float32),
        lax.psum_scatter(
            sum_value.astype(jnp.bfloat16), "seq", scatter_dimension=0, tiled=True
        ).astype(jnp.float32),
        lax.psum_scatter(
            sum_headgate.astype(jnp.bfloat16), "seq", scatter_dimension=0, tiled=True
        ).astype(jnp.float32),
        lax.psum_scatter(
            sum_output.astype(jnp.bfloat16), "seq", scatter_dimension=1, tiled=True
        ).astype(jnp.float32),
        lax.psum_scatter(
            sum_gate.astype(jnp.bfloat16), "seq", scatter_dimension=0, tiled=True
        ).astype(jnp.float32),
        lax.psum_scatter(
            sum_upward.astype(jnp.bfloat16), "seq", scatter_dimension=0, tiled=True
        ).astype(jnp.float32),
        lax.psum_scatter(
            sum_down.astype(jnp.bfloat16), "seq", scatter_dimension=1, tiled=True
        ).astype(jnp.float32),
    )
    query_gain_total, key_gain_total = lax.psum((sum_query_gain, sum_key_gain), ("seq", "kv"))
    return (
        jnp.stack(results, axis=0),
        jnp.stack(input_grads, axis=0),
        attention_total,
        feedforward_total,
        query_gain_total,
        key_gain_total,
        query_total,
        key_total,
        value_total,
        headgate_total,
        output_total,
        gate_total,
        upward_total,
        down_total,
    )


BF = jnp.bfloat16
F32 = jnp.float32
ANY = pl.BlockSpec(memory_space=pl.ANY)
VM = pl.BlockSpec(memory_space=pltpu.VMEM)
DMA = pltpu.SemaphoreType.DMA


def place():
    s = lax.axis_index("seq")
    k = lax.axis_index("kv")
    return (lax.div(s, 2), lax.rem(s, 2), lax.div(k, 2), lax.rem(k, 2))


def device(l, x, y, c):
    return (l * 2 + x, y * 2 + c)


def remote(src, dst, send, recv, target):
    return pltpu.make_async_remote_copy(
        src_ref=src,
        dst_ref=dst,
        send_sem=send,
        recv_sem=recv,
        device_id=target,
        device_id_type=pl.DeviceIdType.MESH,
    )


def greet(partners):
    barrier = pltpu.get_barrier_semaphore()
    count = 0
    for target, there in partners:

        def call(target=target):
            pl.semaphore_signal(
                barrier, inc=1, device_id=target, device_id_type=pl.DeviceIdType.MESH
            )

        if there is None:
            call()
            count = count + 1
        else:
            pl.when(there)(call)
            count = count + jnp.where(there, 1, 0)
    pl.semaphore_wait(barrier, count)


class Line:
    def __init__(self, length, g, ag_send, ag_recv, land=None, rs_send=None, rs_recv=None):
        self.n = length
        self.g, self.ag_send, self.ag_recv = g, ag_send, ag_recv
        self.land, self.rs_send, self.rs_recv = land, rs_send, rs_recv
        self.l, self.x, self.y, self.c = place()

    def partners(self):
        l, x, y, c = self.l, self.x, self.y, self.c
        return [
            (device(l - 1, x, y, c), l >= 1),
            (device(l + 1, x, y, c), l <= self.n - 2),
        ]

    def block(self, item, b):
        return self.g.at[item, pl.ds(2 * b, 2)]

    def _ag(self, item, way, b):
        step = -1 if way == 0 else 1
        return remote(
            self.block(item, b),
            self.block(item, b),
            self.ag_send.at[item, way, b],
            self.ag_recv.at[item, b],
            device(self.l + step, self.x, self.y, self.c),
        )

    def ag_start(self, item):
        l = self.l
        pl.when(l >= 1)(lambda: self._ag(item, 0, l).start())
        pl.when(l <= self.n - 2)(lambda: self._ag(item, 1, l).start())

    def ag_left(self, item):
        pl.when(self.l >= 1)(lambda: self._ag(item, 0, self.l).start())

    def ag_right(self, item):
        l, n = self.l, self.n
        pl.when((l >= 1) & (l <= n - 2))(lambda: self._ag(item, 1, l).start())

    def ag_right_end(self, item):
        pl.when(self.l == 0)(lambda: self._ag(item, 1, self.l).start())

    def ag_step(self, item, t):
        l, n = self.l, self.n

        @pl.when(l + t <= n - 1)
        def _():
            self._ag(item, 0, l + t).wait_recv()
            pl.when(l >= 1)(lambda: self._ag(item, 0, l + t).start())

        @pl.when(l - t >= 0)
        def _():
            self._ag(item, 1, l - t).wait_recv()
            pl.when(l <= n - 2)(lambda: self._ag(item, 1, l - t).start())

    def pump(self, item, t):
        l, n = self.l, self.n

        @pl.when((l + t <= n - 1) & (l >= 1))
        def _():
            self._ag(item, 0, l + t).wait_recv()
            self._ag(item, 0, l + t).start()

        @pl.when((l - t >= 0) & (l <= n - 2))
        def _():
            self._ag(item, 1, l - t).wait_recv()
            self._ag(item, 1, l - t).start()

    def collect(self, item):
        l, n = self.l, self.n
        for t in range(1, n):
            pl.when(l == 0)(lambda t=t: self._ag(item, 0, t).wait_recv())
            pl.when(l == n - 1)(lambda t=t: self._ag(item, 1, n - 1 - t).wait_recv())

    def ag_end(self, item):
        l, n = self.l, self.n
        for b in range(n):
            pl.when((l >= 1) & (l <= b))(lambda b=b: self._ag(item, 0, b).wait_send())
            pl.when((l <= n - 2) & (l >= b))(lambda b=b: self._ag(item, 1, b).wait_send())

    @staticmethod
    def seat(item):
        return item + 3 if item < 3 else item

    @staticmethod
    def berth(item):
        return item + 3 if item < 3 else (item - 3) % 6

    def sum_block(self, item, b):
        return self.g.at[self.seat(item), pl.ds(2 * b, 2)]

    def _slot(self, item, slot):
        return self.land.at[self.berth(item), pl.ds(2 * slot, 2)]

    def _rs(self, item, way, o):
        if way == 0:
            target = self.l - 1
            slot = jnp.where(target == o, self.n, o)
        else:
            target = self.l + 1
            slot = o
        return remote(
            self.sum_block(item, o),
            self._slot(item, slot),
            self.rs_send.at[item, way, o],
            self.rs_recv.at[item, slot],
            device(target, self.x, self.y, self.c),
        )

    def _take(self, item, o, slot):
        here = self._slot(item, slot)
        pltpu.make_async_copy(here, here, self.rs_recv.at[item, slot]).wait()
        seat, berth = self.seat(item), self.berth(item)
        for h in range(2):
            total = self.g[seat, 2 * o + h].astype(F32) + self.land[berth, 2 * slot + h].astype(F32)
            self.g[seat, 2 * o + h] = total.astype(BF)

    def rs_fire(self, item):
        l, n = self.l, self.n
        for o in range(n - 1, 0, -1):
            pl.when(l == 0)(lambda o=o: self._rs(item, 1, o).start())
            pl.when(l == n - 1)(lambda o=o: self._rs(item, 0, n - 1 - o).start())

    def rs_near(self, item):
        l, n = self.l, self.n

        @pl.when(l == 1)
        def _():
            for o in range(n - 1, 1, -1):
                self._take(item, o, o)
                self._rs(item, 1, o).start()

        @pl.when(l == n - 2)
        def _():
            for o in range(n - 2):
                self._take(item, o, o)
                self._rs(item, 0, o).start()

    def rs_far(self, item):
        l, n = self.l, self.n

        @pl.when(l == 1)
        def _():
            self._take(item, 0, 0)
            self._rs(item, 0, 0).start()

        @pl.when(l == n - 2)
        def _():
            self._take(item, n - 1, n - 1)
            self._rs(item, 1, n - 1).start()

    def rs_final(self, item):
        l, n = self.l, self.n
        pl.when(l >= 1)(lambda: self._take(item, l, l))
        pl.when(l <= n - 2)(lambda: self._take(item, l, n))

    def rs_end(self, item):
        l, n = self.l, self.n
        for o in range(n):
            pl.when(l < o)(lambda o=o: self._rs(item, 1, o).wait_send())
            pl.when(l > o)(lambda o=o: self._rs(item, 0, o).wait_send())


def each(count, body):
    def step(i, unused):
        body(i)
        return 0

    lax.fori_loop(0, count, step, 0)


class Pair:
    def __init__(self, line, refs, send, recv, local, half):
        self.line, self.refs = line, refs
        self.send, self.recv, self.local, self.half = send, recv, local, half

    def partner(self):
        line = self.line
        return (device(line.l, 1 - line.x, line.y, line.c), None)

    def _part(self, ref, kind, j, x):
        half = self.half if isinstance(self.half, int) else self.half[kind]
        at = pl.multiple_of(x * half + j * 256, 256)
        return ref.at[pl.ds(at, 256), :] if kind == 2 else ref.at[:, pl.ds(at, 256)]

    def _copies(self, item, kind, j):
        line = self.line
        mine = line.g.at[item, 2 * line.l + line.x]
        out = remote(
            self._part(self.refs[kind], kind, j, 1 - line.x),
            mine,
            self.send.at[item],
            self.recv.at[item],
            self.partner()[0],
        )
        here = pltpu.make_async_copy(
            self._part(self.refs[kind], kind, j, line.x), mine, self.local.at[item]
        )
        return out, here

    def start(self, item, kind, j):
        for copy in self._copies(item, kind, j):
            copy.start()

    def end(self, item, kind, j):
        out, here = self._copies(item, kind, j)
        here.wait()
        out.wait_send()
        out.wait_recv()


class Back(Pair):
    def _copies(self, item, kind, j):
        line = self.line
        home = self._part(self.refs[kind], kind, j, line.x)
        out = remote(
            line.g.at[line.seat(item), 2 * line.l + 1 - line.x],
            home,
            self.send.at[item],
            self.recv.at[item],
            self.partner()[0],
        )
        here = pltpu.make_async_copy(
            line.g.at[line.seat(item), 2 * line.l + line.x], home, self.local.at[item]
        )
        return out, here


def back_wait(back, item, kind, j):
    line = back.line
    out, here = back._copies(item, kind, j)
    here.wait()
    out.wait_send()
    there = back._part(back.refs[kind], kind, j, 1 - line.x)
    pltpu.make_async_copy(there, there, back.recv.at[item]).wait()


def dot(a, b):
    return lax.dot_general(a, b, (((1,), (0,)), ((), ())), preferred_element_type=F32)


def dot_t(a, b):
    return lax.dot_general(a, b, (((1,), (1,)), ((), ())), preferred_element_type=F32)


def layer_kernel(
    n,
    x_any,
    z_any,
    wq,
    wkv,
    wo,
    wg,
    wu,
    wd,
    small,
    cos_ref,
    sin_ref,
    row_range,
    res_out,
    grad_out,
    dq_out,
    dkv_out,
    do_out,
    dgw,
    duw,
    ddw,
    sums_out,
    late_out,
    normed_out,
    dz_out,
    x_v,
    normed,
    normed_t,
    g,
    small_g,
    gain_row,
    heads_row,
    kv,
    q_v,
    qp,
    kp,
    gate_v,
    att,
    tot,
    part,
    core_land,
    low,
    chip_land,
    inner,
    hidden,
    land,
    d_low,
    prod_t,
    kv_land,
    d_hid,
    own_z,
    own_x,
    dl,
    dl_t,
    gain_sum,
    head_sum,
    sums,
    sum_c,
    sum_x,
    sum_y,
    sum_l,
    late,
    late_core,
    late_chip,
    late_l,
    p_send,
    p_recv,
    p_loc,
    ag_send,
    ag_recv,
    sp_sem,
    sa_send,
    sa_recv,
    t_send,
    t_recv,
    z_send,
    z_recv,
    kv_send,
    kv_recv,
    c_send,
    c_recv,
    s_send,
    s_recv,
    i_send,
    i_recv,
    j_send,
    j_recv,
    rs_send,
    rs_recv,
    b_send,
    b_recv,
    b_loc,
    d_send,
    d_recv,
    h_send,
    h_recv,
    u_send,
    u_recv,
    o_loc,
):
    line = Line(n, g, ag_send, ag_recv, land, rs_send, rs_recv)
    l, x, y, c = line.l, line.x, line.y, line.c
    k = y * 2 + c
    group = Group()
    across, mate = device(l, 1 - x, y, c), group.mate
    right = device(l + 1, x, y, c)
    tiny = Line(n, small_g, sa_send, sa_recv)
    scale = HEAD_SIZE ** (-0.5)
    width = 256 * 2 * n
    back = Back(line, (dgw, duw, ddw), b_send, b_recv, b_loc, 768)
    back_first = Back(line, (dq_out, dkv_out, do_out), b_send, b_recv, b_loc, 256)
    left = device(l - 1, x, y, c)
    blocks = 2 * n
    first = Pair(line, (wq, wkv, wo), p_send, p_recv, p_loc, 256)
    rest = Pair(line, (wg, wu, wd), p_send, p_recv, p_loc, 768)

    def swap(item):
        if item < 3:
            return first, item, item, 0
        return rest, item, item % 3, item // 3 - 1

    def swap_start(item):
        pair, item, kind, j = swap(item)
        pair.start(item, kind, j)

    def swap_end(item):
        pair, item, kind, j = swap(item)
        pair.end(item, kind, j)

    used = iter(range(16))

    def put(src, dst):
        copy = pltpu.make_async_copy(src, dst, o_loc.at[next(used)])
        copy.start()
        return copy

    others = [device(lax.rem(l + d, n), x, y, c) for d in range(1, n)]
    greet(
        [(o, None) for o in others] + [(mate, None)] + [(group.chip(i), None) for i in (1, 2, 3)]
    )

    small_here = small_g.at[0, 2 * l + x]
    small_out_copy = remote(small, small_here, sp_sem.at[0], sp_sem.at[1], across)
    small_own = pltpu.make_async_copy(small, small_here, sp_sem.at[2])
    swap_start(0)
    small_out_copy.start()
    small_own.start()
    swap_start(1)
    swap_start(2)
    x_here = pltpu.make_async_copy(x_any, x_v.at[:, x], t_send.at[2])
    x_here.start()
    halves = pl.ds(2 * c, 2)
    x_out = remote(x_any.at[halves], x_v.at[halves, x], t_send.at[0], t_recv.at[0], across)
    x_part = x_v.at[halves, 1 - x]
    x_on = remote(x_part, x_part, t_send.at[1], t_recv.at[1], mate)
    x_out.start()
    for item in range(3, 12):
        swap_start(item)
    z_out = remote(z_any.at[halves], dz_out.at[halves], z_send.at[0], z_recv.at[0], across)
    z_part = dz_out.at[halves]
    z_on = remote(z_part, z_part, z_send.at[1], z_recv.at[1], mate)
    z_out.start()

    swap_end(0)
    line.ag_start(0)
    small_own.wait()
    small_out_copy.wait()
    tiny.ag_start(0)
    swap_end(1)
    line.ag_start(1)
    for t in range(1, n):
        tiny.ag_step(0, t)
    line.pump(0, 1)
    line.pump(1, 1)
    swap_end(2)
    for s in range(2 * n):
        cols = slice(s * 256, (s + 1) * 256)
        heads_row[:, cols] = small_g[0, s]
        gain_row[:, cols] = small_g[0, s, 4:6, :].astype(F32)

    def norm(m, side):
        v = x_v[m, side].reshape(128, 256 * 2 * n).astype(F32)
        mean = jnp.mean(v * v, axis=-1, keepdims=True)
        v = v * lax.rsqrt(mean + EPS) * gain_row[0:1, :]
        normed[m, side] = v.astype(BF).reshape(2, 2, 32, 256 * 2 * n)

    x_here.wait()
    each(4, lambda m: norm(m, x))
    line.pump(0, 2)
    line.pump(1, 2)
    line.ag_start(2)
    x_out.wait_recv()
    x_on.start()
    line.pump(2, 1)
    for item in (3, 4):
        swap_end(item)
        line.ag_left(item)
    x_on.wait_recv()
    each(4, lambda m: norm(m, 1 - x))
    for item in (0, 1):
        line.collect(item)

    def project(m):
        a = normed[m].reshape(256, 256 * 2 * n)
        qf = dot(a, g[0].reshape(256 * 2 * n, 256))
        kf = dot(a, g[1].reshape(256 * 2 * n, 256))
        gate_v[m] = jax.nn.sigmoid(dot_t(a, heads_row[...]))
        qp[m] = qf
        kp[m] = kf[:, :128]
        cosine, sine = cos_ref[m], sin_ref[m]

        def turn(u, gain):
            u = u * lax.rsqrt(jnp.mean(u * u, axis=-1, keepdims=True) + EPS) * gain
            return (u * cosine + pltpu.roll(u, 64, 1) * sine).astype(BF)

        gains = small[8:10, :128].astype(F32)
        q_v[m, :256] = turn(qf[:, :128], gains[0:1])
        q_v[m, 256:] = turn(qf[:, 128:], gains[0:1])
        kv[l, m, :, :128] = turn(kf[:, :128], gains[1:2])
        kv[l, m, :, 128:] = kf[:, 128:].astype(BF)

    def send_kv(b, m):
        return remote(kv.at[b, m], kv.at[b, m], kv_send.at[b, m], kv_recv.at[b, m], right)

    each(4, project)
    z_copy = put(z_any.at[:, k], own_z)
    x_copy = put(x_any.at[:, k], own_x)

    def attend(m, b, diagonal):
        pair = kv[b, m]
        raw = dot_t(q_v[m], pair[:, :128]) * scale
        lo = row_range[m][:, :1] - b * 256
        hi = row_range[m][:, 1:2] - b * 256
        column = lax.broadcasted_iota(jnp.int32, (512, 256), 1)
        allowed = (column >= jnp.concatenate([lo, lo], axis=0)) & (
            column < jnp.concatenate([hi, hi], axis=0)
        )
        e = jnp.where(allowed, jnp.exp(raw), 0.0)
        total = jnp.sum(e, axis=-1, keepdims=True)
        value = dot(e.astype(BF), pair[:, 128:])
        total = jnp.broadcast_to(total, (512, 128))
        if diagonal:
            tot[m] = total
            att[m] = value
        else:
            tot[m] += total
            att[m] += value

    line.pump(2, 2)

    def turned(i):
        m, s = lax.div(i, 2 * n), lax.rem(i, 2 * n)
        tile = normed[m, :, :, :, :, pl.ds(pl.multiple_of(s * 256, 256), 256)].reshape(256, 256)
        normed_t[s, :, pl.ds(pl.multiple_of(m * 256, 256), 256)] = tile.T

    def branch(m):
        total = tot[m]
        lse = jnp.log(total)
        value = att[m] / total
        att[m] = value
        tot[m] = lse
        gates = gate_v[m]
        lo, hi = gates[:, 0:2], gates[:, 2:4]
        gates = jnp.where(x == 0, lo, hi)
        mixed = jnp.concatenate(
            [value[:256] * gates[:, 0:1], value[256:] * gates[:, 1:2]], axis=1
        ).astype(BF)
        for s in range(2 * n):
            part[m, :, :, :, :, s * 256 : (s + 1) * 256] = (
                dot(mixed, g[2, s]).astype(BF).reshape(2, 2, 2, 32, 256)
            )
        mate_copy(m).start()

    sources = (part, normed, part, normed)

    def mate_place(m, r):
        return x_v.at[m, :, pl.ds(0, 2)] if r == 2 else core_land.at[m]

    def chip_place(m, o, r):
        return x_v.at[m, (o - 1) // 2, 2 + (o - 1) % 2] if r == 2 else chip_land.at[o - 1, m]

    def mate_copy(m, r=0):
        return remote(
            sources[r].at[m, :, :, 1 - c], mate_place(m, r), c_send.at[r, m], c_recv.at[r, m], mate
        )

    def chip_copy(m, o, r=0):
        ox, oy = group.other(o)
        return remote(
            low.at[m, ox, oy],
            chip_place(m, o, r),
            s_send.at[r, m, o - 1],
            s_recv.at[r, m, o - 1],
            group.chip(o),
        )

    def to_chips(m, r=0):
        mate_copy(m, r).wait_recv()
        for u in range(2):
            for v in range(2):
                there = x_v[m, u, v] if r == 2 else core_land[m, u, v]
                low[m, u, v] = (sources[r][m, u, v, c].astype(F32) + there.astype(F32)).astype(BF)
        for o in (3, 1, 2):
            chip_copy(m, o, r).start()

    def total_of(m, r=0):
        total = low[m, x, y].astype(F32)
        for o in (1, 2, 3):
            chip_copy(m, o, r).wait_recv()
            there = x_v[m, (o - 1) // 2, 2 + (o - 1) % 2] if r == 2 else chip_land[o - 1, m]
            total = total + there.astype(F32)
        return total

    def sum_end(m, r=0):
        mate_copy(m, r).wait_send()
        for o in (1, 2, 3):
            chip_copy(m, o, r).wait_send()

    def ahead(m):
        pl.when(l <= n - 2)(lambda: send_kv(l, m).start())
        attend(m, l, True)

        def step(t, unused):
            b = l - t
            send_kv(b, m).wait_recv()
            pl.when(l <= n - 2)(lambda: send_kv(b, m).start())
            attend(m, b, False)
            return 0

        lax.fori_loop(1, l + 1, step, 0)

    for m in range(4):
        ahead(m)
        if m == 0:
            each(8 * n, turned)
            line.collect(2)
            normed_copy = put(normed_t, normed_out)
        branch(m)
        if m > 0:
            to_chips(m - 1)
        for item in (3 + 2 * m + 2, 3 + 2 * m + 3):
            if item < 12:
                swap_end(item)
                line.ag_left(item)
    to_chips(3)
    for item in range(3, 12):
        line.ag_right_end(item)
    for item in (3, 4, 5):
        line.ag_right(item)
    for item in (3, 4, 5):
        line.pump(item, 1)

    def inner_copy(m, o, r=0):
        here = inner.at[m, x, y, c]
        return remote(
            here, here, i_send.at[r, m, o - 1], i_recv.at[r, m, o - 1], group.chip(o)
        )

    def inner_mate(m, o, r=0):
        ox, oy = group.other(o)
        there = inner.at[m, ox, oy, c]
        return remote(there, there, j_send.at[r, m, o], j_recv.at[r, m, o], mate)

    def finish(m):
        h = x_v[m, x, k].astype(F32) + total_of(m)
        hidden[m] = h
        mean = jnp.mean(h * h, axis=-1, keepdims=True)
        inner[m, x, y, c] = (h * lax.rsqrt(mean + EPS) * gain_row[1:2, :]).astype(BF)
        for o in (3, 1, 2):
            inner_copy(m, o).start()
        inner_mate(m, 0).start()

    each(4, finish)
    for item in (3, 4, 5):
        line.pump(item, 2)
    for item in (6, 7, 8):
        line.ag_right(item)
    z_out.wait_recv()
    z_on.start()

    def pass_on(m, r=0):
        for o in (1, 2, 3):
            inner_copy(m, o, r).wait_recv()
            inner_mate(m, o, r).start()

    each(4, pass_on)
    for item in (6, 7, 8):
        line.pump(item, 1)
    x_out.wait_send()
    x_on.wait_send()
    z_on.wait_recv()
    dz_own = pltpu.make_async_copy(z_any, x_v.at[:, x], z_send.at[2])
    dz_other = pltpu.make_async_copy(dz_out, x_v.at[:, 1 - x], z_send.at[3])
    dz_own.start()
    dz_other.start()

    def arrive(m, r=0):
        for o in range(4):
            inner_mate(m, o, r).wait_recv()

    def spread_end(m, r=0):
        for o in (1, 2, 3):
            inner_copy(m, o, r).wait_send()
        for o in range(4):
            inner_mate(m, o, r).wait_send()

    each(4, arrive)
    normed_copy.wait()

    def turn_inner(i):
        m, s = lax.div(i, 2 * n), lax.rem(i, 2 * n)
        tile = inner[m, :, :, :, :, pl.ds(pl.multiple_of(s * 256, 256), 256)].reshape(256, 256)
        normed_t[s, :, pl.ds(pl.multiple_of(m * 256, 256), 256)] = tile.T

    each(8 * n, turn_inner)
    each(4, sum_end)
    each(4, spread_end)

    def kv_sent(m):
        for b in range(n):
            pl.when((l >= b) & (l <= n - 2))(lambda b=b: send_kv(b, m).wait_send())

    each(4, kv_sent)
    dz_own.wait()
    dz_other.wait()

    def compute(j):
        base = 3 * j + 3

        def rows(m, unused):
            a = inner[m].reshape(256, width)
            d = x_v[m].reshape(256, width)
            gated = dot(a, g[base].reshape(width, 256))
            upward = dot(a, g[base + 1].reshape(width, 256))
            grad = dot_t(d[:, :256], g[base + 2, 0])
            for s in range(1, 2 * n):
                grad = grad + dot_t(d[:, s * 256 : (s + 1) * 256], g[base + 2, s])
            sigma = jax.nn.sigmoid(gated)
            swish = gated * sigma
            product = (swish * upward).astype(BF)
            d_gated = (grad * upward * sigma * (1.0 + gated * (1.0 - sigma))).astype(BF)
            d_upward = (grad * swish).astype(BF)
            at = pl.ds(pl.multiple_of(m * 256, 256), 256)
            d_low[0, at] = d_gated
            d_low[1, at] = d_upward
            prod_t[:, at] = product.T
            for s in range(2 * n):
                cols = slice(s * 256, (s + 1) * 256)
                o = dot(product, g[base + 2, s])
                i = dot_t(d_gated, g[base, s]) + dot_t(d_upward, g[base + 1, s])
                if j > 0:
                    o = o + part[m, :, :, :, :, cols].reshape(256, 256).astype(F32)
                    i = i + normed[m, :, :, :, :, cols].reshape(256, 256).astype(F32)
                part[m, :, :, :, :, cols] = o.astype(BF).reshape(2, 2, 2, 32, 256)
                normed[m, :, :, :, :, cols] = i.astype(BF).reshape(2, 2, 2, 32, 256)
            return 0

        lax.fori_loop(0, 4, rows, 0)

        def weights(s, unused):
            t = normed_t[s]
            g[base, s] = dot(t, d_low[0]).astype(BF)
            g[base + 1, s] = dot(t, d_low[1]).astype(BF)
            z = x_v[:, :, :, :, pl.ds(pl.multiple_of(s * 256, 256), 256)].reshape(1024, 256)
            g[base + 2, s] = dot(prod_t[...], z).astype(BF)
            return 0

        lax.fori_loop(0, 2 * n, weights, 0)

    def backward(item):
        if item < 3:
            return back_first, item, item, 0
        return back, item, item % 3, item // 3 - 1

    def homeward(item):
        line.rs_final(item)
        way, item, kind, j = backward(item)
        way.start(item, kind, j)

    inside = (l >= 1) & (l <= n - 2)

    def homeward_in(item):
        pl.when(inside)(lambda: homeward(item))

    def homeward_end(item):
        pl.when(jnp.logical_not(inside))(lambda: homeward(item))

    for item in (3, 4, 5):
        line.collect(item)
        line.ag_end(item)
    compute(0)
    for item in (3, 4, 5):
        line.rs_fire(item)
    for item in (6, 7, 8):
        line.pump(item, 2)
    for item in (9, 10, 11):
        line.ag_right(item)
    for item in (9, 10, 11):
        line.pump(item, 1)
    line.rs_near(3)
    line.rs_near(4)
    for item in (6, 7, 8):
        line.collect(item)
        line.ag_end(item)
    compute(1)
    for item in (6, 7, 8):
        line.rs_fire(item)
    for item in (9, 10, 11):
        line.pump(item, 2)
    line.rs_near(5)
    homeward_in(3)
    line.rs_far(3)
    homeward_in(4)
    line.rs_far(4)
    line.rs_near(6)
    homeward_in(5)
    line.rs_far(5)
    line.rs_near(7)
    for item in (9, 10, 11):
        line.collect(item)
        line.ag_end(item)
    compute(2)
    each(4, lambda m: mate_copy(m, 1).start())
    for item in (3, 4, 5):
        homeward_end(item)
    for item in (9, 10, 11):
        line.rs_fire(item)
    gain_sum[...] = jnp.zeros_like(gain_sum)
    head_sum[...] = jnp.zeros_like(head_sum)
    homeward_in(6)
    line.rs_far(6)
    each(4, lambda m: to_chips(m, 1))
    line.rs_near(8)
    homeward_in(7)
    line.rs_far(7)
    homeward_in(8)
    line.rs_far(8)
    z_copy.wait()
    x_copy.wait()
    normed_back_copy = put(normed_out, normed_t)

    def finish_hidden(m):
        total = total_of(m, 1)
        h = hidden[m]
        r = lax.rsqrt(jnp.mean(h * h, axis=-1, keepdims=True) + EPS)
        normal = h * r
        gain_sum[1:2] += jnp.sum(total * normal, axis=0, keepdims=True)
        e = total * gain_row[1:2, :]
        grad = own_z[m].astype(F32) + r * (
            e - normal * jnp.mean(e * normal, axis=-1, keepdims=True)
        )
        d_hid[m] = grad
        inner[m, x, y, c] = grad.astype(BF)
        for o in (3, 1, 2):
            inner_copy(m, o, 1).start()
        inner_mate(m, 0, 1).start()

    each(4, finish_hidden)
    each(4, lambda m: sum_end(m, 1))
    for item in (6, 7, 8):
        homeward_end(item)
    line.rs_near(9)
    each(4, lambda m: pass_on(m, 1))
    each(4, lambda m: mate_copy(m, 2).start())
    line.rs_near(10)
    line.rs_far(9)

    def attend_back(m):
        arrive(m, 1)
        d = inner[m].reshape(256, width)
        gm = dot_t(d[:, :256], g[2, 0])
        for s in range(1, blocks):
            gm = gm + dot_t(d[:, s * 256 : (s + 1) * 256], g[2, s])
        gates = gate_v[m]
        gates = jnp.where(x == 0, gates[:, 0:2], gates[:, 2:4])
        g0, g1 = gates[:, 0:1], gates[:, 1:2]
        a0, a1 = att[m, :256], att[m, 256:]
        d0, d1 = gm[:, :128], gm[:, 128:]
        l0 = jnp.sum(d0 * a0, axis=-1, keepdims=True) * g0 * (1.0 - g0)
        l1 = jnp.sum(d1 * a1, axis=-1, keepdims=True) * g1 * (1.0 - g1)
        lane = lax.broadcasted_iota(jnp.int32, (256, 128), 1)
        logits = jnp.where(lane == 2 * x, l0, 0.0) + jnp.where(lane == 2 * x + 1, l1, 0.0)
        logits = logits.astype(BF)
        dl[m] = logits
        at = pl.ds(pl.multiple_of(m * 256, 256), 256)
        dl_t[:, at] = logits.T[:16]
        mixed = jnp.concatenate([a0 * g0, a1 * g1], axis=1).astype(BF)
        prod_t[:, at] = mixed.T
        da = jnp.concatenate([d0 * g0, d1 * g1], axis=0).astype(BF)
        delta = jnp.sum(da.astype(F32) * att[m], axis=-1, keepdims=True)
        log_total = tot[m][:, :1]
        qm = q_v[m]
        att[m] = jnp.zeros((512, 128), F32)

        def block(b, unused):
            pair = kv[b, m]
            keys, values = pair[:, :128], pair[:, 128:]
            raw = dot_t(qm, keys) * scale
            lo = row_range[m][:, :1] - b * 256
            hi = row_range[m][:, 1:2] - b * 256
            column = lax.broadcasted_iota(jnp.int32, (512, 256), 1)
            allowed = (column >= jnp.concatenate([lo, lo], axis=0)) & (
                column < jnp.concatenate([hi, hi], axis=0)
            )
            p = jnp.where(allowed, jnp.exp(raw - log_total), 0.0)
            ds = (p * (dot_t(da, values) - delta)).astype(BF)
            att[m] += dot(ds, keys)
            dk = dot(ds.T, qm) * scale
            dv = dot(p.astype(BF).T, da)
            kv[b, m] = jnp.concatenate([dk, dv], axis=1).astype(BF)
            return 0

        lax.fori_loop(0, l + 1, block, 0)

    def kv_copy(b, m):
        return remote(
            kv.at[b, m], kv_land.at[b, m], d_send.at[b, m], d_recv.at[b, m], left
        )

    def kv_fire(m):
        for b in range(n - 1):
            pl.when(l == n - 1)(lambda b=b: kv_copy(b, m).start())

    def kv_step(m):
        for b in range(n - 2):

            @pl.when((l > b) & (l <= n - 2))
            def _(b=b):
                kv_copy(b, m).wait_recv()
                kv[b, m] = (kv[b, m].astype(F32) + kv_land[b, m].astype(F32)).astype(BF)
                kv_copy(b, m).start()

    def normal_back(u, d_rot, gain, cosine, sine):
        d = d_rot * cosine - pltpu.roll(d_rot, 64, 1) * sine
        r = lax.rsqrt(jnp.mean(u * u, axis=-1, keepdims=True) + EPS)
        normal = u * r
        e = d * gain
        grad = r * (e - normal * jnp.mean(e * normal, axis=-1, keepdims=True))
        return grad.astype(BF), jnp.sum(d * normal, axis=0, keepdims=True)

    gains = small[8:10, :128].astype(F32)

    def query_back(m):
        for h in range(2):
            cols = slice(h * 128, (h + 1) * 128)
            grad, total = normal_back(
                qp[m][:, cols],
                att[m, h * 256 : (h + 1) * 256] * scale,
                gains[0:1],
                cos_ref[m],
                sin_ref[m],
            )
            d_low[0, pl.ds(pl.multiple_of(m * 256, 256), 256), cols] = grad
            head_sum[0:1, :128] += total

    for m in range(4):
        attend_back(m)
        kv_fire(m)
        if m == 1:
            each(4, lambda m: to_chips(m, 2))
    line.rs_near(11)
    line.rs_far(10)
    for item in (3, 4, 5):
        way, item, kind, j = backward(item)
        back_wait(way, item, kind, j)
        line.rs_end(item)
    each(4, query_back)
    normed_back_copy.wait()

    def output_weights(s, unused):
        z = inner[:, :, :, :, :, pl.ds(pl.multiple_of(s * 256, 256), 256)].reshape(1024, 256)
        g[5, s] = dot(prod_t[...], z).astype(BF)
        return 0

    def query_weights(s, unused):
        g[3, s] = dot(normed_t[s], d_low[0]).astype(BF)
        sums[1, s] = dot_t(dl_t[...], normed_t[s])[:8]
        return 0

    lax.fori_loop(0, blocks, output_weights, 0)
    line.rs_fire(2)
    lax.fori_loop(0, blocks, query_weights, 0)
    line.rs_fire(0)
    for m in range(4):
        kv_step(m)

    def key_back(m):
        pl.when(l <= n - 2)(lambda: kv_copy(l, m).wait_recv())
        pair = kv[l, m].astype(F32)
        pair = pair + jnp.where(l <= n - 2, kv_land[l, m].astype(F32), 0.0)
        grad, total = normal_back(kp[m], pair[:, :128], gains[1:2], cos_ref[m], sin_ref[m])
        at = pl.ds(pl.multiple_of(m * 256, 256), 256)
        d_low[1, at, :128] = grad
        d_low[1, at, 128:] = pair[:, 128:].astype(BF)
        head_sum[0:1, 128:] += total

    each(4, key_back)

    def key_weights(s, unused):
        g[4, s] = dot(normed_t[s], d_low[1]).astype(BF)
        return 0

    lax.fori_loop(0, blocks, key_weights, 0)
    line.rs_fire(1)

    def normed_back(m):
        at = pl.ds(pl.multiple_of(m * 256, 256), 256)
        a, b, e = d_low[0, at], d_low[1, at], dl[m][:, :16]
        for s in range(blocks):
            part = dot_t(a, g[0, s]) + dot_t(b, g[1, s]) + dot(e, small_g[0, s])
            normed[m, :, :, :, :, s * 256 : (s + 1) * 256] = part.astype(BF).reshape(
                2, 2, 2, 32, 256
            )
        mate_copy(m, 3).start()

    def home(i, own, out):
        mine = out.at[:, k]
        there = out.at[:, (1 - y) * 2 + c]
        keep = pltpu.make_async_copy(own, mine, o_loc.at[14 + i])
        over = remote(own, mine, h_send.at[i, 0], h_recv.at[i, 0], group.chip(2))
        beside = remote(own, mine, h_send.at[i, 1], h_recv.at[i, 1], mate)
        on = remote(there, there, h_send.at[i, 2], h_recv.at[i, 2], mate)
        return keep, over, beside, on

    each(4, normed_back)
    line.rs_far(11)
    for s in range(blocks):
        sums[0, s, 0:1] = gain_sum[1:2, s * 256 : (s + 1) * 256]
        sums[0, s, 1:2] = head_sum[0:1]
        sums[0, s, 2:8] = jnp.zeros((6, 256), F32)
    small_c = remote(sums.at[0], sum_c, u_send.at[0], u_recv.at[0], mate)
    small_x = remote(sums, sum_x, u_send.at[1], u_recv.at[1], group.chip(1))
    small_y = remote(sums.at[0], sum_y, u_send.at[2], u_recv.at[2], group.chip(2))
    small_c.start()

    def finish_out(m):
        own_z[m] = (hidden[m] + total_of(m, 2)).astype(BF)

    each(4, finish_out)
    each(4, lambda m: sum_end(m, 2))
    each(4, lambda m: to_chips(m, 3))
    small_c.wait()
    sums[0] = sums[0] + sum_c[...]
    small_x.start()
    res_home = home(0, own_z, res_out)
    for copy in res_home[:3]:
        copy.start()
    line.rs_near(2)
    line.rs_near(0)
    homeward(9)
    line.rs_far(2)
    small_x.wait()
    sums[...] = sums[...] + sum_x[...]
    small_y.start()
    homeward(10)
    homeward(11)
    line.rs_near(1)
    line.rs_far(0)
    small_y.wait()
    sums[0] = sums[0] + sum_y[...]

    def small_line(d):
        to = lax.rem(l + d, n)
        return remote(
            sums.at[:, pl.ds(2 * to, 2)],
            sum_l.at[l],
            u_send.at[2 + d],
            u_recv.at[2 + d],
            device(to, x, y, c),
        )

    for d in range(1, n):
        small_line(d).start()
    sum_l[l] = sums[:, pl.ds(2 * l, 2)]

    def finish_grad(m):
        total = total_of(m, 3)
        v = own_x[m].astype(F32)
        r = lax.rsqrt(jnp.mean(v * v, axis=-1, keepdims=True) + EPS)
        normal = v * r
        gain_sum[0:1] += jnp.sum(total * normal, axis=0, keepdims=True)
        e = total * gain_row[0:1, :]
        own_x[m] = (
            d_hid[m] + r * (e - normal * jnp.mean(e * normal, axis=-1, keepdims=True))
        ).astype(BF)

    each(4, finish_grad)
    for s in range(blocks):
        late[s : s + 1] = gain_sum[0:1, s * 256 : (s + 1) * 256]
    late_c = remote(late, late_core, u_send.at[6], u_recv.at[6], mate)
    late_c.start()
    grad_home = home(1, own_x, grad_out)
    grad_home[0].start()
    grad_home[2].start()
    res_home[1].wait_recv()
    res_home[3].start()
    line.rs_far(1)
    late_c.wait()
    late[...] = late[...] + late_core[...]
    late_s = [
        remote(
            late, late_chip.at[x * 2 + y], u_send.at[6 + o], u_recv.at[6 + o], group.chip(o)
        )
        for o in (1, 2, 3)
    ]
    for copy in late_s:
        copy.start()
    grad_home[1].start()
    late_chip[x * 2 + y] = late[...]
    for copy in late_s:
        copy.wait()
    late[...] = late_chip[0] + late_chip[1] + late_chip[2] + late_chip[3]

    def late_line(d):
        to = lax.rem(l + d, n)
        return remote(
            late, late_l.at[l], u_send.at[9 + d], u_recv.at[9 + d], device(to, x, y, c)
        )

    for d in range(1, n):
        late_line(d).start()
    late_l[l] = late[...]
    homeward(2)
    homeward(0)
    for d in range(1, n):
        small_line(d).wait()
    total = sum_l[0, :, x]
    for i in range(1, n):
        total = total + sum_l[i, :, x]
    sums_out[...] = total
    grad_home[1].wait_recv()
    grad_home[3].start()
    for d in range(1, n):
        late_line(d).wait()
    total = late_l[0]
    for i in range(1, n):
        total = total + late_l[i]
    late_out[...] = total
    homeward(1)
    for item in (6, 7, 8, 9, 10, 11, 2, 0, 1):
        way, item, kind, j = backward(item)
        back_wait(way, item, kind, j)
        line.rs_end(item)
    for copies in (res_home, grad_home):
        keep, over, beside, on = copies
        keep.wait()
        over.wait_send()
        beside.wait()
        on.wait()
    z_out.wait_send()
    z_on.wait_send()
    tiny.ag_end(0)
    each(3, line.ag_end)

    def drain(m):
        sum_end(m, 3)
        spread_end(m, 1)
        for b in range(n - 1):
            pl.when(l > b)(lambda b=b: kv_copy(b, m).wait_send())

    each(4, drain)


def layer(n, x_in, z_in, wq, wkv, wo, wg, wu, wd, small, cosine, sine, row_range):
    d = x_in.shape[-1]
    m = 2 * n
    bf = lambda *shape: jax.ShapeDtypeStruct(shape, BF)
    vb = lambda *shape: pltpu.VMEM(shape, BF)
    vf = lambda *shape: pltpu.VMEM(shape, F32)
    return pl.pallas_call(
        functools.partial(layer_kernel, n),
        out_shape=(
            bf(4, 4, 32, d),
            bf(4, 4, 32, d),
            bf(256, 512),
            bf(256, 512),
            bf(512, 256),
            bf(256, 1536),
            bf(256, 1536),
            bf(1536, 256),
            jax.ShapeDtypeStruct((2, 8, 256), F32),
            jax.ShapeDtypeStruct((m, 256), F32),
            bf(m, 256, 1024),
            bf(4, 4, 32, d),
        ),
        in_specs=[ANY] * 8 + [VM] * 4,
        out_specs=(ANY,) * 8 + (VM,) * 2 + (ANY,) * 2,
        scratch_shapes=[
            vb(4, 2, 4, 32, d),
            vb(4, 2, 2, 2, 32, d),
            vb(m, 256, 1024),
            vb(12, m, 256, 256),
            vb(1, m, 16, 256),
            vf(2, d),
            vb(16, d),
            vb(n, 4, 256, 256),
            vb(4, 512, 128),
            vf(4, 256, 256),
            vf(4, 256, 128),
            vf(4, 256, 16),
            vf(4, 512, 128),
            vf(4, 512, 128),
            vb(4, 2, 2, 2, 32, d),
            vb(4, 2, 2, 32, d),
            vb(4, 2, 2, 32, d),
            vb(3, 4, 32, d),
            vb(4, 2, 2, 2, 32, d),
            vf(4, 32, d),
            vb(6, m + 2, 256, 256),
            vb(2, 1024, 256),
            vb(256, 1024),
            vb(n, 4, 256, 256),
            vf(4, 32, d),
            vb(4, 32, d),
            vb(4, 32, d),
            vb(4, 256, 128),
            vb(16, 1024),
            vf(2, d),
            vf(1, 256),
            vf(2, m, 8, 256),
            vf(m, 8, 256),
            vf(2, m, 8, 256),
            vf(m, 8, 256),
            vf(n, 2, 2, 8, 256),
            vf(m, 256),
            vf(m, 256),
            vf(4, m, 256),
            vf(n, m, 256),
            DMA((12,)),
            DMA((12,)),
            DMA((12,)),
            DMA((12, 2, n)),
            DMA((12, n)),
            DMA((3,)),
            DMA((1, 2, n)),
            DMA((1, n)),
            DMA((3,)),
            DMA((2,)),
            DMA((4,)),
            DMA((2,)),
            DMA((n, 4)),
            DMA((n, 4)),
            DMA((4, 4)),
            DMA((4, 4)),
            DMA((4, 4, 3)),
            DMA((4, 4, 3)),
            DMA((2, 4, 3)),
            DMA((2, 4, 3)),
            DMA((2, 4, 4)),
            DMA((2, 4, 4)),
            DMA((12, 2, n)),
            DMA((12, n + 1)),
            DMA((12,)),
            DMA((12,)),
            DMA((12,)),
            DMA((n, 4)),
            DMA((n, 4)),
            DMA((2, 3)),
            DMA((2, 3)),
            DMA((9 + n,)),
            DMA((9 + n,)),
            DMA((16,)),
        ],
        compiler_params=pltpu.CompilerParams(
            collective_id=0, has_side_effects=True, vmem_limit_bytes=63 * 2**20
        ),
        name="layer",
    )(x_in, z_in, wq, wkv, wo, wg, wu, wd, small, cosine, sine, row_range)

class Group:
    def __init__(self):
        self.l, self.x, self.y, self.c = place()
        self.mate = device(self.l, self.x, self.y, 1 - self.c)

    def other(self, i):
        x = 1 - self.x if i & 1 else self.x
        y = 1 - self.y if i & 2 else self.y
        return x, y

    def chip(self, i):
        x, y = self.other(i)
        return device(self.l, x, y, self.c)

    def partners(self):
        return [(self.mate, None)] + [(self.chip(i), None) for i in (1, 2, 3)]


def row_layout(index, buckets, lengths):
    ends = jnp.cumsum(buckets)
    starts = ends - buckets
    member = (index[:, None] >= starts[None, :]) & (index[:, None] < ends[None, :])
    position = index - jnp.sum(jnp.where(member, starts[None, :], 0), axis=1)
    limit = jnp.sum(jnp.where(member, lengths[None, :], 0), axis=1)
    return (None, position, limit)


def fast_local(
    inputs,
    cotangent,
    bucket_sizes,
    true_lengths,
    attention_gain,
    feedforward_gain,
    query_gain,
    key_gain,
    query_weight,
    key_matrix,
    value_matrix,
    headgate_weight,
    output_weight,
    gate_weight,
    up_weight,
    down_weight,
):
    batches, rows, width = inputs.shape
    n = lax.axis_size("seq") // 2
    seq, kv = lax.axis_index("seq"), lax.axis_index("kv")
    l, x = seq // 2, seq % 2
    scale = HEAD_SIZE ** (-0.5)
    span = 2 * rows
    gain_query = query_gain.astype(F32)
    gain_key = key_gain.astype(F32)

    own_small = jnp.concatenate(
        [
            headgate_weight.T,
            attention_gain[None],
            feedforward_gain[None],
            jnp.zeros((2, 256), BF),
            jnp.pad(jnp.stack([query_gain, key_gain]), ((0, 0), (0, 128))),
            jnp.zeros((6, 256), BF),
        ],
        axis=0,
    )
    paired = jnp.concatenate(
        [key_matrix[:, :128], value_matrix[:, :128], key_matrix[:, 128:], value_matrix[:, 128:]],
        axis=1,
    )

    row_index = l * span + jnp.arange(span, dtype=jnp.int32)
    layouts = [row_layout(row_index, bucket_sizes[b], true_lengths[b]) for b in range(batches)]
    positions = jnp.concatenate([item[1] for item in layouts])
    row_lo = jnp.stack([row_index - item[1] for item in layouts])
    limits = jnp.stack([item[2] for item in layouts])
    row_hi = jnp.minimum(row_index + 1, row_lo + limits)
    cosine, sine = rope_tables(positions, HEAD_SIZE)
    signed = sine * jnp.where(jnp.arange(HEAD_SIZE) < HEAD_SIZE // 2, -1.0, 1.0)
    x_split = inputs.reshape(batches, 4, 32, width)
    z_split = cotangent.reshape(batches, 4, 32, width)
    cosine = cosine.reshape(batches, span, HEAD_SIZE)
    signed = signed.reshape(batches, span, HEAD_SIZE)
    row_range = jnp.where(jnp.arange(128) == 0, row_lo[:, :, None], row_hi[:, :, None])
    own_out, own_grad, dq, dkv, do, d_gate, d_up, d_down, sums, late, unused, unused = layer(
        n,
        x_split,
        z_split,
        query_weight,
        paired,
        output_weight,
        gate_weight,
        up_weight,
        down_weight,
        own_small,
        cosine,
        signed,
        row_range,
    )
    return (
        own_out.reshape(batches, rows, width),
        own_grad.reshape(batches, rows, width),
        lax.dynamic_index_in_dim(late, seq, 0, keepdims=False),
        sums[0, 0],
        sums[0, 1, :HEAD_SIZE],
        sums[0, 1, HEAD_SIZE:],
        dq.astype(F32),
        jnp.concatenate([dkv[:, :128], dkv[:, 256:384]], axis=1).astype(F32),
        jnp.concatenate([dkv[:, 128:256], dkv[:, 384:]], axis=1).astype(F32),
        sums[1, :4].T,
        do.astype(F32),
        d_gate.astype(F32),
        d_up.astype(F32),
        d_down.astype(F32),
    )


def solution(mesh):
    chosen = fast_local if dict(mesh.shape) == {"seq": 8, "kv": 4} else local
    in_specs = (
        P(None, "seq", None),
        P(None, "seq", None),
        P(),
        P(),
        P("seq"),
        P("seq"),
        P(),
        P(),
        P("seq", "kv"),
        P("seq", "kv"),
        P("seq", "kv"),
        P("seq", "kv"),
        P("kv", "seq"),
        P("seq", "kv"),
        P("seq", "kv"),
        P("kv", "seq"),
    )
    out_specs = (
        P(None, "seq", None),
        P(None, "seq", None),
        P("seq"),
        P("seq"),
        P(),
        P(),
        P("seq", "kv"),
        P("seq", "kv"),
        P("seq", "kv"),
        P("seq", "kv"),
        P("kv", "seq"),
        P("seq", "kv"),
        P("seq", "kv"),
        P("kv", "seq"),
    )
    return jax.shard_map(chosen, mesh=mesh, in_specs=in_specs, out_specs=out_specs, check_vma=False)
```

```python
import functools
import math

import jax
import jax.numpy as jnp
from jax import lax
from jax.experimental import pallas as pl
from jax.experimental.pallas import tpu as pltpu
from jax.sharding import PartitionSpec as P

HEAD_SIZE = 128


EPS = 1e-06
ROPE_BASE = 1000000.0
MASKED = -1e30


def rms_scale(values):
    return lax.rsqrt(jnp.mean(values * values, axis=-1, keepdims=True) + EPS)


def norm_backward(grad, normal, factor):
    return factor * (grad - normal * jnp.mean(grad * normal, axis=-1, keepdims=True))


def rope_tables(positions, width):
    half = width // 2
    steps = jnp.arange(half, dtype=jnp.float32) * (2.0 / width)
    inverse = jnp.exp(-steps * math.log(ROPE_BASE))
    angles = positions.astype(jnp.float32)[:, None] * inverse[None, :]
    cosine = jnp.cos(angles)
    sine = jnp.sin(angles)
    return (jnp.concatenate([cosine, cosine], axis=-1), jnp.concatenate([sine, sine], axis=-1))


def rotate_forward(values, cosine, sine):
    half = values.shape[-1] // 2
    turned = jnp.concatenate([-values[..., half:], values[..., :half]], axis=-1)
    return values * cosine[:, None, :] + turned * sine[:, None, :]


def rotate_backward(grad, cosine, sine):
    half = grad.shape[-1] // 2
    moved = grad * sine[:, None, :]
    return grad * cosine[:, None, :] + jnp.concatenate(
        [moved[..., half:], -moved[..., :half]], axis=-1
    )


def token_layout(index, buckets, lengths):
    ends = jnp.cumsum(buckets)
    starts = ends - buckets
    member = (index[:, None] >= starts[None, :]) & (index[:, None] < ends[None, :])
    labels = jnp.arange(buckets.shape[0], dtype=jnp.int32)
    segment = jnp.sum(jnp.where(member, labels[None, :], 0), axis=1)
    position = index - jnp.sum(jnp.where(member, starts[None, :], 0), axis=1)
    limit = jnp.sum(jnp.where(member, lengths[None, :], 0), axis=1)
    return (segment, position, position < limit)


def outer_sum(left, right):
    return lax.dot_general(
        left, right, (((0,), (0,)), ((), ())), preferred_element_type=jnp.float32
    )


def times_transpose(left, weight):
    return lax.dot_general(
        left, weight, (((1,), (1,)), ((), ())), preferred_element_type=jnp.float32
    )


def block_scores(query_kg, key_block, start, row_index, row_segment, buckets, lengths, scale):
    key_index = start + jnp.arange(key_block.shape[0], dtype=jnp.int32)
    key_segment, key_position, key_valid = token_layout(key_index, buckets, lengths)
    allowed = (
        (row_segment[:, None] == key_segment[None, :])
        & (key_index[None, :] <= row_index[:, None])
        & key_valid[None, :]
    )
    raw = (
        jnp.einsum("kgtd,skd->kgts", query_kg, key_block, preferred_element_type=jnp.float32)
        * scale
    )
    return (jnp.where(allowed, raw, MASKED), allowed)


def split_blocks(keys, values, block):
    blocks = keys.shape[0] // block
    key_blocks = keys.reshape(blocks, block, keys.shape[1], keys.shape[2])
    value_blocks = values.reshape(blocks, block, values.shape[1], values.shape[2])
    starts = jnp.arange(blocks) * block
    return (key_blocks, value_blocks, starts)


def attention_forward(
    query_kg, keys, values, row_index, row_segment, buckets, lengths, block, scale
):
    key_blocks, value_blocks, starts = split_blocks(keys, values, block)

    def first_pass(carry, item):
        running_max, total = carry
        key_block, start = item
        masked, allowed = block_scores(
            query_kg, key_block, start, row_index, row_segment, buckets, lengths, scale
        )
        new_max = jnp.maximum(running_max, jnp.max(masked, axis=-1))
        total = total * jnp.exp(running_max - new_max) + jnp.sum(
            jnp.where(allowed, jnp.exp(masked - new_max[..., None]), 0.0), axis=-1
        )
        return ((new_max, total), None)

    begin = (
        jnp.full(query_kg.shape[:3], MASKED, jnp.float32),
        jnp.zeros(query_kg.shape[:3], jnp.float32),
    )
    (running_max, total), unused = lax.scan(first_pass, begin, (key_blocks, starts))
    log_total = running_max + jnp.log(total)

    def second_pass(accumulated, item):
        key_block, value_block, start = item
        masked, allowed = block_scores(
            query_kg, key_block, start, row_index, row_segment, buckets, lengths, scale
        )
        weights = jnp.where(allowed, jnp.exp(masked - log_total[..., None]), 0.0).astype(
            jnp.bfloat16
        )
        return (
            accumulated
            + jnp.einsum(
                "kgts,skd->kgtd", weights, value_block, preferred_element_type=jnp.float32
            ),
            None,
        )

    attended, unused = lax.scan(
        second_pass, jnp.zeros(query_kg.shape, jnp.float32), (key_blocks, value_blocks, starts)
    )
    return (attended, log_total)


def attention_backward(
    query_kg,
    grad_kg,
    log_total,
    delta,
    keys,
    values,
    row_index,
    row_segment,
    buckets,
    lengths,
    block,
    scale,
):
    key_blocks, value_blocks, starts = split_blocks(keys, values, block)

    def step(grad_query, item):
        key_block, value_block, start = item
        masked, allowed = block_scores(
            query_kg, key_block, start, row_index, row_segment, buckets, lengths, scale
        )
        weights = jnp.where(allowed, jnp.exp(masked - log_total[..., None]), 0.0)
        grad_weights = jnp.einsum(
            "kgtd,skd->kgts", grad_kg, value_block, preferred_element_type=jnp.float32
        )
        grad_scores = (weights * (grad_weights - delta[..., None])).astype(jnp.bfloat16)
        grad_query = grad_query + scale * jnp.einsum(
            "kgts,skd->kgtd", grad_scores, key_block, preferred_element_type=jnp.float32
        )
        grad_key = scale * jnp.einsum(
            "kgts,kgtd->skd", grad_scores, query_kg, preferred_element_type=jnp.float32
        )
        grad_value = jnp.einsum(
            "kgts,kgtd->skd",
            weights.astype(jnp.bfloat16),
            grad_kg,
            preferred_element_type=jnp.float32,
        )
        return (grad_query, (grad_key, grad_value))

    grad_query, (grad_keys, grad_values) = lax.scan(
        step, jnp.zeros(query_kg.shape, jnp.float32), (key_blocks, value_blocks, starts)
    )
    return (grad_query, grad_keys.reshape(keys.shape), grad_values.reshape(values.shape))


def local(
    inputs,
    cotangent,
    bucket_sizes,
    true_lengths,
    attention_gain,
    feedforward_gain,
    query_gain,
    key_gain,
    query_weight,
    key_matrix,
    value_matrix,
    headgate_weight,
    output_weight,
    gate_weight,
    up_weight,
    down_weight,
):
    batches, rows, width = inputs.shape
    seq_count = lax.axis_size("seq")
    block = math.gcd(rows * seq_count, 512)
    local_heads = query_weight.shape[1] // HEAD_SIZE
    local_groups = key_matrix.shape[1] // HEAD_SIZE
    group = local_heads // local_groups
    scale = HEAD_SIZE ** (-0.5)
    row_index = lax.axis_index("seq") * rows + jnp.arange(rows, dtype=jnp.int32)
    gain_query = query_gain.astype(jnp.float32)
    gain_key = key_gain.astype(jnp.float32)
    sum_attention_gain = jnp.zeros((width,), jnp.float32)
    sum_feedforward_gain = jnp.zeros((width,), jnp.float32)
    sum_query = jnp.zeros((width, query_weight.shape[1]), jnp.float32)
    sum_key = jnp.zeros((width, key_matrix.shape[1]), jnp.float32)
    sum_value = jnp.zeros((width, value_matrix.shape[1]), jnp.float32)
    sum_headgate = jnp.zeros((width, headgate_weight.shape[1]), jnp.float32)
    sum_output = jnp.zeros((output_weight.shape[0], width), jnp.float32)
    sum_gate = jnp.zeros((width, gate_weight.shape[1]), jnp.float32)
    sum_upward = jnp.zeros((width, up_weight.shape[1]), jnp.float32)
    sum_down = jnp.zeros((down_weight.shape[0], width), jnp.float32)
    sum_query_gain = jnp.zeros((HEAD_SIZE,), jnp.float32)
    sum_key_gain = jnp.zeros((HEAD_SIZE,), jnp.float32)
    results = []
    input_grads = []
    for batch in range(batches):
        gathered = (
            lax.all_gather(attention_gain, "seq", axis=0, tiled=True),
            lax.all_gather(feedforward_gain, "seq", axis=0, tiled=True),
            lax.all_gather(query_weight, "seq", axis=0, tiled=True),
            lax.all_gather(key_matrix, "seq", axis=0, tiled=True),
            lax.all_gather(value_matrix, "seq", axis=0, tiled=True),
            lax.all_gather(headgate_weight, "seq", axis=0, tiled=True),
            lax.all_gather(output_weight, "seq", axis=1, tiled=True),
            lax.all_gather(gate_weight, "seq", axis=0, tiled=True),
            lax.all_gather(up_weight, "seq", axis=0, tiled=True),
            lax.all_gather(down_weight, "seq", axis=1, tiled=True),
        )
        (
            gain_a,
            gain_f,
            w_query,
            key_projection_weight,
            value_projection_weight,
            w_head,
            w_output,
            w_gate,
            w_up,
            w_down,
        ) = gathered
        gain_a = gain_a.astype(jnp.float32)
        gain_f = gain_f.astype(jnp.float32)
        buckets = bucket_sizes[batch]
        lengths = true_lengths[batch]
        row_segment, row_position, row_valid = token_layout(row_index, buckets, lengths)
        cosine, sine = rope_tables(row_position, HEAD_SIZE)
        current = inputs[batch].astype(jnp.float32)
        scale_a = rms_scale(current)
        normal_a = current * scale_a
        normed_input = (normal_a * gain_a).astype(jnp.bfloat16)
        query_proj = jnp.dot(normed_input, w_query, preferred_element_type=jnp.float32).reshape(
            rows, local_heads, HEAD_SIZE
        )
        key_proj = jnp.dot(
            normed_input, key_projection_weight, preferred_element_type=jnp.float32
        ).reshape(rows, local_groups, HEAD_SIZE)
        value_proj = jnp.dot(
            normed_input, value_projection_weight, preferred_element_type=jnp.float32
        )
        query_scale = rms_scale(query_proj)
        query_normal = query_proj * query_scale
        key_scale = rms_scale(key_proj)
        key_normal = key_proj * key_scale
        query_rot = rotate_forward(query_normal * gain_query, cosine, sine).astype(jnp.bfloat16)
        key_rot = rotate_forward(key_normal * gain_key, cosine, sine).astype(jnp.bfloat16)
        value_low = value_proj.astype(jnp.bfloat16).reshape(rows, local_groups, HEAD_SIZE)
        logits = jnp.dot(normed_input, w_head, preferred_element_type=jnp.float32)
        gate = jax.nn.sigmoid(logits)
        all_keys, all_values = (
            lax.all_gather(key_rot, "seq", axis=0, tiled=True),
            lax.all_gather(value_low, "seq", axis=0, tiled=True),
        )
        query_kg = query_rot.reshape(rows, local_groups, group, HEAD_SIZE).transpose(1, 2, 0, 3)
        attended_kg, log_total = attention_forward(
            query_kg, all_keys, all_values, row_index, row_segment, buckets, lengths, block, scale
        )
        attended = attended_kg.transpose(2, 0, 1, 3).reshape(rows, local_heads, HEAD_SIZE)
        mixed = (
            (attended * gate[:, :, None])
            .astype(jnp.bfloat16)
            .reshape(rows, local_heads * HEAD_SIZE)
        )
        hidden = current + lax.psum(
            jnp.dot(mixed, w_output, preferred_element_type=jnp.float32).astype(jnp.bfloat16), "kv"
        ).astype(jnp.float32)
        scale_f = rms_scale(hidden)
        normal_f = hidden * scale_f
        inner = (normal_f * gain_f).astype(jnp.bfloat16)
        gated = jnp.dot(inner, w_gate, preferred_element_type=jnp.float32)
        upward = jnp.dot(inner, w_up, preferred_element_type=jnp.float32)
        sigma = jax.nn.sigmoid(gated)
        swish = gated * sigma
        product = (swish * upward).astype(jnp.bfloat16)
        output = hidden + lax.psum(
            jnp.dot(product, w_down, preferred_element_type=jnp.float32).astype(jnp.bfloat16), "kv"
        ).astype(jnp.float32)
        results.append(output.astype(jnp.bfloat16))
        grad_out = cotangent[batch].astype(jnp.float32)
        grad_low = grad_out.astype(jnp.bfloat16)
        sum_down = sum_down + outer_sum(product, grad_low)
        grad_product = times_transpose(grad_low, w_down)
        grad_gated = (grad_product * upward * sigma * (1.0 + gated * (1.0 - sigma))).astype(
            jnp.bfloat16
        )
        grad_upward = (grad_product * swish).astype(jnp.bfloat16)
        sum_gate = sum_gate + outer_sum(inner, grad_gated)
        sum_upward = sum_upward + outer_sum(inner, grad_upward)
        grad_inner = lax.psum(
            (times_transpose(grad_gated, w_gate) + times_transpose(grad_upward, w_up)).astype(
                jnp.bfloat16
            ),
            "kv",
        ).astype(jnp.float32)
        sum_feedforward_gain = sum_feedforward_gain + jnp.sum(grad_inner * normal_f, axis=0)
        grad_hidden = grad_out + norm_backward(grad_inner * gain_f, normal_f, scale_f)
        grad_branch = grad_hidden.astype(jnp.bfloat16)
        sum_output = sum_output + outer_sum(mixed, grad_branch)
        grad_mixed = times_transpose(grad_branch, w_output).reshape(rows, local_heads, HEAD_SIZE)
        grad_heads = (grad_mixed * gate[:, :, None]).astype(jnp.bfloat16)
        grad_logits = (jnp.sum(grad_mixed * attended, axis=-1) * gate * (1.0 - gate)).astype(
            jnp.bfloat16
        )
        back_keys = lax.all_gather(key_rot, "seq", axis=0, tiled=True)
        back_values = lax.all_gather(value_low, "seq", axis=0, tiled=True)
        grad_kg = grad_heads.reshape(rows, local_groups, group, HEAD_SIZE).transpose(1, 2, 0, 3)
        delta = jnp.sum(grad_kg.astype(jnp.float32) * attended_kg, axis=-1)
        grad_query_kg, grad_keys, grad_values = attention_backward(
            query_kg,
            grad_kg,
            log_total,
            delta,
            back_keys,
            back_values,
            row_index,
            row_segment,
            buckets,
            lengths,
            block,
            scale,
        )
        local_keys, local_values = (
            lax.psum_scatter(
                grad_keys.astype(jnp.bfloat16), "seq", scatter_dimension=0, tiled=True
            ).astype(jnp.float32),
            lax.psum_scatter(
                grad_values.astype(jnp.bfloat16), "seq", scatter_dimension=0, tiled=True
            ).astype(jnp.float32),
        )
        grad_query_rot = grad_query_kg.transpose(2, 0, 1, 3).reshape(rows, local_heads, HEAD_SIZE)
        grad_query_norm = rotate_backward(grad_query_rot, cosine, sine)
        sum_query_gain = sum_query_gain + jnp.sum(grad_query_norm * query_normal, axis=(0, 1))
        grad_query = (
            norm_backward(grad_query_norm * gain_query, query_normal, query_scale)
            .astype(jnp.bfloat16)
            .reshape(rows, local_heads * HEAD_SIZE)
        )
        grad_key_norm = rotate_backward(local_keys, cosine, sine)
        sum_key_gain = sum_key_gain + jnp.sum(grad_key_norm * key_normal, axis=(0, 1))
        grad_key = (
            norm_backward(grad_key_norm * gain_key, key_normal, key_scale)
            .astype(jnp.bfloat16)
            .reshape(rows, local_groups * HEAD_SIZE)
        )
        grad_value = local_values.astype(jnp.bfloat16).reshape(rows, local_groups * HEAD_SIZE)
        sum_query = sum_query + outer_sum(normed_input, grad_query)
        sum_key = sum_key + outer_sum(normed_input, grad_key)
        sum_value = sum_value + outer_sum(normed_input, grad_value)
        sum_headgate = sum_headgate + outer_sum(normed_input, grad_logits)
        grad_partial = (
            times_transpose(grad_query, w_query)
            + times_transpose(grad_key, key_projection_weight)
            + times_transpose(grad_value, value_projection_weight)
            + times_transpose(grad_logits, w_head)
        )
        grad_normed = lax.psum(grad_partial.astype(jnp.bfloat16), "kv").astype(jnp.float32)
        sum_attention_gain = sum_attention_gain + jnp.sum(grad_normed * normal_a, axis=0)
        grad_input = grad_hidden + norm_backward(grad_normed * gain_a, normal_a, scale_a)
        input_grads.append(grad_input.astype(jnp.bfloat16))
    (
        attention_total,
        feedforward_total,
        query_total,
        key_total,
        value_total,
        headgate_total,
        output_total,
        gate_total,
        upward_total,
        down_total,
    ) = (
        lax.psum_scatter(
            sum_attention_gain.astype(jnp.bfloat16), "seq", scatter_dimension=0, tiled=True
        ).astype(jnp.float32),
        lax.psum_scatter(
            sum_feedforward_gain.astype(jnp.bfloat16), "seq", scatter_dimension=0, tiled=True
        ).astype(jnp.float32),
        lax.psum_scatter(
            sum_query.astype(jnp.bfloat16), "seq", scatter_dimension=0, tiled=True
        ).astype(jnp.float32),
        lax.psum_scatter(
            sum_key.astype(jnp.bfloat16), "seq", scatter_dimension=0, tiled=True
        ).astype(jnp.float32),
        lax.psum_scatter(
            sum_value.astype(jnp.bfloat16), "seq", scatter_dimension=0, tiled=True
        ).astype(jnp.float32),
        lax.psum_scatter(
            sum_headgate.astype(jnp.bfloat16), "seq", scatter_dimension=0, tiled=True
        ).astype(jnp.float32),
        lax.psum_scatter(
            sum_output.astype(jnp.bfloat16), "seq", scatter_dimension=1, tiled=True
        ).astype(jnp.float32),
        lax.psum_scatter(
            sum_gate.astype(jnp.bfloat16), "seq", scatter_dimension=0, tiled=True
        ).astype(jnp.float32),
        lax.psum_scatter(
            sum_upward.astype(jnp.bfloat16), "seq", scatter_dimension=0, tiled=True
        ).astype(jnp.float32),
        lax.psum_scatter(
            sum_down.astype(jnp.bfloat16), "seq", scatter_dimension=1, tiled=True
        ).astype(jnp.float32),
    )
    query_gain_total, key_gain_total = lax.psum((sum_query_gain, sum_key_gain), ("seq", "kv"))
    return (
        jnp.stack(results, axis=0),
        jnp.stack(input_grads, axis=0),
        attention_total,
        feedforward_total,
        query_gain_total,
        key_gain_total,
        query_total,
        key_total,
        value_total,
        headgate_total,
        output_total,
        gate_total,
        upward_total,
        down_total,
    )


BF = jnp.bfloat16
F32 = jnp.float32
ANY = pl.BlockSpec(memory_space=pl.ANY)
VM = pl.BlockSpec(memory_space=pltpu.VMEM)
DMA = pltpu.SemaphoreType.DMA


def place():
    s = lax.axis_index("seq")
    k = lax.axis_index("kv")
    return (lax.div(s, 2), lax.rem(s, 2), lax.div(k, 2), lax.rem(k, 2))


def device(l, x, y, c):
    return (l * 2 + x, y * 2 + c)


def remote(src, dst, send, recv, target):
    return pltpu.make_async_remote_copy(
        src_ref=src,
        dst_ref=dst,
        send_sem=send,
        recv_sem=recv,
        device_id=target,
        device_id_type=pl.DeviceIdType.MESH,
    )


def greet(partners):
    barrier = pltpu.get_barrier_semaphore()
    count = 0
    for target, there in partners:

        def call(target=target):
            pl.semaphore_signal(
                barrier, inc=1, device_id=target, device_id_type=pl.DeviceIdType.MESH
            )

        if there is None:
            call()
            count = count + 1
        else:
            pl.when(there)(call)
            count = count + jnp.where(there, 1, 0)
    pl.semaphore_wait(barrier, count)


class Line:
    def __init__(self, length, g, ag_send, ag_recv, land=None, rs_send=None, rs_recv=None):
        self.n = length
        self.g, self.ag_send, self.ag_recv = g, ag_send, ag_recv
        self.land, self.rs_send, self.rs_recv = land, rs_send, rs_recv
        self.l, self.x, self.y, self.c = place()

    def partners(self):
        l, x, y, c = self.l, self.x, self.y, self.c
        return [
            (device(l - 1, x, y, c), l >= 1),
            (device(l + 1, x, y, c), l <= self.n - 2),
        ]

    def block(self, item, b):
        return self.g.at[item, pl.ds(2 * b, 2)]

    def _ag(self, item, way, b):
        step = -1 if way == 0 else 1
        return remote(
            self.block(item, b),
            self.block(item, b),
            self.ag_send.at[item, way, b],
            self.ag_recv.at[item, b],
            device(self.l + step, self.x, self.y, self.c),
        )

    def ag_start(self, item):
        l = self.l
        pl.when(l >= 1)(lambda: self._ag(item, 0, l).start())
        pl.when(l <= self.n - 2)(lambda: self._ag(item, 1, l).start())

    def ag_half(self, item, x, src):
        l, n = self.l, self.n

        def half(way):
            step = -1 if way == 0 else 1
            return remote(
                src,
                self.g.at[item, 2 * l + x],
                self.ag_send.at[item, way, l],
                self.ag_recv.at[item, l],
                device(l + step, self.x, self.y, self.c),
            )

        pl.when(l >= 1)(lambda: half(0).start())
        pl.when(l <= n - 2)(lambda: half(1).start())

    def ag_left(self, item):
        pl.when(self.l >= 1)(lambda: self._ag(item, 0, self.l).start())

    def ag_right(self, item, plane):
        pl.when(self.l == plane)(lambda: self._ag(item, 1, self.l).start())

    def ag_step(self, item, t):
        l, n = self.l, self.n

        @pl.when(l + t <= n - 1)
        def _():
            self._ag(item, 0, l + t).wait_recv()
            pl.when(l >= 1)(lambda: self._ag(item, 0, l + t).start())

        @pl.when(l - t >= 0)
        def _():
            self._ag(item, 1, l - t).wait_recv()
            pl.when(l <= n - 2)(lambda: self._ag(item, 1, l - t).start())

    def pump(self, item, t):
        l, n = self.l, self.n

        @pl.when((l + t <= n - 1) & (l >= 1))
        def _():
            self._ag(item, 0, l + t).wait_recv()
            self._ag(item, 0, l + t).start()

        @pl.when((l - t >= 0) & (l <= n - 2))
        def _():
            self._ag(item, 1, l - t).wait_recv()
            self._ag(item, 1, l - t).start()

    def collect(self, item):
        l, n = self.l, self.n
        for t in range(1, n):
            pl.when(l == 0)(lambda t=t: self._ag(item, 0, t).wait_recv())
            pl.when(l == n - 1)(lambda t=t: self._ag(item, 1, n - 1 - t).wait_recv())

    def ag_end(self, item):
        l, n = self.l, self.n
        for b in range(n):
            pl.when((l >= 1) & (l <= b))(lambda b=b: self._ag(item, 0, b).wait_send())
            pl.when((l <= n - 2) & (l >= b))(lambda b=b: self._ag(item, 1, b).wait_send())

    @staticmethod
    def seat(item):
        return item + 3 if item < 3 else item

    @staticmethod
    def berth(item):
        return item + 3 if item < 3 else (item - 3) % 6

    def sum_block(self, item, b):
        return self.g.at[self.seat(item), pl.ds(2 * b, 2)]

    def _slot(self, item, slot):
        return self.land.at[self.berth(item), pl.ds(2 * slot, 2)]

    def _rs(self, item, way, o):
        if way == 0:
            target = self.l - 1
            slot = jnp.where(target == o, self.n, o)
        else:
            target = self.l + 1
            slot = o
        return remote(
            self.sum_block(item, o),
            self._slot(item, slot),
            self.rs_send.at[item, way, o],
            self.rs_recv.at[item, slot],
            device(target, self.x, self.y, self.c),
        )

    def _take(self, item, o, slot):
        here = self._slot(item, slot)
        pltpu.make_async_copy(here, here, self.rs_recv.at[item, slot]).wait()
        seat, berth = self.seat(item), self.berth(item)
        for h in range(2):
            total = self.g[seat, 2 * o + h].astype(F32) + self.land[berth, 2 * slot + h].astype(F32)
            self.g[seat, 2 * o + h] = total.astype(BF)

    def rs_fire(self, item):
        l, n = self.l, self.n
        for o in range(n - 1, 0, -1):
            pl.when(l == 0)(lambda o=o: self._rs(item, 1, o).start())
            pl.when(l == n - 1)(lambda o=o: self._rs(item, 0, n - 1 - o).start())

    def rs_near(self, item, plane):
        l, n = self.l, self.n
        way = 1 if plane == 1 else 0
        owners = range(n - 1, 1, -1) if plane == 1 else range(n - 2)

        @pl.when(l == plane)
        def _():
            for o in owners:
                self._take(item, o, o)
                self._rs(item, way, o).start()

    def rs_far(self, item, plane):
        l, n = self.l, self.n
        way, o = (0, 0) if plane == 1 else (1, n - 1)

        @pl.when(l == plane)
        def _():
            self._take(item, o, o)
            self._rs(item, way, o).start()

    def rs_final(self, item):
        l, n = self.l, self.n
        pl.when(l >= 1)(lambda: self._take(item, l, l))
        pl.when(l <= n - 2)(lambda: self._take(item, l, n))

    def rs_end(self, item):
        l, n = self.l, self.n
        for o in range(n):
            pl.when(l < o)(lambda o=o: self._rs(item, 1, o).wait_send())
            pl.when(l > o)(lambda o=o: self._rs(item, 0, o).wait_send())


def each(count, body):
    def step(i, unused):
        body(i)
        return 0

    lax.fori_loop(0, count, step, 0)


class Pair:
    def __init__(self, line, refs, send, recv, local, half):
        self.line, self.refs = line, refs
        self.send, self.recv, self.local, self.half = send, recv, local, half

    def partner(self):
        line = self.line
        return (device(line.l, 1 - line.x, line.y, line.c), None)

    def _part(self, ref, kind, j, x):
        at = pl.multiple_of(x * self.half + j * 256, 256)
        return ref.at[pl.ds(at, 256), :] if kind == 2 else ref.at[:, pl.ds(at, 256)]

    def _pieces(self, block, item, kind, j, x):
        ref = self.refs[kind]
        if not isinstance(ref, tuple):
            return [(self._part(ref, kind, j, x), block, item)]
        at = pl.ds(pl.multiple_of(x * (self.half // 2 if item == 1 else self.half) + j * 128, 128), 128)
        return [
            (one.at[:, at], block.at[:, pl.ds(128 * i, 128)], item + 12 * i)
            for i, one in enumerate(ref)
        ]

    def _copies(self, item, kind, j):
        line = self.line
        mine = line.g.at[item, 2 * line.l + line.x]
        away = self._pieces(mine, item, kind, j, 1 - line.x)
        stay = self._pieces(mine, item, kind, j, line.x)
        pairs = []
        for (src, block, sem), (own, unused, unused2) in zip(away, stay):
            out = remote(src, block, self.send.at[sem], self.recv.at[sem], self.partner()[0])
            here = pltpu.make_async_copy(own, block, self.local.at[sem])
            pairs.append((out, here))
        return pairs

    def start(self, item, kind, j):
        for out, here in self._copies(item, kind, j):
            out.start()
            here.start()

    def end(self, item, kind, j):
        for out, here in self._copies(item, kind, j):
            here.wait()
            out.wait_send()
            out.wait_recv()


class Back(Pair):
    def _copies(self, item, kind, j):
        line = self.line
        seat = line.seat(item)
        away = self._pieces(line.g.at[seat, 2 * line.l + 1 - line.x], item, kind, j, line.x)
        stay = self._pieces(line.g.at[seat, 2 * line.l + line.x], item, kind, j, line.x)
        pairs = []
        for (home, block, sem), (unused, own, unused2) in zip(away, stay):
            out = remote(block, home, self.send.at[sem], self.recv.at[sem], self.partner()[0])
            here = pltpu.make_async_copy(own, home, self.local.at[sem])
            pairs.append((out, here))
        return pairs

    def end(self, item, kind, j):
        line = self.line
        block = line.g.at[line.seat(item), 2 * line.l]
        there = self._pieces(block, item, kind, j, 1 - line.x)
        for (out, here), (home, unused, sem) in zip(self._copies(item, kind, j), there):
            here.wait()
            out.wait_send()
            pltpu.make_async_copy(home, home, self.recv.at[sem]).wait()


def dot(a, b):
    return lax.dot_general(a, b, (((1,), (0,)), ((), ())), preferred_element_type=F32)


def dot_t(a, b):
    return lax.dot_general(a, b, (((1,), (1,)), ((), ())), preferred_element_type=F32)


def layer_kernel(
    n,
    x_any,
    z_any,
    wq,
    wk,
    wv,
    wo,
    wg,
    wu,
    wd,
    small,
    sizes,
    lengths,
    res_out,
    grad_out,
    dq_out,
    dk_out,
    dv_out,
    do_out,
    dgw,
    duw,
    ddw,
    sums_out,
    late_out,
    normed_out,
    dz_out,
    x_v,
    normed,
    normed_t,
    g,
    small_g,
    gain_row,
    heads_row,
    kv,
    q_v,
    qp,
    kp,
    gate_v,
    att,
    tot,
    part,
    core_land,
    low,
    chip_land,
    inner,
    hidden,
    land,
    d_low,
    prod_t,
    kv_land,
    d_hid,
    own_z,
    own_x,
    dl,
    dl_t,
    gain_sum,
    head_sum,
    sums,
    sum_c,
    sum_x,
    sum_y,
    sum_l,
    late,
    late_core,
    late_chip,
    late_l,
    cos_ref,
    sin_ref,
    row_range,
    free,
    done,
    p_send,
    p_recv,
    p_loc,
    ag_send,
    ag_recv,
    sp_sem,
    sa_send,
    sa_recv,
    t_send,
    t_recv,
    z_send,
    z_recv,
    kv_send,
    kv_recv,
    c_send,
    c_recv,
    s_send,
    s_recv,
    i_send,
    i_recv,
    j_send,
    j_recv,
    rs_send,
    rs_recv,
    b_send,
    b_recv,
    b_loc,
    d_send,
    d_recv,
    h_send,
    h_recv,
    h_loc,
    u_send,
    u_recv,
    o_loc,
):
    line = Line(n, g, ag_send, ag_recv, land, rs_send, rs_recv)
    l, x, y, c = line.l, line.x, line.y, line.c
    k = y * 2 + c
    group = Group()
    across, mate = device(l, 1 - x, y, c), group.mate
    right = device(l + 1, x, y, c)
    tiny = Line(n, small_g, sa_send, sa_recv)
    scale = HEAD_SIZE ** (-0.5)
    width = 256 * 2 * n
    back = Back(line, ((dgw, duw), (dgw, duw), ddw), b_send, b_recv, b_loc, 768)
    back_first = Back(line, (dq_out, (dk_out, dv_out), do_out), b_send, b_recv, b_loc, 256)
    left = device(l - 1, x, y, c)
    blocks = 2 * n
    first = Pair(line, (wq, (wk, wv), wo), p_send, p_recv, p_loc, 256)
    rest = Pair(line, ((wg, wu), (wg, wu), wd), p_send, p_recv, p_loc, 768)

    def half_of(item):
        chunk = item // 3 - 1
        return chunk if item % 3 == 2 else 2 * chunk + item % 3

    def swap(item):
        if item < 3:
            return first, item, item, 0
        return rest, item, item % 3, half_of(item)

    def swap_start(item):
        pair, item, kind, j = swap(item)
        pair.start(item, kind, j)

    def swap_end(item):
        pair, item, kind, j = swap(item)
        pair.end(item, kind, j)

    used = iter(range(16))

    def put(src, dst):
        copy = pltpu.make_async_copy(src, dst, o_loc.at[next(used)])
        copy.start()
        return copy

    others = [device(lax.rem(l + d, n), x, y, c) for d in range(1, n)]
    greet(
        [(o, None) for o in others] + [(mate, None)] + [(group.chip(i), None) for i in (1, 2, 3)]
    )

    small_here = small_g.at[0, 2 * l + x]
    small_out_copy = remote(small, small_here, sp_sem.at[0], sp_sem.at[1], across)
    small_own = pltpu.make_async_copy(small, small_here, sp_sem.at[2])
    swap_start(0)
    line.ag_half(0, x, first._part(wq, 0, 0, x))
    small_out_copy.start()
    small_own.start()
    swap_start(1)
    swap_start(2)
    x_here = pltpu.make_async_copy(x_any, x_v.at[:, x], t_send.at[2])
    x_here.start()
    halves = pl.ds(2 * c, 2)
    x_out = remote(x_any.at[halves], x_v.at[halves, x], t_send.at[0], t_recv.at[0], across)
    x_part = x_v.at[halves, 1 - x]
    x_on = remote(x_part, x_part, t_send.at[1], t_recv.at[1], mate)
    x_out.start()
    ffn_items = (5, 3, 4, 8, 6, 7, 11, 9, 10)
    for item in ffn_items:
        swap_start(item)
    z_out = remote(z_any.at[halves], dz_out.at[halves], z_send.at[0], z_recv.at[0], across)
    z_part = dz_out.at[halves]
    z_on = remote(z_part, z_part, z_send.at[1], z_recv.at[1], mate)
    z_out.start()

    swap_end(0)
    line.ag_half(0, 1 - x, g.at[0, 2 * l + 1 - x])
    small_own.wait()
    small_out_copy.wait()
    tiny.ag_start(0)
    swap_end(1)
    line.ag_start(1)
    for t in range(1, n):
        tiny.ag_step(0, t)
    line.pump(0, 1)
    line.pump(1, 1)
    swap_end(2)
    for s in range(2 * n):
        cols = slice(s * 256, (s + 1) * 256)
        heads_row[:, cols] = small_g[0, s]
        gain_row[:, cols] = small_g[0, s, 4:6, :].astype(F32)

    def norm(m, side):
        v = x_v[m, side].reshape(128, 256 * 2 * n).astype(F32)
        mean = jnp.mean(v * v, axis=-1, keepdims=True)
        v = v * lax.rsqrt(mean + EPS) * gain_row[0:1, :]
        normed[m, side] = v.astype(BF).reshape(2, 2, 32, 256 * 2 * n)

    def tables(m):
        i = l * 256 + lax.broadcasted_iota(jnp.int32, (256, 128), 0)
        lane = lax.broadcasted_iota(jnp.int32, (256, 128), 1)
        end = sizes[m, 0]
        start = jnp.zeros_like(i)
        valid = jnp.full_like(i, lengths[m, 0])
        for bucket in range(1, sizes.shape[1]):
            start = jnp.where(i >= end, end, start)
            valid = jnp.where(i >= end, lengths[m, bucket], valid)
            end = end + sizes[m, bucket]
        row_range[m] = jnp.where(lane == 0, start, jnp.minimum(i + 1, start + valid))
        steps = (lane & 63).astype(F32) * (2.0 / HEAD_SIZE)
        angle = (i - start).astype(F32) * jnp.exp(-steps * math.log(ROPE_BASE))
        cos_ref[m] = jnp.cos(angle)
        sin_ref[m] = jnp.sin(angle) * jnp.where(lane < 64, -1.0, 1.0)

    x_here.wait()
    each(4, lambda m: norm(m, x))
    line.pump(0, 2)
    line.pump(1, 2)
    line.ag_start(2)
    each(4, tables)
    x_out.wait_recv()
    x_on.start()
    line.pump(2, 1)
    for item in ffn_items[:2]:
        swap_end(item)
        line.ag_left(item)
    x_on.wait_recv()
    each(4, lambda m: norm(m, 1 - x))
    for item in (0, 1):
        line.collect(item)

    def project(m):
        a = normed[m].reshape(256, 256 * 2 * n)
        qf = dot(a, g[0].reshape(256 * 2 * n, 256))
        kf = dot(a, g[1].reshape(256 * 2 * n, 256))
        gate_v[m] = jax.nn.sigmoid(dot_t(a, heads_row[...]))
        qp[m] = qf
        kp[m] = kf[:, :128]
        cosine, sine = cos_ref[m], sin_ref[m]

        def turn(u, gain):
            u = u * lax.rsqrt(jnp.mean(u * u, axis=-1, keepdims=True) + EPS) * gain
            return (u * cosine + pltpu.roll(u, 64, 1) * sine).astype(BF)

        gains = small[8:10, :128].astype(F32)
        q_v[m, :256] = turn(qf[:, :128], gains[0:1])
        q_v[m, 256:] = turn(qf[:, 128:], gains[0:1])
        kv[l, m, :, :128] = turn(kf[:, :128], gains[1:2])
        kv[l, m, :, 128:] = kf[:, 128:].astype(BF)

    def send_kv(b, m):
        return remote(kv.at[b, m], kv.at[b, m], kv_send.at[b, m], kv_recv.at[b, m], right)

    each(4, project)
    z_copy = put(z_any.at[:, k], own_z)
    x_copy = put(x_any.at[:, k], own_x)

    def attend(m, b, diagonal):
        pair = kv[b, m]
        raw = dot_t(q_v[m], pair[:, :128]) * scale
        lo = row_range[m][:, :1] - b * 256
        hi = row_range[m][:, 1:2] - b * 256
        column = lax.broadcasted_iota(jnp.int32, (512, 256), 1)
        allowed = (column >= jnp.concatenate([lo, lo], axis=0)) & (
            column < jnp.concatenate([hi, hi], axis=0)
        )
        e = jnp.where(allowed, jnp.exp(raw), 0.0)
        total = jnp.sum(e, axis=-1, keepdims=True)
        value = dot(e.astype(BF), pair[:, 128:])
        total = jnp.broadcast_to(total, (512, 128))
        if diagonal:
            tot[m] = total
            att[m] = value
        else:
            tot[m] += total
            att[m] += value

    line.pump(2, 2)

    def turned(i):
        m, s = lax.div(i, 2 * n), lax.rem(i, 2 * n)
        tile = normed[m, :, :, :, :, pl.ds(pl.multiple_of(s * 256, 256), 256)].reshape(256, 256)
        normed_t[s, :, pl.ds(pl.multiple_of(m * 256, 256), 256)] = tile.T

    def branch(m):
        total = tot[m]
        lse = jnp.log(total)
        value = att[m] / total
        att[m] = value
        tot[m] = lse
        gates = gate_v[m]
        lo, hi = gates[:, 0:2], gates[:, 2:4]
        gates = jnp.where(x == 0, lo, hi)
        mixed = jnp.concatenate(
            [value[:256] * gates[:, 0:1], value[256:] * gates[:, 1:2]], axis=1
        ).astype(BF)
        for s in range(2 * n):
            part[m, :, :, :, :, s * 256 : (s + 1) * 256] = (
                dot(mixed, g[2, s]).astype(BF).reshape(2, 2, 2, 32, 256)
            )
        mate_copy(m).start()

    sources = (part, normed, part, normed)

    def mate_place(m, r):
        return x_v.at[m, :, pl.ds(0, 2)] if r == 2 else core_land.at[m]

    def chip_place(m, o, r):
        return x_v.at[m, (o - 1) // 2, 2 + (o - 1) % 2] if r == 2 else chip_land.at[o - 1, m]

    def mate_copy(m, r=0):
        return remote(
            sources[r].at[m, :, :, 1 - c], mate_place(m, r), c_send.at[r, m], c_recv.at[r, m], mate
        )

    def chip_copy(m, o, r=0):
        ox, oy = group.other(o)
        return remote(
            low.at[m, ox, oy],
            chip_place(m, o, r),
            s_send.at[r, m, o - 1],
            s_recv.at[r, m, o - 1],
            group.chip(o),
        )

    def to_chips(m, r=0):
        mate_copy(m, r).wait_recv()
        for u in range(2):
            for v in range(2):
                there = x_v[m, u, v] if r == 2 else core_land[m, u, v]
                low[m, u, v] = (sources[r][m, u, v, c].astype(F32) + there.astype(F32)).astype(BF)
        for o in (3, 1, 2):
            chip_copy(m, o, r).start()

    def total_of(m, r=0):
        total = low[m, x, y].astype(F32)
        for o in (1, 2, 3):
            chip_copy(m, o, r).wait_recv()
            there = x_v[m, (o - 1) // 2, 2 + (o - 1) % 2] if r == 2 else chip_land[o - 1, m]
            total = total + there.astype(F32)
        return total

    def sum_end(m, r=0):
        mate_copy(m, r).wait_send()
        for o in (1, 2, 3):
            chip_copy(m, o, r).wait_send()

    def ahead(m):
        pl.when(l <= n - 2)(lambda: send_kv(l, m).start())
        attend(m, l, True)

        def step(t, unused):
            b = l - t
            send_kv(b, m).wait_recv()
            pl.when(l <= n - 2)(lambda: send_kv(b, m).start())
            attend(m, b, False)
            return 0

        lax.fori_loop(1, l + 1, step, 0)

    for m in range(4):
        ahead(m)
        if m == 0:
            each(8 * n, turned)
            line.collect(2)
            normed_copy = put(normed_t, normed_out)
        branch(m)
        if m > 0:
            to_chips(m - 1)
        for item in ffn_items[2 + 2 * m : 4 + 2 * m]:
            swap_end(item)
            line.ag_left(item)
    to_chips(3)
    for item in ffn_items:
        line.ag_right(item, 0)
    for item in (5, 3, 4):
        line.ag_right(item, 1)
    for item in (5, 3):
        line.ag_right(item, 2)
    for item in (5, 3):
        line.pump(item, 1)

    def inner_copy(m, o, r=0):
        here = inner.at[m, x, y, c]
        return remote(
            here, here, i_send.at[r, m, o - 1], i_recv.at[r, m, o - 1], group.chip(o)
        )

    def inner_mate(m, o, r=0):
        ox, oy = group.other(o)
        there = inner.at[m, ox, oy, c]
        return remote(there, there, j_send.at[r, m, o], j_recv.at[r, m, o], mate)

    def finish(m):
        h = x_v[m, x, k].astype(F32) + total_of(m)
        hidden[m] = h
        mean = jnp.mean(h * h, axis=-1, keepdims=True)
        inner[m, x, y, c] = (h * lax.rsqrt(mean + EPS) * gain_row[1:2, :]).astype(BF)
        for o in (3, 1, 2):
            inner_copy(m, o).start()
        inner_mate(m, 0).start()

    each(4, finish)
    for item in (5, 3):
        line.pump(item, 2)
    line.ag_right(4, 2)
    line.pump(4, 1)
    z_out.wait_recv()
    z_on.start()

    def pass_on(m, r=0):
        for o in (1, 2, 3):
            inner_copy(m, o, r).wait_recv()
            inner_mate(m, o, r).start()

    each(4, pass_on)
    line.pump(4, 2)
    for item in (8, 6, 7):
        line.ag_right(item, 1)
    for item in (8, 6):
        line.ag_right(item, 2)
    for item in (8, 6):
        line.pump(item, 1)
    x_out.wait_send()
    x_on.wait_send()
    z_on.wait_recv()
    dz_own = pltpu.make_async_copy(z_any, x_v.at[:, x], z_send.at[2])
    dz_other = pltpu.make_async_copy(dz_out, x_v.at[:, 1 - x], z_send.at[3])
    dz_own.start()
    dz_other.start()

    def arrive(m, r=0):
        for o in range(4):
            inner_mate(m, o, r).wait_recv()

    def spread_end(m, r=0):
        for o in (1, 2, 3):
            inner_copy(m, o, r).wait_send()
        for o in range(4):
            inner_mate(m, o, r).wait_send()

    each(4, arrive)
    normed_copy.wait()

    def turn_inner(i):
        m, s = lax.div(i, 2 * n), lax.rem(i, 2 * n)
        tile = inner[m, :, :, :, :, pl.ds(pl.multiple_of(s * 256, 256), 256)].reshape(256, 256)
        normed_t[s, :, pl.ds(pl.multiple_of(m * 256, 256), 256)] = tile.T

    each(8 * n, turn_inner)
    each(4, sum_end)
    each(4, spread_end)

    def kv_sent(m):
        for b in range(n):
            pl.when((l >= b) & (l <= n - 2))(lambda b=b: send_kv(b, m).wait_send())

    each(4, kv_sent)
    dz_own.wait()
    dz_other.wait()

    def compute(j, h):
        pair_of, down_of = 3 * j + 3 + h, 3 * j + 5
        here = slice(128 * h, 128 * h + 128)

        def rows(m, unused):
            a = inner[m].reshape(256, width)
            d = x_v[m].reshape(256, width)
            both = dot(a, g[pair_of].reshape(width, 256))
            gated, upward = both[:, :128], both[:, 128:]
            grad = dot_t(d[:, :256], g[down_of, 0, here])
            for s in range(1, 2 * n):
                grad = grad + dot_t(d[:, s * 256 : (s + 1) * 256], g[down_of, s, here])
            sigma = jax.nn.sigmoid(gated)
            swish = gated * sigma
            product = (swish * upward).astype(BF)
            d_both = jnp.concatenate(
                [grad * upward * sigma * (1.0 + gated * (1.0 - sigma)), grad * swish], axis=1
            ).astype(BF)
            at = pl.ds(pl.multiple_of(m * 256, 256), 256)
            d_low[0, at] = d_both
            prod_t[:128, at] = product.T
            for s in range(2 * n):
                cols = slice(s * 256, (s + 1) * 256)
                o = dot(product, g[down_of, s, here])
                i = dot_t(d_both, g[pair_of, s])
                if j + h > 0:
                    o = o + part[m, :, :, :, :, cols].reshape(256, 256).astype(F32)
                    i = i + normed[m, :, :, :, :, cols].reshape(256, 256).astype(F32)
                part[m, :, :, :, :, cols] = o.astype(BF).reshape(2, 2, 2, 32, 256)
                normed[m, :, :, :, :, cols] = i.astype(BF).reshape(2, 2, 2, 32, 256)
            return 0

        lax.fori_loop(0, 4, rows, 0)

        def weights(s):
            g[pair_of, s] = dot(normed_t[s], d_low[0]).astype(BF)
            z = x_v[:, :, :, :, pl.ds(pl.multiple_of(s * 256, 256), 256)].reshape(1024, 256)
            g[down_of, s, here] = dot(prod_t[:128], z).astype(BF)

        each(2 * n, weights)

    def backward(item):
        if item < 3:
            return back_first, item, item, 0
        return back, item, item % 3, half_of(item)

    def near(*items):
        for item in items:
            line.rs_near(item, 1)
            line.rs_near(item, n - 2)

    def far(*items):
        for item in items:
            line.rs_far(item, 1)
            line.rs_far(item, n - 2)

    def send_home(item):
        way, item, kind, j = backward(item)
        way.start(item, kind, j)

    inside = (l >= 1) & (l <= n - 2)

    def final_in(item):
        pl.when(inside)(lambda: line.rs_final(item))

    def final_end(item):
        pl.when(jnp.logical_not(inside))(lambda: line.rs_final(item))

    def ready(*items):
        for item in items:
            line.collect(item)
            line.ag_end(item)

    def free_give(i):
        def tell(target):
            pl.semaphore_signal(
                free.at[i], inc=1, device_id=target, device_id_type=pl.DeviceIdType.MESH
            )

        pl.when(l == 1)(lambda: tell(device(l - 1, x, y, c)))
        pl.when(l == n - 2)(lambda: tell(device(l + 1, x, y, c)))

    def done_give(i):
        def tell(target):
            pl.semaphore_signal(
                done.at[i], inc=1, device_id=target, device_id_type=pl.DeviceIdType.MESH
            )

        pl.when(l == 0)(lambda: tell(device(l + 1, x, y, c)))
        pl.when(l == n - 1)(lambda: tell(device(l - 1, x, y, c)))

    def done_take(i):
        pl.when(inside)(lambda: pl.semaphore_wait(done.at[i], 1))

    def free_take(i):
        pl.when(jnp.logical_not(inside))(lambda: pl.semaphore_wait(free.at[i], 1))

    ready(5, 3)
    compute(0, 0)
    line.rs_fire(3)
    for item in (8, 6):
        line.pump(item, 2)
    line.ag_right(7, 2)
    line.pump(7, 1)
    ready(4)
    compute(0, 1)
    line.rs_fire(4)
    line.rs_fire(5)
    line.pump(7, 2)
    for item in (11, 9, 10):
        line.ag_right(item, 1)
    for item in (11, 9):
        line.ag_right(item, 2)
    for item in (11, 9):
        line.pump(item, 1)
    near(3)
    ready(8, 6)
    compute(1, 0)
    line.rs_fire(6)
    for item in (11, 9):
        line.pump(item, 2)
    line.ag_right(10, 2)
    line.pump(10, 1)
    near(4)
    final_in(3)
    free_give(0)
    ready(7)
    compute(1, 1)
    line.rs_fire(7)
    line.rs_fire(8)
    line.pump(10, 2)
    near(5)
    far(3)
    final_in(4)
    free_give(1)
    near(6)
    final_in(5)
    free_give(2)
    far(4)
    ready(11, 9)
    compute(2, 0)
    free_take(0)
    line.rs_fire(9)
    ready(10)
    compute(2, 1)
    each(4, lambda m: mate_copy(m, 1).start())
    free_take(1)
    line.rs_fire(10)
    free_take(2)
    line.rs_fire(11)
    gain_sum[...] = jnp.zeros_like(gain_sum)
    head_sum[...] = jnp.zeros_like(head_sum)
    each(4, lambda m: to_chips(m, 1))
    near(7)
    far(5)
    final_in(6)
    far(6)
    near(8)
    line.rs_near(9, 1)
    z_copy.wait()
    x_copy.wait()
    normed_back_copy = put(normed_out, normed_t)

    def finish_hidden(m):
        total = total_of(m, 1)
        h = hidden[m]
        r = lax.rsqrt(jnp.mean(h * h, axis=-1, keepdims=True) + EPS)
        normal = h * r
        gain_sum[1:2] += jnp.sum(total * normal, axis=0, keepdims=True)
        e = total * gain_row[1:2, :]
        grad = own_z[m].astype(F32) + r * (
            e - normal * jnp.mean(e * normal, axis=-1, keepdims=True)
        )
        d_hid[m] = grad
        inner[m, x, y, c] = grad.astype(BF)
        for o in (3, 1, 2):
            inner_copy(m, o, 1).start()
        inner_mate(m, 0, 1).start()

    each(4, finish_hidden)
    each(4, lambda m: sum_end(m, 1))
    for item in (3, 4, 5):
        final_end(item)
        send_home(item)
    done_give(0)
    line.rs_near(9, 2)
    final_in(7)
    far(7)
    line.rs_near(10, 1)

    def attend_back(m):
        arrive(m, 1)
        d = inner[m].reshape(256, width)
        gm = dot_t(d[:, :256], g[2, 0])
        for s in range(1, blocks):
            gm = gm + dot_t(d[:, s * 256 : (s + 1) * 256], g[2, s])
        gates = gate_v[m]
        gates = jnp.where(x == 0, gates[:, 0:2], gates[:, 2:4])
        g0, g1 = gates[:, 0:1], gates[:, 1:2]
        a0, a1 = att[m, :256], att[m, 256:]
        d0, d1 = gm[:, :128], gm[:, 128:]
        l0 = jnp.sum(d0 * a0, axis=-1, keepdims=True) * g0 * (1.0 - g0)
        l1 = jnp.sum(d1 * a1, axis=-1, keepdims=True) * g1 * (1.0 - g1)
        lane = lax.broadcasted_iota(jnp.int32, (256, 128), 1)
        logits = jnp.where(lane == 2 * x, l0, 0.0) + jnp.where(lane == 2 * x + 1, l1, 0.0)
        logits = logits.astype(BF)
        dl[m] = logits
        at = pl.ds(pl.multiple_of(m * 256, 256), 256)
        dl_t[:, at] = logits.T[:16]
        mixed = jnp.concatenate([a0 * g0, a1 * g1], axis=1).astype(BF)
        prod_t[:, at] = mixed.T
        da = jnp.concatenate([d0 * g0, d1 * g1], axis=0).astype(BF)
        delta = jnp.sum(da.astype(F32) * att[m], axis=-1, keepdims=True)
        log_total = tot[m][:, :1]
        qm = q_v[m]
        att[m] = jnp.zeros((512, 128), F32)

        def block(b, unused):
            pair = kv[b, m]
            keys, values = pair[:, :128], pair[:, 128:]
            raw = dot_t(qm, keys) * scale
            lo = row_range[m][:, :1] - b * 256
            hi = row_range[m][:, 1:2] - b * 256
            column = lax.broadcasted_iota(jnp.int32, (512, 256), 1)
            allowed = (column >= jnp.concatenate([lo, lo], axis=0)) & (
                column < jnp.concatenate([hi, hi], axis=0)
            )
            p = jnp.where(allowed, jnp.exp(raw - log_total), 0.0)
            ds = (p * (dot_t(da, values) - delta)).astype(BF)
            att[m] += dot(ds, keys)
            dk = dot(ds.T, qm) * scale
            dv = dot(p.astype(BF).T, da)
            kv[b, m] = jnp.concatenate([dk, dv], axis=1).astype(BF)
            return 0

        lax.fori_loop(0, l + 1, block, 0)

    def kv_copy(b, m):
        return remote(
            kv.at[b, m], kv_land.at[b, m], d_send.at[b, m], d_recv.at[b, m], left
        )

    def kv_fire(m):
        for b in range(n - 1):
            pl.when(l == n - 1)(lambda b=b: kv_copy(b, m).start())

    def kv_step(m):
        for b in range(n - 2):

            @pl.when((l > b) & (l <= n - 2))
            def _(b=b):
                kv_copy(b, m).wait_recv()
                kv[b, m] = (kv[b, m].astype(F32) + kv_land[b, m].astype(F32)).astype(BF)
                kv_copy(b, m).start()

    def normal_back(u, d_rot, gain, cosine, sine):
        d = d_rot * cosine - pltpu.roll(d_rot, 64, 1) * sine
        r = lax.rsqrt(jnp.mean(u * u, axis=-1, keepdims=True) + EPS)
        normal = u * r
        e = d * gain
        grad = r * (e - normal * jnp.mean(e * normal, axis=-1, keepdims=True))
        return grad.astype(BF), jnp.sum(d * normal, axis=0, keepdims=True)

    gains = small[8:10, :128].astype(F32)

    def query_back(m):
        for h in range(2):
            cols = slice(h * 128, (h + 1) * 128)
            grad, total = normal_back(
                qp[m][:, cols],
                att[m, h * 256 : (h + 1) * 256] * scale,
                gains[0:1],
                cos_ref[m],
                sin_ref[m],
            )
            d_low[0, pl.ds(pl.multiple_of(m * 256, 256), 256), cols] = grad
            head_sum[0:1, :128] += total

    pass_on(0, 1)
    for m in range(4):
        if m < 3:
            pass_on(m + 1, 1)
        if m == 2:
            each(4, lambda m: mate_copy(m, 2).start())
        attend_back(m)
        kv_fire(m)
        if m == 0:
            line.rs_near(10, 2)
    each(4, lambda m: to_chips(m, 2))
    final_in(8)
    far(8)
    line.rs_near(11, 1)
    for item in (6, 7, 8):
        final_end(item)
        send_home(item)
    done_give(1)
    done_take(0)
    far(9)
    for item in (3, 4, 5):
        way, item, kind, j = backward(item)
        way.end(item, kind, j)
        line.rs_end(item)
    each(4, query_back)
    normed_back_copy.wait()

    def output_weights(s, unused):
        z = inner[:, :, :, :, :, pl.ds(pl.multiple_of(s * 256, 256), 256)].reshape(1024, 256)
        g[5, s] = dot(prod_t[...], z).astype(BF)
        return 0

    def query_weights(s, unused):
        g[3, s] = dot(normed_t[s], d_low[0]).astype(BF)
        sums[1, s] = dot_t(dl_t[...], normed_t[s])[:8]
        return 0

    lax.fori_loop(0, blocks, output_weights, 0)
    line.rs_fire(2)
    lax.fori_loop(0, blocks, query_weights, 0)
    line.rs_fire(0)
    for m in range(4):
        kv_step(m)
    line.rs_near(11, 2)
    line.rs_near(2, 1)
    line.rs_near(0, 1)
    far(10)

    def home(i, m, own, out):
        mine = out.at[m, k]
        there = out.at[m, (1 - y) * 2 + c]
        keep = pltpu.make_async_copy(own.at[m], mine, h_loc.at[i, m])
        over = remote(own.at[m], mine, h_send.at[i, m, 0], h_recv.at[i, m, 0], group.chip(2))
        beside = remote(own.at[m], mine, h_send.at[i, m, 1], h_recv.at[i, m, 1], mate)
        on = remote(there, there, h_send.at[i, m, 2], h_recv.at[i, m, 2], mate)
        return keep, over, beside, on

    homes = ((own_z, res_out), (own_x, grad_out))

    def home_start(i, m):
        for copy in home(i, m, *homes[i])[:3]:
            copy.start()

    def home_on(i, m):
        keep, over, beside, on = home(i, m, *homes[i])
        over.wait_recv()
        on.start()

    def home_end(i, m):
        keep, over, beside, on = home(i, m, *homes[i])
        keep.wait()
        over.wait_send()
        beside.wait()
        on.wait()

    def finish_out(m):
        own_z[m] = (hidden[m] + total_of(m, 2)).astype(BF)
        home_start(0, m)

    each(4, finish_out)
    each(4, lambda m: sum_end(m, 2))

    def key_back(m):
        pl.when(l <= n - 2)(lambda: kv_copy(l, m).wait_recv())
        pair = kv[l, m].astype(F32)
        pair = pair + jnp.where(l <= n - 2, kv_land[l, m].astype(F32), 0.0)
        grad, total = normal_back(kp[m], pair[:, :128], gains[1:2], cos_ref[m], sin_ref[m])
        at = pl.ds(pl.multiple_of(m * 256, 256), 256)
        d_low[1, at, :128] = grad
        d_low[1, at, 128:] = pair[:, 128:].astype(BF)
        head_sum[0:1, 128:] += total

    each(4, key_back)

    def key_weights(s, unused):
        g[4, s] = dot(normed_t[s], d_low[1]).astype(BF)
        return 0

    lax.fori_loop(0, blocks, key_weights, 0)
    line.rs_fire(1)

    def normed_back(m):
        at = pl.ds(pl.multiple_of(m * 256, 256), 256)
        a, b, e = d_low[0, at], d_low[1, at], dl[m][:, :16]
        for s in range(blocks):
            part = dot_t(a, g[0, s]) + dot_t(b, g[1, s]) + dot(e, small_g[0, s])
            normed[m, :, :, :, :, s * 256 : (s + 1) * 256] = part.astype(BF).reshape(
                2, 2, 2, 32, 256
            )
        mate_copy(m, 3).start()

    each(4, normed_back)
    far(11)
    for s in range(blocks):
        sums[0, s, 0:1] = gain_sum[1:2, s * 256 : (s + 1) * 256]
        sums[0, s, 1:2] = head_sum[0:1]
        sums[0, s, 2:8] = jnp.zeros((6, 256), F32)
    small_c = remote(sums.at[0], sum_c, u_send.at[0], u_recv.at[0], mate)
    small_x = remote(sums, sum_x, u_send.at[1], u_recv.at[1], group.chip(1))
    small_y = remote(sums.at[0], sum_y, u_send.at[2], u_recv.at[2], group.chip(2))
    small_c.start()
    each(4, lambda m: to_chips(m, 3))
    small_c.wait()
    sums[0] = sums[0] + sum_c[...]
    done_take(1)
    line.rs_far(2, 2)
    line.rs_near(2, 2)
    for item in (9, 10, 11):
        line.rs_final(item)
    line.rs_far(0, 2)
    line.rs_near(1, 1)

    def small_line(d):
        to = lax.rem(l + d, n)
        return remote(
            sums.at[:, pl.ds(2 * to, 2)],
            sum_l.at[l],
            u_send.at[2 + d],
            u_recv.at[2 + d],
            device(to, x, y, c),
        )

    def finish_grad(m):
        total = total_of(m, 3)
        v = own_x[m].astype(F32)
        r = lax.rsqrt(jnp.mean(v * v, axis=-1, keepdims=True) + EPS)
        normal = v * r
        gain_sum[0:1] += jnp.sum(total * normal, axis=0, keepdims=True)
        e = total * gain_row[0:1, :]
        own_x[m] = (
            d_hid[m] + r * (e - normal * jnp.mean(e * normal, axis=-1, keepdims=True))
        ).astype(BF)
        home_start(1, m)

    each(4, finish_grad)
    for s in range(blocks):
        late[s : s + 1] = gain_sum[0:1, s * 256 : (s + 1) * 256]
    late_c = remote(late, late_core, u_send.at[6], u_recv.at[6], mate)
    late_c.start()
    small_x.start()
    each(4, lambda m: home_on(0, m))
    for item in (9, 10, 11):
        send_home(item)
    line.rs_near(0, 2)
    line.rs_far(1, 2)
    line.rs_far(2, 1)
    late_c.wait()
    late[...] = late[...] + late_core[...]
    late_s = [
        remote(
            late, late_chip.at[x * 2 + y], u_send.at[6 + o], u_recv.at[6 + o], group.chip(o)
        )
        for o in (1, 2, 3)
    ]
    for copy in late_s:
        copy.start()
    late_chip[x * 2 + y] = late[...]
    small_x.wait()
    sums[...] = sums[...] + sum_x[...]
    small_y.start()
    each(4, lambda m: home_on(1, m))
    for copy in late_s:
        copy.wait()
    late[...] = late_chip[0] + late_chip[1] + late_chip[2] + late_chip[3]

    def late_line(d):
        to = lax.rem(l + d, n)
        return remote(
            late, late_l.at[l], u_send.at[9 + d], u_recv.at[9 + d], device(to, x, y, c)
        )

    for d in range(1, n):
        late_line(d).start()
    late_l[l] = late[...]
    small_y.wait()
    sums[0] = sums[0] + sum_y[...]
    for d in range(1, n):
        small_line(d).start()
    sum_l[l] = sums[:, pl.ds(2 * l, 2)]
    line.rs_near(1, 2)
    line.rs_far(0, 1)
    line.rs_final(2)
    send_home(2)
    line.rs_far(1, 1)
    line.rs_final(0)
    send_home(0)
    for d in range(1, n):
        small_line(d).wait()
    total = sum_l[0, :, x]
    for i in range(1, n):
        total = total + sum_l[i, :, x]
    sums_out[...] = total
    for d in range(1, n):
        late_line(d).wait()
    total = late_l[0]
    for i in range(1, n):
        total = total + late_l[i]
    late_out[...] = total
    line.rs_final(1)
    send_home(1)
    for item in (6, 7, 8, 9, 10, 11, 2, 0, 1):
        way, item, kind, j = backward(item)
        way.end(item, kind, j)
        line.rs_end(item)
    z_out.wait_send()
    z_on.wait_send()
    tiny.ag_end(0)
    each(3, line.ag_end)

    def drain(m):
        sum_end(m, 3)
        spread_end(m, 1)
        home_end(0, m)
        home_end(1, m)
        for b in range(n - 1):
            pl.when(l > b)(lambda b=b: kv_copy(b, m).wait_send())

    each(4, drain)


def layer(n, x_in, z_in, wq, wk, wv, wo, wg, wu, wd, small, sizes, lengths):
    d = x_in.shape[-1]
    m = 2 * n
    bf = lambda *shape: jax.ShapeDtypeStruct(shape, BF)
    vb = lambda *shape: pltpu.VMEM(shape, BF)
    vf = lambda *shape: pltpu.VMEM(shape, F32)
    return pl.pallas_call(
        functools.partial(layer_kernel, n),
        out_shape=(
            bf(4, 4, 32, d),
            bf(4, 4, 32, d),
            bf(256, 512),
            bf(256, 256),
            bf(256, 256),
            bf(512, 256),
            bf(256, 1536),
            bf(256, 1536),
            bf(1536, 256),
            jax.ShapeDtypeStruct((2, 8, 256), F32),
            jax.ShapeDtypeStruct((m, 256), F32),
            bf(m, 256, 1024),
            bf(4, 4, 32, d),
        ),
        in_specs=[ANY] * 9 + [VM] + [pl.BlockSpec(memory_space=pltpu.SMEM)] * 2,
        out_specs=(ANY,) * 9 + (VM,) * 2 + (ANY,) * 2,
        scratch_shapes=[
            vb(4, 2, 4, 32, d),
            vb(4, 2, 2, 2, 32, d),
            vb(m, 256, 1024),
            vb(12, m, 256, 256),
            vb(1, m, 16, 256),
            vf(2, d),
            vb(16, d),
            vb(n, 4, 256, 256),
            vb(4, 512, 128),
            vf(4, 256, 256),
            vf(4, 256, 128),
            vf(4, 256, 16),
            vf(4, 512, 128),
            vf(4, 512, 128),
            vb(4, 2, 2, 2, 32, d),
            vb(4, 2, 2, 32, d),
            vb(4, 2, 2, 32, d),
            vb(3, 4, 32, d),
            vb(4, 2, 2, 2, 32, d),
            vf(4, 32, d),
            vb(6, m + 2, 256, 256),
            vb(2, 1024, 256),
            vb(256, 1024),
            vb(n, 4, 256, 256),
            vf(4, 32, d),
            vb(4, 32, d),
            vb(4, 32, d),
            vb(4, 256, 128),
            vb(16, 1024),
            vf(2, d),
            vf(1, 256),
            vf(2, m, 8, 256),
            vf(m, 8, 256),
            vf(2, m, 8, 256),
            vf(m, 8, 256),
            vf(n, 2, 2, 8, 256),
            vf(m, 256),
            vf(m, 256),
            vf(4, m, 256),
            vf(n, m, 256),
            vf(4, 256, 128),
            vf(4, 256, 128),
            pltpu.VMEM((4, 256, 128), jnp.int32),
            pltpu.SemaphoreType.REGULAR((3,)),
            pltpu.SemaphoreType.REGULAR((2,)),
            DMA((24,)),
            DMA((24,)),
            DMA((24,)),
            DMA((12, 2, n)),
            DMA((12, n)),
            DMA((3,)),
            DMA((1, 2, n)),
            DMA((1, n)),
            DMA((3,)),
            DMA((2,)),
            DMA((4,)),
            DMA((2,)),
            DMA((n, 4)),
            DMA((n, 4)),
            DMA((4, 4)),
            DMA((4, 4)),
            DMA((4, 4, 3)),
            DMA((4, 4, 3)),
            DMA((2, 4, 3)),
            DMA((2, 4, 3)),
            DMA((2, 4, 4)),
            DMA((2, 4, 4)),
            DMA((12, 2, n)),
            DMA((12, n + 1)),
            DMA((24,)),
            DMA((24,)),
            DMA((24,)),
            DMA((n, 4)),
            DMA((n, 4)),
            DMA((2, 4, 3)),
            DMA((2, 4, 3)),
            DMA((2, 4)),
            DMA((9 + n,)),
            DMA((9 + n,)),
            DMA((16,)),
        ],
        compiler_params=pltpu.CompilerParams(
            collective_id=0, has_side_effects=True, vmem_limit_bytes=63 * 2**20
        ),
        name="layer",
    )(x_in, z_in, wq, wk, wv, wo, wg, wu, wd, small, sizes, lengths)

class Group:
    def __init__(self):
        self.l, self.x, self.y, self.c = place()
        self.mate = device(self.l, self.x, self.y, 1 - self.c)

    def other(self, i):
        x = 1 - self.x if i & 1 else self.x
        y = 1 - self.y if i & 2 else self.y
        return x, y

    def chip(self, i):
        x, y = self.other(i)
        return device(self.l, x, y, self.c)

    def partners(self):
        return [(self.mate, None)] + [(self.chip(i), None) for i in (1, 2, 3)]


def fast_local(
    inputs,
    cotangent,
    bucket_sizes,
    true_lengths,
    attention_gain,
    feedforward_gain,
    query_gain,
    key_gain,
    query_weight,
    key_matrix,
    value_matrix,
    headgate_weight,
    output_weight,
    gate_weight,
    up_weight,
    down_weight,
):
    batches, rows, width = inputs.shape
    n = lax.axis_size("seq") // 2
    seq, kv = lax.axis_index("seq"), lax.axis_index("kv")
    l, x = seq // 2, seq % 2
    scale = HEAD_SIZE ** (-0.5)
    span = 2 * rows
    gain_query = query_gain.astype(F32)
    gain_key = key_gain.astype(F32)

    own_small = jnp.concatenate(
        [
            headgate_weight.T,
            attention_gain[None],
            feedforward_gain[None],
            jnp.zeros((2, 256), BF),
            jnp.pad(jnp.stack([query_gain, key_gain]), ((0, 0), (0, 128))),
            jnp.zeros((6, 256), BF),
        ],
        axis=0,
    )
    x_split = inputs.reshape(batches, 4, 32, width)
    z_split = cotangent.reshape(batches, 4, 32, width)
    own_out, own_grad, dq, dk, dv, do, d_gate, d_up, d_down, sums, late, unused, unused = layer(
        n,
        x_split,
        z_split,
        query_weight,
        key_matrix,
        value_matrix,
        output_weight,
        gate_weight,
        up_weight,
        down_weight,
        own_small,
        bucket_sizes,
        true_lengths,
    )
    return (
        own_out.reshape(batches, rows, width),
        own_grad.reshape(batches, rows, width),
        lax.dynamic_index_in_dim(late, seq, 0, keepdims=False),
        sums[0, 0],
        sums[0, 1, :HEAD_SIZE],
        sums[0, 1, HEAD_SIZE:],
        dq.astype(F32),
        dk.astype(F32),
        dv.astype(F32),
        sums[1, :4].T,
        do.astype(F32),
        d_gate.astype(F32),
        d_up.astype(F32),
        d_down.astype(F32),
    )


def solution(mesh):
    chosen = fast_local if dict(mesh.shape) == {"seq": 8, "kv": 4} else local
    in_specs = (
        P(None, "seq", None),
        P(None, "seq", None),
        P(),
        P(),
        P("seq"),
        P("seq"),
        P(),
        P(),
        P("seq", "kv"),
        P("seq", "kv"),
        P("seq", "kv"),
        P("seq", "kv"),
        P("kv", "seq"),
        P("seq", "kv"),
        P("seq", "kv"),
        P("kv", "seq"),
    )
    out_specs = (
        P(None, "seq", None),
        P(None, "seq", None),
        P("seq"),
        P("seq"),
        P(),
        P(),
        P("seq", "kv"),
        P("seq", "kv"),
        P("seq", "kv"),
        P("seq", "kv"),
        P("kv", "seq"),
        P("seq", "kv"),
        P("seq", "kv"),
        P("kv", "seq"),
    )
    return jax.shard_map(chosen, mesh=mesh, in_specs=in_specs, out_specs=out_specs, check_vma=False)
```

```python
import functools
import math

import jax
import jax.numpy as jnp
from jax import lax
from jax.experimental import pallas as pl
from jax.experimental.pallas import tpu as pltpu
from jax.sharding import PartitionSpec as P

HEAD_SIZE = 128


EPS = 1e-06
ROPE_BASE = 1000000.0
MASKED = -1e30


def rms_scale(values):
    return lax.rsqrt(jnp.mean(values * values, axis=-1, keepdims=True) + EPS)


def norm_backward(grad, normal, factor):
    return factor * (grad - normal * jnp.mean(grad * normal, axis=-1, keepdims=True))


def rope_tables(positions, width):
    half = width // 2
    steps = jnp.arange(half, dtype=jnp.float32) * (2.0 / width)
    inverse = jnp.exp(-steps * math.log(ROPE_BASE))
    angles = positions.astype(jnp.float32)[:, None] * inverse[None, :]
    cosine = jnp.cos(angles)
    sine = jnp.sin(angles)
    return (jnp.concatenate([cosine, cosine], axis=-1), jnp.concatenate([sine, sine], axis=-1))


def rotate_forward(values, cosine, sine):
    half = values.shape[-1] // 2
    turned = jnp.concatenate([-values[..., half:], values[..., :half]], axis=-1)
    return values * cosine[:, None, :] + turned * sine[:, None, :]


def rotate_backward(grad, cosine, sine):
    half = grad.shape[-1] // 2
    moved = grad * sine[:, None, :]
    return grad * cosine[:, None, :] + jnp.concatenate(
        [moved[..., half:], -moved[..., :half]], axis=-1
    )


def token_layout(index, buckets, lengths):
    ends = jnp.cumsum(buckets)
    starts = ends - buckets
    member = (index[:, None] >= starts[None, :]) & (index[:, None] < ends[None, :])
    labels = jnp.arange(buckets.shape[0], dtype=jnp.int32)
    segment = jnp.sum(jnp.where(member, labels[None, :], 0), axis=1)
    position = index - jnp.sum(jnp.where(member, starts[None, :], 0), axis=1)
    limit = jnp.sum(jnp.where(member, lengths[None, :], 0), axis=1)
    return (segment, position, position < limit)


def outer_sum(left, right):
    return lax.dot_general(
        left, right, (((0,), (0,)), ((), ())), preferred_element_type=jnp.float32
    )


def times_transpose(left, weight):
    return lax.dot_general(
        left, weight, (((1,), (1,)), ((), ())), preferred_element_type=jnp.float32
    )


def block_scores(query_kg, key_block, start, row_index, row_segment, buckets, lengths, scale):
    key_index = start + jnp.arange(key_block.shape[0], dtype=jnp.int32)
    key_segment, key_position, key_valid = token_layout(key_index, buckets, lengths)
    allowed = (
        (row_segment[:, None] == key_segment[None, :])
        & (key_index[None, :] <= row_index[:, None])
        & key_valid[None, :]
    )
    raw = (
        jnp.einsum("kgtd,skd->kgts", query_kg, key_block, preferred_element_type=jnp.float32)
        * scale
    )
    return (jnp.where(allowed, raw, MASKED), allowed)


def split_blocks(keys, values, block):
    blocks = keys.shape[0] // block
    key_blocks = keys.reshape(blocks, block, keys.shape[1], keys.shape[2])
    value_blocks = values.reshape(blocks, block, values.shape[1], values.shape[2])
    starts = jnp.arange(blocks) * block
    return (key_blocks, value_blocks, starts)


def attention_forward(
    query_kg, keys, values, row_index, row_segment, buckets, lengths, block, scale
):
    key_blocks, value_blocks, starts = split_blocks(keys, values, block)

    def first_pass(carry, item):
        running_max, total = carry
        key_block, start = item
        masked, allowed = block_scores(
            query_kg, key_block, start, row_index, row_segment, buckets, lengths, scale
        )
        new_max = jnp.maximum(running_max, jnp.max(masked, axis=-1))
        total = total * jnp.exp(running_max - new_max) + jnp.sum(
            jnp.where(allowed, jnp.exp(masked - new_max[..., None]), 0.0), axis=-1
        )
        return ((new_max, total), None)

    begin = (
        jnp.full(query_kg.shape[:3], MASKED, jnp.float32),
        jnp.zeros(query_kg.shape[:3], jnp.float32),
    )
    (running_max, total), unused = lax.scan(first_pass, begin, (key_blocks, starts))
    log_total = running_max + jnp.log(total)

    def second_pass(accumulated, item):
        key_block, value_block, start = item
        masked, allowed = block_scores(
            query_kg, key_block, start, row_index, row_segment, buckets, lengths, scale
        )
        weights = jnp.where(allowed, jnp.exp(masked - log_total[..., None]), 0.0).astype(
            jnp.bfloat16
        )
        return (
            accumulated
            + jnp.einsum(
                "kgts,skd->kgtd", weights, value_block, preferred_element_type=jnp.float32
            ),
            None,
        )

    attended, unused = lax.scan(
        second_pass, jnp.zeros(query_kg.shape, jnp.float32), (key_blocks, value_blocks, starts)
    )
    return (attended, log_total)


def attention_backward(
    query_kg,
    grad_kg,
    log_total,
    delta,
    keys,
    values,
    row_index,
    row_segment,
    buckets,
    lengths,
    block,
    scale,
):
    key_blocks, value_blocks, starts = split_blocks(keys, values, block)

    def step(grad_query, item):
        key_block, value_block, start = item
        masked, allowed = block_scores(
            query_kg, key_block, start, row_index, row_segment, buckets, lengths, scale
        )
        weights = jnp.where(allowed, jnp.exp(masked - log_total[..., None]), 0.0)
        grad_weights = jnp.einsum(
            "kgtd,skd->kgts", grad_kg, value_block, preferred_element_type=jnp.float32
        )
        grad_scores = (weights * (grad_weights - delta[..., None])).astype(jnp.bfloat16)
        grad_query = grad_query + scale * jnp.einsum(
            "kgts,skd->kgtd", grad_scores, key_block, preferred_element_type=jnp.float32
        )
        grad_key = scale * jnp.einsum(
            "kgts,kgtd->skd", grad_scores, query_kg, preferred_element_type=jnp.float32
        )
        grad_value = jnp.einsum(
            "kgts,kgtd->skd",
            weights.astype(jnp.bfloat16),
            grad_kg,
            preferred_element_type=jnp.float32,
        )
        return (grad_query, (grad_key, grad_value))

    grad_query, (grad_keys, grad_values) = lax.scan(
        step, jnp.zeros(query_kg.shape, jnp.float32), (key_blocks, value_blocks, starts)
    )
    return (grad_query, grad_keys.reshape(keys.shape), grad_values.reshape(values.shape))


def local(
    inputs,
    cotangent,
    bucket_sizes,
    true_lengths,
    attention_gain,
    feedforward_gain,
    query_gain,
    key_gain,
    query_weight,
    key_matrix,
    value_matrix,
    headgate_weight,
    output_weight,
    gate_weight,
    up_weight,
    down_weight,
):
    batches, rows, width = inputs.shape
    seq_count = lax.axis_size("seq")
    block = math.gcd(rows * seq_count, 512)
    local_heads = query_weight.shape[1] // HEAD_SIZE
    local_groups = key_matrix.shape[1] // HEAD_SIZE
    group = local_heads // local_groups
    scale = HEAD_SIZE ** (-0.5)
    row_index = lax.axis_index("seq") * rows + jnp.arange(rows, dtype=jnp.int32)
    gain_query = query_gain.astype(jnp.float32)
    gain_key = key_gain.astype(jnp.float32)
    sum_attention_gain = jnp.zeros((width,), jnp.float32)
    sum_feedforward_gain = jnp.zeros((width,), jnp.float32)
    sum_query = jnp.zeros((width, query_weight.shape[1]), jnp.float32)
    sum_key = jnp.zeros((width, key_matrix.shape[1]), jnp.float32)
    sum_value = jnp.zeros((width, value_matrix.shape[1]), jnp.float32)
    sum_headgate = jnp.zeros((width, headgate_weight.shape[1]), jnp.float32)
    sum_output = jnp.zeros((output_weight.shape[0], width), jnp.float32)
    sum_gate = jnp.zeros((width, gate_weight.shape[1]), jnp.float32)
    sum_upward = jnp.zeros((width, up_weight.shape[1]), jnp.float32)
    sum_down = jnp.zeros((down_weight.shape[0], width), jnp.float32)
    sum_query_gain = jnp.zeros((HEAD_SIZE,), jnp.float32)
    sum_key_gain = jnp.zeros((HEAD_SIZE,), jnp.float32)
    results = []
    input_grads = []
    for batch in range(batches):
        gathered = (
            lax.all_gather(attention_gain, "seq", axis=0, tiled=True),
            lax.all_gather(feedforward_gain, "seq", axis=0, tiled=True),
            lax.all_gather(query_weight, "seq", axis=0, tiled=True),
            lax.all_gather(key_matrix, "seq", axis=0, tiled=True),
            lax.all_gather(value_matrix, "seq", axis=0, tiled=True),
            lax.all_gather(headgate_weight, "seq", axis=0, tiled=True),
            lax.all_gather(output_weight, "seq", axis=1, tiled=True),
            lax.all_gather(gate_weight, "seq", axis=0, tiled=True),
            lax.all_gather(up_weight, "seq", axis=0, tiled=True),
            lax.all_gather(down_weight, "seq", axis=1, tiled=True),
        )
        (
            gain_a,
            gain_f,
            w_query,
            key_projection_weight,
            value_projection_weight,
            w_head,
            w_output,
            w_gate,
            w_up,
            w_down,
        ) = gathered
        gain_a = gain_a.astype(jnp.float32)
        gain_f = gain_f.astype(jnp.float32)
        buckets = bucket_sizes[batch]
        lengths = true_lengths[batch]
        row_segment, row_position, row_valid = token_layout(row_index, buckets, lengths)
        cosine, sine = rope_tables(row_position, HEAD_SIZE)
        current = inputs[batch].astype(jnp.float32)
        scale_a = rms_scale(current)
        normal_a = current * scale_a
        normed_input = (normal_a * gain_a).astype(jnp.bfloat16)
        query_proj = jnp.dot(normed_input, w_query, preferred_element_type=jnp.float32).reshape(
            rows, local_heads, HEAD_SIZE
        )
        key_proj = jnp.dot(
            normed_input, key_projection_weight, preferred_element_type=jnp.float32
        ).reshape(rows, local_groups, HEAD_SIZE)
        value_proj = jnp.dot(
            normed_input, value_projection_weight, preferred_element_type=jnp.float32
        )
        query_scale = rms_scale(query_proj)
        query_normal = query_proj * query_scale
        key_scale = rms_scale(key_proj)
        key_normal = key_proj * key_scale
        query_rot = rotate_forward(query_normal * gain_query, cosine, sine).astype(jnp.bfloat16)
        key_rot = rotate_forward(key_normal * gain_key, cosine, sine).astype(jnp.bfloat16)
        value_low = value_proj.astype(jnp.bfloat16).reshape(rows, local_groups, HEAD_SIZE)
        logits = jnp.dot(normed_input, w_head, preferred_element_type=jnp.float32)
        gate = jax.nn.sigmoid(logits)
        all_keys, all_values = (
            lax.all_gather(key_rot, "seq", axis=0, tiled=True),
            lax.all_gather(value_low, "seq", axis=0, tiled=True),
        )
        query_kg = query_rot.reshape(rows, local_groups, group, HEAD_SIZE).transpose(1, 2, 0, 3)
        attended_kg, log_total = attention_forward(
            query_kg, all_keys, all_values, row_index, row_segment, buckets, lengths, block, scale
        )
        attended = attended_kg.transpose(2, 0, 1, 3).reshape(rows, local_heads, HEAD_SIZE)
        mixed = (
            (attended * gate[:, :, None])
            .astype(jnp.bfloat16)
            .reshape(rows, local_heads * HEAD_SIZE)
        )
        hidden = current + lax.psum(
            jnp.dot(mixed, w_output, preferred_element_type=jnp.float32).astype(jnp.bfloat16), "kv"
        ).astype(jnp.float32)
        scale_f = rms_scale(hidden)
        normal_f = hidden * scale_f
        inner = (normal_f * gain_f).astype(jnp.bfloat16)
        gated = jnp.dot(inner, w_gate, preferred_element_type=jnp.float32)
        upward = jnp.dot(inner, w_up, preferred_element_type=jnp.float32)
        sigma = jax.nn.sigmoid(gated)
        swish = gated * sigma
        product = (swish * upward).astype(jnp.bfloat16)
        output = hidden + lax.psum(
            jnp.dot(product, w_down, preferred_element_type=jnp.float32).astype(jnp.bfloat16), "kv"
        ).astype(jnp.float32)
        results.append(output.astype(jnp.bfloat16))
        grad_out = cotangent[batch].astype(jnp.float32)
        grad_low = grad_out.astype(jnp.bfloat16)
        sum_down = sum_down + outer_sum(product, grad_low)
        grad_product = times_transpose(grad_low, w_down)
        grad_gated = (grad_product * upward * sigma * (1.0 + gated * (1.0 - sigma))).astype(
            jnp.bfloat16
        )
        grad_upward = (grad_product * swish).astype(jnp.bfloat16)
        sum_gate = sum_gate + outer_sum(inner, grad_gated)
        sum_upward = sum_upward + outer_sum(inner, grad_upward)
        grad_inner = lax.psum(
            (times_transpose(grad_gated, w_gate) + times_transpose(grad_upward, w_up)).astype(
                jnp.bfloat16
            ),
            "kv",
        ).astype(jnp.float32)
        sum_feedforward_gain = sum_feedforward_gain + jnp.sum(grad_inner * normal_f, axis=0)
        grad_hidden = grad_out + norm_backward(grad_inner * gain_f, normal_f, scale_f)
        grad_branch = grad_hidden.astype(jnp.bfloat16)
        sum_output = sum_output + outer_sum(mixed, grad_branch)
        grad_mixed = times_transpose(grad_branch, w_output).reshape(rows, local_heads, HEAD_SIZE)
        grad_heads = (grad_mixed * gate[:, :, None]).astype(jnp.bfloat16)
        grad_logits = (jnp.sum(grad_mixed * attended, axis=-1) * gate * (1.0 - gate)).astype(
            jnp.bfloat16
        )
        back_keys = lax.all_gather(key_rot, "seq", axis=0, tiled=True)
        back_values = lax.all_gather(value_low, "seq", axis=0, tiled=True)
        grad_kg = grad_heads.reshape(rows, local_groups, group, HEAD_SIZE).transpose(1, 2, 0, 3)
        delta = jnp.sum(grad_kg.astype(jnp.float32) * attended_kg, axis=-1)
        grad_query_kg, grad_keys, grad_values = attention_backward(
            query_kg,
            grad_kg,
            log_total,
            delta,
            back_keys,
            back_values,
            row_index,
            row_segment,
            buckets,
            lengths,
            block,
            scale,
        )
        local_keys, local_values = (
            lax.psum_scatter(
                grad_keys.astype(jnp.bfloat16), "seq", scatter_dimension=0, tiled=True
            ).astype(jnp.float32),
            lax.psum_scatter(
                grad_values.astype(jnp.bfloat16), "seq", scatter_dimension=0, tiled=True
            ).astype(jnp.float32),
        )
        grad_query_rot = grad_query_kg.transpose(2, 0, 1, 3).reshape(rows, local_heads, HEAD_SIZE)
        grad_query_norm = rotate_backward(grad_query_rot, cosine, sine)
        sum_query_gain = sum_query_gain + jnp.sum(grad_query_norm * query_normal, axis=(0, 1))
        grad_query = (
            norm_backward(grad_query_norm * gain_query, query_normal, query_scale)
            .astype(jnp.bfloat16)
            .reshape(rows, local_heads * HEAD_SIZE)
        )
        grad_key_norm = rotate_backward(local_keys, cosine, sine)
        sum_key_gain = sum_key_gain + jnp.sum(grad_key_norm * key_normal, axis=(0, 1))
        grad_key = (
            norm_backward(grad_key_norm * gain_key, key_normal, key_scale)
            .astype(jnp.bfloat16)
            .reshape(rows, local_groups * HEAD_SIZE)
        )
        grad_value = local_values.astype(jnp.bfloat16).reshape(rows, local_groups * HEAD_SIZE)
        sum_query = sum_query + outer_sum(normed_input, grad_query)
        sum_key = sum_key + outer_sum(normed_input, grad_key)
        sum_value = sum_value + outer_sum(normed_input, grad_value)
        sum_headgate = sum_headgate + outer_sum(normed_input, grad_logits)
        grad_partial = (
            times_transpose(grad_query, w_query)
            + times_transpose(grad_key, key_projection_weight)
            + times_transpose(grad_value, value_projection_weight)
            + times_transpose(grad_logits, w_head)
        )
        grad_normed = lax.psum(grad_partial.astype(jnp.bfloat16), "kv").astype(jnp.float32)
        sum_attention_gain = sum_attention_gain + jnp.sum(grad_normed * normal_a, axis=0)
        grad_input = grad_hidden + norm_backward(grad_normed * gain_a, normal_a, scale_a)
        input_grads.append(grad_input.astype(jnp.bfloat16))
    (
        attention_total,
        feedforward_total,
        query_total,
        key_total,
        value_total,
        headgate_total,
        output_total,
        gate_total,
        upward_total,
        down_total,
    ) = (
        lax.psum_scatter(
            sum_attention_gain.astype(jnp.bfloat16), "seq", scatter_dimension=0, tiled=True
        ).astype(jnp.float32),
        lax.psum_scatter(
            sum_feedforward_gain.astype(jnp.bfloat16), "seq", scatter_dimension=0, tiled=True
        ).astype(jnp.float32),
        lax.psum_scatter(
            sum_query.astype(jnp.bfloat16), "seq", scatter_dimension=0, tiled=True
        ).astype(jnp.float32),
        lax.psum_scatter(
            sum_key.astype(jnp.bfloat16), "seq", scatter_dimension=0, tiled=True
        ).astype(jnp.float32),
        lax.psum_scatter(
            sum_value.astype(jnp.bfloat16), "seq", scatter_dimension=0, tiled=True
        ).astype(jnp.float32),
        lax.psum_scatter(
            sum_headgate.astype(jnp.bfloat16), "seq", scatter_dimension=0, tiled=True
        ).astype(jnp.float32),
        lax.psum_scatter(
            sum_output.astype(jnp.bfloat16), "seq", scatter_dimension=1, tiled=True
        ).astype(jnp.float32),
        lax.psum_scatter(
            sum_gate.astype(jnp.bfloat16), "seq", scatter_dimension=0, tiled=True
        ).astype(jnp.float32),
        lax.psum_scatter(
            sum_upward.astype(jnp.bfloat16), "seq", scatter_dimension=0, tiled=True
        ).astype(jnp.float32),
        lax.psum_scatter(
            sum_down.astype(jnp.bfloat16), "seq", scatter_dimension=1, tiled=True
        ).astype(jnp.float32),
    )
    query_gain_total, key_gain_total = lax.psum((sum_query_gain, sum_key_gain), ("seq", "kv"))
    return (
        jnp.stack(results, axis=0),
        jnp.stack(input_grads, axis=0),
        attention_total,
        feedforward_total,
        query_gain_total,
        key_gain_total,
        query_total,
        key_total,
        value_total,
        headgate_total,
        output_total,
        gate_total,
        upward_total,
        down_total,
    )


BF = jnp.bfloat16
F32 = jnp.float32
ANY = pl.BlockSpec(memory_space=pl.ANY)
VM = pl.BlockSpec(memory_space=pltpu.VMEM)
DMA = pltpu.SemaphoreType.DMA


def place():
    s = lax.axis_index("seq")
    k = lax.axis_index("kv")
    return (lax.div(s, 2), lax.rem(s, 2), lax.div(k, 2), lax.rem(k, 2))


def device(l, x, y, c):
    return (l * 2 + x, y * 2 + c)


def remote(src, dst, send, recv, target):
    return pltpu.make_async_remote_copy(
        src_ref=src,
        dst_ref=dst,
        send_sem=send,
        recv_sem=recv,
        device_id=target,
        device_id_type=pl.DeviceIdType.MESH,
    )


def greet(partners):
    barrier = pltpu.get_barrier_semaphore()
    count = 0
    for target, there in partners:

        def call(target=target):
            pl.semaphore_signal(
                barrier, inc=1, device_id=target, device_id_type=pl.DeviceIdType.MESH
            )

        if there is None:
            call()
            count = count + 1
        else:
            pl.when(there)(call)
            count = count + jnp.where(there, 1, 0)
    pl.semaphore_wait(barrier, count)


class Line:
    def __init__(self, length, g, ag_send, ag_recv, land=None, rs_send=None, rs_recv=None):
        self.n = length
        self.g, self.ag_send, self.ag_recv = g, ag_send, ag_recv
        self.land, self.rs_send, self.rs_recv = land, rs_send, rs_recv
        self.l, self.x, self.y, self.c = place()

    def partners(self):
        l, x, y, c = self.l, self.x, self.y, self.c
        return [
            (device(l - 1, x, y, c), l >= 1),
            (device(l + 1, x, y, c), l <= self.n - 2),
        ]

    def block(self, item, b):
        return self.g.at[item, pl.ds(2 * b, 2)]

    def _ag(self, item, way, b):
        step = -1 if way == 0 else 1
        return remote(
            self.block(item, b),
            self.block(item, b),
            self.ag_send.at[item, way, b],
            self.ag_recv.at[item, b],
            device(self.l + step, self.x, self.y, self.c),
        )

    def ag_start(self, item):
        l = self.l
        pl.when(l >= 1)(lambda: self._ag(item, 0, l).start())
        pl.when(l <= self.n - 2)(lambda: self._ag(item, 1, l).start())

    def ag_half(self, item, x, src):
        l, n = self.l, self.n

        def half(way):
            step = -1 if way == 0 else 1
            return remote(
                src,
                self.g.at[item, 2 * l + x],
                self.ag_send.at[item, way, l],
                self.ag_recv.at[item, l],
                device(l + step, self.x, self.y, self.c),
            )

        pl.when(l >= 1)(lambda: half(0).start())
        pl.when(l <= n - 2)(lambda: half(1).start())

    def ag_left(self, item):
        pl.when(self.l >= 1)(lambda: self._ag(item, 0, self.l).start())

    def ag_right(self, item, plane):
        pl.when(self.l == plane)(lambda: self._ag(item, 1, self.l).start())

    def ag_step(self, item, t):
        l, n = self.l, self.n

        @pl.when(l + t <= n - 1)
        def _():
            self._ag(item, 0, l + t).wait_recv()
            pl.when(l >= 1)(lambda: self._ag(item, 0, l + t).start())

        @pl.when(l - t >= 0)
        def _():
            self._ag(item, 1, l - t).wait_recv()
            pl.when(l <= n - 2)(lambda: self._ag(item, 1, l - t).start())

    def pump(self, item, t):
        l, n = self.l, self.n

        @pl.when((l + t <= n - 1) & (l >= 1))
        def _():
            self._ag(item, 0, l + t).wait_recv()
            self._ag(item, 0, l + t).start()

        @pl.when((l - t >= 0) & (l <= n - 2))
        def _():
            self._ag(item, 1, l - t).wait_recv()
            self._ag(item, 1, l - t).start()

    def collect(self, item):
        l, n = self.l, self.n
        for t in range(1, n):
            pl.when(l == 0)(lambda t=t: self._ag(item, 0, t).wait_recv())
            pl.when(l == n - 1)(lambda t=t: self._ag(item, 1, n - 1 - t).wait_recv())

    def ag_end(self, item):
        l, n = self.l, self.n
        for b in range(n):
            pl.when((l >= 1) & (l <= b))(lambda b=b: self._ag(item, 0, b).wait_send())
            pl.when((l <= n - 2) & (l >= b))(lambda b=b: self._ag(item, 1, b).wait_send())

    @staticmethod
    def seat(item):
        return item + 3 if item < 3 else item

    @staticmethod
    def berth(item):
        return item + 3 if item < 3 else (item - 3) % 6

    def sum_block(self, item, b):
        return self.g.at[self.seat(item), pl.ds(2 * b, 2)]

    def _slot(self, item, slot):
        return self.land.at[self.berth(item), pl.ds(2 * slot, 2)]

    def _rs(self, item, way, o):
        if way == 0:
            target = self.l - 1
            slot = jnp.where(target == o, self.n, o)
        else:
            target = self.l + 1
            slot = o
        return remote(
            self.sum_block(item, o),
            self._slot(item, slot),
            self.rs_send.at[item, way, o],
            self.rs_recv.at[item, slot],
            device(target, self.x, self.y, self.c),
        )

    def _take(self, item, o, slot):
        here = self._slot(item, slot)
        pltpu.make_async_copy(here, here, self.rs_recv.at[item, slot]).wait()
        seat, berth = self.seat(item), self.berth(item)
        for h in range(2):
            total = self.g[seat, 2 * o + h].astype(F32) + self.land[berth, 2 * slot + h].astype(F32)
            self.g[seat, 2 * o + h] = total.astype(BF)

    def rs_fire(self, item):
        l, n = self.l, self.n
        for o in range(n - 1, 0, -1):
            pl.when(l == 0)(lambda o=o: self._rs(item, 1, o).start())
            pl.when(l == n - 1)(lambda o=o: self._rs(item, 0, n - 1 - o).start())

    def rs_near(self, item, plane):
        l, n = self.l, self.n
        way = 1 if plane == 1 else 0
        owners = range(n - 1, 1, -1) if plane == 1 else range(n - 2)

        @pl.when(l == plane)
        def _():
            for o in owners:
                self._take(item, o, o)
                self._rs(item, way, o).start()

    def rs_far(self, item, plane):
        l, n = self.l, self.n
        way, o = (0, 0) if plane == 1 else (1, n - 1)

        @pl.when(l == plane)
        def _():
            self._take(item, o, o)
            self._rs(item, way, o).start()

    def rs_final(self, item):
        l, n = self.l, self.n
        pl.when(l >= 1)(lambda: self._take(item, l, l))
        pl.when(l <= n - 2)(lambda: self._take(item, l, n))

    def rs_end(self, item):
        l, n = self.l, self.n
        for o in range(n):
            pl.when(l < o)(lambda o=o: self._rs(item, 1, o).wait_send())
            pl.when(l > o)(lambda o=o: self._rs(item, 0, o).wait_send())


def each(count, body):
    def step(i, unused):
        body(i)
        return 0

    lax.fori_loop(0, count, step, 0)


class Pair:
    def __init__(self, line, refs, send, recv, local, half):
        self.line, self.refs = line, refs
        self.send, self.recv, self.local, self.half = send, recv, local, half

    def partner(self):
        line = self.line
        return (device(line.l, 1 - line.x, line.y, line.c), None)

    def _part(self, ref, kind, j, x):
        at = pl.multiple_of(x * self.half + j * 256, 256)
        return ref.at[pl.ds(at, 256), :] if kind == 2 else ref.at[:, pl.ds(at, 256)]

    def _pieces(self, block, item, kind, j, x):
        ref = self.refs[kind]
        if not isinstance(ref, tuple):
            return [(self._part(ref, kind, j, x), block, item)]
        at = pl.ds(pl.multiple_of(x * (self.half // 2 if item == 1 else self.half) + j * 128, 128), 128)
        return [
            (one.at[:, at], block.at[:, pl.ds(128 * i, 128)], item + 12 * i)
            for i, one in enumerate(ref)
        ]

    def _copies(self, item, kind, j):
        line = self.line
        mine = line.g.at[item, 2 * line.l + line.x]
        away = self._pieces(mine, item, kind, j, 1 - line.x)
        stay = self._pieces(mine, item, kind, j, line.x)
        pairs = []
        for (src, block, sem), (own, unused, unused2) in zip(away, stay):
            out = remote(src, block, self.send.at[sem], self.recv.at[sem], self.partner()[0])
            here = pltpu.make_async_copy(own, block, self.local.at[sem])
            pairs.append((out, here))
        return pairs

    def start(self, item, kind, j):
        for out, here in self._copies(item, kind, j):
            out.start()
            here.start()

    def end(self, item, kind, j):
        for out, here in self._copies(item, kind, j):
            here.wait()
            out.wait_send()
            out.wait_recv()


class Back(Pair):
    def _copies(self, item, kind, j):
        line = self.line
        seat = line.seat(item)
        away = self._pieces(line.g.at[seat, 2 * line.l + 1 - line.x], item, kind, j, line.x)
        stay = self._pieces(line.g.at[seat, 2 * line.l + line.x], item, kind, j, line.x)
        pairs = []
        for (home, block, sem), (unused, own, unused2) in zip(away, stay):
            out = remote(block, home, self.send.at[sem], self.recv.at[sem], self.partner()[0])
            here = pltpu.make_async_copy(own, home, self.local.at[sem])
            pairs.append((out, here))
        return pairs

    def end(self, item, kind, j):
        line = self.line
        block = line.g.at[line.seat(item), 2 * line.l]
        there = self._pieces(block, item, kind, j, 1 - line.x)
        for (out, here), (home, unused, sem) in zip(self._copies(item, kind, j), there):
            here.wait()
            out.wait_send()
            pltpu.make_async_copy(home, home, self.recv.at[sem]).wait()


def dot(a, b):
    return lax.dot_general(a, b, (((1,), (0,)), ((), ())), preferred_element_type=F32)


def dot_t(a, b):
    return lax.dot_general(a, b, (((1,), (1,)), ((), ())), preferred_element_type=F32)


def layer_kernel(
    n,
    x_any,
    z_any,
    wq,
    wk,
    wv,
    wo,
    wg,
    wu,
    wd,
    small,
    sizes,
    lengths,
    res_out,
    grad_out,
    dq_out,
    dk_out,
    dv_out,
    do_out,
    dgw,
    duw,
    ddw,
    sums_out,
    late_out,
    normed_out,
    dz_out,
    x_v,
    normed,
    normed_t,
    g,
    small_g,
    gain_row,
    heads_row,
    kv,
    q_v,
    qp,
    kp,
    gate_v,
    att,
    tot,
    part,
    core_land,
    low,
    chip_land,
    inner,
    hidden,
    land,
    d_low,
    prod_t,
    kv_land,
    d_hid,
    own_z,
    own_x,
    dl,
    dl_t,
    gain_sum,
    head_sum,
    sums,
    sum_c,
    sum_x,
    sum_y,
    sum_l,
    late,
    late_core,
    late_chip,
    late_l,
    cos_ref,
    sin_ref,
    row_range,
    free,
    done,
    p_send,
    p_recv,
    p_loc,
    ag_send,
    ag_recv,
    sp_sem,
    sa_send,
    sa_recv,
    t_send,
    t_recv,
    z_send,
    z_recv,
    kv_send,
    kv_recv,
    c_send,
    c_recv,
    s_send,
    s_recv,
    i_send,
    i_recv,
    j_send,
    j_recv,
    rs_send,
    rs_recv,
    b_send,
    b_recv,
    b_loc,
    d_send,
    d_recv,
    h_send,
    h_recv,
    h_loc,
    u_send,
    u_recv,
    o_loc,
):
    line = Line(n, g, ag_send, ag_recv, land, rs_send, rs_recv)
    l, x, y, c = line.l, line.x, line.y, line.c
    k = y * 2 + c
    group = Group()
    across, mate = device(l, 1 - x, y, c), group.mate
    right = device(l + 1, x, y, c)
    tiny = Line(n, small_g, sa_send, sa_recv)
    scale = HEAD_SIZE ** (-0.5)
    width = 256 * 2 * n
    back = Back(line, ((dgw, duw), (dgw, duw), ddw), b_send, b_recv, b_loc, 768)
    back_first = Back(line, (dq_out, (dk_out, dv_out), do_out), b_send, b_recv, b_loc, 256)
    left = device(l - 1, x, y, c)
    blocks = 2 * n
    first = Pair(line, (wq, (wk, wv), wo), p_send, p_recv, p_loc, 256)
    rest = Pair(line, ((wg, wu), (wg, wu), wd), p_send, p_recv, p_loc, 768)

    def half_of(item):
        chunk = item // 3 - 1
        return chunk if item % 3 == 2 else 2 * chunk + item % 3

    def swap(item):
        if item < 3:
            return first, item, item, 0
        return rest, item, item % 3, half_of(item)

    def swap_start(item):
        pair, item, kind, j = swap(item)
        pair.start(item, kind, j)

    def swap_end(item):
        pair, item, kind, j = swap(item)
        pair.end(item, kind, j)

    used = iter(range(16))

    def put(src, dst):
        copy = pltpu.make_async_copy(src, dst, o_loc.at[next(used)])
        copy.start()
        return copy

    others = [device(lax.rem(l + d, n), x, y, c) for d in range(1, n)]
    greet(
        [(o, None) for o in others] + [(mate, None)] + [(group.chip(i), None) for i in (1, 2, 3)]
    )

    small_here = small_g.at[0, 2 * l + x]
    small_out_copy = remote(small, small_here, sp_sem.at[0], sp_sem.at[1], across)
    small_own = pltpu.make_async_copy(small, small_here, sp_sem.at[2])
    swap_start(0)
    line.ag_half(0, x, first._part(wq, 0, 0, x))
    small_out_copy.start()
    small_own.start()
    swap_start(1)
    swap_start(2)
    x_here = pltpu.make_async_copy(x_any, x_v.at[:, x], t_send.at[2])
    x_here.start()
    halves = pl.ds(2 * c, 2)
    x_out = remote(x_any.at[halves], x_v.at[halves, x], t_send.at[0], t_recv.at[0], across)
    x_part = x_v.at[halves, 1 - x]
    x_on = remote(x_part, x_part, t_send.at[1], t_recv.at[1], mate)
    x_out.start()
    ffn_items = (5, 3, 4, 8, 6, 7, 11, 9, 10)
    for item in ffn_items:
        swap_start(item)
    z_out = remote(z_any.at[halves], dz_out.at[halves], z_send.at[0], z_recv.at[0], across)
    z_part = dz_out.at[halves]
    z_on = remote(z_part, z_part, z_send.at[1], z_recv.at[1], mate)
    z_out.start()

    swap_end(0)
    line.ag_half(0, 1 - x, g.at[0, 2 * l + 1 - x])
    small_own.wait()
    small_out_copy.wait()
    tiny.ag_start(0)
    swap_end(1)
    line.ag_start(1)
    for t in range(1, n):
        tiny.ag_step(0, t)
    line.pump(0, 1)
    line.pump(1, 1)
    swap_end(2)
    for s in range(2 * n):
        cols = slice(s * 256, (s + 1) * 256)
        heads_row[:, cols] = small_g[0, s]
        gain_row[:, cols] = small_g[0, s, 4:6, :].astype(F32)

    def norm(m, side):
        v = x_v[m, side].reshape(128, 256 * 2 * n).astype(F32)
        mean = jnp.mean(v * v, axis=-1, keepdims=True)
        v = v * lax.rsqrt(mean + EPS) * gain_row[0:1, :]
        normed[m, side] = v.astype(BF).reshape(2, 2, 32, 256 * 2 * n)

    def tables(m):
        i = l * 256 + lax.broadcasted_iota(jnp.int32, (256, 128), 0)
        lane = lax.broadcasted_iota(jnp.int32, (256, 128), 1)
        end = sizes[m, 0]
        start = jnp.zeros_like(i)
        valid = jnp.full_like(i, lengths[m, 0])
        for bucket in range(1, sizes.shape[1]):
            start = jnp.where(i >= end, end, start)
            valid = jnp.where(i >= end, lengths[m, bucket], valid)
            end = end + sizes[m, bucket]
        row_range[m] = jnp.where(lane == 0, start, jnp.minimum(i + 1, start + valid))
        steps = (lane & 63).astype(F32) * (2.0 / HEAD_SIZE)
        angle = (i - start).astype(F32) * jnp.exp(-steps * math.log(ROPE_BASE))
        cos_ref[m] = jnp.cos(angle)
        sin_ref[m] = jnp.sin(angle) * jnp.where(lane < 64, -1.0, 1.0)

    x_here.wait()
    each(4, lambda m: norm(m, x))
    line.pump(0, 2)
    line.pump(1, 2)
    line.ag_start(2)
    each(4, tables)
    x_out.wait_recv()
    x_on.start()
    line.pump(2, 1)
    for item in ffn_items[:2]:
        swap_end(item)
        line.ag_left(item)
    x_on.wait_recv()
    each(4, lambda m: norm(m, 1 - x))
    for item in (0, 1):
        line.collect(item)

    def project(m):
        a = normed[m].reshape(256, 256 * 2 * n)
        qf = dot(a, g[0].reshape(256 * 2 * n, 256))
        kf = dot(a, g[1].reshape(256 * 2 * n, 256))
        gate_v[m] = jax.nn.sigmoid(dot_t(a, heads_row[...]))
        qp[m] = qf
        kp[m] = kf[:, :128]
        cosine, sine = cos_ref[m], sin_ref[m]

        def turn(u, gain):
            u = u * lax.rsqrt(jnp.mean(u * u, axis=-1, keepdims=True) + EPS) * gain
            return (u * cosine + pltpu.roll(u, 64, 1) * sine).astype(BF)

        gains = small[8:10, :128].astype(F32)
        q_v[m, :256] = turn(qf[:, :128], gains[0:1])
        q_v[m, 256:] = turn(qf[:, 128:], gains[0:1])
        kv[l, m, :, :128] = turn(kf[:, :128], gains[1:2])
        kv[l, m, :, 128:] = kf[:, 128:].astype(BF)

    def send_kv(b, m):
        return remote(kv.at[b, m], kv.at[b, m], kv_send.at[b, m], kv_recv.at[b, m], right)

    each(4, project)
    z_copy = put(z_any.at[:, k], own_z)
    x_copy = put(x_any.at[:, k], own_x)

    def attend(m, b, diagonal):
        pair = kv[b, m]
        raw = dot_t(q_v[m], pair[:, :128]) * scale
        lo = row_range[m][:, :1] - b * 256
        hi = row_range[m][:, 1:2] - b * 256
        column = lax.broadcasted_iota(jnp.int32, (512, 256), 1)
        allowed = (column >= jnp.concatenate([lo, lo], axis=0)) & (
            column < jnp.concatenate([hi, hi], axis=0)
        )
        e = jnp.where(allowed, jnp.exp(raw), 0.0)
        total = jnp.sum(e, axis=-1, keepdims=True)
        value = dot(e.astype(BF), pair[:, 128:])
        total = jnp.broadcast_to(total, (512, 128))
        if diagonal:
            tot[m] = total
            att[m] = value
        else:
            tot[m] += total
            att[m] += value

    line.pump(2, 2)

    def turned(i):
        m, s = lax.div(i, 2 * n), lax.rem(i, 2 * n)
        tile = normed[m, :, :, :, :, pl.ds(pl.multiple_of(s * 256, 256), 256)].reshape(256, 256)
        normed_t[s, :, pl.ds(pl.multiple_of(m * 256, 256), 256)] = tile.T

    def branch(m):
        total = tot[m]
        lse = jnp.log(total)
        value = att[m] / total
        att[m] = value
        tot[m] = lse
        gates = gate_v[m]
        lo, hi = gates[:, 0:2], gates[:, 2:4]
        gates = jnp.where(x == 0, lo, hi)
        mixed = jnp.concatenate(
            [value[:256] * gates[:, 0:1], value[256:] * gates[:, 1:2]], axis=1
        ).astype(BF)
        for s in range(2 * n):
            part[m, :, :, :, :, s * 256 : (s + 1) * 256] = (
                dot(mixed, g[2, s]).astype(BF).reshape(2, 2, 2, 32, 256)
            )
        mate_copy(m).start()

    sources = (part, normed, part, normed)

    def mate_place(m, r):
        return x_v.at[m, :, pl.ds(0, 2)] if r == 2 else core_land.at[m]

    def chip_place(m, o, r):
        return x_v.at[m, (o - 1) // 2, 2 + (o - 1) % 2] if r == 2 else chip_land.at[o - 1, m]

    def mate_copy(m, r=0):
        return remote(
            sources[r].at[m, :, :, 1 - c], mate_place(m, r), c_send.at[r, m], c_recv.at[r, m], mate
        )

    def chip_copy(m, o, r=0):
        ox, oy = group.other(o)
        return remote(
            low.at[m, ox, oy],
            chip_place(m, o, r),
            s_send.at[r, m, o - 1],
            s_recv.at[r, m, o - 1],
            group.chip(o),
        )

    def to_chips(m, r=0):
        mate_copy(m, r).wait_recv()
        for u in range(2):
            for v in range(2):
                there = x_v[m, u, v] if r == 2 else core_land[m, u, v]
                low[m, u, v] = (sources[r][m, u, v, c].astype(F32) + there.astype(F32)).astype(BF)
        for o in (3, 1, 2):
            chip_copy(m, o, r).start()

    def total_of(m, r=0):
        total = low[m, x, y].astype(F32)
        for o in (1, 2, 3):
            chip_copy(m, o, r).wait_recv()
            there = x_v[m, (o - 1) // 2, 2 + (o - 1) % 2] if r == 2 else chip_land[o - 1, m]
            total = total + there.astype(F32)
        return total

    def sum_end(m, r=0):
        mate_copy(m, r).wait_send()
        for o in (1, 2, 3):
            chip_copy(m, o, r).wait_send()

    def ahead(m):
        pl.when(l <= n - 2)(lambda: send_kv(l, m).start())
        attend(m, l, True)

        def step(t, unused):
            b = l - t
            send_kv(b, m).wait_recv()
            pl.when(l <= n - 2)(lambda: send_kv(b, m).start())
            attend(m, b, False)
            return 0

        lax.fori_loop(1, l + 1, step, 0)

    for m in range(4):
        ahead(m)
        if m == 0:
            each(8 * n, turned)
            line.collect(2)
            normed_copy = put(normed_t, normed_out)
        branch(m)
        if m > 0:
            to_chips(m - 1)
        for item in ffn_items[2 + 2 * m : 4 + 2 * m]:
            swap_end(item)
            line.ag_left(item)
    to_chips(3)
    for item in ffn_items:
        line.ag_right(item, 0)
    for item in (5, 3, 4):
        line.ag_right(item, 1)
    for item in (5, 3):
        line.ag_right(item, 2)
    for item in (5, 3):
        line.pump(item, 1)

    def inner_copy(m, o, r=0):
        here = inner.at[m, x, y, c]
        return remote(
            here, here, i_send.at[r, m, o - 1], i_recv.at[r, m, o - 1], group.chip(o)
        )

    def inner_mate(m, o, r=0):
        ox, oy = group.other(o)
        there = inner.at[m, ox, oy, c]
        return remote(there, there, j_send.at[r, m, o], j_recv.at[r, m, o], mate)

    def finish(m):
        h = x_v[m, x, k].astype(F32) + total_of(m)
        hidden[m] = h
        mean = jnp.mean(h * h, axis=-1, keepdims=True)
        inner[m, x, y, c] = (h * lax.rsqrt(mean + EPS) * gain_row[1:2, :]).astype(BF)
        for o in (3, 1, 2):
            inner_copy(m, o).start()
        inner_mate(m, 0).start()

    each(4, finish)
    for item in (5, 3):
        line.pump(item, 2)
    line.ag_right(4, 2)
    line.pump(4, 1)
    z_out.wait_recv()
    z_on.start()

    def pass_on(m, r=0):
        for o in (1, 2, 3):
            inner_copy(m, o, r).wait_recv()
            inner_mate(m, o, r).start()

    each(4, pass_on)
    line.pump(4, 2)
    for item in (8, 6, 7):
        line.ag_right(item, 1)
    for item in (8, 6):
        line.ag_right(item, 2)
    for item in (8, 6):
        line.pump(item, 1)
    x_out.wait_send()
    x_on.wait_send()
    z_on.wait_recv()
    dz_own = pltpu.make_async_copy(z_any, x_v.at[:, x], z_send.at[2])
    dz_other = pltpu.make_async_copy(dz_out, x_v.at[:, 1 - x], z_send.at[3])
    dz_own.start()
    dz_other.start()

    def arrive(m, r=0):
        for o in range(4):
            inner_mate(m, o, r).wait_recv()

    def spread_end(m, r=0):
        for o in (1, 2, 3):
            inner_copy(m, o, r).wait_send()
        for o in range(4):
            inner_mate(m, o, r).wait_send()

    each(4, arrive)
    normed_copy.wait()

    def turn_inner(i):
        m, s = lax.div(i, 2 * n), lax.rem(i, 2 * n)
        tile = inner[m, :, :, :, :, pl.ds(pl.multiple_of(s * 256, 256), 256)].reshape(256, 256)
        normed_t[s, :, pl.ds(pl.multiple_of(m * 256, 256), 256)] = tile.T

    each(8 * n, turn_inner)
    each(4, sum_end)
    each(4, spread_end)

    def kv_sent(m):
        for b in range(n):
            pl.when((l >= b) & (l <= n - 2))(lambda b=b: send_kv(b, m).wait_send())

    each(4, kv_sent)
    dz_own.wait()
    dz_other.wait()

    def compute(j, h):
        pair_of, down_of = 3 * j + 3 + h, 3 * j + 5
        here = slice(128 * h, 128 * h + 128)

        def rows(m, unused):
            a = inner[m].reshape(256, width)
            d = x_v[m].reshape(256, width)
            both = dot(a, g[pair_of].reshape(width, 256))
            gated, upward = both[:, :128], both[:, 128:]
            grad = dot_t(d[:, :256], g[down_of, 0, here])
            for s in range(1, 2 * n):
                grad = grad + dot_t(d[:, s * 256 : (s + 1) * 256], g[down_of, s, here])
            sigma = jax.nn.sigmoid(gated)
            swish = gated * sigma
            product = (swish * upward).astype(BF)
            d_both = jnp.concatenate(
                [grad * upward * sigma * (1.0 + gated * (1.0 - sigma)), grad * swish], axis=1
            ).astype(BF)
            at = pl.ds(pl.multiple_of(m * 256, 256), 256)
            d_low[0, at] = d_both
            prod_t[:128, at] = product.T
            for s in range(2 * n):
                cols = slice(s * 256, (s + 1) * 256)
                o = dot(product, g[down_of, s, here])
                i = dot_t(d_both, g[pair_of, s])
                if j + h > 0:
                    o = o + part[m, :, :, :, :, cols].reshape(256, 256).astype(F32)
                    i = i + normed[m, :, :, :, :, cols].reshape(256, 256).astype(F32)
                part[m, :, :, :, :, cols] = o.astype(BF).reshape(2, 2, 2, 32, 256)
                normed[m, :, :, :, :, cols] = i.astype(BF).reshape(2, 2, 2, 32, 256)
            return 0

        lax.fori_loop(0, 4, rows, 0)

        def weights(s):
            g[pair_of, s] = dot(normed_t[s], d_low[0]).astype(BF)
            z = x_v[:, :, :, :, pl.ds(pl.multiple_of(s * 256, 256), 256)].reshape(1024, 256)
            g[down_of, s, here] = dot(prod_t[:128], z).astype(BF)

        each(2 * n, weights)

    def backward(item):
        if item < 3:
            return back_first, item, item, 0
        return back, item, item % 3, half_of(item)

    def near(*items):
        for item in items:
            line.rs_near(item, 1)
            line.rs_near(item, n - 2)

    def far(*items):
        for item in items:
            line.rs_far(item, 1)
            line.rs_far(item, n - 2)

    def send_home(item):
        way, item, kind, j = backward(item)
        way.start(item, kind, j)

    inside = (l >= 1) & (l <= n - 2)

    def final_in(item):
        pl.when(inside)(lambda: line.rs_final(item))

    def final_end(item):
        pl.when(jnp.logical_not(inside))(lambda: line.rs_final(item))

    def ready(*items):
        for item in items:
            line.collect(item)
            line.ag_end(item)

    def free_give(i):
        def tell(target):
            pl.semaphore_signal(
                free.at[i], inc=1, device_id=target, device_id_type=pl.DeviceIdType.MESH
            )

        pl.when(l == 1)(lambda: tell(device(l - 1, x, y, c)))
        pl.when(l == n - 2)(lambda: tell(device(l + 1, x, y, c)))

    def done_give(i):
        def tell(target):
            pl.semaphore_signal(
                done.at[i], inc=1, device_id=target, device_id_type=pl.DeviceIdType.MESH
            )

        pl.when(l == 0)(lambda: tell(device(l + 1, x, y, c)))
        pl.when(l == n - 1)(lambda: tell(device(l - 1, x, y, c)))

    def done_take(i):
        pl.when(inside)(lambda: pl.semaphore_wait(done.at[i], 1))

    def free_take(i):
        pl.when(jnp.logical_not(inside))(lambda: pl.semaphore_wait(free.at[i], 1))

    ready(5, 3)
    compute(0, 0)
    line.rs_fire(3)
    for item in (8, 6):
        line.pump(item, 2)
    line.ag_right(7, 2)
    line.pump(7, 1)
    ready(4)
    compute(0, 1)
    line.rs_fire(4)
    line.rs_fire(5)
    line.pump(7, 2)
    for item in (11, 9, 10):
        line.ag_right(item, 1)
    for item in (11, 9):
        line.ag_right(item, 2)
    for item in (11, 9):
        line.pump(item, 1)
    near(3)
    ready(8, 6)
    compute(1, 0)
    line.rs_fire(6)
    for item in (11, 9):
        line.pump(item, 2)
    line.ag_right(10, 2)
    line.pump(10, 1)
    near(4)
    final_in(3)
    free_give(0)
    ready(7)
    compute(1, 1)
    line.rs_fire(7)
    line.rs_fire(8)
    line.pump(10, 2)
    near(5)
    far(3)
    final_in(4)
    free_give(1)
    near(6)
    final_in(5)
    free_give(2)
    far(4)
    ready(11, 9)
    compute(2, 0)
    free_take(0)
    line.rs_fire(9)
    ready(10)
    compute(2, 1)
    each(4, lambda m: mate_copy(m, 1).start())
    free_take(1)
    line.rs_fire(10)
    free_take(2)
    line.rs_fire(11)
    gain_sum[...] = jnp.zeros_like(gain_sum)
    head_sum[...] = jnp.zeros_like(head_sum)
    each(4, lambda m: to_chips(m, 1))
    near(7)
    far(5)
    final_in(6)
    far(6)
    near(8)
    line.rs_near(9, 1)
    z_copy.wait()
    x_copy.wait()
    normed_back_copy = put(normed_out, normed_t)

    def finish_hidden(m):
        total = total_of(m, 1)
        h = hidden[m]
        r = lax.rsqrt(jnp.mean(h * h, axis=-1, keepdims=True) + EPS)
        normal = h * r
        gain_sum[1:2] += jnp.sum(total * normal, axis=0, keepdims=True)
        e = total * gain_row[1:2, :]
        grad = own_z[m].astype(F32) + r * (
            e - normal * jnp.mean(e * normal, axis=-1, keepdims=True)
        )
        d_hid[m] = grad
        inner[m, x, y, c] = grad.astype(BF)
        for o in (3, 1, 2):
            inner_copy(m, o, 1).start()
        inner_mate(m, 0, 1).start()

    each(4, finish_hidden)
    each(4, lambda m: sum_end(m, 1))
    for item in (3, 4, 5):
        final_end(item)
        send_home(item)
    done_give(0)
    line.rs_near(9, 2)
    final_in(7)
    far(7)
    line.rs_near(10, 1)

    def attend_back(m):
        arrive(m, 1)
        d = inner[m].reshape(256, width)
        gm = dot_t(d[:, :256], g[2, 0])
        for s in range(1, blocks):
            gm = gm + dot_t(d[:, s * 256 : (s + 1) * 256], g[2, s])
        gates = gate_v[m]
        gates = jnp.where(x == 0, gates[:, 0:2], gates[:, 2:4])
        g0, g1 = gates[:, 0:1], gates[:, 1:2]
        a0, a1 = att[m, :256], att[m, 256:]
        d0, d1 = gm[:, :128], gm[:, 128:]
        l0 = jnp.sum(d0 * a0, axis=-1, keepdims=True) * g0 * (1.0 - g0)
        l1 = jnp.sum(d1 * a1, axis=-1, keepdims=True) * g1 * (1.0 - g1)
        lane = lax.broadcasted_iota(jnp.int32, (256, 128), 1)
        logits = jnp.where(lane == 2 * x, l0, 0.0) + jnp.where(lane == 2 * x + 1, l1, 0.0)
        logits = logits.astype(BF)
        dl[m] = logits
        at = pl.ds(pl.multiple_of(m * 256, 256), 256)
        dl_t[:, at] = logits.T[:16]
        mixed = jnp.concatenate([a0 * g0, a1 * g1], axis=1).astype(BF)
        prod_t[:, at] = mixed.T
        da = jnp.concatenate([d0 * g0, d1 * g1], axis=0).astype(BF)
        delta = jnp.sum(da.astype(F32) * att[m], axis=-1, keepdims=True)
        log_total = tot[m][:, :1]
        qm = q_v[m]
        att[m] = jnp.zeros((512, 128), F32)

        def block(b, unused):
            pair = kv[b, m]
            keys, values = pair[:, :128], pair[:, 128:]
            raw = dot_t(qm, keys) * scale
            lo = row_range[m][:, :1] - b * 256
            hi = row_range[m][:, 1:2] - b * 256
            column = lax.broadcasted_iota(jnp.int32, (512, 256), 1)
            allowed = (column >= jnp.concatenate([lo, lo], axis=0)) & (
                column < jnp.concatenate([hi, hi], axis=0)
            )
            p = jnp.where(allowed, jnp.exp(raw - log_total), 0.0)
            ds = (p * (dot_t(da, values) - delta)).astype(BF)
            att[m] += dot(ds, keys)
            dk = dot(ds.T, qm) * scale
            dv = dot(p.astype(BF).T, da)
            kv[b, m] = jnp.concatenate([dk, dv], axis=1).astype(BF)
            return 0

        lax.fori_loop(0, l + 1, block, 0)

    def kv_copy(b, m):
        return remote(
            kv.at[b, m], kv_land.at[b, m], d_send.at[b, m], d_recv.at[b, m], left
        )

    def kv_fire(m):
        for b in range(n - 1):
            pl.when(l == n - 1)(lambda b=b: kv_copy(b, m).start())

    def kv_step(m):
        for b in range(n - 2):

            @pl.when((l > b) & (l <= n - 2))
            def _(b=b):
                kv_copy(b, m).wait_recv()
                kv[b, m] = (kv[b, m].astype(F32) + kv_land[b, m].astype(F32)).astype(BF)
                kv_copy(b, m).start()

    def normal_back(u, d_rot, gain, cosine, sine):
        d = d_rot * cosine - pltpu.roll(d_rot, 64, 1) * sine
        r = lax.rsqrt(jnp.mean(u * u, axis=-1, keepdims=True) + EPS)
        normal = u * r
        e = d * gain
        grad = r * (e - normal * jnp.mean(e * normal, axis=-1, keepdims=True))
        return grad.astype(BF), jnp.sum(d * normal, axis=0, keepdims=True)

    gains = small[8:10, :128].astype(F32)

    def query_back(m):
        for h in range(2):
            cols = slice(h * 128, (h + 1) * 128)
            grad, total = normal_back(
                qp[m][:, cols],
                att[m, h * 256 : (h + 1) * 256] * scale,
                gains[0:1],
                cos_ref[m],
                sin_ref[m],
            )
            d_low[0, pl.ds(pl.multiple_of(m * 256, 256), 256), cols] = grad
            head_sum[0:1, :128] += total

    pass_on(0, 1)
    for m in range(4):
        if m < 3:
            pass_on(m + 1, 1)
        if m == 2:
            each(4, lambda m: mate_copy(m, 2).start())
        attend_back(m)
        kv_fire(m)
        if m == 0:
            line.rs_near(10, 2)
    each(4, lambda m: to_chips(m, 2))
    final_in(8)
    far(8)
    line.rs_near(11, 1)
    for item in (6, 7, 8):
        final_end(item)
        send_home(item)
    done_give(1)
    done_take(0)
    far(9)
    for item in (3, 4, 5):
        way, item, kind, j = backward(item)
        way.end(item, kind, j)
        line.rs_end(item)
    each(4, query_back)
    normed_back_copy.wait()

    def output_weights(s, unused):
        z = inner[:, :, :, :, :, pl.ds(pl.multiple_of(s * 256, 256), 256)].reshape(1024, 256)
        g[5, s] = dot(prod_t[...], z).astype(BF)
        return 0

    def query_weights(s, unused):
        g[3, s] = dot(normed_t[s], d_low[0]).astype(BF)
        sums[1, s] = dot_t(dl_t[...], normed_t[s])[:8]
        return 0

    lax.fori_loop(0, blocks, output_weights, 0)
    line.rs_fire(2)
    lax.fori_loop(0, blocks, query_weights, 0)
    line.rs_fire(0)
    for m in range(4):
        kv_step(m)
    line.rs_near(11, 2)
    line.rs_near(2, 1)
    line.rs_near(0, 1)
    far(10)

    def home(i, m, own, out):
        mine = out.at[m, k]
        there = out.at[m, (1 - y) * 2 + c]
        keep = pltpu.make_async_copy(own.at[m], mine, h_loc.at[i, m])
        over = remote(own.at[m], mine, h_send.at[i, m, 0], h_recv.at[i, m, 0], group.chip(2))
        beside = remote(own.at[m], mine, h_send.at[i, m, 1], h_recv.at[i, m, 1], mate)
        on = remote(there, there, h_send.at[i, m, 2], h_recv.at[i, m, 2], mate)
        return keep, over, beside, on

    homes = ((own_z, res_out), (own_x, grad_out))

    def home_start(i, m):
        for copy in home(i, m, *homes[i])[:3]:
            copy.start()

    def home_on(i, m):
        keep, over, beside, on = home(i, m, *homes[i])
        over.wait_recv()
        on.start()

    def home_end(i, m):
        keep, over, beside, on = home(i, m, *homes[i])
        keep.wait()
        over.wait_send()
        beside.wait()
        on.wait()

    def finish_out(m):
        own_z[m] = (hidden[m] + total_of(m, 2)).astype(BF)
        home_start(0, m)

    each(4, finish_out)
    each(4, lambda m: sum_end(m, 2))

    def key_back(m):
        pl.when(l <= n - 2)(lambda: kv_copy(l, m).wait_recv())
        pair = kv[l, m].astype(F32)
        pair = pair + jnp.where(l <= n - 2, kv_land[l, m].astype(F32), 0.0)
        grad, total = normal_back(kp[m], pair[:, :128], gains[1:2], cos_ref[m], sin_ref[m])
        at = pl.ds(pl.multiple_of(m * 256, 256), 256)
        d_low[1, at, :128] = grad
        d_low[1, at, 128:] = pair[:, 128:].astype(BF)
        head_sum[0:1, 128:] += total

    each(4, key_back)

    def key_weights(s, unused):
        g[4, s] = dot(normed_t[s], d_low[1]).astype(BF)
        return 0

    lax.fori_loop(0, blocks, key_weights, 0)
    line.rs_fire(1)

    def normed_back(m):
        at = pl.ds(pl.multiple_of(m * 256, 256), 256)
        a, b, e = d_low[0, at], d_low[1, at], dl[m][:, :16]
        for s in range(blocks):
            part = dot_t(a, g[0, s]) + dot_t(b, g[1, s]) + dot(e, small_g[0, s])
            normed[m, :, :, :, :, s * 256 : (s + 1) * 256] = part.astype(BF).reshape(
                2, 2, 2, 32, 256
            )
        mate_copy(m, 3).start()

    each(4, normed_back)
    far(11)
    for s in range(blocks):
        sums[0, s, 0:1] = gain_sum[1:2, s * 256 : (s + 1) * 256]
        sums[0, s, 1:2] = head_sum[0:1]
        sums[0, s, 2:8] = jnp.zeros((6, 256), F32)
    small_c = remote(sums.at[0], sum_c, u_send.at[0], u_recv.at[0], mate)
    small_x = remote(sums, sum_x, u_send.at[1], u_recv.at[1], group.chip(1))
    small_y = remote(sums.at[0], sum_y, u_send.at[2], u_recv.at[2], group.chip(2))
    small_c.start()
    each(4, lambda m: to_chips(m, 3))
    small_c.wait()
    sums[0] = sums[0] + sum_c[...]
    done_take(1)
    line.rs_far(2, 2)
    line.rs_near(2, 2)
    for item in (9, 10, 11):
        line.rs_final(item)
    line.rs_far(0, 2)
    line.rs_near(1, 1)

    def small_line(d):
        to = lax.rem(l + d, n)
        return remote(
            sums.at[:, pl.ds(2 * to, 2)],
            sum_l.at[l],
            u_send.at[2 + d],
            u_recv.at[2 + d],
            device(to, x, y, c),
        )

    def finish_grad(m):
        total = total_of(m, 3)
        v = own_x[m].astype(F32)
        r = lax.rsqrt(jnp.mean(v * v, axis=-1, keepdims=True) + EPS)
        normal = v * r
        gain_sum[0:1] += jnp.sum(total * normal, axis=0, keepdims=True)
        e = total * gain_row[0:1, :]
        own_x[m] = (
            d_hid[m] + r * (e - normal * jnp.mean(e * normal, axis=-1, keepdims=True))
        ).astype(BF)
        home_start(1, m)

    each(4, finish_grad)
    for s in range(blocks):
        late[s : s + 1] = gain_sum[0:1, s * 256 : (s + 1) * 256]
    late_c = remote(late, late_core, u_send.at[6], u_recv.at[6], mate)
    late_c.start()
    small_x.start()
    each(4, lambda m: home_on(0, m))
    for item in (9, 10, 11):
        send_home(item)
    line.rs_near(0, 2)
    line.rs_far(1, 2)
    line.rs_far(2, 1)
    line.rs_far(0, 1)
    late_c.wait()
    late[...] = late[...] + late_core[...]
    late_s = [
        remote(
            late, late_chip.at[x * 2 + y], u_send.at[6 + o], u_recv.at[6 + o], group.chip(o)
        )
        for o in (1, 2, 3)
    ]
    for copy in late_s:
        copy.start()
    late_chip[x * 2 + y] = late[...]
    small_x.wait()
    sums[...] = sums[...] + sum_x[...]
    small_y.start()
    each(4, lambda m: home_on(1, m))
    line.rs_near(1, 2)
    line.rs_far(1, 1)
    for copy in late_s:
        copy.wait()
    late[...] = late_chip[0] + late_chip[1] + late_chip[2] + late_chip[3]

    def late_line(d):
        to = lax.rem(l + d, n)
        return remote(
            late, late_l.at[l], u_send.at[9 + d], u_recv.at[9 + d], device(to, x, y, c)
        )

    for d in range(1, n):
        late_line(d).start()
    late_l[l] = late[...]
    small_y.wait()
    sums[0] = sums[0] + sum_y[...]
    for d in range(1, n):
        small_line(d).start()
    sum_l[l] = sums[:, pl.ds(2 * l, 2)]
    line.rs_final(2)
    send_home(2)
    line.rs_final(0)
    send_home(0)
    for d in range(1, n):
        small_line(d).wait()
    total = sum_l[0, :, x]
    for i in range(1, n):
        total = total + sum_l[i, :, x]
    sums_out[...] = total
    for d in range(1, n):
        late_line(d).wait()
    total = late_l[0]
    for i in range(1, n):
        total = total + late_l[i]
    late_out[...] = total
    line.rs_final(1)
    send_home(1)
    for item in (6, 7, 8, 9, 10, 11, 2, 0, 1):
        way, item, kind, j = backward(item)
        way.end(item, kind, j)
        line.rs_end(item)
    z_out.wait_send()
    z_on.wait_send()
    tiny.ag_end(0)
    each(3, line.ag_end)

    def drain(m):
        sum_end(m, 3)
        spread_end(m, 1)
        home_end(0, m)
        home_end(1, m)
        for b in range(n - 1):
            pl.when(l > b)(lambda b=b: kv_copy(b, m).wait_send())

    each(4, drain)


def layer(n, x_in, z_in, wq, wk, wv, wo, wg, wu, wd, small, sizes, lengths):
    d = x_in.shape[-1]
    m = 2 * n
    bf = lambda *shape: jax.ShapeDtypeStruct(shape, BF)
    vb = lambda *shape: pltpu.VMEM(shape, BF)
    vf = lambda *shape: pltpu.VMEM(shape, F32)
    return pl.pallas_call(
        functools.partial(layer_kernel, n),
        out_shape=(
            bf(4, 4, 32, d),
            bf(4, 4, 32, d),
            bf(256, 512),
            bf(256, 256),
            bf(256, 256),
            bf(512, 256),
            bf(256, 1536),
            bf(256, 1536),
            bf(1536, 256),
            jax.ShapeDtypeStruct((2, 8, 256), F32),
            jax.ShapeDtypeStruct((m, 256), F32),
            bf(m, 256, 1024),
            bf(4, 4, 32, d),
        ),
        in_specs=[ANY] * 9 + [VM] + [pl.BlockSpec(memory_space=pltpu.SMEM)] * 2,
        out_specs=(ANY,) * 9 + (VM,) * 2 + (ANY,) * 2,
        scratch_shapes=[
            vb(4, 2, 4, 32, d),
            vb(4, 2, 2, 2, 32, d),
            vb(m, 256, 1024),
            vb(12, m, 256, 256),
            vb(1, m, 16, 256),
            vf(2, d),
            vb(16, d),
            vb(n, 4, 256, 256),
            vb(4, 512, 128),
            vf(4, 256, 256),
            vf(4, 256, 128),
            vf(4, 256, 16),
            vf(4, 512, 128),
            vf(4, 512, 128),
            vb(4, 2, 2, 2, 32, d),
            vb(4, 2, 2, 32, d),
            vb(4, 2, 2, 32, d),
            vb(3, 4, 32, d),
            vb(4, 2, 2, 2, 32, d),
            vf(4, 32, d),
            vb(6, m + 2, 256, 256),
            vb(2, 1024, 256),
            vb(256, 1024),
            vb(n, 4, 256, 256),
            vf(4, 32, d),
            vb(4, 32, d),
            vb(4, 32, d),
            vb(4, 256, 128),
            vb(16, 1024),
            vf(2, d),
            vf(1, 256),
            vf(2, m, 8, 256),
            vf(m, 8, 256),
            vf(2, m, 8, 256),
            vf(m, 8, 256),
            vf(n, 2, 2, 8, 256),
            vf(m, 256),
            vf(m, 256),
            vf(4, m, 256),
            vf(n, m, 256),
            vf(4, 256, 128),
            vf(4, 256, 128),
            pltpu.VMEM((4, 256, 128), jnp.int32),
            pltpu.SemaphoreType.REGULAR((3,)),
            pltpu.SemaphoreType.REGULAR((2,)),
            DMA((24,)),
            DMA((24,)),
            DMA((24,)),
            DMA((12, 2, n)),
            DMA((12, n)),
            DMA((3,)),
            DMA((1, 2, n)),
            DMA((1, n)),
            DMA((3,)),
            DMA((2,)),
            DMA((4,)),
            DMA((2,)),
            DMA((n, 4)),
            DMA((n, 4)),
            DMA((4, 4)),
            DMA((4, 4)),
            DMA((4, 4, 3)),
            DMA((4, 4, 3)),
            DMA((2, 4, 3)),
            DMA((2, 4, 3)),
            DMA((2, 4, 4)),
            DMA((2, 4, 4)),
            DMA((12, 2, n)),
            DMA((12, n + 1)),
            DMA((24,)),
            DMA((24,)),
            DMA((24,)),
            DMA((n, 4)),
            DMA((n, 4)),
            DMA((2, 4, 3)),
            DMA((2, 4, 3)),
            DMA((2, 4)),
            DMA((9 + n,)),
            DMA((9 + n,)),
            DMA((16,)),
        ],
        compiler_params=pltpu.CompilerParams(
            collective_id=0, has_side_effects=True, vmem_limit_bytes=63 * 2**20
        ),
        name="layer",
    )(x_in, z_in, wq, wk, wv, wo, wg, wu, wd, small, sizes, lengths)

class Group:
    def __init__(self):
        self.l, self.x, self.y, self.c = place()
        self.mate = device(self.l, self.x, self.y, 1 - self.c)

    def other(self, i):
        x = 1 - self.x if i & 1 else self.x
        y = 1 - self.y if i & 2 else self.y
        return x, y

    def chip(self, i):
        x, y = self.other(i)
        return device(self.l, x, y, self.c)

    def partners(self):
        return [(self.mate, None)] + [(self.chip(i), None) for i in (1, 2, 3)]


def outputs_kernel(count, *refs):
    ins, small, outs = refs[:count], refs[count : count + 2], refs[count + 2 : 2 * count + 2]
    attention, feedforward, query, key, heads = refs[2 * count + 2 : 2 * count + 7]
    held = refs[2 * count + 7 : 3 * count + 7]
    wide = refs[3 * count + 7 : 4 * count + 5]
    in_sem, out_sem = refs[-2:]
    reads = [
        pltpu.make_async_copy(ins[i], held[i], in_sem.at[i]) for i in range(count)
    ]
    writes = [
        pltpu.make_async_copy(held[i] if i < 2 else wide[i - 2], outs[i], out_sem.at[i])
        for i in range(count)
    ]
    order = list(range(2, count)) + [0, 1]
    for i in order:
        reads[i].start()
    s = lax.axis_index("seq")
    sums, late = small
    row = lax.broadcasted_iota(jnp.int32, late.shape, 0)
    attention[...] = jnp.sum(jnp.where(row == s, late[...], 0.0), axis=0, keepdims=True)
    feedforward[...] = sums[0, 0:1]
    query[...] = sums[0, 1:2, :HEAD_SIZE]
    key[...] = sums[0, 1:2, HEAD_SIZE:]
    heads[...] = sums[1].T[:, :4]
    for i in order:
        reads[i].wait()
        if i >= 2:
            src, dst = held[i], wide[i - 2]

            def widen(part, src=src, dst=dst):
                at = pl.ds(pl.multiple_of(part * 64, 64), 64)
                dst[at] = src[at].astype(F32)

            each(src.shape[0] // 64, widen)
        writes[i].start()
    for copy in writes:
        copy.wait()


def outputs(arrays, sums, late):
    count = len(arrays)
    f32 = lambda *shape: jax.ShapeDtypeStruct(shape, F32)
    kept = [jax.ShapeDtypeStruct(a.shape, a.dtype) for a in arrays[:2]]
    return pl.pallas_call(
        functools.partial(outputs_kernel, count),
        out_shape=(
            *kept,
            *[f32(*a.shape) for a in arrays[2:]],
            f32(1, 256),
            f32(1, 256),
            f32(1, HEAD_SIZE),
            f32(1, HEAD_SIZE),
            f32(256, 4),
        ),
        in_specs=[ANY] * count + [VM] * 2,
        out_specs=(ANY,) * count + (VM,) * 5,
        scratch_shapes=[
            *[pltpu.VMEM(a.shape, a.dtype) for a in arrays],
            *[pltpu.VMEM(a.shape, F32) for a in arrays[2:]],
            DMA((count,)),
            DMA((count,)),
        ],
        compiler_params=pltpu.CompilerParams(vmem_limit_bytes=63 * 2**20),
        name="outputs",
    )(*arrays, sums, late)


def fast_local(
    inputs,
    cotangent,
    bucket_sizes,
    true_lengths,
    attention_gain,
    feedforward_gain,
    query_gain,
    key_gain,
    query_weight,
    key_matrix,
    value_matrix,
    headgate_weight,
    output_weight,
    gate_weight,
    up_weight,
    down_weight,
):
    batches, rows, width = inputs.shape
    n = lax.axis_size("seq") // 2
    seq, kv = lax.axis_index("seq"), lax.axis_index("kv")
    l, x = seq // 2, seq % 2
    scale = HEAD_SIZE ** (-0.5)
    span = 2 * rows
    gain_query = query_gain.astype(F32)
    gain_key = key_gain.astype(F32)

    own_small = jnp.concatenate(
        [
            headgate_weight.T,
            attention_gain[None],
            feedforward_gain[None],
            jnp.zeros((2, 256), BF),
            jnp.pad(jnp.stack([query_gain, key_gain]), ((0, 0), (0, 128))),
            jnp.zeros((6, 256), BF),
        ],
        axis=0,
    )
    x_split = inputs.reshape(batches, 4, 32, width)
    z_split = cotangent.reshape(batches, 4, 32, width)
    own_out, own_grad, dq, dk, dv, do, d_gate, d_up, d_down, sums, late, unused, unused = layer(
        n,
        x_split,
        z_split,
        query_weight,
        key_matrix,
        value_matrix,
        output_weight,
        gate_weight,
        up_weight,
        down_weight,
        own_small,
        bucket_sizes,
        true_lengths,
    )
    res, grad, dq, dk, dv, do, dg, du, dd, attention, feedforward, query, key, heads = outputs(
        [
            own_out.reshape(batches, rows, width),
            own_grad.reshape(batches, rows, width),
            dq,
            dk,
            dv,
            do,
            d_gate,
            d_up,
            d_down,
        ],
        sums,
        late,
    )
    return (
        res,
        grad,
        attention[0],
        feedforward[0],
        query[0],
        key[0],
        dq,
        dk,
        dv,
        heads,
        do,
        dg,
        du,
        dd,
    )


def solution(mesh):
    chosen = fast_local if dict(mesh.shape) == {"seq": 8, "kv": 4} else local
    in_specs = (
        P(None, "seq", None),
        P(None, "seq", None),
        P(),
        P(),
        P("seq"),
        P("seq"),
        P(),
        P(),
        P("seq", "kv"),
        P("seq", "kv"),
        P("seq", "kv"),
        P("seq", "kv"),
        P("kv", "seq"),
        P("seq", "kv"),
        P("seq", "kv"),
        P("kv", "seq"),
    )
    out_specs = (
        P(None, "seq", None),
        P(None, "seq", None),
        P("seq"),
        P("seq"),
        P(),
        P(),
        P("seq", "kv"),
        P("seq", "kv"),
        P("seq", "kv"),
        P("seq", "kv"),
        P("kv", "seq"),
        P("seq", "kv"),
        P("seq", "kv"),
        P("kv", "seq"),
    )
    return jax.shard_map(chosen, mesh=mesh, in_specs=in_specs, out_specs=out_specs, check_vma=False)
```

```python
import functools
import math

import jax
import jax.numpy as jnp
from jax import lax
from jax.experimental import pallas as pl
from jax.experimental.pallas import tpu as pltpu
from jax.sharding import PartitionSpec as P

HEAD_SIZE = 128


EPS = 1e-06
ROPE_BASE = 1000000.0
MASKED = -1e30


def rms_scale(values):
    return lax.rsqrt(jnp.mean(values * values, axis=-1, keepdims=True) + EPS)


def norm_backward(grad, normal, factor):
    return factor * (grad - normal * jnp.mean(grad * normal, axis=-1, keepdims=True))


def rope_tables(positions, width):
    half = width // 2
    steps = jnp.arange(half, dtype=jnp.float32) * (2.0 / width)
    inverse = jnp.exp(-steps * math.log(ROPE_BASE))
    angles = positions.astype(jnp.float32)[:, None] * inverse[None, :]
    cosine = jnp.cos(angles)
    sine = jnp.sin(angles)
    return (jnp.concatenate([cosine, cosine], axis=-1), jnp.concatenate([sine, sine], axis=-1))


def rotate_forward(values, cosine, sine):
    half = values.shape[-1] // 2
    turned = jnp.concatenate([-values[..., half:], values[..., :half]], axis=-1)
    return values * cosine[:, None, :] + turned * sine[:, None, :]


def rotate_backward(grad, cosine, sine):
    half = grad.shape[-1] // 2
    moved = grad * sine[:, None, :]
    return grad * cosine[:, None, :] + jnp.concatenate(
        [moved[..., half:], -moved[..., :half]], axis=-1
    )


def token_layout(index, buckets, lengths):
    ends = jnp.cumsum(buckets)
    starts = ends - buckets
    member = (index[:, None] >= starts[None, :]) & (index[:, None] < ends[None, :])
    labels = jnp.arange(buckets.shape[0], dtype=jnp.int32)
    segment = jnp.sum(jnp.where(member, labels[None, :], 0), axis=1)
    position = index - jnp.sum(jnp.where(member, starts[None, :], 0), axis=1)
    limit = jnp.sum(jnp.where(member, lengths[None, :], 0), axis=1)
    return (segment, position, position < limit)


def outer_sum(left, right):
    return lax.dot_general(
        left, right, (((0,), (0,)), ((), ())), preferred_element_type=jnp.float32
    )


def times_transpose(left, weight):
    return lax.dot_general(
        left, weight, (((1,), (1,)), ((), ())), preferred_element_type=jnp.float32
    )


def block_scores(query_kg, key_block, start, row_index, row_segment, buckets, lengths, scale):
    key_index = start + jnp.arange(key_block.shape[0], dtype=jnp.int32)
    key_segment, key_position, key_valid = token_layout(key_index, buckets, lengths)
    allowed = (
        (row_segment[:, None] == key_segment[None, :])
        & (key_index[None, :] <= row_index[:, None])
        & key_valid[None, :]
    )
    raw = (
        jnp.einsum("kgtd,skd->kgts", query_kg, key_block, preferred_element_type=jnp.float32)
        * scale
    )
    return (jnp.where(allowed, raw, MASKED), allowed)


def split_blocks(keys, values, block):
    blocks = keys.shape[0] // block
    key_blocks = keys.reshape(blocks, block, keys.shape[1], keys.shape[2])
    value_blocks = values.reshape(blocks, block, values.shape[1], values.shape[2])
    starts = jnp.arange(blocks) * block
    return (key_blocks, value_blocks, starts)


def attention_forward(
    query_kg, keys, values, row_index, row_segment, buckets, lengths, block, scale
):
    key_blocks, value_blocks, starts = split_blocks(keys, values, block)

    def first_pass(carry, item):
        running_max, total = carry
        key_block, start = item
        masked, allowed = block_scores(
            query_kg, key_block, start, row_index, row_segment, buckets, lengths, scale
        )
        new_max = jnp.maximum(running_max, jnp.max(masked, axis=-1))
        total = total * jnp.exp(running_max - new_max) + jnp.sum(
            jnp.where(allowed, jnp.exp(masked - new_max[..., None]), 0.0), axis=-1
        )
        return ((new_max, total), None)

    begin = (
        jnp.full(query_kg.shape[:3], MASKED, jnp.float32),
        jnp.zeros(query_kg.shape[:3], jnp.float32),
    )
    (running_max, total), unused = lax.scan(first_pass, begin, (key_blocks, starts))
    log_total = running_max + jnp.log(total)

    def second_pass(accumulated, item):
        key_block, value_block, start = item
        masked, allowed = block_scores(
            query_kg, key_block, start, row_index, row_segment, buckets, lengths, scale
        )
        weights = jnp.where(allowed, jnp.exp(masked - log_total[..., None]), 0.0).astype(
            jnp.bfloat16
        )
        return (
            accumulated
            + jnp.einsum(
                "kgts,skd->kgtd", weights, value_block, preferred_element_type=jnp.float32
            ),
            None,
        )

    attended, unused = lax.scan(
        second_pass, jnp.zeros(query_kg.shape, jnp.float32), (key_blocks, value_blocks, starts)
    )
    return (attended, log_total)


def attention_backward(
    query_kg,
    grad_kg,
    log_total,
    delta,
    keys,
    values,
    row_index,
    row_segment,
    buckets,
    lengths,
    block,
    scale,
):
    key_blocks, value_blocks, starts = split_blocks(keys, values, block)

    def step(grad_query, item):
        key_block, value_block, start = item
        masked, allowed = block_scores(
            query_kg, key_block, start, row_index, row_segment, buckets, lengths, scale
        )
        weights = jnp.where(allowed, jnp.exp(masked - log_total[..., None]), 0.0)
        grad_weights = jnp.einsum(
            "kgtd,skd->kgts", grad_kg, value_block, preferred_element_type=jnp.float32
        )
        grad_scores = (weights * (grad_weights - delta[..., None])).astype(jnp.bfloat16)
        grad_query = grad_query + scale * jnp.einsum(
            "kgts,skd->kgtd", grad_scores, key_block, preferred_element_type=jnp.float32
        )
        grad_key = scale * jnp.einsum(
            "kgts,kgtd->skd", grad_scores, query_kg, preferred_element_type=jnp.float32
        )
        grad_value = jnp.einsum(
            "kgts,kgtd->skd",
            weights.astype(jnp.bfloat16),
            grad_kg,
            preferred_element_type=jnp.float32,
        )
        return (grad_query, (grad_key, grad_value))

    grad_query, (grad_keys, grad_values) = lax.scan(
        step, jnp.zeros(query_kg.shape, jnp.float32), (key_blocks, value_blocks, starts)
    )
    return (grad_query, grad_keys.reshape(keys.shape), grad_values.reshape(values.shape))


def local(
    inputs,
    cotangent,
    bucket_sizes,
    true_lengths,
    attention_gain,
    feedforward_gain,
    query_gain,
    key_gain,
    query_weight,
    key_matrix,
    value_matrix,
    headgate_weight,
    output_weight,
    gate_weight,
    up_weight,
    down_weight,
):
    batches, rows, width = inputs.shape
    seq_count = lax.axis_size("seq")
    block = math.gcd(rows * seq_count, 512)
    local_heads = query_weight.shape[1] // HEAD_SIZE
    local_groups = key_matrix.shape[1] // HEAD_SIZE
    group = local_heads // local_groups
    scale = HEAD_SIZE ** (-0.5)
    row_index = lax.axis_index("seq") * rows + jnp.arange(rows, dtype=jnp.int32)
    gain_query = query_gain.astype(jnp.float32)
    gain_key = key_gain.astype(jnp.float32)
    sum_attention_gain = jnp.zeros((width,), jnp.float32)
    sum_feedforward_gain = jnp.zeros((width,), jnp.float32)
    sum_query = jnp.zeros((width, query_weight.shape[1]), jnp.float32)
    sum_key = jnp.zeros((width, key_matrix.shape[1]), jnp.float32)
    sum_value = jnp.zeros((width, value_matrix.shape[1]), jnp.float32)
    sum_headgate = jnp.zeros((width, headgate_weight.shape[1]), jnp.float32)
    sum_output = jnp.zeros((output_weight.shape[0], width), jnp.float32)
    sum_gate = jnp.zeros((width, gate_weight.shape[1]), jnp.float32)
    sum_upward = jnp.zeros((width, up_weight.shape[1]), jnp.float32)
    sum_down = jnp.zeros((down_weight.shape[0], width), jnp.float32)
    sum_query_gain = jnp.zeros((HEAD_SIZE,), jnp.float32)
    sum_key_gain = jnp.zeros((HEAD_SIZE,), jnp.float32)
    results = []
    input_grads = []
    for batch in range(batches):
        gathered = (
            lax.all_gather(attention_gain, "seq", axis=0, tiled=True),
            lax.all_gather(feedforward_gain, "seq", axis=0, tiled=True),
            lax.all_gather(query_weight, "seq", axis=0, tiled=True),
            lax.all_gather(key_matrix, "seq", axis=0, tiled=True),
            lax.all_gather(value_matrix, "seq", axis=0, tiled=True),
            lax.all_gather(headgate_weight, "seq", axis=0, tiled=True),
            lax.all_gather(output_weight, "seq", axis=1, tiled=True),
            lax.all_gather(gate_weight, "seq", axis=0, tiled=True),
            lax.all_gather(up_weight, "seq", axis=0, tiled=True),
            lax.all_gather(down_weight, "seq", axis=1, tiled=True),
        )
        (
            gain_a,
            gain_f,
            w_query,
            key_projection_weight,
            value_projection_weight,
            w_head,
            w_output,
            w_gate,
            w_up,
            w_down,
        ) = gathered
        gain_a = gain_a.astype(jnp.float32)
        gain_f = gain_f.astype(jnp.float32)
        buckets = bucket_sizes[batch]
        lengths = true_lengths[batch]
        row_segment, row_position, row_valid = token_layout(row_index, buckets, lengths)
        cosine, sine = rope_tables(row_position, HEAD_SIZE)
        current = inputs[batch].astype(jnp.float32)
        scale_a = rms_scale(current)
        normal_a = current * scale_a
        normed_input = (normal_a * gain_a).astype(jnp.bfloat16)
        query_proj = jnp.dot(normed_input, w_query, preferred_element_type=jnp.float32).reshape(
            rows, local_heads, HEAD_SIZE
        )
        key_proj = jnp.dot(
            normed_input, key_projection_weight, preferred_element_type=jnp.float32
        ).reshape(rows, local_groups, HEAD_SIZE)
        value_proj = jnp.dot(
            normed_input, value_projection_weight, preferred_element_type=jnp.float32
        )
        query_scale = rms_scale(query_proj)
        query_normal = query_proj * query_scale
        key_scale = rms_scale(key_proj)
        key_normal = key_proj * key_scale
        query_rot = rotate_forward(query_normal * gain_query, cosine, sine).astype(jnp.bfloat16)
        key_rot = rotate_forward(key_normal * gain_key, cosine, sine).astype(jnp.bfloat16)
        value_low = value_proj.astype(jnp.bfloat16).reshape(rows, local_groups, HEAD_SIZE)
        logits = jnp.dot(normed_input, w_head, preferred_element_type=jnp.float32)
        gate = jax.nn.sigmoid(logits)
        all_keys, all_values = (
            lax.all_gather(key_rot, "seq", axis=0, tiled=True),
            lax.all_gather(value_low, "seq", axis=0, tiled=True),
        )
        query_kg = query_rot.reshape(rows, local_groups, group, HEAD_SIZE).transpose(1, 2, 0, 3)
        attended_kg, log_total = attention_forward(
            query_kg, all_keys, all_values, row_index, row_segment, buckets, lengths, block, scale
        )
        attended = attended_kg.transpose(2, 0, 1, 3).reshape(rows, local_heads, HEAD_SIZE)
        mixed = (
            (attended * gate[:, :, None])
            .astype(jnp.bfloat16)
            .reshape(rows, local_heads * HEAD_SIZE)
        )
        hidden = current + lax.psum(
            jnp.dot(mixed, w_output, preferred_element_type=jnp.float32).astype(jnp.bfloat16), "kv"
        ).astype(jnp.float32)
        scale_f = rms_scale(hidden)
        normal_f = hidden * scale_f
        inner = (normal_f * gain_f).astype(jnp.bfloat16)
        gated = jnp.dot(inner, w_gate, preferred_element_type=jnp.float32)
        upward = jnp.dot(inner, w_up, preferred_element_type=jnp.float32)
        sigma = jax.nn.sigmoid(gated)
        swish = gated * sigma
        product = (swish * upward).astype(jnp.bfloat16)
        output = hidden + lax.psum(
            jnp.dot(product, w_down, preferred_element_type=jnp.float32).astype(jnp.bfloat16), "kv"
        ).astype(jnp.float32)
        results.append(output.astype(jnp.bfloat16))
        grad_out = cotangent[batch].astype(jnp.float32)
        grad_low = grad_out.astype(jnp.bfloat16)
        sum_down = sum_down + outer_sum(product, grad_low)
        grad_product = times_transpose(grad_low, w_down)
        grad_gated = (grad_product * upward * sigma * (1.0 + gated * (1.0 - sigma))).astype(
            jnp.bfloat16
        )
        grad_upward = (grad_product * swish).astype(jnp.bfloat16)
        sum_gate = sum_gate + outer_sum(inner, grad_gated)
        sum_upward = sum_upward + outer_sum(inner, grad_upward)
        grad_inner = lax.psum(
            (times_transpose(grad_gated, w_gate) + times_transpose(grad_upward, w_up)).astype(
                jnp.bfloat16
            ),
            "kv",
        ).astype(jnp.float32)
        sum_feedforward_gain = sum_feedforward_gain + jnp.sum(grad_inner * normal_f, axis=0)
        grad_hidden = grad_out + norm_backward(grad_inner * gain_f, normal_f, scale_f)
        grad_branch = grad_hidden.astype(jnp.bfloat16)
        sum_output = sum_output + outer_sum(mixed, grad_branch)
        grad_mixed = times_transpose(grad_branch, w_output).reshape(rows, local_heads, HEAD_SIZE)
        grad_heads = (grad_mixed * gate[:, :, None]).astype(jnp.bfloat16)
        grad_logits = (jnp.sum(grad_mixed * attended, axis=-1) * gate * (1.0 - gate)).astype(
            jnp.bfloat16
        )
        back_keys = lax.all_gather(key_rot, "seq", axis=0, tiled=True)
        back_values = lax.all_gather(value_low, "seq", axis=0, tiled=True)
        grad_kg = grad_heads.reshape(rows, local_groups, group, HEAD_SIZE).transpose(1, 2, 0, 3)
        delta = jnp.sum(grad_kg.astype(jnp.float32) * attended_kg, axis=-1)
        grad_query_kg, grad_keys, grad_values = attention_backward(
            query_kg,
            grad_kg,
            log_total,
            delta,
            back_keys,
            back_values,
            row_index,
            row_segment,
            buckets,
            lengths,
            block,
            scale,
        )
        local_keys, local_values = (
            lax.psum_scatter(
                grad_keys.astype(jnp.bfloat16), "seq", scatter_dimension=0, tiled=True
            ).astype(jnp.float32),
            lax.psum_scatter(
                grad_values.astype(jnp.bfloat16), "seq", scatter_dimension=0, tiled=True
            ).astype(jnp.float32),
        )
        grad_query_rot = grad_query_kg.transpose(2, 0, 1, 3).reshape(rows, local_heads, HEAD_SIZE)
        grad_query_norm = rotate_backward(grad_query_rot, cosine, sine)
        sum_query_gain = sum_query_gain + jnp.sum(grad_query_norm * query_normal, axis=(0, 1))
        grad_query = (
            norm_backward(grad_query_norm * gain_query, query_normal, query_scale)
            .astype(jnp.bfloat16)
            .reshape(rows, local_heads * HEAD_SIZE)
        )
        grad_key_norm = rotate_backward(local_keys, cosine, sine)
        sum_key_gain = sum_key_gain + jnp.sum(grad_key_norm * key_normal, axis=(0, 1))
        grad_key = (
            norm_backward(grad_key_norm * gain_key, key_normal, key_scale)
            .astype(jnp.bfloat16)
            .reshape(rows, local_groups * HEAD_SIZE)
        )
        grad_value = local_values.astype(jnp.bfloat16).reshape(rows, local_groups * HEAD_SIZE)
        sum_query = sum_query + outer_sum(normed_input, grad_query)
        sum_key = sum_key + outer_sum(normed_input, grad_key)
        sum_value = sum_value + outer_sum(normed_input, grad_value)
        sum_headgate = sum_headgate + outer_sum(normed_input, grad_logits)
        grad_partial = (
            times_transpose(grad_query, w_query)
            + times_transpose(grad_key, key_projection_weight)
            + times_transpose(grad_value, value_projection_weight)
            + times_transpose(grad_logits, w_head)
        )
        grad_normed = lax.psum(grad_partial.astype(jnp.bfloat16), "kv").astype(jnp.float32)
        sum_attention_gain = sum_attention_gain + jnp.sum(grad_normed * normal_a, axis=0)
        grad_input = grad_hidden + norm_backward(grad_normed * gain_a, normal_a, scale_a)
        input_grads.append(grad_input.astype(jnp.bfloat16))
    (
        attention_total,
        feedforward_total,
        query_total,
        key_total,
        value_total,
        headgate_total,
        output_total,
        gate_total,
        upward_total,
        down_total,
    ) = (
        lax.psum_scatter(
            sum_attention_gain.astype(jnp.bfloat16), "seq", scatter_dimension=0, tiled=True
        ).astype(jnp.float32),
        lax.psum_scatter(
            sum_feedforward_gain.astype(jnp.bfloat16), "seq", scatter_dimension=0, tiled=True
        ).astype(jnp.float32),
        lax.psum_scatter(
            sum_query.astype(jnp.bfloat16), "seq", scatter_dimension=0, tiled=True
        ).astype(jnp.float32),
        lax.psum_scatter(
            sum_key.astype(jnp.bfloat16), "seq", scatter_dimension=0, tiled=True
        ).astype(jnp.float32),
        lax.psum_scatter(
            sum_value.astype(jnp.bfloat16), "seq", scatter_dimension=0, tiled=True
        ).astype(jnp.float32),
        lax.psum_scatter(
            sum_headgate.astype(jnp.bfloat16), "seq", scatter_dimension=0, tiled=True
        ).astype(jnp.float32),
        lax.psum_scatter(
            sum_output.astype(jnp.bfloat16), "seq", scatter_dimension=1, tiled=True
        ).astype(jnp.float32),
        lax.psum_scatter(
            sum_gate.astype(jnp.bfloat16), "seq", scatter_dimension=0, tiled=True
        ).astype(jnp.float32),
        lax.psum_scatter(
            sum_upward.astype(jnp.bfloat16), "seq", scatter_dimension=0, tiled=True
        ).astype(jnp.float32),
        lax.psum_scatter(
            sum_down.astype(jnp.bfloat16), "seq", scatter_dimension=1, tiled=True
        ).astype(jnp.float32),
    )
    query_gain_total, key_gain_total = lax.psum((sum_query_gain, sum_key_gain), ("seq", "kv"))
    return (
        jnp.stack(results, axis=0),
        jnp.stack(input_grads, axis=0),
        attention_total,
        feedforward_total,
        query_gain_total,
        key_gain_total,
        query_total,
        key_total,
        value_total,
        headgate_total,
        output_total,
        gate_total,
        upward_total,
        down_total,
    )


BF = jnp.bfloat16
F32 = jnp.float32
ANY = pl.BlockSpec(memory_space=pl.ANY)
VM = pl.BlockSpec(memory_space=pltpu.VMEM)
DMA = pltpu.SemaphoreType.DMA


def place():
    s = lax.axis_index("seq")
    k = lax.axis_index("kv")
    return (lax.div(s, 2), lax.rem(s, 2), lax.div(k, 2), lax.rem(k, 2))


def device(l, x, y, c):
    return (l * 2 + x, y * 2 + c)


def remote(src, dst, send, recv, target):
    return pltpu.make_async_remote_copy(
        src_ref=src,
        dst_ref=dst,
        send_sem=send,
        recv_sem=recv,
        device_id=target,
        device_id_type=pl.DeviceIdType.MESH,
    )


def greet(partners):
    barrier = pltpu.get_barrier_semaphore()
    count = 0
    for target, there in partners:

        def call(target=target):
            pl.semaphore_signal(
                barrier, inc=1, device_id=target, device_id_type=pl.DeviceIdType.MESH
            )

        if there is None:
            call()
            count = count + 1
        else:
            pl.when(there)(call)
            count = count + jnp.where(there, 1, 0)
    pl.semaphore_wait(barrier, count)


class Line:
    def __init__(self, length, g, ag_send, ag_recv, land=None, rs_send=None, rs_recv=None):
        self.n = length
        self.g, self.ag_send, self.ag_recv = g, ag_send, ag_recv
        self.land, self.rs_send, self.rs_recv = land, rs_send, rs_recv
        self.l, self.x, self.y, self.c = place()

    def partners(self):
        l, x, y, c = self.l, self.x, self.y, self.c
        return [
            (device(l - 1, x, y, c), l >= 1),
            (device(l + 1, x, y, c), l <= self.n - 2),
        ]

    def block(self, item, b):
        return self.g.at[item, pl.ds(2 * b, 2)]

    def _ag(self, item, way, b):
        step = -1 if way == 0 else 1
        return remote(
            self.block(item, b),
            self.block(item, b),
            self.ag_send.at[item, way, b],
            self.ag_recv.at[item, b],
            device(self.l + step, self.x, self.y, self.c),
        )

    def ag_start(self, item):
        l = self.l
        pl.when(l >= 1)(lambda: self._ag(item, 0, l).start())
        pl.when(l <= self.n - 2)(lambda: self._ag(item, 1, l).start())

    def ag_half(self, item, x, src):
        l, n = self.l, self.n

        def half(way):
            step = -1 if way == 0 else 1
            return remote(
                src,
                self.g.at[item, 2 * l + x],
                self.ag_send.at[item, way, l],
                self.ag_recv.at[item, l],
                device(l + step, self.x, self.y, self.c),
            )

        pl.when(l >= 1)(lambda: half(0).start())
        pl.when(l <= n - 2)(lambda: half(1).start())

    def ag_left(self, item):
        pl.when(self.l >= 1)(lambda: self._ag(item, 0, self.l).start())

    def ag_right(self, item, plane):
        pl.when(self.l == plane)(lambda: self._ag(item, 1, self.l).start())

    def ag_step(self, item, t):
        l, n = self.l, self.n

        @pl.when(l + t <= n - 1)
        def _():
            self._ag(item, 0, l + t).wait_recv()
            pl.when(l >= 1)(lambda: self._ag(item, 0, l + t).start())

        @pl.when(l - t >= 0)
        def _():
            self._ag(item, 1, l - t).wait_recv()
            pl.when(l <= n - 2)(lambda: self._ag(item, 1, l - t).start())

    def pump(self, item, t):
        l, n = self.l, self.n

        @pl.when((l + t <= n - 1) & (l >= 1))
        def _():
            self._ag(item, 0, l + t).wait_recv()
            self._ag(item, 0, l + t).start()

        @pl.when((l - t >= 0) & (l <= n - 2))
        def _():
            self._ag(item, 1, l - t).wait_recv()
            self._ag(item, 1, l - t).start()

    def collect(self, item):
        l, n = self.l, self.n
        for t in range(1, n):
            pl.when(l == 0)(lambda t=t: self._ag(item, 0, t).wait_recv())
            pl.when(l == n - 1)(lambda t=t: self._ag(item, 1, n - 1 - t).wait_recv())

    def ag_end(self, item):
        l, n = self.l, self.n
        for b in range(n):
            pl.when((l >= 1) & (l <= b))(lambda b=b: self._ag(item, 0, b).wait_send())
            pl.when((l <= n - 2) & (l >= b))(lambda b=b: self._ag(item, 1, b).wait_send())

    @staticmethod
    def seat(item):
        return item + 3 if item < 3 else item

    @staticmethod
    def berth(item):
        return item + 3 if item < 3 else (item - 3) % 6

    def sum_block(self, item, b):
        return self.g.at[self.seat(item), pl.ds(2 * b, 2)]

    def _slot(self, item, slot):
        return self.land.at[self.berth(item), pl.ds(2 * slot, 2)]

    def _rs(self, item, way, o):
        if way == 0:
            target = self.l - 1
            slot = jnp.where(target == o, self.n, o)
        else:
            target = self.l + 1
            slot = o
        return remote(
            self.sum_block(item, o),
            self._slot(item, slot),
            self.rs_send.at[item, way, o],
            self.rs_recv.at[item, slot],
            device(target, self.x, self.y, self.c),
        )

    def _take(self, item, o, slot):
        here = self._slot(item, slot)
        pltpu.make_async_copy(here, here, self.rs_recv.at[item, slot]).wait()
        seat, berth = self.seat(item), self.berth(item)
        for h in range(2):
            total = self.g[seat, 2 * o + h].astype(F32) + self.land[berth, 2 * slot + h].astype(F32)
            self.g[seat, 2 * o + h] = total.astype(BF)

    def rs_fire(self, item, first=0, last=3):
        l, n = self.l, self.n
        for o in range(n - 1 - first, n - 1 - last, -1):
            pl.when(l == 0)(lambda o=o: self._rs(item, 1, o).start())
            pl.when(l == n - 1)(lambda o=o: self._rs(item, 0, n - 1 - o).start())

    def rs_near(self, item, plane):
        l, n = self.l, self.n
        way = 1 if plane == 1 else 0
        owners = range(n - 1, 1, -1) if plane == 1 else range(n - 2)

        @pl.when(l == plane)
        def _():
            for o in owners:
                self._take(item, o, o)
                self._rs(item, way, o).start()

    def rs_far(self, item, plane):
        l, n = self.l, self.n
        way, o = (0, 0) if plane == 1 else (1, n - 1)

        @pl.when(l == plane)
        def _():
            self._take(item, o, o)
            self._rs(item, way, o).start()

    def rs_final(self, item):
        l, n = self.l, self.n
        pl.when(l >= 1)(lambda: self._take(item, l, l))
        pl.when(l <= n - 2)(lambda: self._take(item, l, n))

    def rs_end(self, item):
        l, n = self.l, self.n
        for o in range(n):
            pl.when(l < o)(lambda o=o: self._rs(item, 1, o).wait_send())
            pl.when(l > o)(lambda o=o: self._rs(item, 0, o).wait_send())


def each(count, body):
    def step(i, unused):
        body(i)
        return 0

    lax.fori_loop(0, count, step, 0)


class Pair:
    def __init__(self, line, refs, send, recv, local, half):
        self.line, self.refs = line, refs
        self.send, self.recv, self.local, self.half = send, recv, local, half

    def partner(self):
        line = self.line
        return (device(line.l, 1 - line.x, line.y, line.c), None)

    def _part(self, ref, kind, j, x):
        at = pl.multiple_of(x * self.half + j * 256, 256)
        return ref.at[pl.ds(at, 256), :] if kind == 2 else ref.at[:, pl.ds(at, 256)]

    def _pieces(self, block, item, kind, j, x):
        ref = self.refs[kind]
        if not isinstance(ref, tuple):
            return [(self._part(ref, kind, j, x), block, item)]
        at = pl.ds(pl.multiple_of(x * (self.half // 2 if item == 1 else self.half) + j * 128, 128), 128)
        return [
            (one.at[:, at], block.at[:, pl.ds(128 * i, 128)], item + 12 * i)
            for i, one in enumerate(ref)
        ]

    def _copies(self, item, kind, j):
        line = self.line
        mine = line.g.at[item, 2 * line.l + line.x]
        away = self._pieces(mine, item, kind, j, 1 - line.x)
        stay = self._pieces(mine, item, kind, j, line.x)
        pairs = []
        for (src, block, sem), (own, unused, unused2) in zip(away, stay):
            out = remote(src, block, self.send.at[sem], self.recv.at[sem], self.partner()[0])
            here = pltpu.make_async_copy(own, block, self.local.at[sem])
            pairs.append((out, here))
        return pairs

    def start(self, item, kind, j):
        for out, here in self._copies(item, kind, j):
            out.start()
            here.start()

    def end(self, item, kind, j):
        for out, here in self._copies(item, kind, j):
            here.wait()
            out.wait_send()
            out.wait_recv()


class Back(Pair):
    def _copies(self, item, kind, j):
        line = self.line
        seat = line.seat(item)
        away = self._pieces(line.g.at[seat, 2 * line.l + 1 - line.x], item, kind, j, line.x)
        stay = self._pieces(line.g.at[seat, 2 * line.l + line.x], item, kind, j, line.x)
        pairs = []
        for (home, block, sem), (unused, own, unused2) in zip(away, stay):
            out = remote(block, home, self.send.at[sem], self.recv.at[sem], self.partner()[0])
            here = pltpu.make_async_copy(own, home, self.local.at[sem])
            pairs.append((out, here))
        return pairs

    def end(self, item, kind, j):
        line = self.line
        block = line.g.at[line.seat(item), 2 * line.l]
        there = self._pieces(block, item, kind, j, 1 - line.x)
        for (out, here), (home, unused, sem) in zip(self._copies(item, kind, j), there):
            here.wait()
            out.wait_send()
            pltpu.make_async_copy(home, home, self.recv.at[sem]).wait()


def dot(a, b):
    return lax.dot_general(a, b, (((1,), (0,)), ((), ())), preferred_element_type=F32)


def dot_t(a, b):
    return lax.dot_general(a, b, (((1,), (1,)), ((), ())), preferred_element_type=F32)


def layer_kernel(
    n,
    x_any,
    z_any,
    wq,
    wk,
    wv,
    wo,
    wg,
    wu,
    wd,
    small,
    sizes,
    lengths,
    res_out,
    grad_out,
    dq_out,
    dk_out,
    dv_out,
    do_out,
    dgw,
    duw,
    ddw,
    sums_out,
    late_out,
    normed_out,
    dz_out,
    x_v,
    normed,
    normed_t,
    g,
    small_g,
    gain_row,
    heads_row,
    kv,
    q_v,
    qp,
    kp,
    gate_v,
    att,
    tot,
    part,
    core_land,
    low,
    chip_land,
    inner,
    hidden,
    land,
    d_low,
    prod_t,
    kv_land,
    d_hid,
    own_z,
    own_x,
    dl,
    dl_t,
    gain_sum,
    head_sum,
    sums,
    sum_c,
    sum_x,
    sum_y,
    sum_l,
    late,
    late_core,
    late_chip,
    late_l,
    cos_ref,
    sin_ref,
    row_range,
    free,
    done,
    p_send,
    p_recv,
    p_loc,
    ag_send,
    ag_recv,
    sp_sem,
    sa_send,
    sa_recv,
    t_send,
    t_recv,
    z_send,
    z_recv,
    kv_send,
    kv_recv,
    c_send,
    c_recv,
    s_send,
    s_recv,
    i_send,
    i_recv,
    j_send,
    j_recv,
    rs_send,
    rs_recv,
    b_send,
    b_recv,
    b_loc,
    d_send,
    d_recv,
    h_send,
    h_recv,
    h_loc,
    u_send,
    u_recv,
    o_loc,
):
    line = Line(n, g, ag_send, ag_recv, land, rs_send, rs_recv)
    l, x, y, c = line.l, line.x, line.y, line.c
    k = y * 2 + c
    group = Group()
    across, mate = device(l, 1 - x, y, c), group.mate
    right = device(l + 1, x, y, c)
    tiny = Line(n, small_g, sa_send, sa_recv)
    scale = HEAD_SIZE ** (-0.5)
    width = 256 * 2 * n
    back = Back(line, ((dgw, duw), (dgw, duw), ddw), b_send, b_recv, b_loc, 768)
    back_first = Back(line, (dq_out, (dk_out, dv_out), do_out), b_send, b_recv, b_loc, 256)
    left = device(l - 1, x, y, c)
    blocks = 2 * n
    first = Pair(line, (wq, (wk, wv), wo), p_send, p_recv, p_loc, 256)
    rest = Pair(line, ((wg, wu), (wg, wu), wd), p_send, p_recv, p_loc, 768)

    def half_of(item):
        chunk = item // 3 - 1
        return chunk if item % 3 == 2 else 2 * chunk + item % 3

    def swap(item):
        if item < 3:
            return first, item, item, 0
        return rest, item, item % 3, half_of(item)

    def swap_start(item):
        pair, item, kind, j = swap(item)
        pair.start(item, kind, j)

    def swap_end(item):
        pair, item, kind, j = swap(item)
        pair.end(item, kind, j)

    used = iter(range(16))

    def put(src, dst):
        copy = pltpu.make_async_copy(src, dst, o_loc.at[next(used)])
        copy.start()
        return copy

    others = [device(lax.rem(l + d, n), x, y, c) for d in range(1, n)]
    greet(
        [(o, None) for o in others] + [(mate, None)] + [(group.chip(i), None) for i in (1, 2, 3)]
    )

    small_here = small_g.at[0, 2 * l + x]
    small_out_copy = remote(small, small_here, sp_sem.at[0], sp_sem.at[1], across)
    small_own = pltpu.make_async_copy(small, small_here, sp_sem.at[2])
    swap_start(0)
    line.ag_half(0, x, first._part(wq, 0, 0, x))
    small_out_copy.start()
    small_own.start()
    swap_start(1)
    swap_start(2)
    x_here = pltpu.make_async_copy(x_any, x_v.at[:, x], t_send.at[2])
    x_here.start()
    halves = pl.ds(2 * c, 2)
    x_out = remote(x_any.at[halves], x_v.at[halves, x], t_send.at[0], t_recv.at[0], across)
    x_part = x_v.at[halves, 1 - x]
    x_on = remote(x_part, x_part, t_send.at[1], t_recv.at[1], mate)
    x_out.start()
    ffn_items = (5, 3, 4, 8, 6, 7, 11, 9, 10)
    for item in ffn_items:
        swap_start(item)
    z_out = remote(z_any.at[halves], dz_out.at[halves], z_send.at[0], z_recv.at[0], across)
    z_part = dz_out.at[halves]
    z_on = remote(z_part, z_part, z_send.at[1], z_recv.at[1], mate)
    z_out.start()

    swap_end(0)
    line.ag_half(0, 1 - x, g.at[0, 2 * l + 1 - x])
    small_own.wait()
    small_out_copy.wait()
    tiny.ag_start(0)
    swap_end(1)
    line.ag_start(1)
    for t in range(1, n):
        tiny.ag_step(0, t)
    line.pump(0, 1)
    line.pump(1, 1)
    swap_end(2)
    for s in range(2 * n):
        cols = slice(s * 256, (s + 1) * 256)
        heads_row[:, cols] = small_g[0, s]
        gain_row[:, cols] = small_g[0, s, 4:6, :].astype(F32)

    def norm(m, side):
        v = x_v[m, side].reshape(128, 256 * 2 * n).astype(F32)
        mean = jnp.mean(v * v, axis=-1, keepdims=True)
        v = v * lax.rsqrt(mean + EPS) * gain_row[0:1, :]
        normed[m, side] = v.astype(BF).reshape(2, 2, 32, 256 * 2 * n)

    def tables(m):
        i = l * 256 + lax.broadcasted_iota(jnp.int32, (256, 128), 0)
        lane = lax.broadcasted_iota(jnp.int32, (256, 128), 1)
        end = sizes[m, 0]
        start = jnp.zeros_like(i)
        valid = jnp.full_like(i, lengths[m, 0])
        for bucket in range(1, sizes.shape[1]):
            start = jnp.where(i >= end, end, start)
            valid = jnp.where(i >= end, lengths[m, bucket], valid)
            end = end + sizes[m, bucket]
        row_range[m] = jnp.where(lane == 0, start, jnp.minimum(i + 1, start + valid))
        steps = (lane & 63).astype(F32) * (2.0 / HEAD_SIZE)
        angle = (i - start).astype(F32) * jnp.exp(-steps * math.log(ROPE_BASE))
        cos_ref[m] = jnp.cos(angle)
        sin_ref[m] = jnp.sin(angle) * jnp.where(lane < 64, -1.0, 1.0)

    x_here.wait()
    each(4, lambda m: norm(m, x))
    line.pump(0, 2)
    line.pump(1, 2)
    line.ag_start(2)
    each(4, tables)
    x_out.wait_recv()
    x_on.start()
    line.pump(2, 1)
    for item in ffn_items[:2]:
        swap_end(item)
        line.ag_left(item)
    x_on.wait_recv()
    each(4, lambda m: norm(m, 1 - x))
    for item in (0, 1):
        line.collect(item)

    def project(m):
        a = normed[m].reshape(256, 256 * 2 * n)
        qf = dot(a, g[0].reshape(256 * 2 * n, 256))
        kf = dot(a, g[1].reshape(256 * 2 * n, 256))
        gate_v[m] = jax.nn.sigmoid(dot_t(a, heads_row[...]))
        qp[m] = qf
        kp[m] = kf[:, :128]
        cosine, sine = cos_ref[m], sin_ref[m]

        def turn(u, gain):
            u = u * lax.rsqrt(jnp.mean(u * u, axis=-1, keepdims=True) + EPS) * gain
            return (u * cosine + pltpu.roll(u, 64, 1) * sine).astype(BF)

        gains = small[8:10, :128].astype(F32)
        q_v[m, :256] = turn(qf[:, :128], gains[0:1])
        q_v[m, 256:] = turn(qf[:, 128:], gains[0:1])
        kv[l, m, :, :128] = turn(kf[:, :128], gains[1:2])
        kv[l, m, :, 128:] = kf[:, 128:].astype(BF)

    def send_kv(b, m):
        return remote(kv.at[b, m], kv.at[b, m], kv_send.at[b, m], kv_recv.at[b, m], right)

    each(4, project)
    z_copy = put(z_any.at[:, k], own_z)
    x_copy = put(x_any.at[:, k], own_x)

    def attend(m, b, diagonal):
        pair = kv[b, m]
        raw = dot_t(q_v[m], pair[:, :128]) * scale
        lo = row_range[m][:, :1] - b * 256
        hi = row_range[m][:, 1:2] - b * 256
        column = lax.broadcasted_iota(jnp.int32, (512, 256), 1)
        allowed = (column >= jnp.concatenate([lo, lo], axis=0)) & (
            column < jnp.concatenate([hi, hi], axis=0)
        )
        e = jnp.where(allowed, jnp.exp(raw), 0.0)
        total = jnp.sum(e, axis=-1, keepdims=True)
        value = dot(e.astype(BF), pair[:, 128:])
        total = jnp.broadcast_to(total, (512, 128))
        if diagonal:
            tot[m] = total
            att[m] = value
        else:
            tot[m] += total
            att[m] += value

    line.pump(2, 2)

    def turned(i):
        m, s = lax.div(i, 2 * n), lax.rem(i, 2 * n)
        tile = normed[m, :, :, :, :, pl.ds(pl.multiple_of(s * 256, 256), 256)].reshape(256, 256)
        normed_t[s, :, pl.ds(pl.multiple_of(m * 256, 256), 256)] = tile.T

    def branch(m):
        total = tot[m]
        lse = jnp.log(total)
        value = att[m] / total
        att[m] = value
        tot[m] = lse
        gates = gate_v[m]
        lo, hi = gates[:, 0:2], gates[:, 2:4]
        gates = jnp.where(x == 0, lo, hi)
        mixed = jnp.concatenate(
            [value[:256] * gates[:, 0:1], value[256:] * gates[:, 1:2]], axis=1
        ).astype(BF)
        for s in range(2 * n):
            part[m, :, :, :, :, s * 256 : (s + 1) * 256] = (
                dot(mixed, g[2, s]).astype(BF).reshape(2, 2, 2, 32, 256)
            )
        mate_copy(m).start()

    sources = (part, normed, part, normed)

    def mate_place(m, r):
        return x_v.at[m, :, pl.ds(0, 2)] if r == 2 else core_land.at[m]

    def chip_place(m, o, r):
        return x_v.at[m, (o - 1) // 2, 2 + (o - 1) % 2] if r == 2 else chip_land.at[o - 1, m]

    def mate_copy(m, r=0):
        return remote(
            sources[r].at[m, :, :, 1 - c], mate_place(m, r), c_send.at[r, m], c_recv.at[r, m], mate
        )

    def chip_copy(m, o, r=0):
        ox, oy = group.other(o)
        return remote(
            low.at[m, ox, oy],
            chip_place(m, o, r),
            s_send.at[r, m, o - 1],
            s_recv.at[r, m, o - 1],
            group.chip(o),
        )

    def to_chips(m, r=0):
        mate_copy(m, r).wait_recv()
        for u in range(2):
            for v in range(2):
                there = x_v[m, u, v] if r == 2 else core_land[m, u, v]
                low[m, u, v] = (sources[r][m, u, v, c].astype(F32) + there.astype(F32)).astype(BF)
        for o in (3, 1, 2):
            chip_copy(m, o, r).start()

    def total_of(m, r=0):
        total = low[m, x, y].astype(F32)
        for o in (1, 2, 3):
            chip_copy(m, o, r).wait_recv()
            there = x_v[m, (o - 1) // 2, 2 + (o - 1) % 2] if r == 2 else chip_land[o - 1, m]
            total = total + there.astype(F32)
        return total

    def sum_end(m, r=0):
        mate_copy(m, r).wait_send()
        for o in (1, 2, 3):
            chip_copy(m, o, r).wait_send()

    def ahead(m):
        pl.when(l <= n - 2)(lambda: send_kv(l, m).start())
        attend(m, l, True)

        def step(t, unused):
            b = l - t
            send_kv(b, m).wait_recv()
            pl.when(l <= n - 2)(lambda: send_kv(b, m).start())
            attend(m, b, False)
            return 0

        lax.fori_loop(1, l + 1, step, 0)

    for m in range(4):
        ahead(m)
        if m == 0:
            each(8 * n, turned)
            line.collect(2)
            normed_copy = put(normed_t, normed_out)
        branch(m)
        if m > 0:
            to_chips(m - 1)
        for item in ffn_items[2 + 2 * m : 4 + 2 * m]:
            swap_end(item)
            line.ag_left(item)
    to_chips(3)
    for item in ffn_items:
        line.ag_right(item, 0)
    for item in (5, 3, 4):
        line.ag_right(item, 1)
    for item in (5, 3):
        line.ag_right(item, 2)
    for item in (5, 3):
        line.pump(item, 1)

    def inner_copy(m, o, r=0):
        here = inner.at[m, x, y, c]
        return remote(
            here, here, i_send.at[r, m, o - 1], i_recv.at[r, m, o - 1], group.chip(o)
        )

    def inner_mate(m, o, r=0):
        ox, oy = group.other(o)
        there = inner.at[m, ox, oy, c]
        return remote(there, there, j_send.at[r, m, o], j_recv.at[r, m, o], mate)

    def finish(m):
        h = x_v[m, x, k].astype(F32) + total_of(m)
        hidden[m] = h
        mean = jnp.mean(h * h, axis=-1, keepdims=True)
        inner[m, x, y, c] = (h * lax.rsqrt(mean + EPS) * gain_row[1:2, :]).astype(BF)
        for o in (3, 1, 2):
            inner_copy(m, o).start()
        inner_mate(m, 0).start()

    each(4, finish)
    for item in (5, 3):
        line.pump(item, 2)
    line.ag_right(4, 2)
    line.pump(4, 1)
    z_out.wait_recv()
    z_on.start()

    def pass_on(m, r=0):
        for o in (1, 2, 3):
            inner_copy(m, o, r).wait_recv()
            inner_mate(m, o, r).start()

    each(4, pass_on)
    line.pump(4, 2)
    for item in (8, 6, 7):
        line.ag_right(item, 1)
    for item in (8, 6):
        line.ag_right(item, 2)
    for item in (8, 6):
        line.pump(item, 1)
    x_out.wait_send()
    x_on.wait_send()
    z_on.wait_recv()
    dz_own = pltpu.make_async_copy(z_any, x_v.at[:, x], z_send.at[2])
    dz_other = pltpu.make_async_copy(dz_out, x_v.at[:, 1 - x], z_send.at[3])
    dz_own.start()
    dz_other.start()

    def arrive(m, r=0):
        for o in range(4):
            inner_mate(m, o, r).wait_recv()

    def spread_end(m, r=0):
        for o in (1, 2, 3):
            inner_copy(m, o, r).wait_send()
        for o in range(4):
            inner_mate(m, o, r).wait_send()

    each(4, arrive)
    normed_copy.wait()

    def turn_inner(i):
        m, s = lax.div(i, 2 * n), lax.rem(i, 2 * n)
        tile = inner[m, :, :, :, :, pl.ds(pl.multiple_of(s * 256, 256), 256)].reshape(256, 256)
        normed_t[s, :, pl.ds(pl.multiple_of(m * 256, 256), 256)] = tile.T

    each(8 * n, turn_inner)
    each(4, sum_end)
    each(4, spread_end)

    def kv_sent(m):
        for b in range(n):
            pl.when((l >= b) & (l <= n - 2))(lambda b=b: send_kv(b, m).wait_send())

    each(4, kv_sent)
    dz_own.wait()
    dz_other.wait()

    def compute(j, h):
        pair_of, down_of = 3 * j + 3 + h, 3 * j + 5
        here = slice(128 * h, 128 * h + 128)

        def rows(m, unused):
            a = inner[m].reshape(256, width)
            d = x_v[m].reshape(256, width)
            both = dot(a, g[pair_of].reshape(width, 256))
            gated, upward = both[:, :128], both[:, 128:]
            grad = dot_t(d[:, :256], g[down_of, 0, here])
            for s in range(1, 2 * n):
                grad = grad + dot_t(d[:, s * 256 : (s + 1) * 256], g[down_of, s, here])
            sigma = jax.nn.sigmoid(gated)
            swish = gated * sigma
            product = (swish * upward).astype(BF)
            d_both = jnp.concatenate(
                [grad * upward * sigma * (1.0 + gated * (1.0 - sigma)), grad * swish], axis=1
            ).astype(BF)
            at = pl.ds(pl.multiple_of(m * 256, 256), 256)
            d_low[0, at] = d_both
            prod_t[:128, at] = product.T
            for s in range(2 * n):
                cols = slice(s * 256, (s + 1) * 256)
                o = dot(product, g[down_of, s, here])
                i = dot_t(d_both, g[pair_of, s])
                if j + h > 0:
                    o = o + part[m, :, :, :, :, cols].reshape(256, 256).astype(F32)
                    i = i + normed[m, :, :, :, :, cols].reshape(256, 256).astype(F32)
                part[m, :, :, :, :, cols] = o.astype(BF).reshape(2, 2, 2, 32, 256)
                normed[m, :, :, :, :, cols] = i.astype(BF).reshape(2, 2, 2, 32, 256)
            return 0

        lax.fori_loop(0, 4, rows, 0)

        def weights(s):
            g[pair_of, s] = dot(normed_t[s], d_low[0]).astype(BF)
            z = x_v[:, :, :, :, pl.ds(pl.multiple_of(s * 256, 256), 256)].reshape(1024, 256)
            g[down_of, s, here] = dot(prod_t[:128], z).astype(BF)

        each(2 * n, weights)

    def backward(item):
        if item < 3:
            return back_first, item, item, 0
        return back, item, item % 3, half_of(item)

    def near(*items):
        for item in items:
            line.rs_near(item, 1)
            line.rs_near(item, n - 2)

    def far(*items):
        for item in items:
            line.rs_far(item, 1)
            line.rs_far(item, n - 2)

    def send_home(item):
        way, item, kind, j = backward(item)
        way.start(item, kind, j)

    inside = (l >= 1) & (l <= n - 2)

    def final_in(item):
        pl.when(inside)(lambda: line.rs_final(item))

    def final_end(item):
        pl.when(jnp.logical_not(inside))(lambda: line.rs_final(item))

    def ready(*items):
        for item in items:
            line.collect(item)
            line.ag_end(item)

    def free_give(i):
        def tell(target):
            pl.semaphore_signal(
                free.at[i], inc=1, device_id=target, device_id_type=pl.DeviceIdType.MESH
            )

        pl.when(l == 1)(lambda: tell(device(l - 1, x, y, c)))
        pl.when(l == n - 2)(lambda: tell(device(l + 1, x, y, c)))

    def done_give(i):
        def tell(target):
            pl.semaphore_signal(
                done.at[i], inc=1, device_id=target, device_id_type=pl.DeviceIdType.MESH
            )

        pl.when(l == 0)(lambda: tell(device(l + 1, x, y, c)))
        pl.when(l == n - 1)(lambda: tell(device(l - 1, x, y, c)))

    def done_take(i):
        pl.when(inside)(lambda: pl.semaphore_wait(done.at[i], 1))

    def free_take(i):
        pl.when(jnp.logical_not(inside))(lambda: pl.semaphore_wait(free.at[i], 1))

    ready(5, 3)
    compute(0, 0)
    line.rs_fire(3)
    for item in (8, 6):
        line.pump(item, 2)
    line.ag_right(7, 2)
    line.pump(7, 1)
    ready(4)
    compute(0, 1)
    line.rs_fire(4)
    line.rs_fire(5)
    line.pump(7, 2)
    for item in (11, 9, 10):
        line.ag_right(item, 1)
    for item in (11, 9):
        line.ag_right(item, 2)
    for item in (11, 9):
        line.pump(item, 1)
    near(3)
    ready(8, 6)
    compute(1, 0)
    line.rs_fire(6)
    for item in (11, 9):
        line.pump(item, 2)
    line.ag_right(10, 2)
    line.pump(10, 1)
    near(4)
    final_in(3)
    free_give(0)
    ready(7)
    compute(1, 1)
    line.rs_fire(7)
    line.rs_fire(8)
    line.pump(10, 2)
    near(5)
    far(3)
    final_in(4)
    free_give(1)
    near(6)
    final_in(5)
    free_give(2)
    far(4)
    ready(11, 9)
    compute(2, 0)
    free_take(0)
    line.rs_fire(9)
    ready(10)
    compute(2, 1)
    each(4, lambda m: mate_copy(m, 1).start())
    free_take(1)
    line.rs_fire(10)
    free_take(2)
    line.rs_fire(11, 0, 2)
    gain_sum[...] = jnp.zeros_like(gain_sum)
    head_sum[...] = jnp.zeros_like(head_sum)
    each(4, lambda m: to_chips(m, 1))
    near(7)
    far(5)
    final_in(6)
    far(6)
    near(8)
    line.rs_near(9, 1)
    z_copy.wait()
    x_copy.wait()
    normed_back_copy = put(normed_out, normed_t)

    def finish_hidden(m):
        total = total_of(m, 1)
        h = hidden[m]
        r = lax.rsqrt(jnp.mean(h * h, axis=-1, keepdims=True) + EPS)
        normal = h * r
        gain_sum[1:2] += jnp.sum(total * normal, axis=0, keepdims=True)
        e = total * gain_row[1:2, :]
        grad = own_z[m].astype(F32) + r * (
            e - normal * jnp.mean(e * normal, axis=-1, keepdims=True)
        )
        d_hid[m] = grad
        inner[m, x, y, c] = grad.astype(BF)
        for o in (3, 1, 2):
            inner_copy(m, o, 1).start()
        inner_mate(m, 0, 1).start()

    each(4, finish_hidden)
    each(4, lambda m: sum_end(m, 1))
    for item in (3, 4, 5):
        final_end(item)
        send_home(item)
    done_give(0)
    line.rs_near(9, 2)
    final_in(7)
    far(7)
    line.rs_near(10, 1)

    def attend_back(m):
        arrive(m, 1)
        d = inner[m].reshape(256, width)
        gm = dot_t(d[:, :256], g[2, 0])
        for s in range(1, blocks):
            gm = gm + dot_t(d[:, s * 256 : (s + 1) * 256], g[2, s])
        gates = gate_v[m]
        gates = jnp.where(x == 0, gates[:, 0:2], gates[:, 2:4])
        g0, g1 = gates[:, 0:1], gates[:, 1:2]
        a0, a1 = att[m, :256], att[m, 256:]
        d0, d1 = gm[:, :128], gm[:, 128:]
        l0 = jnp.sum(d0 * a0, axis=-1, keepdims=True) * g0 * (1.0 - g0)
        l1 = jnp.sum(d1 * a1, axis=-1, keepdims=True) * g1 * (1.0 - g1)
        lane = lax.broadcasted_iota(jnp.int32, (256, 128), 1)
        logits = jnp.where(lane == 2 * x, l0, 0.0) + jnp.where(lane == 2 * x + 1, l1, 0.0)
        logits = logits.astype(BF)
        dl[m] = logits
        at = pl.ds(pl.multiple_of(m * 256, 256), 256)
        dl_t[:, at] = logits.T[:16]
        mixed = jnp.concatenate([a0 * g0, a1 * g1], axis=1).astype(BF)
        prod_t[:, at] = mixed.T
        da = jnp.concatenate([d0 * g0, d1 * g1], axis=0).astype(BF)
        delta = jnp.sum(da.astype(F32) * att[m], axis=-1, keepdims=True)
        log_total = tot[m][:, :1]
        qm = q_v[m]
        att[m] = jnp.zeros((512, 128), F32)

        def block(b, unused):
            pair = kv[b, m]
            keys, values = pair[:, :128], pair[:, 128:]
            raw = dot_t(qm, keys) * scale
            lo = row_range[m][:, :1] - b * 256
            hi = row_range[m][:, 1:2] - b * 256
            column = lax.broadcasted_iota(jnp.int32, (512, 256), 1)
            allowed = (column >= jnp.concatenate([lo, lo], axis=0)) & (
                column < jnp.concatenate([hi, hi], axis=0)
            )
            p = jnp.where(allowed, jnp.exp(raw - log_total), 0.0)
            ds = (p * (dot_t(da, values) - delta)).astype(BF)
            att[m] += dot(ds, keys)
            dk = dot(ds.T, qm) * scale
            dv = dot(p.astype(BF).T, da)
            kv[b, m] = jnp.concatenate([dk, dv], axis=1).astype(BF)
            return 0

        lax.fori_loop(0, l + 1, block, 0)

    def kv_copy(b, m):
        return remote(
            kv.at[b, m], kv_land.at[b, m], d_send.at[b, m], d_recv.at[b, m], left
        )

    def kv_fire(m):
        for b in range(n - 1):
            pl.when(l == n - 1)(lambda b=b: kv_copy(b, m).start())

    def kv_step(m):
        for b in range(n - 2):

            @pl.when((l > b) & (l <= n - 2))
            def _(b=b):
                kv_copy(b, m).wait_recv()
                kv[b, m] = (kv[b, m].astype(F32) + kv_land[b, m].astype(F32)).astype(BF)
                kv_copy(b, m).start()

    def normal_back(u, d_rot, gain, cosine, sine):
        d = d_rot * cosine - pltpu.roll(d_rot, 64, 1) * sine
        r = lax.rsqrt(jnp.mean(u * u, axis=-1, keepdims=True) + EPS)
        normal = u * r
        e = d * gain
        grad = r * (e - normal * jnp.mean(e * normal, axis=-1, keepdims=True))
        return grad.astype(BF), jnp.sum(d * normal, axis=0, keepdims=True)

    gains = small[8:10, :128].astype(F32)

    def query_back(m):
        for h in range(2):
            cols = slice(h * 128, (h + 1) * 128)
            grad, total = normal_back(
                qp[m][:, cols],
                att[m, h * 256 : (h + 1) * 256] * scale,
                gains[0:1],
                cos_ref[m],
                sin_ref[m],
            )
            d_low[0, pl.ds(pl.multiple_of(m * 256, 256), 256), cols] = grad
            head_sum[0:1, :128] += total

    pass_on(0, 1)
    for m in range(4):
        attend_back(m)
        kv_fire(m)
        if m == 0:
            line.rs_near(10, 2)
        if m < 3:
            pass_on(m + 1, 1)
        if m == 2:
            each(4, lambda m: mate_copy(m, 2).start())
    line.rs_fire(11, 2, 3)
    each(4, lambda m: to_chips(m, 2))
    final_in(8)
    far(8)
    line.rs_near(11, 1)
    for item in (6, 7, 8):
        final_end(item)
        send_home(item)
    done_give(1)
    done_take(0)
    far(9)
    for item in (3, 4, 5):
        way, item, kind, j = backward(item)
        way.end(item, kind, j)
        line.rs_end(item)
    kv_step(0)
    each(4, query_back)
    kv_step(1)
    normed_back_copy.wait()

    def output_weights(s, unused):
        z = inner[:, :, :, :, :, pl.ds(pl.multiple_of(s * 256, 256), 256)].reshape(1024, 256)
        g[5, s] = dot(prod_t[...], z).astype(BF)
        return 0

    def query_weights(s, unused):
        g[3, s] = dot(normed_t[s], d_low[0]).astype(BF)
        sums[1, s] = dot_t(dl_t[...], normed_t[s])[:8]
        return 0

    lax.fori_loop(0, blocks, output_weights, 0)
    line.rs_fire(2)
    kv_step(2)
    lax.fori_loop(0, blocks, query_weights, 0)
    line.rs_fire(0)
    kv_step(3)
    line.rs_near(11, 2)
    line.rs_near(2, 1)
    line.rs_near(0, 1)
    far(10)

    def home(i, m, own, out):
        mine = out.at[m, k]
        there = out.at[m, (1 - y) * 2 + c]
        keep = pltpu.make_async_copy(own.at[m], mine, h_loc.at[i, m])
        over = remote(own.at[m], mine, h_send.at[i, m, 0], h_recv.at[i, m, 0], group.chip(2))
        beside = remote(own.at[m], mine, h_send.at[i, m, 1], h_recv.at[i, m, 1], mate)
        on = remote(there, there, h_send.at[i, m, 2], h_recv.at[i, m, 2], mate)
        return keep, over, beside, on

    homes = ((own_z, res_out), (own_x, grad_out))

    def home_start(i, m):
        for copy in home(i, m, *homes[i])[:3]:
            copy.start()

    def home_on(i, m):
        keep, over, beside, on = home(i, m, *homes[i])
        over.wait_recv()
        on.start()

    def home_end(i, m):
        keep, over, beside, on = home(i, m, *homes[i])
        keep.wait()
        over.wait_send()
        beside.wait()
        on.wait()

    def finish_out(m):
        own_z[m] = (hidden[m] + total_of(m, 2)).astype(BF)
        home_start(0, m)

    each(4, finish_out)
    each(4, lambda m: sum_end(m, 2))

    def key_back(m):
        pl.when(l <= n - 2)(lambda: kv_copy(l, m).wait_recv())
        pair = kv[l, m].astype(F32)
        pair = pair + jnp.where(l <= n - 2, kv_land[l, m].astype(F32), 0.0)
        grad, total = normal_back(kp[m], pair[:, :128], gains[1:2], cos_ref[m], sin_ref[m])
        at = pl.ds(pl.multiple_of(m * 256, 256), 256)
        d_low[1, at, :128] = grad
        d_low[1, at, 128:] = pair[:, 128:].astype(BF)
        head_sum[0:1, 128:] += total

    each(4, key_back)

    def key_weights(s, unused):
        g[4, s] = dot(normed_t[s], d_low[1]).astype(BF)
        return 0

    lax.fori_loop(0, blocks, key_weights, 0)
    line.rs_fire(1)

    def normed_back(m):
        at = pl.ds(pl.multiple_of(m * 256, 256), 256)
        a, b, e = d_low[0, at], d_low[1, at], dl[m][:, :16]
        for s in range(blocks):
            part = dot_t(a, g[0, s]) + dot_t(b, g[1, s]) + dot(e, small_g[0, s])
            normed[m, :, :, :, :, s * 256 : (s + 1) * 256] = part.astype(BF).reshape(
                2, 2, 2, 32, 256
            )
        mate_copy(m, 3).start()

    each(4, normed_back)
    far(11)
    for s in range(blocks):
        sums[0, s, 0:1] = gain_sum[1:2, s * 256 : (s + 1) * 256]
        sums[0, s, 1:2] = head_sum[0:1]
        sums[0, s, 2:8] = jnp.zeros((6, 256), F32)
    small_c = remote(sums.at[0], sum_c, u_send.at[0], u_recv.at[0], mate)
    small_x = remote(sums, sum_x, u_send.at[1], u_recv.at[1], group.chip(1))
    small_y = remote(sums.at[0], sum_y, u_send.at[2], u_recv.at[2], group.chip(2))
    small_c.start()
    each(4, lambda m: to_chips(m, 3))
    small_c.wait()
    sums[0] = sums[0] + sum_c[...]
    done_take(1)
    line.rs_far(2, 2)
    line.rs_near(2, 2)
    for item in (9, 10, 11):
        line.rs_final(item)
    line.rs_far(0, 2)
    line.rs_near(1, 1)

    def small_line(d):
        to = lax.rem(l + d, n)
        return remote(
            sums.at[:, pl.ds(2 * to, 2)],
            sum_l.at[l],
            u_send.at[2 + d],
            u_recv.at[2 + d],
            device(to, x, y, c),
        )

    def finish_grad(m):
        total = total_of(m, 3)
        v = own_x[m].astype(F32)
        r = lax.rsqrt(jnp.mean(v * v, axis=-1, keepdims=True) + EPS)
        normal = v * r
        gain_sum[0:1] += jnp.sum(total * normal, axis=0, keepdims=True)
        e = total * gain_row[0:1, :]
        own_x[m] = (
            d_hid[m] + r * (e - normal * jnp.mean(e * normal, axis=-1, keepdims=True))
        ).astype(BF)
        home_start(1, m)

    each(4, finish_grad)
    for s in range(blocks):
        late[s : s + 1] = gain_sum[0:1, s * 256 : (s + 1) * 256]
    late_c = remote(late, late_core, u_send.at[6], u_recv.at[6], mate)
    late_c.start()
    small_x.start()
    each(4, lambda m: home_on(0, m))
    for item in (9, 10, 11):
        send_home(item)
    line.rs_near(0, 2)
    line.rs_far(1, 2)
    line.rs_far(2, 1)
    line.rs_far(0, 1)
    late_c.wait()
    late[...] = late[...] + late_core[...]
    late_s = [
        remote(
            late, late_chip.at[x * 2 + y], u_send.at[6 + o], u_recv.at[6 + o], group.chip(o)
        )
        for o in (1, 2, 3)
    ]
    for copy in late_s:
        copy.start()
    late_chip[x * 2 + y] = late[...]
    small_x.wait()
    sums[...] = sums[...] + sum_x[...]
    small_y.start()
    each(4, lambda m: home_on(1, m))
    line.rs_near(1, 2)
    line.rs_far(1, 1)
    for copy in late_s:
        copy.wait()
    late[...] = late_chip[0] + late_chip[1] + late_chip[2] + late_chip[3]

    def late_line(d):
        to = lax.rem(l + d, n)
        return remote(
            late, late_l.at[l], u_send.at[9 + d], u_recv.at[9 + d], device(to, x, y, c)
        )

    for d in range(1, n):
        late_line(d).start()
    late_l[l] = late[...]
    small_y.wait()
    sums[0] = sums[0] + sum_y[...]
    for d in range(1, n):
        small_line(d).start()
    sum_l[l] = sums[:, pl.ds(2 * l, 2)]
    line.rs_final(2)
    send_home(2)
    line.rs_final(0)
    send_home(0)
    for d in range(1, n):
        small_line(d).wait()
    total = sum_l[0, :, x]
    for i in range(1, n):
        total = total + sum_l[i, :, x]
    sums_out[...] = total
    for d in range(1, n):
        late_line(d).wait()
    total = late_l[0]
    for i in range(1, n):
        total = total + late_l[i]
    late_out[...] = total
    line.rs_final(1)
    send_home(1)
    for item in (6, 7, 8, 9, 10, 11, 2, 0, 1):
        way, item, kind, j = backward(item)
        way.end(item, kind, j)
        line.rs_end(item)
    z_out.wait_send()
    z_on.wait_send()
    tiny.ag_end(0)
    each(3, line.ag_end)

    def drain(m):
        sum_end(m, 3)
        spread_end(m, 1)
        home_end(0, m)
        home_end(1, m)
        for b in range(n - 1):
            pl.when(l > b)(lambda b=b: kv_copy(b, m).wait_send())

    each(4, drain)


def layer(n, x_in, z_in, wq, wk, wv, wo, wg, wu, wd, small, sizes, lengths):
    d = x_in.shape[-1]
    m = 2 * n
    bf = lambda *shape: jax.ShapeDtypeStruct(shape, BF)
    vb = lambda *shape: pltpu.VMEM(shape, BF)
    vf = lambda *shape: pltpu.VMEM(shape, F32)
    return pl.pallas_call(
        functools.partial(layer_kernel, n),
        out_shape=(
            bf(4, 4, 32, d),
            bf(4, 4, 32, d),
            bf(256, 512),
            bf(256, 256),
            bf(256, 256),
            bf(512, 256),
            bf(256, 1536),
            bf(256, 1536),
            bf(1536, 256),
            jax.ShapeDtypeStruct((2, 8, 256), F32),
            jax.ShapeDtypeStruct((m, 256), F32),
            bf(m, 256, 1024),
            bf(4, 4, 32, d),
        ),
        in_specs=[ANY] * 9 + [VM] + [pl.BlockSpec(memory_space=pltpu.SMEM)] * 2,
        out_specs=(ANY,) * 9 + (VM,) * 2 + (ANY,) * 2,
        scratch_shapes=[
            vb(4, 2, 4, 32, d),
            vb(4, 2, 2, 2, 32, d),
            vb(m, 256, 1024),
            vb(12, m, 256, 256),
            vb(1, m, 16, 256),
            vf(2, d),
            vb(16, d),
            vb(n, 4, 256, 256),
            vb(4, 512, 128),
            vf(4, 256, 256),
            vf(4, 256, 128),
            vf(4, 256, 16),
            vf(4, 512, 128),
            vf(4, 512, 128),
            vb(4, 2, 2, 2, 32, d),
            vb(4, 2, 2, 32, d),
            vb(4, 2, 2, 32, d),
            vb(3, 4, 32, d),
            vb(4, 2, 2, 2, 32, d),
            vf(4, 32, d),
            vb(6, m + 2, 256, 256),
            vb(2, 1024, 256),
            vb(256, 1024),
            vb(n, 4, 256, 256),
            vf(4, 32, d),
            vb(4, 32, d),
            vb(4, 32, d),
            vb(4, 256, 128),
            vb(16, 1024),
            vf(2, d),
            vf(1, 256),
            vf(2, m, 8, 256),
            vf(m, 8, 256),
            vf(2, m, 8, 256),
            vf(m, 8, 256),
            vf(n, 2, 2, 8, 256),
            vf(m, 256),
            vf(m, 256),
            vf(4, m, 256),
            vf(n, m, 256),
            vf(4, 256, 128),
            vf(4, 256, 128),
            pltpu.VMEM((4, 256, 128), jnp.int32),
            pltpu.SemaphoreType.REGULAR((3,)),
            pltpu.SemaphoreType.REGULAR((2,)),
            DMA((24,)),
            DMA((24,)),
            DMA((24,)),
            DMA((12, 2, n)),
            DMA((12, n)),
            DMA((3,)),
            DMA((1, 2, n)),
            DMA((1, n)),
            DMA((3,)),
            DMA((2,)),
            DMA((4,)),
            DMA((2,)),
            DMA((n, 4)),
            DMA((n, 4)),
            DMA((4, 4)),
            DMA((4, 4)),
            DMA((4, 4, 3)),
            DMA((4, 4, 3)),
            DMA((2, 4, 3)),
            DMA((2, 4, 3)),
            DMA((2, 4, 4)),
            DMA((2, 4, 4)),
            DMA((12, 2, n)),
            DMA((12, n + 1)),
            DMA((24,)),
            DMA((24,)),
            DMA((24,)),
            DMA((n, 4)),
            DMA((n, 4)),
            DMA((2, 4, 3)),
            DMA((2, 4, 3)),
            DMA((2, 4)),
            DMA((9 + n,)),
            DMA((9 + n,)),
            DMA((16,)),
        ],
        compiler_params=pltpu.CompilerParams(
            collective_id=0, has_side_effects=True, vmem_limit_bytes=63 * 2**20
        ),
        name="layer",
    )(x_in, z_in, wq, wk, wv, wo, wg, wu, wd, small, sizes, lengths)

class Group:
    def __init__(self):
        self.l, self.x, self.y, self.c = place()
        self.mate = device(self.l, self.x, self.y, 1 - self.c)

    def other(self, i):
        x = 1 - self.x if i & 1 else self.x
        y = 1 - self.y if i & 2 else self.y
        return x, y

    def chip(self, i):
        x, y = self.other(i)
        return device(self.l, x, y, self.c)

    def partners(self):
        return [(self.mate, None)] + [(self.chip(i), None) for i in (1, 2, 3)]


def outputs_kernel(count, *refs):
    ins, small, outs = refs[:count], refs[count : count + 2], refs[count + 2 : 2 * count + 2]
    attention, feedforward, query, key, heads = refs[2 * count + 2 : 2 * count + 7]
    held = refs[2 * count + 7 : 3 * count + 7]
    wide = refs[3 * count + 7 : 4 * count + 5]
    in_sem, out_sem = refs[-2:]
    reads = [
        pltpu.make_async_copy(ins[i], held[i], in_sem.at[i]) for i in range(count)
    ]
    writes = [
        pltpu.make_async_copy(held[i] if i < 2 else wide[i - 2], outs[i], out_sem.at[i])
        for i in range(count)
    ]
    order = list(range(2, count)) + [0, 1]
    for i in order:
        reads[i].start()
    s = lax.axis_index("seq")
    sums, late = small
    row = lax.broadcasted_iota(jnp.int32, late.shape, 0)
    attention[...] = jnp.sum(jnp.where(row == s, late[...], 0.0), axis=0, keepdims=True)
    feedforward[...] = sums[0, 0:1]
    query[...] = sums[0, 1:2, :HEAD_SIZE]
    key[...] = sums[0, 1:2, HEAD_SIZE:]
    heads[...] = sums[1].T[:, :4]
    for i in order:
        reads[i].wait()
        if i >= 2:
            src, dst = held[i], wide[i - 2]

            def widen(part, src=src, dst=dst):
                at = pl.ds(pl.multiple_of(part * 64, 64), 64)
                dst[at] = src[at].astype(F32)

            each(src.shape[0] // 64, widen)
        writes[i].start()
    for copy in writes:
        copy.wait()


def outputs(arrays, sums, late):
    count = len(arrays)
    f32 = lambda *shape: jax.ShapeDtypeStruct(shape, F32)
    kept = [jax.ShapeDtypeStruct(a.shape, a.dtype) for a in arrays[:2]]
    return pl.pallas_call(
        functools.partial(outputs_kernel, count),
        out_shape=(
            *kept,
            *[f32(*a.shape) for a in arrays[2:]],
            f32(1, 256),
            f32(1, 256),
            f32(1, HEAD_SIZE),
            f32(1, HEAD_SIZE),
            f32(256, 4),
        ),
        in_specs=[ANY] * count + [VM] * 2,
        out_specs=(ANY,) * count + (VM,) * 5,
        scratch_shapes=[
            *[pltpu.VMEM(a.shape, a.dtype) for a in arrays],
            *[pltpu.VMEM(a.shape, F32) for a in arrays[2:]],
            DMA((count,)),
            DMA((count,)),
        ],
        compiler_params=pltpu.CompilerParams(vmem_limit_bytes=63 * 2**20),
        name="outputs",
    )(*arrays, sums, late)


def fast_local(
    inputs,
    cotangent,
    bucket_sizes,
    true_lengths,
    attention_gain,
    feedforward_gain,
    query_gain,
    key_gain,
    query_weight,
    key_matrix,
    value_matrix,
    headgate_weight,
    output_weight,
    gate_weight,
    up_weight,
    down_weight,
):
    batches, rows, width = inputs.shape
    n = lax.axis_size("seq") // 2
    seq, kv = lax.axis_index("seq"), lax.axis_index("kv")
    l, x = seq // 2, seq % 2
    scale = HEAD_SIZE ** (-0.5)
    span = 2 * rows
    gain_query = query_gain.astype(F32)
    gain_key = key_gain.astype(F32)

    own_small = jnp.concatenate(
        [
            headgate_weight.T,
            attention_gain[None],
            feedforward_gain[None],
            jnp.zeros((2, 256), BF),
            jnp.pad(jnp.stack([query_gain, key_gain]), ((0, 0), (0, 128))),
            jnp.zeros((6, 256), BF),
        ],
        axis=0,
    )
    x_split = inputs.reshape(batches, 4, 32, width)
    z_split = cotangent.reshape(batches, 4, 32, width)
    own_out, own_grad, dq, dk, dv, do, d_gate, d_up, d_down, sums, late, unused, unused = layer(
        n,
        x_split,
        z_split,
        query_weight,
        key_matrix,
        value_matrix,
        output_weight,
        gate_weight,
        up_weight,
        down_weight,
        own_small,
        bucket_sizes,
        true_lengths,
    )
    res, grad, dq, dk, dv, do, dg, du, dd, attention, feedforward, query, key, heads = outputs(
        [
            own_out.reshape(batches, rows, width),
            own_grad.reshape(batches, rows, width),
            dq,
            dk,
            dv,
            do,
            d_gate,
            d_up,
            d_down,
        ],
        sums,
        late,
    )
    return (
        res,
        grad,
        attention[0],
        feedforward[0],
        query[0],
        key[0],
        dq,
        dk,
        dv,
        heads,
        do,
        dg,
        du,
        dd,
    )


def solution(mesh):
    chosen = fast_local if dict(mesh.shape) == {"seq": 8, "kv": 4} else local
    in_specs = (
        P(None, "seq", None),
        P(None, "seq", None),
        P(),
        P(),
        P("seq"),
        P("seq"),
        P(),
        P(),
        P("seq", "kv"),
        P("seq", "kv"),
        P("seq", "kv"),
        P("seq", "kv"),
        P("kv", "seq"),
        P("seq", "kv"),
        P("seq", "kv"),
        P("kv", "seq"),
    )
    out_specs = (
        P(None, "seq", None),
        P(None, "seq", None),
        P("seq"),
        P("seq"),
        P(),
        P(),
        P("seq", "kv"),
        P("seq", "kv"),
        P("seq", "kv"),
        P("seq", "kv"),
        P("kv", "seq"),
        P("seq", "kv"),
        P("seq", "kv"),
        P("kv", "seq"),
    )
    return jax.shard_map(chosen, mesh=mesh, in_specs=in_specs, out_specs=out_specs, check_vma=False)
```
